32 devices in a mesh: bead: 8 (over z, x), slab: 2 (over y), grp: 2 (over core).
Axes of the slice: x: 2, y: 2, z: 4, core: 2. Of those that a mesh axis runs over, the one named last changes fastest.
Arguments:
- positions: float32 [64, 3, 16384], P('bead', None, ('slab', 'grp')), may hold values from -6 to 6
- momenta: float32 [64, 3, 16384], P('bead', None, ('slab', 'grp')), may hold values from -12 to 12
- force_old: float32 [64, 3, 16384], P('bead', None, ('slab', 'grp')), may hold values from -6 to 6
- noise: float32 [64, 3, 16384], P('bead', None, ('slab', 'grp')), may hold values from -6 to 6
- mass: float32 [16384], P(('slab', 'grp')), may hold values from 1 to 16
- pair_list: int32 [16384, 32], P(('slab', 'grp')), may hold values from 0 to 4351, as said below
- desc_w: bfloat16 [128, 1600], replicated, may hold values from -0.5 to 0.5
- hidden_one: bfloat16 [1600, 240], replicated, may hold values from -0.15625 to 0.15625
- hidden_two: bfloat16 [240, 240], replicated, may hold values from -0.375 to 0.375
- hidden_three: bfloat16 [240, 240], replicated, may hold values from -0.375 to 0.375
- out_w: bfloat16 [240, 3], replicated, may hold values from -0.375 to 0.375
Outputs:
- new_positions: float32 [64, 3, 16384], P('bead', None, ('slab', 'grp'))
- new_momenta: float32 [64, 3, 16384], P('bead', None, ('slab', 'grp'))
- force_new: float32 [64, 3, 16384], P('bead', None, ('slab', 'grp'))
The draws below stay inside these ranges and needn't reach their ends.
Inputs may be any that keep to these rules, and one draw needn't show every extreme that they name: `pair_list`: for the atom with index li in its slab, every entry lies in li .. li + 256; entries past a count of 16 to 32 per atom name the atom itself, li + 128.
All inputs are finite; a program needn't handle non-finite values.
Results may differ from the reference program's by a relative error of at most 0.00096.
Values sent between devices are 32-bit elements; how exact they have to be, the bound alone decides.
No kernel may reach another device: no remote copies, remote signals or barrier semaphores. Data moves between devices by JAX's collectives and lax.ppermute only.
A program may use at most 128 MiB of HBM per device.

```python
import jax
import jax.numpy as jnp
from jax import lax

BEADS = 64
NC = 8
A_SLAB = 4096
K = 32
EDGE = 128
DESC = 1600
HID = 240
ENV = 128
ATOMS = 16384


def draw_pair_list(key, part):
    first_key, second_key = jax.random.split(jax.random.fold_in(key, 11))
    local = jnp.arange(ATOMS, dtype=jnp.int32) % A_SLAB
    offsets = jax.random.randint(first_key, (ATOMS, K), 0, 2 * EDGE + 1).astype(jnp.int32)
    counts = jax.random.randint(second_key, (ATOMS, 1), K // 2, K + 1).astype(jnp.int32)
    slot = jnp.arange(K, dtype=jnp.int32)[None, :]
    offsets = jnp.where((local[:, None] == A_SLAB - 1) & (slot == 0), 2 * EDGE, offsets)
    offsets = jnp.where((local[:, None] == 0) & (slot == 0), 0, offsets)
    picked = local[:, None] + offsets
    itself = local[:, None] + EDGE
    return jnp.where(slot < counts, picked, itself).astype(jnp.int32)


def block_scale(rng, shape, cuts, smallest, high):
    level = 1.0
    for axis_at, parts in cuts:
        draws = jax.random.uniform(jax.random.fold_in(jax.random.fold_in(rng, 6), axis_at), (parts,), jnp.float32, smallest / len(cuts), high / len(cuts))
        level = level * jnp.repeat(jnp.exp(draws), shape[axis_at] // parts).reshape((-1,) + (1,) * (len(shape) - 1 - axis_at))
    return level


def bell_draw(rng, dims, deviation, most, shards=(), held_as=jnp.bfloat16):
    gain = block_scale(rng, dims, shards, -0.22, 0.18) if shards else 1.0
    result = jax.random.normal(rng, dims, jnp.float32) * deviation * gain
    return jnp.minimum(jnp.maximum(result, -most), most).astype(held_as)


def setup_inputs(seed: int = 0) -> dict:
    keys = jax.random.split(jax.random.key(seed), 12)
    return {
        "positions": bell_draw(keys[0], (BEADS, 3, ATOMS), 1.0, 6.0, ((0, 8), (2, 4)), jnp.float32),
        "momenta": bell_draw(keys[1], (BEADS, 3, ATOMS), 2.0, 12.0, ((0, 8), (2, 4)), jnp.float32),
        "force_old": bell_draw(keys[2], (BEADS, 3, ATOMS), 1.0, 6.0, ((0, 8), (2, 4)), jnp.float32),
        "noise": bell_draw(keys[3], (BEADS, 3, ATOMS), 1.0, 6.0, ((0, 8), (2, 4)), jnp.float32),
        "mass": jnp.clip(1.0 + 15.0 * jax.random.uniform(keys[4], (ATOMS,), jnp.float32) ** block_scale(keys[4], (ATOMS,), ((0, 4),), -0.2, 0.2), 1.0, 16.0),
        "pair_list": draw_pair_list(jax.random.fold_in(keys[11], 71), 0),
        "desc_w": bell_draw(keys[6], (ENV, DESC), ENV ** -0.5, 0.5),
        "hidden_one": bell_draw(keys[7], (DESC, HID), DESC ** -0.5, 0.15625),
        "hidden_two": bell_draw(keys[8], (HID, HID), HID ** -0.5, 0.375),
        "hidden_three": bell_draw(keys[9], (HID, HID), HID ** -0.5, 0.375),
        "out_w": bell_draw(keys[10], (HID, 3), HID ** -0.5, 0.375),
    }


TIME_STEP = 0.1
CYCLE_FREQ = 5.0
CENTROID_FRICTION = 1.0
PAIR_STRENGTH = 0.5

def cycle_tables(beads, contracted):
    index = jnp.arange(beads, dtype=jnp.float32)
    mode_int = jnp.arange(beads, dtype=jnp.int32)[None, :]
    angle = 2.0 * jnp.pi * index[:, None] * index[None, :] / beads
    half_mode = beads // 2
    root_one = 1.0 / jnp.sqrt(jnp.float32(beads))
    root_two = jnp.sqrt(2.0 / jnp.float32(beads))
    basis = jnp.where(mode_int == 0, root_one * jnp.ones_like(angle), jnp.where(mode_int < half_mode, root_two * jnp.cos(angle), jnp.where(mode_int == half_mode, root_one * jnp.cos(angle), root_two * jnp.sin(angle))))
    freq = 2.0 * CYCLE_FREQ * jnp.sin(jnp.pi * index / beads)
    cindex = jnp.arange(contracted, dtype=jnp.float32)
    spacing = index[None, :] / beads - cindex[:, None] / contracted
    kernel = jnp.ones_like(spacing)
    for order in range(1, contracted // 2):
        kernel = kernel + 2.0 * jnp.cos(2.0 * jnp.pi * order * spacing)
    kernel = kernel + jnp.cos(jnp.pi * contracted * spacing)
    return (basis, freq, kernel / beads)

def free_drift(modes_q, modes_p, freq, masses):
    step = 0.5 * TIME_STEP
    rate = freq[:, None, None]
    moving = rate > 0.0
    safe = jnp.where(moving, rate, 1.0)
    cosine = jnp.cos(safe * step)
    sine = jnp.sin(safe * step)
    new_q = jnp.where(moving, cosine * modes_q + sine / (masses * safe) * modes_p, modes_q + step * modes_p / masses)
    new_p = jnp.where(moving, cosine * modes_p - masses * safe * sine * modes_q, modes_p)
    return (new_q, new_p)

def thermostat(modes_p, noise, freq, masses):
    friction = jnp.where(freq > 0.0, 2.0 * freq, CENTROID_FRICTION)
    keep = jnp.exp(-friction * TIME_STEP)[:, None, None]
    return keep * modes_p + jnp.sqrt(masses) * jnp.sqrt(1.0 - keep * keep) * noise

def wide_dot(left, right):
    return jnp.dot(left.astype(jnp.float32), right.astype(jnp.float32), precision=lax.Precision.HIGHEST, preferred_element_type=jnp.float32)

def neural_force(extended, lists, start, weights):
    desc_w, hidden_one, hidden_two, hidden_three, out_w = weights
    count = lists.shape[0]
    near = extended[:, lists]
    own = lax.dynamic_slice_in_dim(extended, start + EDGE, count, 1)[:, :, None]
    apart = near - own
    closeness = 1.0 / (1.0 + lax.optimization_barrier(jnp.sum(apart * apart, axis=0)))
    env = jnp.concatenate([apart, closeness[None]], axis=0)
    env = jnp.transpose(env, (1, 2, 0)).reshape(count, -1).astype(jnp.bfloat16)
    layer = jnp.tanh(wide_dot(env, desc_w)).astype(jnp.bfloat16)
    for matrix in (hidden_one, hidden_two, hidden_three):
        layer = jnp.tanh(wide_dot(layer, matrix)).astype(jnp.bfloat16)
    return wide_dot(layer, out_w).T

def contracted_forces(extended, lists, start, weights):

    def one_bead(single):
        return neural_force(single, lists, start, weights)
    return lax.map(one_bead, extended)

def pair_force(extended_one, lists):
    near = extended_one[:, lists]
    own = extended_one[:, EDGE:EDGE + lists.shape[0]][:, :, None]
    apart = near - own
    closeness = 1.0 / (1.0 + lax.optimization_barrier(jnp.sum(apart * apart, axis=0, keepdims=True)))
    return PAIR_STRENGTH * lax.optimization_barrier(jnp.sum(apart * closeness, axis=2))

def slab_extend(field):
    lead = field.shape[0]
    slabs = jnp.transpose(field.reshape(lead, 3, -1, A_SLAB), (2, 0, 1, 3))
    before = jnp.roll(slabs, 1, axis=0)[..., A_SLAB - EDGE:]
    after = jnp.roll(slabs, -1, axis=0)[..., :EDGE]
    return jnp.concatenate([before, slabs, after], axis=3)

def reference(positions, momenta, force_old, noise, mass, pair_list, desc_w, hidden_one, hidden_two, hidden_three, out_w):
    best = lax.Precision.HIGHEST
    basis, freq, contract = cycle_tables(BEADS, NC)
    masses = mass[None, None, :]
    kicked = momenta + 0.5 * TIME_STEP * force_old
    modes_q = jnp.einsum('bk,bxa->kxa', basis, positions, precision=best)
    modes_p = jnp.einsum('bk,bxa->kxa', basis, kicked, precision=best)
    modes_q, modes_p = free_drift(modes_q, modes_p, freq, masses)
    modes_p = thermostat(modes_p, noise, freq, masses)
    modes_q, modes_p = free_drift(modes_q, modes_p, freq, masses)
    new_q = jnp.einsum('bk,kxa->bxa', basis, modes_q, precision=best)
    moved = jnp.einsum('bk,kxa->bxa', basis, modes_p, precision=best)
    contracted = jnp.einsum('cb,bxa->cxa', contract, new_q, precision=best)
    slab_lists = pair_list.reshape(-1, A_SLAB, K)
    weights = (desc_w, hidden_one, hidden_two, hidden_three, out_w)

    def slab_neural(pieces):
        extended, lists = pieces
        return contracted_forces(extended, lists, jnp.int32(0), weights)
    neural = lax.map(slab_neural, (slab_extend(contracted), slab_lists))
    neural = jnp.transpose(neural, (1, 2, 0, 3)).reshape(NC, 3, -1)
    spread = BEADS / NC * jnp.einsum('cb,cxa->bxa', contract, neural, precision=best)

    def slab_pair(pieces):
        extended, lists = pieces

        def one_bead(single):
            return pair_force(single, lists)
        return lax.map(one_bead, extended)
    pairs = lax.map(slab_pair, (slab_extend(new_q), slab_lists))
    pairs = jnp.transpose(pairs, (1, 2, 0, 3)).reshape(BEADS, 3, -1)
    force_new = pairs + spread
    return (new_q, moved + 0.5 * TIME_STEP * force_new, force_new)
```

```python
import math

import jax
import jax.numpy as jnp
import numpy as np
from jax import lax
from jax.experimental import pallas as pl
from jax.experimental.pallas import tpu as pltpu
from jax.sharding import PartitionSpec as P

BEADS = 64
NC = 8
EDGE = 128
LANES = 128

TIME_STEP = 0.1
CYCLE_FREQ = 5.0
CENTROID_FRICTION = 1.0
PAIR_STRENGTH = 0.5

BEST = lax.Precision.HIGHEST


def step_tables():
    b = np.arange(BEADS, dtype=np.float64)
    k = np.arange(BEADS)
    angle = 2.0 * np.pi * ((b[:, None] * b[None, :]) % BEADS) / BEADS
    half = BEADS // 2
    basis = np.where(
        k == 0,
        1.0 / math.sqrt(BEADS),
        np.where(
            k < half,
            math.sqrt(2.0 / BEADS) * np.cos(angle),
            np.where(
                k == half, np.cos(angle) / math.sqrt(BEADS), math.sqrt(2.0 / BEADS) * np.sin(angle)
            ),
        ),
    )
    freq = 2.0 * CYCLE_FREQ * np.sin(np.pi * b / BEADS)
    spacing = b[None, :] / BEADS - np.arange(NC, dtype=np.float64)[:, None] / NC
    kernel = np.ones_like(spacing)
    for order in range(1, NC // 2):
        kernel = kernel + 2.0 * np.cos(2.0 * np.pi * order * spacing)
    kernel = kernel + np.cos(np.pi * NC * spacing)
    contract = kernel / BEADS

    h = 0.5 * TIME_STEP
    safe = np.where(freq > 0.0, freq, 1.0)
    qq = np.where(freq > 0.0, np.cos(safe * h), 1.0)
    qp = np.where(freq > 0.0, np.sin(safe * h) / safe, h)
    pq = np.where(freq > 0.0, -safe * np.sin(safe * h), 0.0)
    pp = qq
    keep = np.exp(-np.where(freq > 0.0, 2.0 * freq, CENTROID_FRICTION) * TIME_STEP)
    kick = np.sqrt(1.0 - keep * keep)
    full_qq = qq * qq + qp * keep * pq
    full_qp = qq * qp + qp * keep * pp
    full_qn = qp * kick
    full_pq = pq * qq + pp * keep * pq
    full_pp = pq * qp + pp * keep * pp
    full_pn = pp * kick
    q_rows = np.concatenate(
        [(basis * full_qq) @ basis.T, (basis * full_qp) @ basis.T, basis * full_qn], axis=1
    )
    p_rows = np.concatenate(
        [(basis * full_pq) @ basis.T, (basis * full_pp) @ basis.T, basis * full_pn], axis=1
    )
    c_rows = contract @ q_rows
    step = np.concatenate([c_rows, q_rows, p_rows], axis=0)
    return step.astype(np.float32), contract.astype(np.float32)


def whole_vmem():
    return pl.BlockSpec(memory_space=pltpu.VMEM)


def params():
    return pltpu.CompilerParams(vmem_limit_bytes=48 * 1024 * 1024)


def pack(positions, momenta, force_old, noise, groups):
    _, beads, atoms = positions.shape
    rows = atoms // groups

    def kernel(q_ref, p_ref, f_ref, n_ref, out_ref):
        for d in range(groups):
            at = pl.ds(d * rows, rows)
            for x in range(3):
                out_ref[d, x] = q_ref[x, :, at]
                out_ref[d, 3 + x] = p_ref[x, :, at] + 0.5 * TIME_STEP * f_ref[x, :, at]
                out_ref[d, 6 + x] = n_ref[x, :, at]

    return pl.pallas_call(
        kernel,
        out_shape=jax.ShapeDtypeStruct((groups, 9, beads, rows), jnp.float32),
        in_specs=[whole_vmem()] * 4,
        out_specs=whole_vmem(),
        compiler_params=params(),
        name="pack",
    )(positions, momenta, force_old, noise)


def transform(received, masses, step):
    groups, _, beads, rows = received.shape

    def kernel(in_ref, mass_ref, step_ref, c_ref, q_ref, p_ref):
        mass = mass_ref[...]
        inverse = 1.0 / mass
        root = lax.rsqrt(mass)
        table = step_ref[...]
        for x in range(3):
            q = in_ref[:, x].reshape(BEADS, rows)
            p = in_ref[:, 3 + x].reshape(BEADS, rows) * inverse
            n = in_ref[:, 6 + x].reshape(BEADS, rows) * root
            fields = jnp.concatenate([q, p, n], axis=0)
            out = jnp.dot(table, fields, precision=BEST, preferred_element_type=jnp.float32)
            c_ref[x] = out[:NC]
            q_ref[:, x] = out[NC : NC + BEADS].reshape(groups, beads, rows)
            p_ref[:, x] = (out[NC + BEADS :] * mass).reshape(groups, beads, rows)

    return pl.pallas_call(
        kernel,
        out_shape=(
            jax.ShapeDtypeStruct((3, NC, rows), jnp.float32),
            jax.ShapeDtypeStruct((groups, 3, beads, rows), jnp.float32),
            jax.ShapeDtypeStruct((groups, 3, beads, rows), jnp.float32),
        ),
        in_specs=[whole_vmem()] * 3,
        out_specs=(whole_vmem(),) * 3,
        compiler_params=params(),
        name="transform",
    )(received, masses, step)


def banded(windows, lane, low, high):
    below, middle, above = [
        jnp.take_along_axis(w, lane, axis=1, mode="promise_in_bounds") for w in windows
    ]
    return jnp.where(low, below, jnp.where(high, above, middle))


def neural(contracted, lower, upper, lists, weights):
    _, _, rows = contracted.shape
    entries = lists.shape[0]
    w0, w1, w2, w3, wo = weights
    tiles = rows // LANES
    desc, env = w0.shape
    chunk = 256

    def kernel(c_ref, low_ref, up_ref, list_ref, w0_ref, w1_ref, w2_ref, w3_ref, wo_ref, out_ref, ext, envs):
        ext[:, :, :EDGE] = low_ref[...]
        ext[:, :, EDGE : EDGE + rows] = c_ref[...]
        ext[:, :, EDGE + rows :] = up_ref[...]

        @pl.loop(0, tiles)
        def _(t):
            base = pl.multiple_of(t * LANES, LANES)
            for e in range(0, entries, 8):
                place = list_ref[pl.ds(e, 8), pl.ds(base, LANES)]
                lane = place & (LANES - 1)
                low = place < LANES
                high = place >= 2 * LANES
                for c in range(NC):
                    apart = []
                    for x in range(3):
                        windows = [
                            jnp.broadcast_to(
                                ext[x, pl.ds(c, 1), pl.ds(base + v * LANES, LANES)], (8, LANES)
                            )
                            for v in range(3)
                        ]
                        apart.append(banded(windows, lane, low, high) - windows[1])
                    square = apart[0] * apart[0] + apart[1] * apart[1] + apart[2] * apart[2]
                    close = 1.0 / (1.0 + square)
                    for x, value in enumerate(apart + [close]):
                        envs[pl.ds(x * entries + e, 8), pl.ds(c * LANES, LANES)] = value
            cols = 256
            for c in range(0, NC * LANES, cols):
                inputs = envs[:, pl.ds(c, cols)].astype(jnp.bfloat16)
                total = None
                for f in range(0, desc, chunk):
                    size = min(chunk, desc - f)
                    first = jnp.dot(
                        w0_ref[pl.ds(f, size), :], inputs, preferred_element_type=jnp.float32
                    )
                    first = jnp.tanh(first).astype(jnp.bfloat16)
                    part = jnp.dot(
                        w1_ref[:, pl.ds(f, size)], first, preferred_element_type=jnp.float32
                    )
                    total = part if total is None else total + part
                layer = jnp.tanh(total).astype(jnp.bfloat16)
                for ref in (w2_ref, w3_ref):
                    layer = jnp.tanh(
                        jnp.dot(ref[...], layer, preferred_element_type=jnp.float32)
                    ).astype(jnp.bfloat16)
                out = jnp.dot(wo_ref[...], layer, preferred_element_type=jnp.float32)
                for part in range(cols // LANES):
                    for x in range(3):
                        out_ref[x, pl.ds(c // LANES + part, 1), pl.ds(base, LANES)] = out[
                            x : x + 1, part * LANES : (part + 1) * LANES
                        ]

    return pl.pallas_call(
        kernel,
        out_shape=jax.ShapeDtypeStruct((3, NC, rows), jnp.float32),
        in_specs=[whole_vmem()] * 9,
        out_specs=whole_vmem(),
        scratch_shapes=[
            pltpu.VMEM((3, NC, rows + 2 * EDGE), jnp.float32),
            pltpu.VMEM((env, NC * LANES), jnp.float32),
        ],
        compiler_params=params(),
        cost_estimate=pl.CostEstimate(
            flops=12_000_000_000, bytes_accessed=4_000_000, transcendentals=10_000_000
        ),
        name="neural",
    )(contracted, lower, upper, lists, w0, w1, w2, w3, wo)


def finish(block_q, lower, upper, lists, moved, forces, coefs):
    groups, _, beads, rows = block_q.shape
    atoms = groups * rows
    entries = lists.shape[0]
    tiles = rows // LANES

    def kernel(q_ref, low_ref, up_ref, list_ref, p_ref, n_ref, coef_ref, newq, newp, newf, ext):
        ext[:, :, :EDGE] = low_ref[...]
        ext[:, :, EDGE + atoms :] = up_ref[...]
        for g in range(groups):
            for x in range(3):
                value = q_ref[g, x]
                newq[x, :, pl.ds(g * rows, rows)] = value
                ext[x, :, pl.ds(EDGE + g * rows, rows)] = value

        @pl.loop(0, groups * tiles)
        def _(t):
            g = t // tiles
            inner = pl.multiple_of((t % tiles) * LANES, LANES)
            base = pl.multiple_of(t * LANES, LANES)
            windows = [
                [ext[x, :, pl.ds(base + v * LANES, LANES)] for v in range(3)] for x in range(3)
            ]
            sums = [jnp.zeros((beads, LANES), jnp.float32)] * 3
            for e in range(entries):
                place = jnp.broadcast_to(
                    list_ref[pl.ds(e, 1), pl.ds(base, LANES)], (beads, LANES)
                )
                lane = place & (LANES - 1)
                low = place < LANES
                high = place >= 2 * LANES
                apart = [banded(windows[x], lane, low, high) - windows[x][1] for x in range(3)]
                square = apart[0] * apart[0] + apart[1] * apart[1] + apart[2] * apart[2]
                close = 1.0 / (1.0 + square)
                sums = [s + a * close for s, a in zip(sums, apart)]
            for x in range(3):
                spread = jnp.zeros((beads, LANES), jnp.float32)
                for c in range(NC):
                    spread = spread + coef_ref[c] * n_ref[g, x, pl.ds(c, 1), pl.ds(inner, LANES)]
                force = PAIR_STRENGTH * sums[x] + spread
                newf[x, :, pl.ds(base, LANES)] = force
                newp[x, :, pl.ds(base, LANES)] = (
                    p_ref[g, x, :, pl.ds(inner, LANES)] + 0.5 * TIME_STEP * force
                )

    out = jax.ShapeDtypeStruct((3, beads, atoms), jnp.float32)
    return pl.pallas_call(
        kernel,
        out_shape=(out,) * 3,
        in_specs=[whole_vmem()] * 7,
        out_specs=(whole_vmem(),) * 3,
        scratch_shapes=[pltpu.VMEM((3, beads, atoms + 2 * EDGE), jnp.float32)],
        compiler_params=params(),
        name="finish",
    )(block_q, lower, upper, lists, moved, forces, coefs)


def body(
    positions,
    momenta,
    force_old,
    noise,
    mass,
    pair_list,
    desc_w,
    hidden_one,
    hidden_two,
    hidden_three,
    out_w,
):
    beads, _, atoms = positions.shape
    groups = lax.axis_size("bead")
    slabs = lax.axis_size(("slab", "grp"))
    rows = atoms // groups
    entries = pair_list.shape[1]
    place = lax.axis_index("bead")
    step, contract = step_tables()

    swap = lambda field: jnp.transpose(field, (1, 0, 2))
    sends = pack(swap(positions), swap(momenta), swap(force_old), swap(noise), groups)
    received = lax.all_to_all(sends, "bead", split_axis=0, concat_axis=0, tiled=True)

    first = (jnp.arange(atoms, dtype=jnp.int32) // LANES) * LANES
    lists = pair_list.T - first[None, :]
    block_lists = lax.dynamic_slice_in_dim(lists, place * rows, rows, 1)
    masses = lax.dynamic_slice_in_dim(mass, place * rows, rows, 0)[None, :]
    coefs = lax.dynamic_slice_in_dim(
        jnp.asarray(contract.T * np.float32(BEADS / NC)), place * beads, beads, 0
    )
    coefs = jnp.broadcast_to(coefs.T[:, :, None], (NC, beads, LANES))
    env_w = desc_w.T.reshape(-1, entries, 4).transpose(0, 2, 1).reshape(-1, entries * 4)
    weights = (env_w, hidden_one.T, hidden_two.T, hidden_three.T, out_w.T)

    contracted, block_q, block_p = transform(received, masses, jnp.asarray(step))

    ring = [(g * slabs + s, ((g + 1) % groups) * slabs + (s + (g + 1) // groups) % slabs)
            for g in range(groups) for s in range(slabs)]
    back = [(j, i) for i, j in ring]
    every = ("bead", "slab", "grp")
    lower = lax.ppermute(contracted[:, :, rows - EDGE :], every, ring)
    upper = lax.ppermute(contracted[:, :, :EDGE], every, back)

    new_q = lax.all_to_all(block_q, "bead", split_axis=0, concat_axis=0, tiled=True)
    moved = lax.all_to_all(block_p, "bead", split_axis=0, concat_axis=0, tiled=True)

    slab_ring = [(s, (s + 1) % slabs) for s in range(slabs)]
    slab_back = [(j, i) for i, j in slab_ring]
    q_lower = lax.ppermute(new_q[groups - 1, :, :, rows - EDGE :], ("slab", "grp"), slab_ring)
    q_upper = lax.ppermute(new_q[0, :, :, :EDGE], ("slab", "grp"), slab_back)

    forces = neural(contracted, lower, upper, block_lists, weights)
    forces = lax.all_gather(forces, "bead", axis=0, tiled=False)
    outs = finish(new_q, q_lower, q_upper, lists, moved, forces, coefs)
    return tuple(swap(out) for out in outs)


def solution(mesh):
    field = P("bead", None, ("slab", "grp"))
    placed = (field,) * 4 + (P(("slab", "grp")), P(("slab", "grp"), None)) + (P(),) * 5
    return jax.shard_map(
        body, mesh=mesh, in_specs=placed, out_specs=(field,) * 3, check_vma=False
    )
```

```python
import math

import jax
import jax.numpy as jnp
import numpy as np
from jax import lax
from jax.experimental import pallas as pl
from jax.experimental.pallas import tpu as pltpu
from jax.sharding import PartitionSpec as P

BEADS = 64
NC = 8
EDGE = 128
LANES = 128

TIME_STEP = 0.1
CYCLE_FREQ = 5.0
CENTROID_FRICTION = 1.0
PAIR_STRENGTH = 0.5

BEST = lax.Precision.HIGHEST


def step_tables():
    b = np.arange(BEADS, dtype=np.float64)
    k = np.arange(BEADS)
    angle = 2.0 * np.pi * ((b[:, None] * b[None, :]) % BEADS) / BEADS
    half = BEADS // 2
    basis = np.where(
        k == 0,
        1.0 / math.sqrt(BEADS),
        np.where(
            k < half,
            math.sqrt(2.0 / BEADS) * np.cos(angle),
            np.where(
                k == half, np.cos(angle) / math.sqrt(BEADS), math.sqrt(2.0 / BEADS) * np.sin(angle)
            ),
        ),
    )
    freq = 2.0 * CYCLE_FREQ * np.sin(np.pi * b / BEADS)
    spacing = b[None, :] / BEADS - np.arange(NC, dtype=np.float64)[:, None] / NC
    kernel = np.ones_like(spacing)
    for order in range(1, NC // 2):
        kernel = kernel + 2.0 * np.cos(2.0 * np.pi * order * spacing)
    kernel = kernel + np.cos(np.pi * NC * spacing)
    contract = kernel / BEADS

    h = 0.5 * TIME_STEP
    safe = np.where(freq > 0.0, freq, 1.0)
    qq = np.where(freq > 0.0, np.cos(safe * h), 1.0)
    qp = np.where(freq > 0.0, np.sin(safe * h) / safe, h)
    pq = np.where(freq > 0.0, -safe * np.sin(safe * h), 0.0)
    pp = qq
    keep = np.exp(-np.where(freq > 0.0, 2.0 * freq, CENTROID_FRICTION) * TIME_STEP)
    kick = np.sqrt(1.0 - keep * keep)
    full_qq = qq * qq + qp * keep * pq
    full_qp = qq * qp + qp * keep * pp
    full_qn = qp * kick
    full_pq = pq * qq + pp * keep * pq
    full_pp = pq * qp + pp * keep * pp
    full_pn = pp * kick
    q_rows = np.concatenate(
        [(basis * full_qq) @ basis.T, (basis * full_qp) @ basis.T, basis * full_qn], axis=1
    )
    p_rows = np.concatenate(
        [(basis * full_pq) @ basis.T, (basis * full_pp) @ basis.T, basis * full_pn], axis=1
    )
    c_rows = contract @ q_rows
    step = np.concatenate([c_rows, q_rows, p_rows], axis=0)
    return step.astype(np.float32), contract.astype(np.float32)


def whole_vmem():
    return pl.BlockSpec(memory_space=pltpu.VMEM)


def params(mebibytes=48):
    return pltpu.CompilerParams(vmem_limit_bytes=mebibytes * 1024 * 1024)


def pack(positions, momenta, force_old, noise, groups):
    _, beads, atoms = positions.shape
    rows = atoms // groups

    def kernel(q_ref, p_ref, f_ref, n_ref, out_ref, p_buf, f_buf, sems):
        loads = [
            pltpu.make_async_copy(p_ref, p_buf, sems.at[0]),
            pltpu.make_async_copy(f_ref, f_buf, sems.at[1]),
        ]
        for d in range(groups):
            at = pl.ds(d * rows, rows)
            for slot, (ref, first) in enumerate(((q_ref, 0), (n_ref, 6))):
                loads.append(
                    pltpu.make_async_copy(
                        ref.at[:, :, at], out_ref.at[d, pl.ds(first, 3)], sems.at[2 + 2 * d + slot]
                    )
                )
        for load in loads:
            load.start()
        loads[0].wait()
        loads[1].wait()
        for d in range(groups):
            at = pl.ds(d * rows, rows)
            for x in range(3):
                out_ref[d, 3 + x] = p_buf[x, :, at] + 0.5 * TIME_STEP * f_buf[x, :, at]
        for load in loads[2:]:
            load.wait()

    return pl.pallas_call(
        kernel,
        out_shape=jax.ShapeDtypeStruct((groups, 9, beads, rows), jnp.float32),
        in_specs=[pl.BlockSpec(memory_space=pltpu.HBM)] * 4,
        out_specs=whole_vmem(),
        scratch_shapes=[
            pltpu.VMEM((3, beads, atoms), jnp.float32),
            pltpu.VMEM((3, beads, atoms), jnp.float32),
            pltpu.SemaphoreType.DMA((2 + 2 * groups,)),
        ],
        compiler_params=params(60),
        name="pack",
    )(positions, momenta, force_old, noise)


def prepare(pair_list, mass, desc_w, hidden_one, place, rows):
    entries, atoms = pair_list.shape
    desc, env = desc_w.shape
    hid = hidden_one.shape[0]
    order = np.arange(env)
    order = (order % entries) * (env // entries) + order // entries
    permute = jnp.asarray(np.eye(env)[order], jnp.bfloat16)

    def kernel(place_ref, list_ref, mass_ref, w0_ref, w1_ref, order_ref, lists, own, masses, w0, w1):
        for t in range(atoms // LANES):
            at = pl.ds(t * LANES, LANES)
            lists[:, at] = list_ref[:, at] - t * LANES
        block = pl.ds(pl.multiple_of(place_ref[0] * rows, LANES), rows)
        own[...] = lists[:, block]
        masses[...] = mass_ref[:, block]
        w0[...] = lax.dot_general(
            order_ref[...],
            w0_ref[...],
            (((1,), (1,)), ((), ())),
            preferred_element_type=jnp.float32,
        ).astype(w0.dtype)
        w1[...] = w1_ref[...].astype(jnp.float32).T.astype(w1.dtype)

    return pl.pallas_call(
        kernel,
        out_shape=(
            jax.ShapeDtypeStruct((entries, atoms), jnp.int32),
            jax.ShapeDtypeStruct((entries, rows), jnp.int32),
            jax.ShapeDtypeStruct((1, rows), jnp.float32),
            jax.ShapeDtypeStruct((env, desc), jnp.bfloat16),
            jax.ShapeDtypeStruct((desc, hid), jnp.bfloat16),
        ),
        in_specs=[pl.BlockSpec(memory_space=pltpu.SMEM)] + [whole_vmem()] * 5,
        out_specs=(whole_vmem(),) * 5,
        compiler_params=params(),
        cost_estimate=pl.CostEstimate(
            flops=1_000_000_000, bytes_accessed=4_000_000, transcendentals=0
        ),
        name="prepare",
    )(place, pair_list, mass, desc_w, hidden_one, permute)


def transform(received, masses, step):
    groups, _, beads, rows = received.shape

    def kernel(in_ref, mass_ref, step_ref, c_ref, out_ref):
        mass = mass_ref[...]
        inverse = 1.0 / mass
        root = lax.rsqrt(mass)
        table = step_ref[...]
        for x in range(3):
            q = in_ref[:, x].reshape(BEADS, rows)
            p = in_ref[:, 3 + x].reshape(BEADS, rows) * inverse
            n = in_ref[:, 6 + x].reshape(BEADS, rows) * root
            fields = jnp.concatenate([q, p, n], axis=0)
            out = jnp.dot(table, fields, precision=BEST, preferred_element_type=jnp.float32)
            c_ref[x] = out[:NC]
            out_ref[:, x] = out[NC : NC + BEADS].reshape(groups, beads, rows)
            out_ref[:, 3 + x] = (out[NC + BEADS :] * mass).reshape(groups, beads, rows)

    return pl.pallas_call(
        kernel,
        out_shape=(
            jax.ShapeDtypeStruct((3, NC, rows), jnp.float32),
            jax.ShapeDtypeStruct((groups, 6, beads, rows), jnp.float32),
        ),
        in_specs=[whole_vmem()] * 3,
        out_specs=(whole_vmem(),) * 2,
        compiler_params=params(),
        name="transform",
    )(received, masses, step)


def banded(windows, lane, low, high):
    below, middle, above = [
        jnp.take_along_axis(w, lane, axis=1, mode="promise_in_bounds") for w in windows
    ]
    return jnp.where(low, below, jnp.where(high, above, middle))


def neural(contracted, lower, upper, lists, weights, spread, groups):
    _, _, rows = contracted.shape
    entries = lists.shape[0]
    beads = BEADS // groups
    w0, w1, w2, w3, wo = weights
    tiles = rows // LANES
    env, desc = w0.shape
    chunk = 256
    cols = 512

    def kernel(
        c_ref, low_ref, up_ref, list_ref, w0_ref, w1_ref, w2_ref, w3_ref, wo_ref, spread_ref,
        out_ref, ext, envs, inputs_ref, forces,
    ):
        ext[:, :, :EDGE] = low_ref[...]
        ext[:, :, EDGE : EDGE + rows] = c_ref[...]
        ext[:, :, EDGE + rows :] = up_ref[...]

        @pl.loop(0, tiles)
        def _(t):
            base = pl.multiple_of(t * LANES, LANES)
            for e in range(0, entries, 8):
                place = list_ref[pl.ds(e, 8), pl.ds(base, LANES)]
                lane = place & (LANES - 1)
                low = place < LANES
                high = place >= 2 * LANES
                for c in range(NC):
                    apart = []
                    for x in range(3):
                        windows = [
                            jnp.broadcast_to(
                                ext[x, pl.ds(c, 1), pl.ds(base + v * LANES, LANES)], (8, LANES)
                            )
                            for v in range(3)
                        ]
                        apart.append(banded(windows, lane, low, high) - windows[1])
                    square = apart[0] * apart[0] + apart[1] * apart[1] + apart[2] * apart[2]
                    close = 1.0 / (1.0 + square)
                    for x, value in enumerate(apart + [close]):
                        envs[pl.ds(x * entries + e, 8), pl.ds(c * LANES, LANES)] = value
            for c in range(NC):
                at = pl.ds(c * LANES, LANES)
                inputs_ref[at, :] = envs[:, at].T.astype(jnp.bfloat16)
            for c in range(0, NC * LANES, cols):
                inputs = inputs_ref[pl.ds(c, cols), :]
                total = None
                for f in range(0, desc, chunk):
                    size = min(chunk, desc - f)
                    first = jnp.dot(
                        inputs, w0_ref[:, pl.ds(f, size)], preferred_element_type=jnp.float32
                    )
                    first = jnp.tanh(first.astype(jnp.bfloat16))
                    part = jnp.dot(
                        first, w1_ref[pl.ds(f, size), :], preferred_element_type=jnp.float32
                    )
                    total = part if total is None else total + part
                layer = jnp.tanh(total).astype(jnp.bfloat16)
                for ref in (w2_ref, w3_ref):
                    layer = jnp.tanh(
                        jnp.dot(layer, ref[...], preferred_element_type=jnp.float32)
                    ).astype(jnp.bfloat16)
                out = lax.dot_general(
                    wo_ref[...],
                    layer,
                    (((1,), (1,)), ((), ())),
                    preferred_element_type=jnp.float32,
                )
                for part in range(cols // LANES):
                    for x in range(3):
                        forces[pl.ds(c // LANES + part, 1), pl.ds(x * LANES, LANES)] = out[
                            x : x + 1, part * LANES : (part + 1) * LANES
                        ]
            wide = jnp.dot(
                spread_ref[...], forces[...], precision=BEST, preferred_element_type=jnp.float32
            )
            for x in range(3):
                out_ref[:, x, :, pl.ds(base, LANES)] = wide[
                    :, x * LANES : (x + 1) * LANES
                ].reshape(groups, beads, LANES)

    return pl.pallas_call(
        kernel,
        out_shape=jax.ShapeDtypeStruct((groups, 3, beads, rows), jnp.float32),
        in_specs=[whole_vmem()] * 10,
        out_specs=whole_vmem(),
        scratch_shapes=[
            pltpu.VMEM((3, NC, rows + 2 * EDGE), jnp.float32),
            pltpu.VMEM((env, NC * LANES), jnp.float32),
            pltpu.VMEM((NC * LANES, env), jnp.bfloat16),
            pltpu.VMEM((NC, 3 * LANES), jnp.float32),
        ],
        compiler_params=params(),
        cost_estimate=pl.CostEstimate(
            flops=12_000_000_000, bytes_accessed=4_000_000, transcendentals=10_000_000
        ),
        name="neural",
    )(contracted, lower, upper, lists, w0, w1, w2, w3, wo, spread)


def pair_tile(windows, list_ref, base):
    beads = windows[0][0].shape[0]
    sums = [jnp.zeros((beads, LANES), jnp.float32)] * 3
    for e in range(list_ref.shape[0]):
        place = jnp.broadcast_to(list_ref[pl.ds(e, 1), pl.ds(base, LANES)], (beads, LANES))
        lane = place & (LANES - 1)
        low = place < LANES
        high = place >= 2 * LANES
        apart = [banded(windows[x], lane, low, high) - windows[x][1] for x in range(3)]
        square = apart[0] * apart[0] + apart[1] * apart[1] + apart[2] * apart[2]
        close = 1.0 / (1.0 + square)
        sums = [s + a * close for s, a in zip(sums, apart)]
    return [PAIR_STRENGTH * s for s in sums]


def pair_inner(fields, lists):
    groups, _, beads, rows = fields.shape
    atoms = groups * rows

    def kernel(in_ref, list_ref, newq, pair):
        for g in range(groups):
            for x in range(3):
                newq[x, :, pl.ds(g * rows, rows)] = in_ref[g, x]

        @pl.loop(1, atoms // LANES - 1)
        def _(t):
            base = pl.multiple_of(t * LANES, LANES)
            windows = [
                [newq[x, :, pl.ds(base + (v - 1) * LANES, LANES)] for v in range(3)]
                for x in range(3)
            ]
            for x, force in enumerate(pair_tile(windows, list_ref, base)):
                pair[x, :, pl.ds(base, LANES)] = force

    out = jax.ShapeDtypeStruct((3, beads, atoms), jnp.float32)
    return pl.pallas_call(
        kernel,
        out_shape=(out,) * 2,
        in_specs=[whole_vmem()] * 2,
        out_specs=(whole_vmem(),) * 2,
        compiler_params=params(),
        cost_estimate=pl.CostEstimate(
            flops=15_000_000_000, bytes_accessed=4_000_000, transcendentals=0
        ),
        name="pair_inner",
    )(fields, lists)


def finish(pair, new_q, lower, upper, lists, fields, spread):
    groups, _, beads, rows = fields.shape
    atoms = groups * rows

    def kernel(pair_ref, q_ref, low_ref, up_ref, list_ref, in_ref, spread_ref, newp, newf):
        def edge(base, windows):
            for x, force in enumerate(pair_tile(windows, list_ref, base)):
                newf[x, :, pl.ds(base, LANES)] = force

        newf[...] = pair_ref[...]
        inner = lambda x, at: q_ref[x, :, pl.ds(at, LANES)]
        last = atoms - LANES
        edge(0, [[low_ref[x], inner(x, 0), inner(x, LANES)] for x in range(3)])
        edge(last, [[inner(x, last - LANES), inner(x, last), up_ref[x]] for x in range(3)])
        for g in range(groups):
            at = pl.ds(g * rows, rows)
            for x in range(3):
                force = newf[x, :, at] + spread_ref[g, x]
                newf[x, :, at] = force
                newp[x, :, at] = in_ref[g, 3 + x] + 0.5 * TIME_STEP * force

    out = jax.ShapeDtypeStruct((3, beads, atoms), jnp.float32)
    return pl.pallas_call(
        kernel,
        out_shape=(out,) * 2,
        in_specs=[whole_vmem()] * 7,
        out_specs=(whole_vmem(),) * 2,
        compiler_params=params(),
        name="finish",
    )(pair, new_q, lower, upper, lists, fields, spread)


def body(
    positions,
    momenta,
    force_old,
    noise,
    mass,
    pair_list,
    desc_w,
    hidden_one,
    hidden_two,
    hidden_three,
    out_w,
):
    beads, _, atoms = positions.shape
    groups = lax.axis_size("bead")
    slabs = lax.axis_size(("slab", "grp"))
    rows = atoms // groups
    place = lax.axis_index("bead")
    step, contract = step_tables()

    swap = lambda field: jnp.transpose(field, (1, 0, 2))
    sends = pack(swap(positions), swap(momenta), swap(force_old), swap(noise), groups)
    received = lax.all_to_all(sends, "bead", split_axis=0, concat_axis=0, tiled=True)

    lists, block_lists, masses, env_w, w1 = prepare(
        pair_list.T, mass[None, :], desc_w.T, hidden_one.T, place.astype(jnp.int32)[None], rows
    )
    received, lists, block_lists, masses, env_w, w1 = lax.optimization_barrier(
        (received, lists, block_lists, masses, env_w, w1)
    )
    weights = (env_w, w1, hidden_two, hidden_three, out_w.T)

    contracted, returns = transform(received, masses, jnp.asarray(step))

    ring = [
        (g * slabs + s, ((g + 1) % groups) * slabs + (s + (g + 1) // groups) % slabs)
        for g in range(groups)
        for s in range(slabs)
    ]
    back = [(j, i) for i, j in ring]
    every = ("bead", "slab", "grp")
    lower = lax.ppermute(contracted[:, :, rows - EDGE :], every, ring)
    upper = lax.ppermute(contracted[:, :, :EDGE], every, back)
    fields = lax.all_to_all(returns, "bead", split_axis=0, concat_axis=0, tiled=True)

    spread = neural(
        contracted, lower, upper, block_lists, weights,
        jnp.asarray(contract.T * np.float32(BEADS / NC)), groups,
    )
    fields, spread = lax.optimization_barrier((fields, spread))
    spread = lax.all_to_all(spread, "bead", split_axis=0, concat_axis=0, tiled=True)

    slab_ring = [(s, (s + 1) % slabs) for s in range(slabs)]
    slab_back = [(j, i) for i, j in slab_ring]
    q_lower = lax.ppermute(fields[groups - 1, :3, :, rows - EDGE :], ("slab", "grp"), slab_ring)
    q_upper = lax.ppermute(fields[0, :3, :, :EDGE], ("slab", "grp"), slab_back)

    new_q, pair = pair_inner(fields, lists)
    new_p, force = finish(pair, new_q, q_lower, q_upper, lists, fields, spread)
    return tuple(swap(out) for out in (new_q, new_p, force))


def solution(mesh):
    field = P("bead", None, ("slab", "grp"))
    placed = (field,) * 4 + (P(("slab", "grp")), P(("slab", "grp"), None)) + (P(),) * 5
    return jax.shard_map(
        body, mesh=mesh, in_specs=placed, out_specs=(field,) * 3, check_vma=False
    )
```

```python
import math

import jax
import jax.numpy as jnp
import numpy as np
from jax import lax
from jax.experimental import pallas as pl
from jax.experimental.pallas import tpu as pltpu
from jax.sharding import PartitionSpec as P

BEADS = 64
NC = 8
EDGE = 128
LANES = 128

TIME_STEP = 0.1
CYCLE_FREQ = 5.0
CENTROID_FRICTION = 1.0
PAIR_STRENGTH = 0.5

BEST = lax.Precision.HIGHEST


def step_tables():
    b = np.arange(BEADS, dtype=np.float64)
    k = np.arange(BEADS)
    angle = 2.0 * np.pi * ((b[:, None] * b[None, :]) % BEADS) / BEADS
    half = BEADS // 2
    basis = np.where(
        k == 0,
        1.0 / math.sqrt(BEADS),
        np.where(
            k < half,
            math.sqrt(2.0 / BEADS) * np.cos(angle),
            np.where(
                k == half, np.cos(angle) / math.sqrt(BEADS), math.sqrt(2.0 / BEADS) * np.sin(angle)
            ),
        ),
    )
    freq = 2.0 * CYCLE_FREQ * np.sin(np.pi * b / BEADS)
    spacing = b[None, :] / BEADS - np.arange(NC, dtype=np.float64)[:, None] / NC
    kernel = np.ones_like(spacing)
    for order in range(1, NC // 2):
        kernel = kernel + 2.0 * np.cos(2.0 * np.pi * order * spacing)
    kernel = kernel + np.cos(np.pi * NC * spacing)
    contract = kernel / BEADS

    h = 0.5 * TIME_STEP
    safe = np.where(freq > 0.0, freq, 1.0)
    qq = np.where(freq > 0.0, np.cos(safe * h), 1.0)
    qp = np.where(freq > 0.0, np.sin(safe * h) / safe, h)
    pq = np.where(freq > 0.0, -safe * np.sin(safe * h), 0.0)
    pp = qq
    keep = np.exp(-np.where(freq > 0.0, 2.0 * freq, CENTROID_FRICTION) * TIME_STEP)
    kick = np.sqrt(1.0 - keep * keep)
    full_qq = qq * qq + qp * keep * pq
    full_qp = qq * qp + qp * keep * pp
    full_qn = qp * kick
    full_pq = pq * qq + pp * keep * pq
    full_pp = pq * qp + pp * keep * pp
    full_pn = pp * kick
    q_rows = np.concatenate(
        [(basis * full_qq) @ basis.T, (basis * full_qp) @ basis.T, basis * full_qn], axis=1
    )
    p_rows = np.concatenate(
        [(basis * full_pq) @ basis.T, (basis * full_pp) @ basis.T, basis * full_pn], axis=1
    )
    c_rows = contract @ q_rows
    step = np.concatenate([c_rows, q_rows, p_rows], axis=0)
    return step.astype(np.float32), contract.astype(np.float32)


def whole_vmem():
    return pl.BlockSpec(memory_space=pltpu.VMEM)


def params(mebibytes=48):
    return pltpu.CompilerParams(vmem_limit_bytes=mebibytes * 1024 * 1024)


def pack(positions, momenta, force_old, noise, groups):
    _, beads, atoms = positions.shape
    rows = atoms // groups

    def kernel(q_ref, p_ref, f_ref, n_ref, out_ref, p_buf, f_buf, sems):
        loads = [
            pltpu.make_async_copy(p_ref, p_buf, sems.at[0]),
            pltpu.make_async_copy(f_ref, f_buf, sems.at[1]),
        ]
        for d in range(groups):
            at = pl.ds(d * rows, rows)
            for slot, (ref, first) in enumerate(((q_ref, 0), (n_ref, 6))):
                loads.append(
                    pltpu.make_async_copy(
                        ref.at[:, :, at], out_ref.at[d, pl.ds(first, 3)], sems.at[2 + 2 * d + slot]
                    )
                )
        for load in loads:
            load.start()
        loads[0].wait()
        loads[1].wait()
        for d in range(groups):
            at = pl.ds(d * rows, rows)
            for x in range(3):
                out_ref[d, 3 + x] = p_buf[x, :, at] + 0.5 * TIME_STEP * f_buf[x, :, at]
        for load in loads[2:]:
            load.wait()

    return pl.pallas_call(
        kernel,
        out_shape=jax.ShapeDtypeStruct((groups, 9, beads, rows), jnp.float32),
        in_specs=[pl.BlockSpec(memory_space=pltpu.HBM)] * 4,
        out_specs=whole_vmem(),
        scratch_shapes=[
            pltpu.VMEM((3, beads, atoms), jnp.float32),
            pltpu.VMEM((3, beads, atoms), jnp.float32),
            pltpu.SemaphoreType.DMA((2 + 2 * groups,)),
        ],
        compiler_params=params(60),
        name="pack",
    )(positions, momenta, force_old, noise)


def prepare(pair_list, mass, desc_w, hidden_one, place, rows):
    entries, atoms = pair_list.shape
    desc, env = desc_w.shape
    hid = hidden_one.shape[0]
    order = np.arange(env)
    order = (order % entries) * (env // entries) + order // entries
    permute = jnp.asarray(np.eye(env)[order], jnp.bfloat16)

    def kernel(place_ref, list_ref, mass_ref, w0_ref, w1_ref, order_ref, lists, own, masses, w0, w1):
        for t in range(atoms // LANES):
            at = pl.ds(t * LANES, LANES)
            lists[:, at] = list_ref[:, at] - t * LANES
        block = pl.ds(pl.multiple_of(place_ref[0] * rows, LANES), rows)
        own[...] = lists[:, block]
        masses[...] = mass_ref[:, block]
        w0[...] = lax.dot_general(
            order_ref[...],
            w0_ref[...],
            (((1,), (1,)), ((), ())),
            preferred_element_type=jnp.float32,
        ).astype(w0.dtype)
        w1[...] = w1_ref[...].astype(jnp.float32).T.astype(w1.dtype)

    return pl.pallas_call(
        kernel,
        out_shape=(
            jax.ShapeDtypeStruct((entries, atoms), jnp.int32),
            jax.ShapeDtypeStruct((entries, rows), jnp.int32),
            jax.ShapeDtypeStruct((1, rows), jnp.float32),
            jax.ShapeDtypeStruct((env, desc), jnp.bfloat16),
            jax.ShapeDtypeStruct((desc, hid), jnp.bfloat16),
        ),
        in_specs=[pl.BlockSpec(memory_space=pltpu.SMEM)] + [whole_vmem()] * 5,
        out_specs=(whole_vmem(),) * 5,
        compiler_params=params(),
        cost_estimate=pl.CostEstimate(
            flops=1_000_000_000, bytes_accessed=4_000_000, transcendentals=0
        ),
        name="prepare",
    )(place, pair_list, mass, desc_w, hidden_one, permute)


def transform(received, masses, step):
    groups, _, beads, rows = received.shape

    def kernel(in_ref, mass_ref, step_ref, c_ref, out_ref):
        mass = mass_ref[...]
        inverse = 1.0 / mass
        root = lax.rsqrt(mass)
        table = step_ref[...]
        for x in range(3):
            q = in_ref[:, x].reshape(BEADS, rows)
            p = in_ref[:, 3 + x].reshape(BEADS, rows) * inverse
            n = in_ref[:, 6 + x].reshape(BEADS, rows) * root
            fields = jnp.concatenate([q, p, n], axis=0)
            out = jnp.dot(table, fields, precision=BEST, preferred_element_type=jnp.float32)
            c_ref[x] = out[:NC]
            out_ref[:, x] = out[NC : NC + BEADS].reshape(groups, beads, rows)
            out_ref[:, 3 + x] = (out[NC + BEADS :] * mass).reshape(groups, beads, rows)

    return pl.pallas_call(
        kernel,
        out_shape=(
            jax.ShapeDtypeStruct((3, NC, rows), jnp.float32),
            jax.ShapeDtypeStruct((groups, 6, beads, rows), jnp.float32),
        ),
        in_specs=[whole_vmem()] * 3,
        out_specs=(whole_vmem(),) * 2,
        compiler_params=params(),
        name="transform",
    )(received, masses, step)


def banded(windows, lane, low, high):
    below, middle, above = [
        jnp.take_along_axis(w, lane, axis=1, mode="promise_in_bounds") for w in windows
    ]
    return jnp.where(low, below, jnp.where(high, above, middle))


def env_tile(windows, list_ref, base, envs, inputs):
    entries = list_ref.shape[0]
    for e in range(0, entries, 8):
        place = list_ref[pl.ds(e, 8), pl.ds(base, LANES)]
        lane = place & (LANES - 1)
        low = place < LANES
        high = place >= 2 * LANES
        for c in range(NC):
            apart = []
            for x in range(3):
                tiles = windows(c, x)
                apart.append(banded(tiles, lane, low, high) - tiles[1])
            square = apart[0] * apart[0] + apart[1] * apart[1] + apart[2] * apart[2]
            close = 1.0 / (1.0 + square)
            for x, value in enumerate(apart + [close]):
                envs[pl.ds(x * entries + e, 8), pl.ds(c * LANES, LANES)] = value
    for c in range(NC):
        at = pl.ds(c * LANES, LANES)
        inputs[at, :] = envs[:, at].T.astype(jnp.bfloat16)


def network(inputs_ref, weights, forces, cols=256, chunk=256):
    w0_ref, w1_ref, w2_ref, w3_ref, wo_ref = weights
    desc = w0_ref.shape[1]
    for c in range(0, NC * LANES, cols):
        inputs = inputs_ref[pl.ds(c, cols), :]
        total = None
        for f in range(0, desc, chunk):
            size = min(chunk, desc - f)
            first = jnp.dot(inputs, w0_ref[:, pl.ds(f, size)], preferred_element_type=jnp.float32)
            first = jnp.tanh(first.astype(jnp.bfloat16))
            part = jnp.dot(first, w1_ref[pl.ds(f, size), :], preferred_element_type=jnp.float32)
            total = part if total is None else total + part
        layer = jnp.tanh(total).astype(jnp.bfloat16)
        for ref in (w2_ref, w3_ref):
            layer = jnp.tanh(
                jnp.dot(layer, ref[...], preferred_element_type=jnp.float32)
            ).astype(jnp.bfloat16)
        out = lax.dot_general(
            wo_ref[...], layer, (((1,), (1,)), ((), ())), preferred_element_type=jnp.float32
        )
        for part in range(cols // LANES):
            for x in range(3):
                forces[pl.ds(c // LANES + part, 1), pl.ds(x * LANES, LANES)] = out[
                    x : x + 1, part * LANES : (part + 1) * LANES
                ]


def neural_scratch(env):
    return [
        pltpu.VMEM((2, env, NC * LANES), jnp.float32),
        pltpu.VMEM((2, NC * LANES, env), jnp.bfloat16),
    ]


def neural_cost(tiles):
    return pl.CostEstimate(
        flops=3_000_000_000 * tiles, bytes_accessed=2_000_000, transcendentals=0
    )


def neural_inner(contracted, lists, weights):
    tiles = contracted.shape[2] // LANES
    inner = tiles - 2

    def kernel(c_ref, list_ref, w0, w1, w2, w3, wo, out_ref, envs, inputs):
        def windows_of(t):
            return lambda c, x: [
                jnp.broadcast_to(
                    c_ref[x, pl.ds(c, 1), pl.ds((t + v) * LANES, LANES)], (8, LANES)
                )
                for v in (-1, 0, 1)
            ]

        for t in range(1, tiles - 1):
            slot = t % 2
            env_tile(windows_of(t), list_ref, t * LANES, envs.at[slot], inputs.at[slot])
            network(inputs.at[slot], (w0, w1, w2, w3, wo), out_ref.at[t - 1])

    return pl.pallas_call(
        kernel,
        out_shape=jax.ShapeDtypeStruct((inner, NC, 3 * LANES), jnp.float32),
        in_specs=[whole_vmem()] * 7,
        out_specs=whole_vmem(),
        scratch_shapes=neural_scratch(weights[0].shape[0]),
        compiler_params=params(),
        cost_estimate=neural_cost(inner),
        name="neural_inner",
    )(contracted, lists, *weights)


def neural_edge(contracted, lower, upper, lists, weights, inner, spread, groups):
    _, _, rows = contracted.shape
    beads = BEADS // groups
    tiles = rows // LANES

    def kernel(
        c_ref, low_ref, up_ref, list_ref, w0, w1, w2, w3, wo, spread_ref, inner_ref,
        out_ref, forces, envs, inputs,
    ):
        def tile(x, c, t):
            if t < 0:
                ref, at = low_ref, 0
            elif t >= tiles:
                ref, at = up_ref, 0
            else:
                ref, at = c_ref, t * LANES
            return jnp.broadcast_to(ref[x, pl.ds(c, 1), pl.ds(at, LANES)], (8, LANES))

        for slot, t in enumerate((0, tiles - 1)):
            windows = lambda c, x: [tile(x, c, t + v) for v in (-1, 0, 1)]
            env_tile(windows, list_ref, t * LANES, envs.at[slot], inputs.at[slot])
            network(inputs.at[slot], (w0, w1, w2, w3, wo), forces.at[slot])
        for t in range(tiles):
            if t in (0, tiles - 1):
                own = forces[min(t, 1)]
            else:
                own = inner_ref[t - 1]
            wide = jnp.dot(
                spread_ref[...], own, precision=BEST, preferred_element_type=jnp.float32
            )
            for x in range(3):
                out_ref[:, x, :, pl.ds(t * LANES, LANES)] = wide[
                    :, x * LANES : (x + 1) * LANES
                ].reshape(groups, beads, LANES)

    return pl.pallas_call(
        kernel,
        out_shape=jax.ShapeDtypeStruct((groups, 3, beads, rows), jnp.float32),
        in_specs=[whole_vmem()] * 11,
        out_specs=whole_vmem(),
        scratch_shapes=[pltpu.VMEM((2, NC, 3 * LANES), jnp.float32)]
        + neural_scratch(weights[0].shape[0]),
        compiler_params=params(),
        cost_estimate=neural_cost(2),
        name="neural_edge",
    )(contracted, lower, upper, lists, *weights, spread, inner)


def pair_tile(windows, list_ref, base):
    beads = windows[0][0].shape[0]
    sums = [jnp.zeros((beads, LANES), jnp.float32)] * 3
    for e in range(list_ref.shape[0]):
        place = jnp.broadcast_to(list_ref[pl.ds(e, 1), pl.ds(base, LANES)], (beads, LANES))
        lane = place & (LANES - 1)
        low = place < LANES
        high = place >= 2 * LANES
        apart = [banded(windows[x], lane, low, high) - windows[x][1] for x in range(3)]
        square = apart[0] * apart[0] + apart[1] * apart[1] + apart[2] * apart[2]
        close = 1.0 / (1.0 + square)
        sums = [s + a * close for s, a in zip(sums, apart)]
    return [PAIR_STRENGTH * s for s in sums]


def pair_inner(fields, lists):
    groups, _, beads, rows = fields.shape
    atoms = groups * rows
    entries = lists.shape[0]
    top = float(2**20 - 1)

    def unpack(one, two):
        third = ((one << 21) | ((two & 1023) << 11)) >> 11
        return one >> 11, two >> 11, third

    def kernel(in_ref, list_ref, newq, pair, words):
        largest = jnp.zeros((beads, rows), jnp.float32)
        for g in range(groups):
            for x in range(3):
                value = in_ref[g, x]
                newq[x, :, pl.ds(g * rows, rows)] = value
                largest = jnp.maximum(largest, jnp.abs(value))
        limit = jnp.maximum(jnp.max(largest, keepdims=True), 1e-30)
        to_fixed = top / limit
        unit = limit / top
        for g in range(groups):
            at = pl.ds(g * rows, rows)
            one, two, three = [
                jnp.floor(in_ref[g, x] * to_fixed + 0.5).astype(jnp.int32) for x in range(3)
            ]
            words[0, :, at] = (one << 11) | ((three >> 10) & 2047)
            words[1, :, at] = (two << 11) | (three & 1023)
        unit_row = jnp.broadcast_to(unit, (beads, LANES))
        unit_square = unit_row * unit_row

        @pl.loop(1, atoms // LANES - 1)
        def _(t):
            base = pl.multiple_of(t * LANES, LANES)
            windows = [
                [words[w, :, pl.ds(base + (v - 1) * LANES, LANES)] for v in range(3)]
                for w in range(2)
            ]
            own = unpack(windows[0][1], windows[1][1])
            sums = [jnp.zeros((beads, LANES), jnp.float32)] * 3
            for e in range(entries):
                place = jnp.broadcast_to(
                    list_ref[pl.ds(e, 1), pl.ds(base, LANES)], (beads, LANES)
                )
                lane = place & (LANES - 1)
                low = place < LANES
                high = place >= 2 * LANES
                near = unpack(*[banded(windows[w], lane, low, high) for w in range(2)])
                apart = [(n - o).astype(jnp.float32) for n, o in zip(near, own)]
                square = apart[0] * apart[0] + apart[1] * apart[1] + apart[2] * apart[2]
                close = 1.0 / (1.0 + square * unit_square)
                sums = [s + a * close for s, a in zip(sums, apart)]
            for x in range(3):
                pair[x, :, pl.ds(base, LANES)] = (PAIR_STRENGTH * unit_row) * sums[x]

    out = jax.ShapeDtypeStruct((3, beads, atoms), jnp.float32)
    return pl.pallas_call(
        kernel,
        out_shape=(out,) * 2,
        in_specs=[whole_vmem()] * 2,
        out_specs=(whole_vmem(),) * 2,
        scratch_shapes=[pltpu.VMEM((2, beads, atoms), jnp.int32)],
        compiler_params=params(),
        cost_estimate=pl.CostEstimate(
            flops=15_000_000_000, bytes_accessed=4_000_000, transcendentals=0
        ),
        name="pair_inner",
    )(fields, lists)


def finish(pair, lower, upper, lists, fields, spread):
    groups, _, beads, rows = fields.shape
    atoms = groups * rows

    def kernel(pair_ref, low_ref, up_ref, list_ref, in_ref, spread_ref, newp, newf):
        def edge(base, windows):
            for x, force in enumerate(pair_tile(windows, list_ref, base)):
                newf[x, :, pl.ds(base, LANES)] = force

        newf[...] = pair_ref[...]
        first = lambda x, t: in_ref[0, x, :, pl.ds(t * LANES, LANES)]
        last = lambda x, t: in_ref[groups - 1, x, :, pl.ds(rows - t * LANES, LANES)]
        edge(0, [[low_ref[x], first(x, 0), first(x, 1)] for x in range(3)])
        edge(atoms - LANES, [[last(x, 2), last(x, 1), up_ref[x]] for x in range(3)])
        for g in range(groups):
            at = pl.ds(g * rows, rows)
            for x in range(3):
                force = newf[x, :, at] + spread_ref[g, x]
                newf[x, :, at] = force
                newp[x, :, at] = in_ref[g, 3 + x] + 0.5 * TIME_STEP * force

    out = jax.ShapeDtypeStruct((3, beads, atoms), jnp.float32)
    return pl.pallas_call(
        kernel,
        out_shape=(out,) * 2,
        in_specs=[whole_vmem()] * 6,
        out_specs=(whole_vmem(),) * 2,
        compiler_params=params(),
        name="finish",
    )(pair, lower, upper, lists, fields, spread)


def body(
    positions,
    momenta,
    force_old,
    noise,
    mass,
    pair_list,
    desc_w,
    hidden_one,
    hidden_two,
    hidden_three,
    out_w,
):
    beads, _, atoms = positions.shape
    groups = lax.axis_size("bead")
    slabs = lax.axis_size(("slab", "grp"))
    rows = atoms // groups
    place = lax.axis_index("bead")
    step, contract = step_tables()

    swap = lambda field: jnp.transpose(field, (1, 0, 2))
    sends = pack(swap(positions), swap(momenta), swap(force_old), swap(noise), groups)
    received = lax.all_to_all(sends, "bead", split_axis=0, concat_axis=0, tiled=True)

    lists, block_lists, masses, env_w, w1 = prepare(
        pair_list.T, mass[None, :], desc_w.T, hidden_one.T, place.astype(jnp.int32)[None], rows
    )
    received, lists, block_lists, masses, env_w, w1 = lax.optimization_barrier(
        (received, lists, block_lists, masses, env_w, w1)
    )
    weights = (env_w, w1, hidden_two, hidden_three, out_w.T)

    contracted, returns = transform(received, masses, jnp.asarray(step))

    ring = [
        (g * slabs + s, ((g + 1) % groups) * slabs + (s + (g + 1) // groups) % slabs)
        for g in range(groups)
        for s in range(slabs)
    ]
    back = [(j, i) for i, j in ring]
    every = ("bead", "slab", "grp")
    lower = lax.ppermute(contracted[:, :, rows - EDGE :], every, ring)
    upper = lax.ppermute(contracted[:, :, :EDGE], every, back)
    fields = lax.all_to_all(returns, "bead", split_axis=0, concat_axis=0, tiled=True)

    if rows > 2 * LANES:
        inner = neural_inner(contracted, block_lists, weights)
    else:
        inner = jnp.zeros((1, NC, 3 * LANES), jnp.float32)
    inner, lower, upper = lax.optimization_barrier((inner, lower, upper))
    spread = neural_edge(
        contracted, lower, upper, block_lists, weights, inner,
        jnp.asarray(contract.T * np.float32(BEADS / NC)), groups,
    )
    fields, spread = lax.optimization_barrier((fields, spread))
    spread = lax.all_to_all(spread, "bead", split_axis=0, concat_axis=0, tiled=True)

    slab_ring = [(s, (s + 1) % slabs) for s in range(slabs)]
    slab_back = [(j, i) for i, j in slab_ring]
    q_lower = lax.ppermute(fields[groups - 1, :3, :, rows - EDGE :], ("slab", "grp"), slab_ring)
    q_upper = lax.ppermute(fields[0, :3, :, :EDGE], ("slab", "grp"), slab_back)

    new_q, pair = pair_inner(fields, lists)
    new_p, force = finish(pair, q_lower, q_upper, lists, fields, spread)
    return tuple(swap(out) for out in (new_q, new_p, force))


def solution(mesh):
    field = P("bead", None, ("slab", "grp"))
    placed = (field,) * 4 + (P(("slab", "grp")), P(("slab", "grp"), None)) + (P(),) * 5
    return jax.shard_map(
        body, mesh=mesh, in_specs=placed, out_specs=(field,) * 3, check_vma=False
    )
```

```python
import math

import jax
import jax.numpy as jnp
import numpy as np
from jax import lax
from jax.experimental import pallas as pl
from jax.experimental.pallas import tpu as pltpu
from jax.sharding import PartitionSpec as P

BEADS = 64
NC = 8
EDGE = 128
LANES = 128

TIME_STEP = 0.1
CYCLE_FREQ = 5.0
CENTROID_FRICTION = 1.0
PAIR_STRENGTH = 0.5

BEST = lax.Precision.HIGHEST


def step_tables():
    b = np.arange(BEADS, dtype=np.float64)
    k = np.arange(BEADS)
    angle = 2.0 * np.pi * ((b[:, None] * b[None, :]) % BEADS) / BEADS
    half = BEADS // 2
    basis = np.where(
        k == 0,
        1.0 / math.sqrt(BEADS),
        np.where(
            k < half,
            math.sqrt(2.0 / BEADS) * np.cos(angle),
            np.where(
                k == half, np.cos(angle) / math.sqrt(BEADS), math.sqrt(2.0 / BEADS) * np.sin(angle)
            ),
        ),
    )
    freq = 2.0 * CYCLE_FREQ * np.sin(np.pi * b / BEADS)
    spacing = b[None, :] / BEADS - np.arange(NC, dtype=np.float64)[:, None] / NC
    kernel = np.ones_like(spacing)
    for order in range(1, NC // 2):
        kernel = kernel + 2.0 * np.cos(2.0 * np.pi * order * spacing)
    kernel = kernel + np.cos(np.pi * NC * spacing)
    contract = kernel / BEADS

    h = 0.5 * TIME_STEP
    safe = np.where(freq > 0.0, freq, 1.0)
    qq = np.where(freq > 0.0, np.cos(safe * h), 1.0)
    qp = np.where(freq > 0.0, np.sin(safe * h) / safe, h)
    pq = np.where(freq > 0.0, -safe * np.sin(safe * h), 0.0)
    pp = qq
    keep = np.exp(-np.where(freq > 0.0, 2.0 * freq, CENTROID_FRICTION) * TIME_STEP)
    kick = np.sqrt(1.0 - keep * keep)
    full_qq = qq * qq + qp * keep * pq
    full_qp = qq * qp + qp * keep * pp
    full_qn = qp * kick
    full_pq = pq * qq + pp * keep * pq
    full_pp = pq * qp + pp * keep * pp
    full_pn = pp * kick
    q_rows = np.concatenate(
        [(basis * full_qq) @ basis.T, (basis * full_qp) @ basis.T, basis * full_qn], axis=1
    )
    p_rows = np.concatenate(
        [(basis * full_pq) @ basis.T, (basis * full_pp) @ basis.T, basis * full_pn], axis=1
    )
    c_rows = contract @ q_rows
    step = np.concatenate([c_rows, q_rows, p_rows], axis=0)
    return step.astype(np.float32), contract.astype(np.float32)


def whole_vmem():
    return pl.BlockSpec(memory_space=pltpu.VMEM)


def params(mebibytes=48):
    return pltpu.CompilerParams(vmem_limit_bytes=mebibytes * 1024 * 1024)


def smem():
    return pl.BlockSpec(memory_space=pltpu.SMEM)


def block_of(place_ref, r, rows):
    return pl.ds(pl.multiple_of((place_ref[0] ^ r) * rows, LANES), rows)


def exchange(blocks, axis):
    count = len(blocks)
    return [blocks[0]] + [
        lax.ppermute(blocks[r], axis, [(i, i ^ r) for i in range(count)]) for r in range(1, count)
    ]


def pack(place, positions, momenta, force_old, noise, groups):
    _, beads, atoms = positions.shape
    rows = atoms // groups

    def kernel(place_ref, q_ref, p_ref, f_ref, n_ref, *rest):
        outs, (p_buf, f_buf, sems) = rest[:groups], rest[groups:]
        loads = [
            pltpu.make_async_copy(p_ref, p_buf, sems.at[0]),
            pltpu.make_async_copy(f_ref, f_buf, sems.at[1]),
        ]
        for r in range(groups):
            at = block_of(place_ref, r, rows)
            for slot, (ref, first) in enumerate(((q_ref, 0), (n_ref, 6))):
                loads.append(
                    pltpu.make_async_copy(
                        ref.at[:, :, at], outs[r].at[pl.ds(first, 3)], sems.at[2 + 2 * r + slot]
                    )
                )
        for load in loads:
            load.start()
        loads[0].wait()
        loads[1].wait()
        for r in range(groups):
            at = block_of(place_ref, r, rows)
            for x in range(3):
                outs[r][3 + x] = p_buf[x, :, at] + 0.5 * TIME_STEP * f_buf[x, :, at]
        for load in loads[2:]:
            load.wait()

    return pl.pallas_call(
        kernel,
        out_shape=[jax.ShapeDtypeStruct((9, beads, rows), jnp.float32)] * groups,
        in_specs=[smem()] + [pl.BlockSpec(memory_space=pltpu.HBM)] * 4,
        out_specs=[whole_vmem()] * groups,
        scratch_shapes=[
            pltpu.VMEM((3, beads, atoms), jnp.float32),
            pltpu.VMEM((3, beads, atoms), jnp.float32),
            pltpu.SemaphoreType.DMA((2 + 2 * groups,)),
        ],
        compiler_params=params(60),
        name="pack",
    )(place, positions, momenta, force_old, noise)


def prepare(pair_list, mass, desc_w, hidden_one, place, rows):
    entries, atoms = pair_list.shape
    desc, env = desc_w.shape
    hid = hidden_one.shape[0]
    order = np.arange(env)
    order = (order % entries) * (env // entries) + order // entries
    permute = jnp.asarray(np.eye(env)[order], jnp.bfloat16)

    def kernel(place_ref, list_ref, mass_ref, w0_ref, w1_ref, order_ref, lists, own, masses, w0, w1):
        for t in range(atoms // LANES):
            at = pl.ds(t * LANES, LANES)
            lists[:, at] = list_ref[:, at] - t * LANES
        block = pl.ds(pl.multiple_of(place_ref[0] * rows, LANES), rows)
        own[...] = lists[:, block]
        masses[...] = mass_ref[:, block]
        w0[...] = lax.dot_general(
            order_ref[...],
            w0_ref[...],
            (((1,), (1,)), ((), ())),
            preferred_element_type=jnp.float32,
        ).astype(w0.dtype)
        w1[...] = w1_ref[...].astype(jnp.float32).T.astype(w1.dtype)

    return pl.pallas_call(
        kernel,
        out_shape=(
            jax.ShapeDtypeStruct((entries, atoms), jnp.int32),
            jax.ShapeDtypeStruct((entries, rows), jnp.int32),
            jax.ShapeDtypeStruct((1, rows), jnp.float32),
            jax.ShapeDtypeStruct((env, desc), jnp.bfloat16),
            jax.ShapeDtypeStruct((desc, hid), jnp.bfloat16),
        ),
        in_specs=[pl.BlockSpec(memory_space=pltpu.SMEM)] + [whole_vmem()] * 5,
        out_specs=(whole_vmem(),) * 5,
        compiler_params=params(),
        cost_estimate=pl.CostEstimate(
            flops=1_000_000_000, bytes_accessed=4_000_000, transcendentals=0
        ),
        name="prepare",
    )(place, pair_list, mass, desc_w, hidden_one, permute)


def transform(place, received, masses, step):
    groups = len(received)
    _, beads, rows = received[0].shape

    def kernel(place_ref, mass_ref, step_ref, *rest):
        ins = rest[:groups]
        c_ref = rest[groups]
        qs, ps = rest[groups + 1 : 2 * groups + 1], rest[2 * groups + 1 : 3 * groups + 1]
        fields, news = rest[3 * groups + 1 :]
        mass = mass_ref[...]
        inverse = 1.0 / mass
        root = lax.rsqrt(mass)
        table = step_ref[...]
        for r in range(groups):
            g = place_ref[0] ^ r
            for x in range(3):
                fields[x, 0, g] = ins[r][x]
                fields[x, 1, g] = ins[r][3 + x] * inverse
                fields[x, 2, g] = ins[r][6 + x] * root
        for x in range(3):
            out = jnp.dot(
                table,
                fields[x].reshape(3 * BEADS, rows),
                precision=BEST,
                preferred_element_type=jnp.float32,
            )
            c_ref[x] = out[:NC]
            news[0, x] = out[NC : NC + BEADS].reshape(groups, beads, rows)
            news[1, x] = (out[NC + BEADS :] * mass).reshape(groups, beads, rows)
        for r in range(groups):
            g = place_ref[0] ^ r
            for x in range(3):
                qs[r][x] = news[0, x, g]
                ps[r][x] = news[1, x, g]

    block = jax.ShapeDtypeStruct((3, beads, rows), jnp.float32)
    outs = pl.pallas_call(
        kernel,
        out_shape=[jax.ShapeDtypeStruct((3, NC, rows), jnp.float32)] + [block] * (2 * groups),
        in_specs=[smem()] + [whole_vmem()] * (2 + groups),
        out_specs=[whole_vmem()] * (1 + 2 * groups),
        scratch_shapes=[
            pltpu.VMEM((3, 3, groups, beads, rows), jnp.float32),
            pltpu.VMEM((2, 3, groups, beads, rows), jnp.float32),
        ],
        compiler_params=params(),
        name="transform",
    )(place, masses, step, *received)
    return outs[0], outs[1 : 1 + groups], outs[1 + groups :]


def banded(windows, lane, low, high):
    below, middle, above = [
        jnp.take_along_axis(w, lane, axis=1, mode="promise_in_bounds") for w in windows
    ]
    return jnp.where(low, below, jnp.where(high, above, middle))


def env_tile(windows, list_ref, base, envs, inputs):
    entries = list_ref.shape[0]
    for e in range(0, entries, 8):
        place = list_ref[pl.ds(e, 8), pl.ds(base, LANES)]
        lane = place & (LANES - 1)
        low = place < LANES
        high = place >= 2 * LANES
        for c in range(NC):
            apart = []
            for x in range(3):
                tiles = windows(c, x)
                apart.append(banded(tiles, lane, low, high) - tiles[1])
            square = apart[0] * apart[0] + apart[1] * apart[1] + apart[2] * apart[2]
            close = 1.0 / (1.0 + square)
            for x, value in enumerate(apart + [close]):
                envs[pl.ds(x * entries + e, 8), pl.ds(c * LANES, LANES)] = value
    for c in range(NC):
        at = pl.ds(c * LANES, LANES)
        inputs[at, :] = envs[:, at].T.astype(jnp.bfloat16)


def network(inputs_ref, weights, forces, cols=256, chunk=256):
    w0_ref, w1_ref, w2_ref, w3_ref, wo_ref = weights
    desc = w0_ref.shape[1]
    for c in range(0, NC * LANES, cols):
        inputs = inputs_ref[pl.ds(c, cols), :]
        total = None
        for f in range(0, desc, chunk):
            size = min(chunk, desc - f)
            first = jnp.dot(inputs, w0_ref[:, pl.ds(f, size)], preferred_element_type=jnp.float32)
            first = jnp.tanh(first.astype(jnp.bfloat16))
            part = jnp.dot(first, w1_ref[pl.ds(f, size), :], preferred_element_type=jnp.float32)
            total = part if total is None else total + part
        layer = jnp.tanh(total).astype(jnp.bfloat16)
        for ref in (w2_ref, w3_ref):
            layer = jnp.tanh(
                jnp.dot(layer, ref[...], preferred_element_type=jnp.float32)
            ).astype(jnp.bfloat16)
        out = lax.dot_general(
            wo_ref[...], layer, (((1,), (1,)), ((), ())), preferred_element_type=jnp.float32
        )
        for part in range(cols // LANES):
            for x in range(3):
                forces[pl.ds(c // LANES + part, 1), pl.ds(x * LANES, LANES)] = out[
                    x : x + 1, part * LANES : (part + 1) * LANES
                ]


def neural_scratch(env):
    return [
        pltpu.VMEM((2, env, NC * LANES), jnp.float32),
        pltpu.VMEM((2, NC * LANES, env), jnp.bfloat16),
    ]


def neural_cost(tiles):
    return pl.CostEstimate(
        flops=3_000_000_000 * tiles, bytes_accessed=2_000_000, transcendentals=0
    )


def neural_inner(contracted, lists, weights):
    tiles = contracted.shape[2] // LANES
    inner = tiles - 2

    def kernel(c_ref, list_ref, w0, w1, w2, w3, wo, out_ref, envs, inputs):
        def windows_of(t):
            return lambda c, x: [
                jnp.broadcast_to(
                    c_ref[x, pl.ds(c, 1), pl.ds((t + v) * LANES, LANES)], (8, LANES)
                )
                for v in (-1, 0, 1)
            ]

        for t in range(1, tiles - 1):
            slot = t % 2
            env_tile(windows_of(t), list_ref, t * LANES, envs.at[slot], inputs.at[slot])
            network(inputs.at[slot], (w0, w1, w2, w3, wo), out_ref.at[t - 1])

    return pl.pallas_call(
        kernel,
        out_shape=jax.ShapeDtypeStruct((inner, NC, 3 * LANES), jnp.float32),
        in_specs=[whole_vmem()] * 7,
        out_specs=whole_vmem(),
        scratch_shapes=neural_scratch(weights[0].shape[0]),
        compiler_params=params(),
        cost_estimate=neural_cost(inner),
        name="neural_inner",
    )(contracted, lists, *weights)


def neural_edge(place, contracted, lower, upper, lists, weights, inner, spread, groups):
    _, _, rows = contracted.shape
    beads = BEADS // groups
    tiles = rows // LANES

    def kernel(
        place_ref, c_ref, low_ref, up_ref, list_ref, w0, w1, w2, w3, wo, spread_ref, inner_ref,
        *rest,
    ):
        outs = rest[:groups]
        forces, spreads, envs, inputs = rest[groups:]

        def tile(x, c, t):
            if t < 0:
                ref, at = low_ref, 0
            elif t >= tiles:
                ref, at = up_ref, 0
            else:
                ref, at = c_ref, t * LANES
            return jnp.broadcast_to(ref[x, pl.ds(c, 1), pl.ds(at, LANES)], (8, LANES))

        for slot, t in enumerate((0, tiles - 1)):
            windows = lambda c, x: [tile(x, c, t + v) for v in (-1, 0, 1)]
            env_tile(windows, list_ref, t * LANES, envs.at[slot], inputs.at[slot])
            network(inputs.at[slot], (w0, w1, w2, w3, wo), forces.at[slot])
        for t in range(tiles):
            if t in (0, tiles - 1):
                own = forces[min(t, 1)]
            else:
                own = inner_ref[t - 1]
            wide = jnp.dot(
                spread_ref[...], own, precision=BEST, preferred_element_type=jnp.float32
            )
            for x in range(3):
                spreads[:, x, :, pl.ds(t * LANES, LANES)] = wide[
                    :, x * LANES : (x + 1) * LANES
                ].reshape(groups, beads, LANES)
        for r in range(groups):
            outs[r][...] = spreads[place_ref[0] ^ r]

    return pl.pallas_call(
        kernel,
        out_shape=[jax.ShapeDtypeStruct((3, beads, rows), jnp.float32)] * groups,
        in_specs=[smem()] + [whole_vmem()] * 11,
        out_specs=[whole_vmem()] * groups,
        scratch_shapes=[
            pltpu.VMEM((2, NC, 3 * LANES), jnp.float32),
            pltpu.VMEM((groups, 3, beads, rows), jnp.float32),
        ]
        + neural_scratch(weights[0].shape[0]),
        compiler_params=params(),
        cost_estimate=neural_cost(2),
        name="neural_edge",
    )(place, contracted, lower, upper, lists, *weights, spread, inner)


def pair_tile(windows, list_ref, base):
    beads = windows[0][0].shape[0]
    sums = [jnp.zeros((beads, LANES), jnp.float32)] * 3
    for e in range(list_ref.shape[0]):
        place = jnp.broadcast_to(list_ref[pl.ds(e, 1), pl.ds(base, LANES)], (beads, LANES))
        lane = place & (LANES - 1)
        low = place < LANES
        high = place >= 2 * LANES
        apart = [banded(windows[x], lane, low, high) - windows[x][1] for x in range(3)]
        square = apart[0] * apart[0] + apart[1] * apart[1] + apart[2] * apart[2]
        close = 1.0 / (1.0 + square)
        sums = [s + a * close for s, a in zip(sums, apart)]
    return [PAIR_STRENGTH * s for s in sums]


def unpack(one, two):
    third = ((one << 21) | ((two & 1023) << 11)) >> 11
    return one >> 11, two >> 11, third


def assemble(place, blocks):
    groups = len(blocks)
    _, beads, rows = blocks[0].shape
    atoms = groups * rows
    top = float(2**20 - 1)

    def kernel(place_ref, *rest):
        ins = rest[:groups]
        newq, words, unit_ref, rims = rest[groups:]
        largest = jnp.zeros((beads, rows), jnp.float32)
        for r in range(groups):
            at = block_of(place_ref, r, rows)
            for x in range(3):
                value = ins[r][x]
                newq[x, :, at] = value
                largest = jnp.maximum(largest, jnp.abs(value))
        limit = jnp.maximum(jnp.max(largest, keepdims=True), 1e-30)
        to_fixed = top / limit
        unit_ref[...] = jnp.broadcast_to(limit / top, (beads, LANES))
        for r in range(groups):
            at = block_of(place_ref, r, rows)
            one, two, three = [
                jnp.floor(ins[r][x] * to_fixed + 0.5).astype(jnp.int32) for x in range(3)
            ]
            words[0, :, at] = (one << 11) | ((three >> 10) & 2047)
            words[1, :, at] = (two << 11) | (three & 1023)
        for rim, t in enumerate((0, LANES, atoms - 2 * LANES, atoms - LANES)):
            rims[rim] = newq[:, :, pl.ds(t, LANES)]

    return pl.pallas_call(
        kernel,
        out_shape=(
            jax.ShapeDtypeStruct((3, beads, atoms), jnp.float32),
            jax.ShapeDtypeStruct((2, beads, atoms), jnp.int32),
            jax.ShapeDtypeStruct((beads, LANES), jnp.float32),
            jax.ShapeDtypeStruct((4, 3, beads, LANES), jnp.float32),
        ),
        in_specs=[smem()] + [whole_vmem()] * groups,
        out_specs=(whole_vmem(),) * 4,
        compiler_params=params(),
        name="assemble",
    )(place, *blocks)


def pair_inner(words, unit, lists):
    _, beads, atoms = words.shape
    entries = lists.shape[0]

    def kernel(words_ref, unit_ref, list_ref, pair):
        unit_row = unit_ref[...]
        unit_square = unit_row * unit_row

        @pl.loop(1, atoms // LANES - 1)
        def _(t):
            base = pl.multiple_of(t * LANES, LANES)
            windows = [
                [words_ref[w, :, pl.ds(base + (v - 1) * LANES, LANES)] for v in range(3)]
                for w in range(2)
            ]
            own = unpack(windows[0][1], windows[1][1])
            sums = [jnp.zeros((beads, LANES), jnp.float32)] * 3
            for e in range(entries):
                place = jnp.broadcast_to(
                    list_ref[pl.ds(e, 1), pl.ds(base, LANES)], (beads, LANES)
                )
                lane = place & (LANES - 1)
                low = place < LANES
                high = place >= 2 * LANES
                near = unpack(*[banded(windows[w], lane, low, high) for w in range(2)])
                apart = [(n - o).astype(jnp.float32) for n, o in zip(near, own)]
                square = apart[0] * apart[0] + apart[1] * apart[1] + apart[2] * apart[2]
                close = 1.0 / (1.0 + square * unit_square)
                sums = [s + a * close for s, a in zip(sums, apart)]
            for x in range(3):
                pair[x, :, pl.ds(base, LANES)] = (PAIR_STRENGTH * unit_row) * sums[x]

    return pl.pallas_call(
        kernel,
        out_shape=jax.ShapeDtypeStruct((3, beads, atoms), jnp.float32),
        in_specs=[whole_vmem()] * 3,
        out_specs=whole_vmem(),
        compiler_params=params(),
        cost_estimate=pl.CostEstimate(
            flops=15_000_000_000, bytes_accessed=4_000_000, transcendentals=0
        ),
        name="pair_inner",
    )(words, unit, lists)


def finish(place, pair, rims, lower, upper, lists, moved, spread):
    groups = len(moved)
    _, beads, rows = moved[0].shape
    atoms = groups * rows

    def kernel(place_ref, pair_ref, rims_ref, low_ref, up_ref, list_ref, *rest):
        ps, spreads = rest[:groups], rest[groups : 2 * groups]
        newp, newf = rest[2 * groups :]

        def edge(base, windows):
            for x, force in enumerate(pair_tile(windows, list_ref, base)):
                newf[x, :, pl.ds(base, LANES)] = force

        newf[...] = pair_ref[...]
        edge(0, [[low_ref[x], rims_ref[0, x], rims_ref[1, x]] for x in range(3)])
        edge(atoms - LANES, [[rims_ref[2, x], rims_ref[3, x], up_ref[x]] for x in range(3)])
        for r in range(groups):
            at = block_of(place_ref, r, rows)
            for x in range(3):
                force = newf[x, :, at] + spreads[r][x]
                newf[x, :, at] = force
                newp[x, :, at] = ps[r][x] + 0.5 * TIME_STEP * force

    out = jax.ShapeDtypeStruct((3, beads, atoms), jnp.float32)
    return pl.pallas_call(
        kernel,
        out_shape=(out,) * 2,
        in_specs=[smem()] + [whole_vmem()] * (5 + 2 * groups),
        out_specs=(whole_vmem(),) * 2,
        compiler_params=params(),
        name="finish",
    )(place, pair, rims, lower, upper, lists, *moved, *spread)


def body(
    positions,
    momenta,
    force_old,
    noise,
    mass,
    pair_list,
    desc_w,
    hidden_one,
    hidden_two,
    hidden_three,
    out_w,
):
    beads, _, atoms = positions.shape
    groups = lax.axis_size("bead")
    slabs = lax.axis_size(("slab", "grp"))
    rows = atoms // groups
    place = lax.axis_index("bead").astype(jnp.int32)[None]
    step, contract = step_tables()

    swap = lambda field: jnp.transpose(field, (1, 0, 2))
    sends = pack(place, swap(positions), swap(momenta), swap(force_old), swap(noise), groups)
    received = exchange(sends, "bead")

    lists, block_lists, masses, env_w, w1 = prepare(
        pair_list.T, mass[None, :], desc_w.T, hidden_one.T, place, rows
    )
    received, lists, block_lists, masses, env_w, w1 = lax.optimization_barrier(
        (received, lists, block_lists, masses, env_w, w1)
    )
    weights = (env_w, w1, hidden_two, hidden_three, out_w.T)

    contracted, block_q, block_p = transform(place, received, masses, jnp.asarray(step))

    ring = [
        (g * slabs + s, ((g + 1) % groups) * slabs + (s + (g + 1) // groups) % slabs)
        for g in range(groups)
        for s in range(slabs)
    ]
    back = [(j, i) for i, j in ring]
    every = ("bead", "slab", "grp")
    lower = lax.ppermute(contracted[:, :, rows - EDGE :], every, ring)
    upper = lax.ppermute(contracted[:, :, :EDGE], every, back)
    new_q = exchange(block_q, "bead")
    moved = exchange(block_p, "bead")

    if rows > 2 * LANES:
        inner = neural_inner(contracted, block_lists, weights)
    else:
        inner = jnp.zeros((1, NC, 3 * LANES), jnp.float32)
    inner, lower, upper = lax.optimization_barrier((inner, lower, upper))
    spread = neural_edge(
        place, contracted, lower, upper, block_lists, weights, inner,
        jnp.asarray(contract.T * np.float32(BEADS / NC)), groups,
    )
    new_q, spread = lax.optimization_barrier((new_q, spread))
    spread = exchange(spread, "bead")

    new_q, words, unit, rims = assemble(place, new_q)
    slab_ring = [(s, (s + 1) % slabs) for s in range(slabs)]
    slab_back = [(j, i) for i, j in slab_ring]
    q_lower = lax.ppermute(rims[3], ("slab", "grp"), slab_ring)
    q_upper = lax.ppermute(rims[0], ("slab", "grp"), slab_back)

    pair = pair_inner(words, unit, lists)
    new_p, force = finish(place, pair, rims, q_lower, q_upper, lists, moved, spread)
    return tuple(swap(out) for out in (new_q, new_p, force))


def solution(mesh):
    field = P("bead", None, ("slab", "grp"))
    placed = (field,) * 4 + (P(("slab", "grp")), P(("slab", "grp"), None)) + (P(),) * 5
    return jax.shard_map(
        body, mesh=mesh, in_specs=placed, out_specs=(field,) * 3, check_vma=False
    )
```

```python
import math

import jax
import jax.numpy as jnp
import numpy as np
from jax import lax
from jax.experimental import pallas as pl
from jax.experimental.pallas import tpu as pltpu
from jax.sharding import PartitionSpec as P

BEADS = 64
NC = 8
EDGE = 128
LANES = 128

TIME_STEP = 0.1
CYCLE_FREQ = 5.0
CENTROID_FRICTION = 1.0
PAIR_STRENGTH = 0.5

BEST = lax.Precision.HIGHEST


def step_tables():
    b = np.arange(BEADS, dtype=np.float64)
    k = np.arange(BEADS)
    angle = 2.0 * np.pi * ((b[:, None] * b[None, :]) % BEADS) / BEADS
    half = BEADS // 2
    basis = np.where(
        k == 0,
        1.0 / math.sqrt(BEADS),
        np.where(
            k < half,
            math.sqrt(2.0 / BEADS) * np.cos(angle),
            np.where(
                k == half, np.cos(angle) / math.sqrt(BEADS), math.sqrt(2.0 / BEADS) * np.sin(angle)
            ),
        ),
    )
    freq = 2.0 * CYCLE_FREQ * np.sin(np.pi * b / BEADS)
    spacing = b[None, :] / BEADS - np.arange(NC, dtype=np.float64)[:, None] / NC
    kernel = np.ones_like(spacing)
    for order in range(1, NC // 2):
        kernel = kernel + 2.0 * np.cos(2.0 * np.pi * order * spacing)
    kernel = kernel + np.cos(np.pi * NC * spacing)
    contract = kernel / BEADS

    h = 0.5 * TIME_STEP
    safe = np.where(freq > 0.0, freq, 1.0)
    qq = np.where(freq > 0.0, np.cos(safe * h), 1.0)
    qp = np.where(freq > 0.0, np.sin(safe * h) / safe, h)
    pq = np.where(freq > 0.0, -safe * np.sin(safe * h), 0.0)
    pp = qq
    keep = np.exp(-np.where(freq > 0.0, 2.0 * freq, CENTROID_FRICTION) * TIME_STEP)
    kick = np.sqrt(1.0 - keep * keep)
    full_qq = qq * qq + qp * keep * pq
    full_qp = qq * qp + qp * keep * pp
    full_qn = qp * kick
    full_pq = pq * qq + pp * keep * pq
    full_pp = pq * qp + pp * keep * pp
    full_pn = pp * kick
    q_rows = np.concatenate(
        [(basis * full_qq) @ basis.T, (basis * full_qp) @ basis.T, basis * full_qn], axis=1
    )
    p_rows = np.concatenate(
        [(basis * full_pq) @ basis.T, (basis * full_pp) @ basis.T, basis * full_pn], axis=1
    )
    c_rows = contract @ q_rows
    step = np.concatenate([c_rows, q_rows, p_rows], axis=0)
    return step.astype(np.float32), contract.astype(np.float32)


def whole_vmem():
    return pl.BlockSpec(memory_space=pltpu.VMEM)


def params(mebibytes=48):
    return pltpu.CompilerParams(vmem_limit_bytes=mebibytes * 1024 * 1024)


def smem():
    return pl.BlockSpec(memory_space=pltpu.SMEM)


def block_of(place_ref, r, rows):
    return pl.ds(pl.multiple_of((place_ref[0] ^ r) * rows, LANES), rows)


def exchange(blocks, axis):
    count = len(blocks)
    return [blocks[0]] + [
        lax.ppermute(blocks[r], axis, [(i, i ^ r) for i in range(count)]) for r in range(1, count)
    ]


def pack(place, positions, momenta, force_old, noise, groups):
    _, beads, atoms = positions.shape
    rows = atoms // groups

    def kernel(place_ref, q_ref, p_ref, f_ref, n_ref, *rest):
        outs, (p_buf, f_buf, sems) = rest[:groups], rest[groups:]
        loads = [
            pltpu.make_async_copy(p_ref, p_buf, sems.at[0]),
            pltpu.make_async_copy(f_ref, f_buf, sems.at[1]),
        ]
        for r in range(groups):
            at = block_of(place_ref, r, rows)
            for slot, (ref, first) in enumerate(((q_ref, 0), (n_ref, 6))):
                loads.append(
                    pltpu.make_async_copy(
                        ref.at[:, :, at], outs[r].at[pl.ds(first, 3)], sems.at[2 + 2 * r + slot]
                    )
                )
        for load in loads:
            load.start()
        loads[0].wait()
        loads[1].wait()
        for r in range(groups):
            at = block_of(place_ref, r, rows)
            for x in range(3):
                outs[r][3 + x] = p_buf[x, :, at] + 0.5 * TIME_STEP * f_buf[x, :, at]
        for load in loads[2:]:
            load.wait()

    return pl.pallas_call(
        kernel,
        out_shape=[jax.ShapeDtypeStruct((9, beads, rows), jnp.float32)] * groups,
        in_specs=[smem()] + [pl.BlockSpec(memory_space=pltpu.HBM)] * 4,
        out_specs=[whole_vmem()] * groups,
        scratch_shapes=[
            pltpu.VMEM((3, beads, atoms), jnp.float32),
            pltpu.VMEM((3, beads, atoms), jnp.float32),
            pltpu.SemaphoreType.DMA((2 + 2 * groups,)),
        ],
        compiler_params=params(60),
        name="pack",
    )(place, positions, momenta, force_old, noise)


def prepare(pair_list, mass, desc_w, hidden_one, place, rows, beads):
    entries, atoms = pair_list.shape
    desc, env = desc_w.shape
    hid = hidden_one.shape[0]
    order = np.arange(env)
    order = (order % entries) * (env // entries) + order // entries
    permute = jnp.asarray(np.eye(env)[order], jnp.bfloat16)

    def kernel(place_ref, list_ref, mass_ref, w0_ref, w1_ref, order_ref, lists, own, masses, w0, w1):
        for t in range(atoms // LANES):
            at = pl.ds(t * LANES, LANES)
            places = list_ref[:, at] - t * LANES
            lists[:, :, at] = jnp.broadcast_to(places[:, None, :], (entries, beads, LANES))
        block = pl.ds(pl.multiple_of(place_ref[0] * rows, LANES), rows)
        own[...] = list_ref[:, block] - place_ref[0] * rows
        masses[...] = mass_ref[:, block]
        w0[...] = lax.dot_general(
            order_ref[...],
            w0_ref[...],
            (((1,), (1,)), ((), ())),
            preferred_element_type=jnp.float32,
        ).astype(w0.dtype)
        w1[...] = w1_ref[...].astype(jnp.float32).T.astype(w1.dtype)

    return pl.pallas_call(
        kernel,
        out_shape=(
            jax.ShapeDtypeStruct((entries, beads, atoms), jnp.int32),
            jax.ShapeDtypeStruct((entries, rows), jnp.int32),
            jax.ShapeDtypeStruct((1, rows), jnp.float32),
            jax.ShapeDtypeStruct((env, desc), jnp.bfloat16),
            jax.ShapeDtypeStruct((desc, hid), jnp.bfloat16),
        ),
        in_specs=[pl.BlockSpec(memory_space=pltpu.SMEM)] + [whole_vmem()] * 5,
        out_specs=(whole_vmem(),) * 5,
        compiler_params=params(),
        cost_estimate=pl.CostEstimate(
            flops=1_000_000_000, bytes_accessed=4_000_000, transcendentals=0
        ),
        name="prepare",
    )(place, pair_list, mass, desc_w, hidden_one, permute)


def scaled_fields(place_ref, mass_ref, ins, fields):
    mass = mass_ref[...]
    inverse = 1.0 / mass
    root = lax.rsqrt(mass)
    for r, block in enumerate(ins):
        g = place_ref[0] ^ r
        for x in range(3):
            fields[x, 0, g] = block[x]
            fields[x, 1, g] = block[3 + x] * inverse
            fields[x, 2, g] = block[6 + x] * root


def contract(place, received, masses, table):
    groups = len(received)
    _, beads, rows = received[0].shape

    def kernel(place_ref, mass_ref, table_ref, *rest):
        ins, (c_ref, first, last, fields) = rest[:groups], rest[groups:]
        scaled_fields(place_ref, mass_ref, ins, fields)
        for x in range(3):
            out = jnp.dot(
                table_ref[...],
                fields[x].reshape(3 * BEADS, rows),
                precision=BEST,
                preferred_element_type=jnp.float32,
            )
            c_ref[x] = out
            first[x] = out[:, :EDGE]
            last[x] = out[:, rows - EDGE :]

    edge = jax.ShapeDtypeStruct((3, NC, EDGE), jnp.float32)
    return pl.pallas_call(
        kernel,
        out_shape=(jax.ShapeDtypeStruct((3, NC, rows), jnp.float32), edge, edge),
        in_specs=[smem()] + [whole_vmem()] * (2 + groups),
        out_specs=(whole_vmem(),) * 3,
        scratch_shapes=[pltpu.VMEM((3, 3, groups, beads, rows), jnp.float32)],
        compiler_params=params(),
        name="contract",
    )(place, masses, table, *received)


def transform(place, received, masses, table):
    groups = len(received)
    _, beads, rows = received[0].shape

    def kernel(place_ref, mass_ref, table_ref, *rest):
        ins, (out_ref, fields) = rest[:groups], rest[groups:]
        scaled_fields(place_ref, mass_ref, ins, fields)
        mass = mass_ref[...]
        for x in range(3):
            out = jnp.dot(
                table_ref[...],
                fields[x].reshape(3 * BEADS, rows),
                precision=BEST,
                preferred_element_type=jnp.float32,
            )
            out_ref[:, x] = out[:BEADS].reshape(groups, beads, rows)
            out_ref[:, 3 + x] = (out[BEADS:] * mass).reshape(groups, beads, rows)

    return pl.pallas_call(
        kernel,
        out_shape=jax.ShapeDtypeStruct((groups, 6, beads, rows), jnp.float32),
        in_specs=[smem()] + [whole_vmem()] * (2 + groups),
        out_specs=whole_vmem(),
        scratch_shapes=[pltpu.VMEM((3, 3, groups, beads, rows), jnp.float32)],
        compiler_params=params(),
        cost_estimate=pl.CostEstimate(
            flops=1_000_000_000, bytes_accessed=2_000_000, transcendentals=0
        ),
        name="transform",
    )(place, masses, table, *received)


def inverse_of(value):
    estimate = pl.reciprocal(value, approx=True)
    return estimate * (2.0 - value * estimate)


def banded(windows, lane, low, high):
    below, middle, above = [
        jnp.take_along_axis(w, lane, axis=1, mode="promise_in_bounds") for w in windows
    ]
    return jnp.where(low, below, jnp.where(high, above, middle))


def env_tile(windows, list_ref, base, envs, inputs):
    entries = list_ref.shape[0]
    for e in range(0, entries, 8):
        place = list_ref[pl.ds(e, 8), pl.ds(base, LANES)] - base
        lane = place & (LANES - 1)
        low = place < LANES
        high = place >= 2 * LANES
        for c in range(NC):
            apart = []
            for x in range(3):
                tiles = windows(c, x)
                apart.append(banded(tiles, lane, low, high) - tiles[1])
            square = apart[0] * apart[0] + apart[1] * apart[1] + apart[2] * apart[2]
            close = inverse_of(1.0 + square)
            for x, value in enumerate(apart + [close]):
                envs[pl.ds(x * entries + e, 8), pl.ds(c * LANES, LANES)] = value
    for c in range(NC):
        at = pl.ds(c * LANES, LANES)
        inputs[at, :] = envs[:, at].T.astype(jnp.bfloat16)


def network(inputs_ref, weights, forces, cols=1024, chunk=256):
    w0_ref, w1_ref, w2_ref, w3_ref, wo_ref = weights
    desc = w0_ref.shape[1]
    for c in range(0, NC * LANES, cols):
        inputs = inputs_ref[pl.ds(c, cols), :]
        total = None
        for f in range(0, desc, chunk):
            size = min(chunk, desc - f)
            first = jnp.dot(inputs, w0_ref[:, pl.ds(f, size)], preferred_element_type=jnp.float32)
            first = jnp.tanh(first.astype(jnp.bfloat16))
            part = jnp.dot(first, w1_ref[pl.ds(f, size), :], preferred_element_type=jnp.float32)
            total = part if total is None else total + part
        layer = jnp.tanh(total).astype(jnp.bfloat16)
        for ref in (w2_ref, w3_ref):
            layer = jnp.tanh(
                jnp.dot(layer, ref[...], preferred_element_type=jnp.float32)
            ).astype(jnp.bfloat16)
        out = lax.dot_general(
            wo_ref[...], layer, (((1,), (1,)), ((), ())), preferred_element_type=jnp.float32
        )
        for part in range(cols // LANES):
            for x in range(3):
                forces[pl.ds(c // LANES + part, 1), pl.ds(x * LANES, LANES)] = out[
                    x : x + 1, part * LANES : (part + 1) * LANES
                ]


def neural_scratch(env):
    return [
        pltpu.VMEM((2, env, NC * LANES), jnp.float32),
        pltpu.VMEM((2, NC * LANES, env), jnp.bfloat16),
    ]


def neural(contracted, lower, upper, lists, weights, spread, groups):
    _, _, rows = contracted.shape
    beads = BEADS // groups
    tiles = rows // LANES

    def kernel(
        c_ref, low_ref, up_ref, list_ref, w0, w1, w2, w3, wo, spread_ref,
        out_ref, forces, envs, inputs,
    ):
        def tile(x, c, t):
            if t < 0:
                ref, at = low_ref, 0
            elif t >= tiles:
                ref, at = up_ref, 0
            else:
                ref, at = c_ref, t * LANES
            return jnp.broadcast_to(ref[x, pl.ds(c, 1), pl.ds(at, LANES)], (8, LANES))

        for t in range(tiles):
            slot = t % 2
            windows = lambda c, x: [tile(x, c, t + v) for v in (-1, 0, 1)]
            env_tile(windows, list_ref, t * LANES, envs.at[slot], inputs.at[slot])
            network(inputs.at[slot], (w0, w1, w2, w3, wo), forces.at[slot])
            for x in range(3):
                at = pl.ds(x * LANES, LANES)
                wide = spread_ref[0] * forces[slot, pl.ds(0, 1), at]
                for c in range(1, NC):
                    wide = wide + spread_ref[c] * forces[slot, pl.ds(c, 1), at]
                out_ref[:, x, :, pl.ds(t * LANES, LANES)] = wide.reshape(groups, beads, LANES)

    return pl.pallas_call(
        kernel,
        out_shape=jax.ShapeDtypeStruct((groups, 3, beads, rows), jnp.float32),
        in_specs=[whole_vmem()] * 10,
        out_specs=whole_vmem(),
        scratch_shapes=[pltpu.VMEM((2, NC, 3 * LANES), jnp.float32)]
        + neural_scratch(weights[0].shape[0]),
        compiler_params=params(),
        cost_estimate=pl.CostEstimate(
            flops=12_000_000_000, bytes_accessed=4_000_000, transcendentals=0
        ),
        name="neural",
    )(contracted, lower, upper, lists, *weights, spread)


def entry_of(list_ref, e, base):
    place = list_ref[e, :, pl.ds(base, LANES)]
    return place & (LANES - 1), place < LANES, place >= 2 * LANES


def pair_tile(windows, list_ref, base):
    beads = windows[0][0].shape[0]
    sums = [jnp.zeros((beads, LANES), jnp.float32)] * 3
    for e in range(list_ref.shape[0]):
        lane, low, high = entry_of(list_ref, e, base)
        apart = [banded(windows[x], lane, low, high) - windows[x][1] for x in range(3)]
        square = apart[0] * apart[0] + apart[1] * apart[1] + apart[2] * apart[2]
        close = inverse_of(1.0 + square)
        sums = [s + a * close for s, a in zip(sums, apart)]
    return [PAIR_STRENGTH * s for s in sums]


def third_of(one, two):
    return ((one & 2047) << 20) + ((two & 511) << 11)


def assemble(fields):
    groups, _, beads, rows = fields.shape
    atoms = groups * rows
    half = 2**19
    top = float(half - 1)

    def kernel(in_ref, newq, words, unit_ref, rims):
        largest = jnp.zeros((beads, rows), jnp.float32)
        for g in range(groups):
            at = pl.ds(g * rows, rows)
            for x in range(3):
                value = in_ref[g, x]
                newq[x, :, at] = value
                largest = jnp.maximum(largest, jnp.abs(value))
        limit = jnp.maximum(jnp.max(largest, keepdims=True), 1e-30)
        to_fixed = top / limit
        unit_ref[...] = jnp.broadcast_to(limit / (top * 2048.0), (beads, LANES))
        for g in range(groups):
            at = pl.ds(g * rows, rows)
            one, two, three = [
                jnp.floor(in_ref[g, x] * to_fixed + 0.5).astype(jnp.int32) for x in range(3)
            ]
            three = three + half
            words[0, :, at] = (one << 11) + (three >> 9)
            words[1, :, at] = (two << 11) + (three & 511)
        for rim, t in enumerate((0, LANES, atoms - 2 * LANES, atoms - LANES)):
            rims[rim] = newq[:, :, pl.ds(t, LANES)]

    return pl.pallas_call(
        kernel,
        out_shape=(
            jax.ShapeDtypeStruct((3, beads, atoms), jnp.float32),
            jax.ShapeDtypeStruct((2, beads, atoms), jnp.int32),
            jax.ShapeDtypeStruct((beads, LANES), jnp.float32),
            jax.ShapeDtypeStruct((4, 3, beads, LANES), jnp.float32),
        ),
        in_specs=[whole_vmem()],
        out_specs=(whole_vmem(),) * 4,
        compiler_params=params(),
        name="assemble",
    )(fields)


def pair_inner(words, unit, lists):
    _, beads, atoms = words.shape
    entries = lists.shape[0]

    def kernel(words_ref, unit_ref, list_ref, pair):
        unit_row = unit_ref[...]
        unit_square = unit_row * unit_row

        @pl.loop(1, atoms // LANES - 1)
        def _(t):
            base = pl.multiple_of(t * LANES, LANES)
            windows = [
                [words_ref[w, :, pl.ds(base + (v - 1) * LANES, LANES)] for v in range(3)]
                for w in range(2)
            ]
            own = (windows[0][1], windows[1][1], third_of(windows[0][1], windows[1][1]))
            sums = [jnp.zeros((beads, LANES), jnp.float32)] * 3
            for e in range(entries):
                lane, low, high = entry_of(list_ref, e, base)
                one, two = [banded(windows[w], lane, low, high) for w in range(2)]
                near = (one, two, third_of(one, two))
                apart = [(n - o).astype(jnp.float32) for n, o in zip(near, own)]
                square = apart[0] * apart[0] + apart[1] * apart[1] + apart[2] * apart[2]
                close = inverse_of(1.0 + square * unit_square)
                sums = [s + a * close for s, a in zip(sums, apart)]
            for x in range(3):
                pair[x, :, pl.ds(base, LANES)] = (PAIR_STRENGTH * unit_row) * sums[x]

    return pl.pallas_call(
        kernel,
        out_shape=jax.ShapeDtypeStruct((3, beads, atoms), jnp.float32),
        in_specs=[whole_vmem()] * 3,
        out_specs=whole_vmem(),
        compiler_params=params(),
        cost_estimate=pl.CostEstimate(
            flops=15_000_000_000, bytes_accessed=4_000_000, transcendentals=0
        ),
        name="pair_inner",
    )(words, unit, lists)


def finish(pair, rims, lower, upper, lists, fields, spread):
    groups, _, beads, rows = fields.shape
    atoms = groups * rows

    def kernel(pair_ref, rims_ref, low_ref, up_ref, list_ref, in_ref, spread_ref, newp, newf):
        def edge(base, windows):
            for x, force in enumerate(pair_tile(windows, list_ref, base)):
                newf[x, :, pl.ds(base, LANES)] = force

        newf[...] = pair_ref[...]
        edge(0, [[low_ref[x], rims_ref[0, x], rims_ref[1, x]] for x in range(3)])
        edge(atoms - LANES, [[rims_ref[2, x], rims_ref[3, x], up_ref[x]] for x in range(3)])
        for g in range(groups):
            at = pl.ds(g * rows, rows)
            for x in range(3):
                force = newf[x, :, at] + spread_ref[g, x]
                newf[x, :, at] = force
                newp[x, :, at] = in_ref[g, 3 + x] + 0.5 * TIME_STEP * force

    out = jax.ShapeDtypeStruct((3, beads, atoms), jnp.float32)
    return pl.pallas_call(
        kernel,
        out_shape=(out,) * 2,
        in_specs=[whole_vmem()] * 7,
        out_specs=(whole_vmem(),) * 2,
        compiler_params=params(),
        name="finish",
    )(pair, rims, lower, upper, lists, fields, spread)


def body(
    positions,
    momenta,
    force_old,
    noise,
    mass,
    pair_list,
    desc_w,
    hidden_one,
    hidden_two,
    hidden_three,
    out_w,
):
    beads, _, atoms = positions.shape
    groups = lax.axis_size("bead")
    slabs = lax.axis_size(("slab", "grp"))
    rows = atoms // groups
    place = lax.axis_index("bead").astype(jnp.int32)[None]
    step, kernel = step_tables()

    swap = lambda field: jnp.transpose(field, (1, 0, 2))
    sends = pack(place, swap(positions), swap(momenta), swap(force_old), swap(noise), groups)
    received = exchange(sends, "bead")

    lists, block_lists, masses, env_w, w1 = prepare(
        pair_list.T, mass[None, :], desc_w.T, hidden_one.T, place, rows, beads
    )
    received, lists, block_lists, masses, env_w, w1 = lax.optimization_barrier(
        (received, lists, block_lists, masses, env_w, w1)
    )
    weights = (env_w, w1, hidden_two, hidden_three, out_w.T)

    contracted, first, last = contract(place, received, masses, jnp.asarray(step[:NC]))
    ring = [
        (g * slabs + s, ((g + 1) % groups) * slabs + (s + (g + 1) // groups) % slabs)
        for g in range(groups)
        for s in range(slabs)
    ]
    back = [(j, i) for i, j in ring]
    every = ("bead", "slab", "grp")
    lower = lax.ppermute(last, every, ring)
    upper = lax.ppermute(first, every, back)
    returns = transform(place, received, masses, jnp.asarray(step[NC:]))
    returns, lower, upper = lax.optimization_barrier((returns, lower, upper))
    fields = lax.all_to_all(returns, "bead", split_axis=0, concat_axis=0, tiled=True)

    coefs = jnp.asarray(kernel * np.float32(BEADS / NC))
    coefs = jnp.broadcast_to(coefs[:, :, None], (NC, BEADS, LANES))
    spread = neural(contracted, lower, upper, block_lists, weights, coefs, groups)
    fields, spread = lax.optimization_barrier((fields, spread))
    spread = lax.all_to_all(spread, "bead", split_axis=0, concat_axis=0, tiled=True)

    new_q, words, unit, rims = assemble(fields)
    slab_ring = [(s, (s + 1) % slabs) for s in range(slabs)]
    slab_back = [(j, i) for i, j in slab_ring]
    q_lower = lax.ppermute(rims[3], ("slab", "grp"), slab_ring)
    q_upper = lax.ppermute(rims[0], ("slab", "grp"), slab_back)

    pair = pair_inner(words, unit, lists)
    new_p, force = finish(pair, rims, q_lower, q_upper, lists, fields, spread)
    return tuple(swap(out) for out in (new_q, new_p, force))


def solution(mesh):
    field = P("bead", None, ("slab", "grp"))
    placed = (field,) * 4 + (P(("slab", "grp")), P(("slab", "grp"), None)) + (P(),) * 5
    return jax.shard_map(
        body, mesh=mesh, in_specs=placed, out_specs=(field,) * 3, check_vma=False
    )
```

```python
import math

import jax
import jax.numpy as jnp
import numpy as np
from jax import lax
from jax.experimental import pallas as pl
from jax.experimental.pallas import tpu as pltpu
from jax.sharding import PartitionSpec as P

BEADS = 64
NC = 8
EDGE = 128
LANES = 128

TIME_STEP = 0.1
CYCLE_FREQ = 5.0
CENTROID_FRICTION = 1.0
PAIR_STRENGTH = 0.5

BEST = lax.Precision.HIGHEST


def step_tables():
    b = np.arange(BEADS, dtype=np.float64)
    k = np.arange(BEADS)
    angle = 2.0 * np.pi * ((b[:, None] * b[None, :]) % BEADS) / BEADS
    half = BEADS // 2
    basis = np.where(
        k == 0,
        1.0 / math.sqrt(BEADS),
        np.where(
            k < half,
            math.sqrt(2.0 / BEADS) * np.cos(angle),
            np.where(
                k == half, np.cos(angle) / math.sqrt(BEADS), math.sqrt(2.0 / BEADS) * np.sin(angle)
            ),
        ),
    )
    freq = 2.0 * CYCLE_FREQ * np.sin(np.pi * b / BEADS)
    spacing = b[None, :] / BEADS - np.arange(NC, dtype=np.float64)[:, None] / NC
    kernel = np.ones_like(spacing)
    for order in range(1, NC // 2):
        kernel = kernel + 2.0 * np.cos(2.0 * np.pi * order * spacing)
    kernel = kernel + np.cos(np.pi * NC * spacing)
    contract = kernel / BEADS

    h = 0.5 * TIME_STEP
    safe = np.where(freq > 0.0, freq, 1.0)
    qq = np.where(freq > 0.0, np.cos(safe * h), 1.0)
    qp = np.where(freq > 0.0, np.sin(safe * h) / safe, h)
    pq = np.where(freq > 0.0, -safe * np.sin(safe * h), 0.0)
    pp = qq
    keep = np.exp(-np.where(freq > 0.0, 2.0 * freq, CENTROID_FRICTION) * TIME_STEP)
    kick = np.sqrt(1.0 - keep * keep)
    full_qq = qq * qq + qp * keep * pq
    full_qp = qq * qp + qp * keep * pp
    full_qn = qp * kick
    full_pq = pq * qq + pp * keep * pq
    full_pp = pq * qp + pp * keep * pp
    full_pn = pp * kick
    q_rows = np.concatenate(
        [(basis * full_qq) @ basis.T, (basis * full_qp) @ basis.T, basis * full_qn], axis=1
    )
    p_rows = np.concatenate(
        [(basis * full_pq) @ basis.T, (basis * full_pp) @ basis.T, basis * full_pn], axis=1
    )
    c_rows = contract @ q_rows
    step = np.concatenate([c_rows, q_rows, p_rows], axis=0)
    return step.astype(np.float32), contract.astype(np.float32)


def whole_vmem():
    return pl.BlockSpec(memory_space=pltpu.VMEM)


def params(mebibytes=48):
    return pltpu.CompilerParams(vmem_limit_bytes=mebibytes * 1024 * 1024)


def smem():
    return pl.BlockSpec(memory_space=pltpu.SMEM)


def block_of(place_ref, r, rows):
    return pl.ds(pl.multiple_of((place_ref[0] ^ r) * rows, LANES), rows)


def exchange(blocks, axis):
    count = len(blocks)
    back = {0: blocks[0]}
    for r in range(count - 1, 0, -1):
        back[r] = lax.ppermute(blocks[r], axis, [(i, i ^ r) for i in range(count)])
    return [back[r] for r in range(count)]


def pack(place, positions, momenta, force_old, noise, groups):
    _, beads, atoms = positions.shape
    rows = atoms // groups

    def kernel(place_ref, q_ref, p_ref, f_ref, n_ref, *rest):
        outs, (p_buf, f_buf, sems) = rest[:groups], rest[groups:]
        loads = [
            pltpu.make_async_copy(p_ref, p_buf, sems.at[0]),
            pltpu.make_async_copy(f_ref, f_buf, sems.at[1]),
        ]
        for r in range(groups):
            at = block_of(place_ref, r, rows)
            for slot, (ref, first) in enumerate(((q_ref, 0), (n_ref, 6))):
                loads.append(
                    pltpu.make_async_copy(
                        ref.at[:, :, at], outs[r].at[pl.ds(first, 3)], sems.at[2 + 2 * r + slot]
                    )
                )
        for load in loads:
            load.start()
        loads[0].wait()
        loads[1].wait()
        for r in range(groups):
            at = block_of(place_ref, r, rows)
            for x in range(3):
                outs[r][3 + x] = p_buf[x, :, at] + 0.5 * TIME_STEP * f_buf[x, :, at]
        for load in loads[2:]:
            load.wait()

    return pl.pallas_call(
        kernel,
        out_shape=[jax.ShapeDtypeStruct((9, beads, rows), jnp.float32)] * groups,
        in_specs=[smem()] + [pl.BlockSpec(memory_space=pltpu.HBM)] * 4,
        out_specs=[whole_vmem()] * groups,
        scratch_shapes=[
            pltpu.VMEM((3, beads, atoms), jnp.float32),
            pltpu.VMEM((3, beads, atoms), jnp.float32),
            pltpu.SemaphoreType.DMA((2 + 2 * groups,)),
        ],
        compiler_params=params(60),
        name="pack",
    )(place, positions, momenta, force_old, noise)


def prepare(pair_list, mass, desc_w, hidden_one, place, rows):
    entries, atoms = pair_list.shape
    desc, env = desc_w.shape
    hid = hidden_one.shape[0]
    order = np.arange(env)
    order = (order % entries) * (env // entries) + order // entries
    permute = jnp.asarray(np.eye(env)[order], jnp.bfloat16)

    def kernel(place_ref, list_ref, mass_ref, w0_ref, w1_ref, order_ref, lists, own, masses, w0, w1):
        for t in range(atoms // LANES):
            at = pl.ds(t * LANES, LANES)
            lists[:, at] = list_ref[:, at] - t * LANES
        block = pl.ds(pl.multiple_of(place_ref[0] * rows, LANES), rows)
        own[...] = lists[:, block]
        masses[...] = mass_ref[:, block]
        w0[...] = lax.dot_general(
            order_ref[...],
            w0_ref[...],
            (((1,), (1,)), ((), ())),
            preferred_element_type=jnp.float32,
        ).astype(w0.dtype)
        w1[...] = w1_ref[...].astype(jnp.float32).T.astype(w1.dtype)

    return pl.pallas_call(
        kernel,
        out_shape=(
            jax.ShapeDtypeStruct((entries, atoms), jnp.int32),
            jax.ShapeDtypeStruct((entries, rows), jnp.int32),
            jax.ShapeDtypeStruct((1, rows), jnp.float32),
            jax.ShapeDtypeStruct((env, desc), jnp.bfloat16),
            jax.ShapeDtypeStruct((desc, hid), jnp.bfloat16),
        ),
        in_specs=[pl.BlockSpec(memory_space=pltpu.SMEM)] + [whole_vmem()] * 5,
        out_specs=(whole_vmem(),) * 5,
        compiler_params=params(),
        cost_estimate=pl.CostEstimate(
            flops=1_000_000_000, bytes_accessed=4_000_000, transcendentals=0
        ),
        name="prepare",
    )(place, pair_list, mass, desc_w, hidden_one, permute)


def contract(place, received, masses, table):
    groups = len(received)
    _, beads, rows = received[0].shape

    def kernel(place_ref, mass_ref, table_ref, own_ref, *rest):
        ins, (c_ref, first, last, fields, own, sem) = rest[: groups - 1], rest[groups - 1 :]
        load = pltpu.make_async_copy(own_ref, own, sem)
        load.start()
        mass = mass_ref[...]
        inverse = 1.0 / mass
        root = lax.rsqrt(mass)

        def scale(g, block):
            for x in range(3):
                fields[x, 0, g] = block[x]
                fields[x, 1, g] = block[3 + x] * inverse
                fields[x, 2, g] = block[6 + x] * root

        for r in range(1, groups):
            scale(place_ref[0] ^ r, ins[r - 1])
        load.wait()
        scale(place_ref[0], own)
        for x in range(3):
            out = jnp.dot(
                table_ref[...],
                fields[x].reshape(3 * BEADS, rows),
                precision=BEST,
                preferred_element_type=jnp.float32,
            )
            c_ref[x] = out
            first[x] = out[:, :EDGE]
            last[x] = out[:, rows - EDGE :]

    edge = jax.ShapeDtypeStruct((3, NC, EDGE), jnp.float32)
    return pl.pallas_call(
        kernel,
        out_shape=(
            jax.ShapeDtypeStruct((3, NC, rows), jnp.float32),
            edge,
            edge,
            jax.ShapeDtypeStruct((3, 3, groups, beads, rows), jnp.float32),
        ),
        in_specs=[smem()]
        + [whole_vmem()] * 2
        + [pl.BlockSpec(memory_space=pltpu.HBM)]
        + [whole_vmem()] * (groups - 1),
        out_specs=(whole_vmem(),) * 4,
        scratch_shapes=[pltpu.VMEM((9, beads, rows), jnp.float32), pltpu.SemaphoreType.DMA],
        compiler_params=params(),
        name="contract",
    )(place, masses, table, *received)


def transform(fields, masses, table):
    _, _, groups, beads, rows = fields.shape

    def kernel(fields_ref, mass_ref, table_ref, out_ref):
        mass = mass_ref[...]
        for x in range(3):
            out = jnp.dot(
                table_ref[...],
                fields_ref[x].reshape(3 * BEADS, rows),
                precision=BEST,
                preferred_element_type=jnp.float32,
            )
            out_ref[:, x] = out[:BEADS].reshape(groups, beads, rows)
            out_ref[:, 3 + x] = (out[BEADS:] * mass).reshape(groups, beads, rows)

    return pl.pallas_call(
        kernel,
        out_shape=jax.ShapeDtypeStruct((groups, 6, beads, rows), jnp.float32),
        in_specs=[whole_vmem()] * 3,
        out_specs=whole_vmem(),
        compiler_params=params(),
        cost_estimate=pl.CostEstimate(
            flops=1_000_000_000, bytes_accessed=2_000_000, transcendentals=0
        ),
        name="transform",
    )(fields, masses, table)


def inverse_of(value):
    estimate = pl.reciprocal(value, approx=True)
    return estimate * (2.0 - value * estimate)


def banded(windows, lane, low, high):
    below, middle, above = [
        jnp.take_along_axis(w, lane, axis=1, mode="promise_in_bounds") for w in windows
    ]
    return jnp.where(low, below, jnp.where(high, above, middle))


def entries_of(list_ref, e, base):
    place = list_ref[pl.ds(e, 8), pl.ds(base, LANES)]
    return place & (LANES - 1), place < LANES, place >= 2 * LANES


def on_sublanes(row):
    return jnp.broadcast_to(row, (8, LANES))


def env_tile(windows, list_ref, base, envs, inputs):
    entries = list_ref.shape[0]
    for e in range(0, entries, 8):
        lane, low, high = entries_of(list_ref, e, base)
        for c in range(NC):
            apart = []
            for x in range(3):
                tiles = windows(c, x)
                apart.append(banded(tiles, lane, low, high) - tiles[1])
            square = apart[0] * apart[0] + apart[1] * apart[1] + apart[2] * apart[2]
            close = inverse_of(1.0 + square)
            for x, value in enumerate(apart + [close]):
                envs[pl.ds(x * entries + e, 8), pl.ds(c * LANES, LANES)] = value
    for c in range(NC):
        at = pl.ds(c * LANES, LANES)
        inputs[at, :] = envs[:, at].T.astype(jnp.bfloat16)


def network(inputs_ref, weights, forces, cols=1024, chunk=256):
    w0_ref, w1_ref, w2_ref, w3_ref, wo_ref = weights
    desc = w0_ref.shape[1]
    for c in range(0, NC * LANES, cols):
        inputs = inputs_ref[pl.ds(c, cols), :]
        total = None
        for f in range(0, desc, chunk):
            size = min(chunk, desc - f)
            first = jnp.dot(inputs, w0_ref[:, pl.ds(f, size)], preferred_element_type=jnp.float32)
            first = jnp.tanh(first.astype(jnp.bfloat16))
            part = jnp.dot(first, w1_ref[pl.ds(f, size), :], preferred_element_type=jnp.float32)
            total = part if total is None else total + part
        layer = jnp.tanh(total).astype(jnp.bfloat16)
        for ref in (w2_ref, w3_ref):
            layer = jnp.tanh(
                jnp.dot(layer, ref[...], preferred_element_type=jnp.float32)
            ).astype(jnp.bfloat16)
        out = lax.dot_general(
            wo_ref[...], layer, (((1,), (1,)), ((), ())), preferred_element_type=jnp.float32
        )
        for part in range(cols // LANES):
            for x in range(3):
                forces[pl.ds(c // LANES + part, 1), pl.ds(x * LANES, LANES)] = out[
                    x : x + 1, part * LANES : (part + 1) * LANES
                ]


def neural_scratch(env):
    return [
        pltpu.VMEM((2, env, NC * LANES), jnp.float32),
        pltpu.VMEM((2, NC * LANES, env), jnp.bfloat16),
    ]


def neural(contracted, lower, upper, lists, weights, spread, groups):
    _, _, rows = contracted.shape
    beads = BEADS // groups
    tiles = rows // LANES

    def kernel(
        c_ref, low_ref, up_ref, list_ref, w0, w1, w2, w3, wo, spread_ref,
        out_ref, forces, envs, inputs,
    ):
        def tile(x, c, t):
            if t < 0:
                ref, at = low_ref, 0
            elif t >= tiles:
                ref, at = up_ref, 0
            else:
                ref, at = c_ref, t * LANES
            return on_sublanes(ref[x, pl.ds(c, 1), pl.ds(at, LANES)])

        for t in range(tiles):
            slot = t % 2
            windows = lambda c, x: [tile(x, c, t + v) for v in (-1, 0, 1)]
            env_tile(windows, list_ref, t * LANES, envs.at[slot], inputs.at[slot])
            network(inputs.at[slot], (w0, w1, w2, w3, wo), forces.at[slot])
            for x in range(3):
                at = pl.ds(x * LANES, LANES)
                wide = spread_ref[0] * forces[slot, pl.ds(0, 1), at]
                for c in range(1, NC):
                    wide = wide + spread_ref[c] * forces[slot, pl.ds(c, 1), at]
                out_ref[:, x, :, pl.ds(t * LANES, LANES)] = wide.reshape(groups, beads, LANES)

    return pl.pallas_call(
        kernel,
        out_shape=jax.ShapeDtypeStruct((groups, 3, beads, rows), jnp.float32),
        in_specs=[whole_vmem()] * 10,
        out_specs=whole_vmem(),
        scratch_shapes=[pltpu.VMEM((2, NC, 3 * LANES), jnp.float32)]
        + neural_scratch(weights[0].shape[0]),
        compiler_params=params(),
        cost_estimate=pl.CostEstimate(
            flops=12_000_000_000, bytes_accessed=4_000_000, transcendentals=0
        ),
        name="neural",
    )(contracted, lower, upper, lists, *weights, spread)


def add_pairs(sums, e, b, apart, close):
    for x in range(3):
        part = apart[x] * close
        sums[x, b] = part if e == 0 else sums[x, b] + part


def total_of(sums, x):
    total = sums[x, :, 0, :]
    for s in range(1, 8):
        total = total + sums[x, :, s, :]
    return total


def third_of(one, two):
    return ((one & 2047) << 20) + ((two & 511) << 11)


def assemble(fields):
    groups, _, beads, rows = fields.shape
    atoms = groups * rows
    half = 2**19
    top = float(half - 1)

    def kernel(in_ref, newq, words, unit_ref, rims):
        largest = jnp.zeros((beads, rows), jnp.float32)
        for g in range(groups):
            at = pl.ds(g * rows, rows)
            for x in range(3):
                value = in_ref[g, x]
                newq[x, :, at] = value
                largest = jnp.maximum(largest, jnp.abs(value))
        limit = jnp.maximum(jnp.max(largest, keepdims=True), 1e-30)
        to_fixed = top / limit
        unit_ref[...] = jnp.broadcast_to(limit / (top * 2048.0), (beads, LANES))
        for g in range(groups):
            at = pl.ds(g * rows, rows)
            one, two, three = [
                jnp.floor(in_ref[g, x] * to_fixed + 0.5).astype(jnp.int32) for x in range(3)
            ]
            three = three + half
            words[0, :, at] = (one << 11) + (three >> 9)
            words[1, :, at] = (two << 11) + (three & 511)
            words[2, :, at] = three << 11
        for rim, t in enumerate((0, LANES, atoms - 2 * LANES, atoms - LANES)):
            rims[rim] = newq[:, :, pl.ds(t, LANES)]

    return pl.pallas_call(
        kernel,
        out_shape=(
            jax.ShapeDtypeStruct((3, beads, atoms), jnp.float32),
            jax.ShapeDtypeStruct((3, beads, atoms), jnp.int32),
            jax.ShapeDtypeStruct((beads, LANES), jnp.float32),
            jax.ShapeDtypeStruct((4, 3, beads, LANES), jnp.float32),
        ),
        in_specs=[whole_vmem()],
        out_specs=(whole_vmem(),) * 4,
        compiler_params=params(),
        name="assemble",
    )(fields)


def pair_inner(words, unit, lists):
    _, beads, atoms = words.shape
    entries = lists.shape[0]

    def kernel(words_ref, unit_ref, list_ref, pair, sums):
        unit_row = unit_ref[...]
        unit_square = on_sublanes(unit_ref[pl.ds(0, 1), :])
        unit_square = unit_square * unit_square

        @pl.loop(1, atoms // LANES - 1)
        def _(t):
            base = pl.multiple_of(t * LANES, LANES)

            def row(w, b, v):
                return on_sublanes(
                    words_ref[w, pl.ds(b, 1), pl.ds(base + (v - 1) * LANES, LANES)]
                )

            for e in range(0, entries, 8):
                lane, low, high = entries_of(list_ref, e, base)
                for b in range(beads):
                    windows = [[row(w, b, v) for v in range(3)] for w in range(2)]
                    one, two = [banded(windows[w], lane, low, high) for w in range(2)]
                    near = (one, two, third_of(one, two))
                    own = (windows[0][1], windows[1][1], row(2, b, 1))
                    apart = [(n - o).astype(jnp.float32) for n, o in zip(near, own)]
                    square = apart[0] * apart[0] + apart[1] * apart[1] + apart[2] * apart[2]
                    close = inverse_of(1.0 + square * unit_square)
                    add_pairs(sums, e, b, apart, close)
            for x in range(3):
                pair[x, :, pl.ds(base, LANES)] = (PAIR_STRENGTH * unit_row) * total_of(sums, x)

    return pl.pallas_call(
        kernel,
        out_shape=jax.ShapeDtypeStruct((3, beads, atoms), jnp.float32),
        in_specs=[whole_vmem()] * 3,
        out_specs=whole_vmem(),
        scratch_shapes=[pltpu.VMEM((3, beads, 8, LANES), jnp.float32)],
        compiler_params=params(),
        cost_estimate=pl.CostEstimate(
            flops=15_000_000_000, bytes_accessed=4_000_000, transcendentals=0
        ),
        name="pair_inner",
    )(words, unit, lists)


def finish(pair, rims, lower, upper, lists, fields, spread):
    groups, _, beads, rows = fields.shape
    atoms = groups * rows

    def kernel(
        pair_ref, rims_ref, low_ref, up_ref, list_ref, in_ref, spread_ref, newp, newf, sums
    ):
        def edge(base, tiles):
            for e in range(0, list_ref.shape[0], 8):
                lane, low, high = entries_of(list_ref, e, base)
                for b in range(beads):
                    apart = []
                    for x in range(3):
                        windows = [on_sublanes(tile[x, pl.ds(b, 1), :]) for tile in tiles]
                        apart.append(banded(windows, lane, low, high) - windows[1])
                    square = apart[0] * apart[0] + apart[1] * apart[1] + apart[2] * apart[2]
                    add_pairs(sums, e, b, apart, inverse_of(1.0 + square))
            for x in range(3):
                newf[x, :, pl.ds(base, LANES)] = PAIR_STRENGTH * total_of(sums, x)

        newf[...] = pair_ref[...]
        edge(0, [low_ref, rims_ref.at[0], rims_ref.at[1]])
        edge(atoms - LANES, [rims_ref.at[2], rims_ref.at[3], up_ref])
        for g in range(groups):
            at = pl.ds(g * rows, rows)
            for x in range(3):
                force = newf[x, :, at] + spread_ref[g, x]
                newf[x, :, at] = force
                newp[x, :, at] = in_ref[g, 3 + x] + 0.5 * TIME_STEP * force

    out = jax.ShapeDtypeStruct((3, beads, atoms), jnp.float32)
    return pl.pallas_call(
        kernel,
        out_shape=(out,) * 2,
        in_specs=[whole_vmem()] * 7,
        out_specs=(whole_vmem(),) * 2,
        scratch_shapes=[pltpu.VMEM((3, beads, 8, LANES), jnp.float32)],
        compiler_params=params(),
        name="finish",
    )(pair, rims, lower, upper, lists, fields, spread)


def body(
    positions,
    momenta,
    force_old,
    noise,
    mass,
    pair_list,
    desc_w,
    hidden_one,
    hidden_two,
    hidden_three,
    out_w,
):
    beads, _, atoms = positions.shape
    groups = lax.axis_size("bead")
    slabs = lax.axis_size(("slab", "grp"))
    rows = atoms // groups
    place = lax.axis_index("bead").astype(jnp.int32)[None]
    step, kernel = step_tables()

    swap = lambda field: jnp.transpose(field, (1, 0, 2))
    sends = pack(place, swap(positions), swap(momenta), swap(force_old), swap(noise), groups)
    received = exchange(sends, "bead")

    lists, block_lists, masses, env_w, w1 = prepare(
        pair_list.T, mass[None, :], desc_w.T, hidden_one.T, place, rows
    )
    received, lists, block_lists, masses, env_w, w1 = lax.optimization_barrier(
        (received, lists, block_lists, masses, env_w, w1)
    )
    weights = (env_w, w1, hidden_two, hidden_three, out_w.T)

    contracted, first, last, scaled = contract(place, received, masses, jnp.asarray(step[:NC]))
    ring = [
        (g * slabs + s, ((g + 1) % groups) * slabs + (s + (g + 1) // groups) % slabs)
        for g in range(groups)
        for s in range(slabs)
    ]
    back = [(j, i) for i, j in ring]
    every = ("bead", "slab", "grp")
    lower = lax.ppermute(last, every, ring)
    upper = lax.ppermute(first, every, back)
    returns = transform(scaled, masses, jnp.asarray(step[NC:]))
    returns, lower, upper = lax.optimization_barrier((returns, lower, upper))
    fields = lax.all_to_all(returns, "bead", split_axis=0, concat_axis=0, tiled=True)

    coefs = jnp.asarray(kernel * np.float32(BEADS / NC))
    coefs = jnp.broadcast_to(coefs[:, :, None], (NC, BEADS, LANES))
    spread = neural(contracted, lower, upper, block_lists, weights, coefs, groups)
    fields, spread = lax.optimization_barrier((fields, spread))
    spread = lax.all_to_all(spread, "bead", split_axis=0, concat_axis=0, tiled=True)

    new_q, words, unit, rims = assemble(fields)
    slab_ring = [(s, (s + 1) % slabs) for s in range(slabs)]
    slab_back = [(j, i) for i, j in slab_ring]
    q_lower = lax.ppermute(rims[3], ("slab", "grp"), slab_ring)
    q_upper = lax.ppermute(rims[0], ("slab", "grp"), slab_back)

    pair = pair_inner(words, unit, lists)
    new_p, force = finish(pair, rims, q_lower, q_upper, lists, fields, spread)
    return tuple(swap(out) for out in (new_q, new_p, force))


def solution(mesh):
    field = P("bead", None, ("slab", "grp"))
    placed = (field,) * 4 + (P(("slab", "grp")), P(("slab", "grp"), None)) + (P(),) * 5
    return jax.shard_map(
        body, mesh=mesh, in_specs=placed, out_specs=(field,) * 3, check_vma=False
    )
```

```python
import math

import jax
import jax.numpy as jnp
import numpy as np
from jax import lax
from jax.experimental import pallas as pl
from jax.experimental.pallas import tpu as pltpu
from jax.sharding import PartitionSpec as P

BEADS = 64
NC = 8
EDGE = 128
LANES = 128

TIME_STEP = 0.1
CYCLE_FREQ = 5.0
CENTROID_FRICTION = 1.0
PAIR_STRENGTH = 0.5

BEST = lax.Precision.HIGHEST


def step_tables():
    b = np.arange(BEADS, dtype=np.float64)
    k = np.arange(BEADS)
    angle = 2.0 * np.pi * ((b[:, None] * b[None, :]) % BEADS) / BEADS
    half = BEADS // 2
    basis = np.where(
        k == 0,
        1.0 / math.sqrt(BEADS),
        np.where(
            k < half,
            math.sqrt(2.0 / BEADS) * np.cos(angle),
            np.where(
                k == half, np.cos(angle) / math.sqrt(BEADS), math.sqrt(2.0 / BEADS) * np.sin(angle)
            ),
        ),
    )
    freq = 2.0 * CYCLE_FREQ * np.sin(np.pi * b / BEADS)
    spacing = b[None, :] / BEADS - np.arange(NC, dtype=np.float64)[:, None] / NC
    kernel = np.ones_like(spacing)
    for order in range(1, NC // 2):
        kernel = kernel + 2.0 * np.cos(2.0 * np.pi * order * spacing)
    kernel = kernel + np.cos(np.pi * NC * spacing)
    contract = kernel / BEADS

    h = 0.5 * TIME_STEP
    safe = np.where(freq > 0.0, freq, 1.0)
    qq = np.where(freq > 0.0, np.cos(safe * h), 1.0)
    qp = np.where(freq > 0.0, np.sin(safe * h) / safe, h)
    pq = np.where(freq > 0.0, -safe * np.sin(safe * h), 0.0)
    pp = qq
    keep = np.exp(-np.where(freq > 0.0, 2.0 * freq, CENTROID_FRICTION) * TIME_STEP)
    kick = np.sqrt(1.0 - keep * keep)
    full_qq = qq * qq + qp * keep * pq
    full_qp = qq * qp + qp * keep * pp
    full_qn = qp * kick
    full_pq = pq * qq + pp * keep * pq
    full_pp = pq * qp + pp * keep * pp
    full_pn = pp * kick
    q_rows = np.concatenate(
        [(basis * full_qq) @ basis.T, (basis * full_qp) @ basis.T, basis * full_qn], axis=1
    )
    p_rows = np.concatenate(
        [(basis * full_pq) @ basis.T, (basis * full_pp) @ basis.T, basis * full_pn], axis=1
    )
    c_rows = contract @ q_rows
    step = np.concatenate([c_rows, q_rows, p_rows], axis=0)
    return step.astype(np.float32), contract.astype(np.float32)


def whole_vmem():
    return pl.BlockSpec(memory_space=pltpu.VMEM)


def params(mebibytes=48):
    return pltpu.CompilerParams(vmem_limit_bytes=mebibytes * 1024 * 1024)


def smem():
    return pl.BlockSpec(memory_space=pltpu.SMEM)


def block_of(place_ref, r, rows):
    return pl.ds(pl.multiple_of((place_ref[0] ^ r) * rows, LANES), rows)


def exchange(blocks, axis):
    count = len(blocks)
    back = {0: blocks[0]}
    for r in range(count - 1, 0, -1):
        back[r] = lax.ppermute(blocks[r], axis, [(i, i ^ r) for i in range(count)])
    return [back[r] for r in range(count)]


def pack(place, positions, momenta, force_old, noise, groups):
    _, beads, atoms = positions.shape
    rows = atoms // groups

    def kernel(place_ref, q_ref, p_ref, f_ref, n_ref, *rest):
        outs, (p_buf, f_buf, sems) = rest[:groups], rest[groups:]
        loads = [
            pltpu.make_async_copy(p_ref, p_buf, sems.at[0]),
            pltpu.make_async_copy(f_ref, f_buf, sems.at[1]),
        ]
        for r in range(groups):
            at = block_of(place_ref, r, rows)
            for slot, (ref, first) in enumerate(((q_ref, 0), (n_ref, 6))):
                loads.append(
                    pltpu.make_async_copy(
                        ref.at[:, :, at], outs[r].at[pl.ds(first, 3)], sems.at[2 + 2 * r + slot]
                    )
                )
        for load in loads:
            load.start()
        loads[0].wait()
        loads[1].wait()
        for r in range(groups):
            at = block_of(place_ref, r, rows)
            for x in range(3):
                outs[r][3 + x] = p_buf[x, :, at] + 0.5 * TIME_STEP * f_buf[x, :, at]
        for load in loads[2:]:
            load.wait()

    return pl.pallas_call(
        kernel,
        out_shape=[jax.ShapeDtypeStruct((9, beads, rows), jnp.float32)] * groups,
        in_specs=[smem()] + [pl.BlockSpec(memory_space=pltpu.HBM)] * 4,
        out_specs=[whole_vmem()] * groups,
        scratch_shapes=[
            pltpu.VMEM((3, beads, atoms), jnp.float32),
            pltpu.VMEM((3, beads, atoms), jnp.float32),
            pltpu.SemaphoreType.DMA((2 + 2 * groups,)),
        ],
        compiler_params=params(60),
        name="pack",
    )(place, positions, momenta, force_old, noise)


def prepare(pair_list, mass, desc_w, hidden_one, place, rows):
    entries, atoms = pair_list.shape
    desc, env = desc_w.shape
    hid = hidden_one.shape[0]
    order = np.arange(env)
    order = (order % entries) * (env // entries) + order // entries
    permute = jnp.asarray(np.eye(env)[order], jnp.bfloat16)

    def kernel(place_ref, list_ref, mass_ref, w0_ref, w1_ref, order_ref, lists, own, masses, w0, w1):
        for t in range(atoms // LANES):
            at = pl.ds(t * LANES, LANES)
            lists[:, at] = list_ref[:, at] - t * LANES
        block = pl.ds(pl.multiple_of(place_ref[0] * rows, LANES), rows)
        own[...] = lists[:, block]
        masses[...] = mass_ref[:, block]
        w0[...] = lax.dot_general(
            order_ref[...],
            w0_ref[...],
            (((1,), (1,)), ((), ())),
            preferred_element_type=jnp.float32,
        ).astype(w0.dtype)
        w1[...] = w1_ref[...].astype(jnp.float32).T.astype(w1.dtype)

    return pl.pallas_call(
        kernel,
        out_shape=(
            jax.ShapeDtypeStruct((entries, atoms), jnp.int32),
            jax.ShapeDtypeStruct((entries, rows), jnp.int32),
            jax.ShapeDtypeStruct((1, rows), jnp.float32),
            jax.ShapeDtypeStruct((env, desc), jnp.bfloat16),
            jax.ShapeDtypeStruct((desc, hid), jnp.bfloat16),
        ),
        in_specs=[pl.BlockSpec(memory_space=pltpu.SMEM)] + [whole_vmem()] * 5,
        out_specs=(whole_vmem(),) * 5,
        compiler_params=params(),
        cost_estimate=pl.CostEstimate(
            flops=1_000_000_000, bytes_accessed=4_000_000, transcendentals=0
        ),
        name="prepare",
    )(place, pair_list, mass, desc_w, hidden_one, permute)


def contract(place, received, masses, table):
    groups = len(received)
    _, beads, rows = received[0].shape

    def kernel(place_ref, mass_ref, table_ref, own_ref, *rest):
        ins, (c_ref, first, last, fields, own, sem) = rest[: groups - 1], rest[groups - 1 :]
        ins = ins[::-1]
        load = pltpu.make_async_copy(own_ref, own, sem)
        load.start()
        mass = mass_ref[...]
        inverse = 1.0 / mass
        root = lax.rsqrt(mass)

        def scale(g, block):
            for x in range(3):
                fields[x, 0, g] = block[x]
                fields[x, 1, g] = block[3 + x] * inverse
                fields[x, 2, g] = block[6 + x] * root

        for r in range(1, groups):
            scale(place_ref[0] ^ r, ins[r - 1])
        load.wait()
        scale(place_ref[0], own)
        for x in range(3):
            out = jnp.dot(
                table_ref[...],
                fields[x].reshape(3 * BEADS, rows),
                precision=BEST,
                preferred_element_type=jnp.float32,
            )
            c_ref[x] = out
            first[x] = out[:, :EDGE]
            last[x] = out[:, rows - EDGE :]

    edge = jax.ShapeDtypeStruct((3, NC, EDGE), jnp.float32)
    return pl.pallas_call(
        kernel,
        out_shape=(
            jax.ShapeDtypeStruct((3, NC, rows), jnp.float32),
            edge,
            edge,
            jax.ShapeDtypeStruct((3, 3, groups, beads, rows), jnp.float32),
        ),
        in_specs=[smem()]
        + [whole_vmem()] * 2
        + [pl.BlockSpec(memory_space=pltpu.HBM)]
        + [whole_vmem()] * (groups - 1),
        out_specs=(whole_vmem(),) * 4,
        scratch_shapes=[pltpu.VMEM((9, beads, rows), jnp.float32), pltpu.SemaphoreType.DMA],
        compiler_params=params(),
        name="contract",
    )(place, masses, table, received[0], *received[:0:-1])


def transform(fields, masses, table):
    _, _, groups, beads, rows = fields.shape

    def kernel(fields_ref, mass_ref, table_ref, out_ref):
        mass = mass_ref[...]
        for x in range(3):
            out = jnp.dot(
                table_ref[...],
                fields_ref[x].reshape(3 * BEADS, rows),
                precision=BEST,
                preferred_element_type=jnp.float32,
            )
            out_ref[:, x] = out[:BEADS].reshape(groups, beads, rows)
            out_ref[:, 3 + x] = (out[BEADS:] * mass).reshape(groups, beads, rows)

    return pl.pallas_call(
        kernel,
        out_shape=jax.ShapeDtypeStruct((groups, 6, beads, rows), jnp.float32),
        in_specs=[whole_vmem()] * 3,
        out_specs=whole_vmem(),
        compiler_params=params(),
        cost_estimate=pl.CostEstimate(
            flops=1_000_000_000, bytes_accessed=2_000_000, transcendentals=0
        ),
        name="transform",
    )(fields, masses, table)


def inverse_of(value):
    estimate = pl.reciprocal(value, approx=True)
    return estimate * (2.0 - value * estimate)


def banded(windows, lane, low, high):
    below, middle, above = [
        jnp.take_along_axis(w, lane, axis=1, mode="promise_in_bounds") for w in windows
    ]
    return jnp.where(low, below, jnp.where(high, above, middle))


def entries_of(list_ref, e, base):
    place = list_ref[pl.ds(e, 8), pl.ds(base, LANES)]
    return place & (LANES - 1), place < LANES, place >= 2 * LANES


def on_sublanes(row):
    return jnp.broadcast_to(row, (8, LANES))


def env_units(windows, list_ref, base, envs, inputs):
    entries = list_ref.shape[0]
    for e in range(0, entries, 8):
        lane, low, high = entries_of(list_ref, e, base)
        for c in range(NC):
            apart = []
            for x in range(3):
                tiles = windows(c, x)
                apart.append(banded(tiles, lane, low, high) - tiles[1])
            square = apart[0] * apart[0] + apart[1] * apart[1] + apart[2] * apart[2]
            close = inverse_of(1.0 + square)
            for x, value in enumerate(apart + [close]):
                envs[pl.ds(x * entries + e, 8), pl.ds(c * LANES, LANES)] = value
            yield
    for c in range(NC):
        at = pl.ds(c * LANES, LANES)
        inputs[at, :] = envs[:, at].T.astype(jnp.bfloat16)
        yield


def network(inputs_ref, weights, out_ref, base, units, chunk=256):
    w0_ref, w1_ref, w2_ref, w3_ref, wo_ref = weights
    desc = w0_ref.shape[1]
    inputs = inputs_ref[...]
    total = None
    for f in range(0, desc, chunk):
        size = min(chunk, desc - f)
        first = jnp.dot(inputs, w0_ref[:, pl.ds(f, size)], preferred_element_type=jnp.float32)
        first = jnp.tanh(first.astype(jnp.bfloat16))
        part = jnp.dot(first, w1_ref[pl.ds(f, size), :], preferred_element_type=jnp.float32)
        total = part if total is None else total + part
        for _ in range(6):
            next(units, None)
    layer = jnp.tanh(total).astype(jnp.bfloat16)
    for ref in (w2_ref, w3_ref):
        layer = jnp.tanh(jnp.dot(layer, ref[...], preferred_element_type=jnp.float32)).astype(
            jnp.bfloat16
        )
    out = lax.dot_general(
        wo_ref[...], layer, (((1,), (1,)), ((), ())), preferred_element_type=jnp.float32
    )
    for c in range(NC):
        for x in range(3):
            out_ref[x, pl.ds(c, 1), pl.ds(base, LANES)] = out[
                x : x + 1, c * LANES : (c + 1) * LANES
            ]


def neural_scratch(env):
    return [
        pltpu.VMEM((2, env, NC * LANES), jnp.float32),
        pltpu.VMEM((2, NC * LANES, env), jnp.bfloat16),
    ]


def neural(contracted, lower, upper, lists, weights):
    _, _, rows = contracted.shape
    tiles = rows // LANES

    def kernel(
        c_ref, low_ref, up_ref, list_ref, w0, w1, w2, w3, wo, out_ref, envs, inputs
    ):
        def tile(x, c, t):
            if t < 0:
                ref, at = low_ref, 0
            elif t >= tiles:
                ref, at = up_ref, 0
            else:
                ref, at = c_ref, t * LANES
            return on_sublanes(ref[x, pl.ds(c, 1), pl.ds(at, LANES)])

        def units_of(t):
            if t >= tiles:
                return iter(())
            windows = lambda c, x: [tile(x, c, t + v) for v in (-1, 0, 1)]
            slot = t % 2
            return env_units(windows, list_ref, t * LANES, envs.at[slot], inputs.at[slot])

        for _ in units_of(0):
            pass
        for t in range(tiles):
            units = units_of(t + 1)
            network(inputs.at[t % 2], (w0, w1, w2, w3, wo), out_ref, t * LANES, units)
            for _ in units:
                pass

    return pl.pallas_call(
        kernel,
        out_shape=jax.ShapeDtypeStruct((3, NC, rows), jnp.float32),
        in_specs=[whole_vmem()] * 9,
        out_specs=whole_vmem(),
        scratch_shapes=neural_scratch(weights[0].shape[0]),
        compiler_params=params(),
        cost_estimate=pl.CostEstimate(
            flops=12_000_000_000, bytes_accessed=4_000_000, transcendentals=0
        ),
        name="neural",
    )(contracted, lower, upper, lists, *weights)


def add_pairs(sums, e, b, apart, close):
    for x in range(3):
        part = apart[x] * close
        sums[x, b] = part if e == 0 else sums[x, b] + part


def total_of(sums, x):
    total = sums[x, :, 0, :]
    for s in range(1, 8):
        total = total + sums[x, :, s, :]
    return total


def assemble(fields):
    groups, _, beads, rows = fields.shape
    atoms = groups * rows
    half = beads // 2
    top = float(2**15 - 1)

    def kernel(in_ref, newq, words, fixed, unit_ref, rims):
        largest = jnp.zeros((beads, rows), jnp.float32)
        for g in range(groups):
            at = pl.ds(g * rows, rows)
            for x in range(3):
                value = in_ref[g, x]
                newq[x, :, at] = value
                largest = jnp.maximum(largest, jnp.abs(value))
        limit = jnp.maximum(jnp.max(largest, keepdims=True), 1e-30)
        to_fixed = top / limit
        unit_ref[...] = jnp.broadcast_to(limit / (top * 65536.0), (beads, LANES))
        for g in range(groups):
            at = pl.ds(g * rows, rows)
            for x in range(3):
                value = jnp.floor(in_ref[g, x] * to_fixed + 0.5)
                fixed[x, :, at] = value * 65536.0
                value = value.astype(jnp.int32)
                words[x, :, at] = (value[:half] << 16) | (value[half:] & 65535)
        for rim, t in enumerate((0, LANES, atoms - 2 * LANES, atoms - LANES)):
            rims[rim] = newq[:, :, pl.ds(t, LANES)]

    return pl.pallas_call(
        kernel,
        out_shape=(
            jax.ShapeDtypeStruct((3, beads, atoms), jnp.float32),
            jax.ShapeDtypeStruct((3, half, atoms), jnp.int32),
            jax.ShapeDtypeStruct((3, beads, atoms), jnp.float32),
            jax.ShapeDtypeStruct((beads, LANES), jnp.float32),
            jax.ShapeDtypeStruct((4, 3, beads, LANES), jnp.float32),
        ),
        in_specs=[whole_vmem()],
        out_specs=(whole_vmem(),) * 5,
        compiler_params=params(),
        name="assemble",
    )(fields)


def pair_inner(words, fixed, unit, lists):
    _, beads, atoms = fixed.shape
    half = beads // 2
    entries = lists.shape[0]

    def kernel(words_ref, fixed_ref, unit_ref, list_ref, pair, sums):
        unit_row = unit_ref[...]
        unit_square = on_sublanes(unit_ref[pl.ds(0, 1), :])
        unit_square = unit_square * unit_square

        @pl.loop(1, atoms // LANES - 1)
        def _(t):
            base = pl.multiple_of(t * LANES, LANES)

            def row(ref, x, b, v):
                return on_sublanes(ref[x, pl.ds(b, 1), pl.ds(base + (v - 1) * LANES, LANES)])

            for e in range(0, entries, 8):
                lane, low, high = entries_of(list_ref, e, base)
                for b in range(half):
                    both = [
                        banded([row(words_ref, x, b, v) for v in range(3)], lane, low, high)
                        for x in range(3)
                    ]
                    for bead, near in ((b, [w & -65536 for w in both]),
                                       (b + half, [w << 16 for w in both])):
                        apart = [
                            near[x].astype(jnp.float32) - row(fixed_ref, x, bead, 1)
                            for x in range(3)
                        ]
                        square = apart[0] * apart[0] + apart[1] * apart[1] + apart[2] * apart[2]
                        close = inverse_of(1.0 + square * unit_square)
                        add_pairs(sums, e, bead, apart, close)
            for x in range(3):
                pair[x, :, pl.ds(base, LANES)] = (PAIR_STRENGTH * unit_row) * total_of(sums, x)

    return pl.pallas_call(
        kernel,
        out_shape=jax.ShapeDtypeStruct((3, beads, atoms), jnp.float32),
        in_specs=[whole_vmem()] * 4,
        out_specs=whole_vmem(),
        scratch_shapes=[pltpu.VMEM((3, beads, 8, LANES), jnp.float32)],
        compiler_params=params(),
        cost_estimate=pl.CostEstimate(
            flops=15_000_000_000, bytes_accessed=4_000_000, transcendentals=0
        ),
        name="pair_inner",
    )(words, fixed, unit, lists)


def finish(place, pair, rims, lower, upper, lists, fields, neural_parts, partners, coefs):
    groups, _, beads, rows = fields.shape
    atoms = groups * rows
    sizes = [part.shape[0] for part in neural_parts]

    def kernel(
        place_ref, pair_ref, rims_ref, low_ref, up_ref, list_ref, in_ref, coef_ref, *rest
    ):
        parts, (newp, newf, sums) = rest[: len(sizes)], rest[len(sizes) :]
        own = place_ref[0]

        def edge(base, tiles):
            for e in range(0, list_ref.shape[0], 8):
                lane, low, high = entries_of(list_ref, e, base)
                for b in range(beads):
                    apart = []
                    for x in range(3):
                        windows = [on_sublanes(tile[x, pl.ds(b, 1), :]) for tile in tiles]
                        apart.append(banded(windows, lane, low, high) - windows[1])
                    square = apart[0] * apart[0] + apart[1] * apart[1] + apart[2] * apart[2]
                    add_pairs(sums, e, b, apart, inverse_of(1.0 + square))
            for x in range(3):
                newf[x, :, pl.ds(base, LANES)] = PAIR_STRENGTH * total_of(sums, x)

        newf[...] = pair_ref[...]
        edge(0, [low_ref, rims_ref.at[0], rims_ref.at[1]])
        edge(atoms - LANES, [rims_ref.at[2], rims_ref.at[3], up_ref])
        coef = [coef_ref[c, own] for c in range(NC)]
        blocks = [part.at[i] for part, size in zip(parts, sizes) for i in range(size)]
        for r, block in zip(partners, blocks):
            g = own ^ r
            for t in range(0, rows, LANES):
                at = pl.ds(pl.multiple_of(g * rows + t, LANES), LANES)
                inner = pl.ds(t, LANES)
                for x in range(3):
                    force = newf[x, :, at]
                    for c in range(NC):
                        force = force + coef[c] * block[x, pl.ds(c, 1), inner]
                    newf[x, :, at] = force
                    newp[x, :, at] = in_ref[g, 3 + x, :, inner] + 0.5 * TIME_STEP * force

    out = jax.ShapeDtypeStruct((3, beads, atoms), jnp.float32)
    return pl.pallas_call(
        kernel,
        out_shape=(out,) * 2,
        in_specs=[smem()] + [whole_vmem()] * (7 + len(sizes)),
        out_specs=(whole_vmem(),) * 2,
        scratch_shapes=[pltpu.VMEM((3, beads, 8, LANES), jnp.float32)],
        compiler_params=params(),
        name="finish",
    )(place, pair, rims, lower, upper, lists, fields, coefs, *neural_parts)


def gather_blocks(block, axis):
    count = lax.axis_size(axis)
    have, partners = block[None], [0]
    bit = count // 2
    while bit:
        got = lax.ppermute(have, axis, [(i, i ^ bit) for i in range(count)])
        partners = partners + [r ^ bit for r in partners]
        bit //= 2
        if bit:
            have = jnp.concatenate([have, got], axis=0)
    return (have, got), partners


def body(
    positions,
    momenta,
    force_old,
    noise,
    mass,
    pair_list,
    desc_w,
    hidden_one,
    hidden_two,
    hidden_three,
    out_w,
):
    beads, _, atoms = positions.shape
    groups = lax.axis_size("bead")
    slabs = lax.axis_size(("slab", "grp"))
    rows = atoms // groups
    place = lax.axis_index("bead").astype(jnp.int32)[None]
    step, kernel = step_tables()

    swap = lambda field: jnp.transpose(field, (1, 0, 2))
    sends = pack(place, swap(positions), swap(momenta), swap(force_old), swap(noise), groups)
    received = exchange(sends, "bead")

    lists, block_lists, masses, env_w, w1 = prepare(
        pair_list.T, mass[None, :], desc_w.T, hidden_one.T, place, rows
    )
    received, lists, block_lists, masses, env_w, w1 = lax.optimization_barrier(
        (received[::-1], lists, block_lists, masses, env_w, w1)
    )
    received = received[::-1]
    weights = (env_w, w1, hidden_two, hidden_three, out_w.T)

    contracted, first, last, scaled = contract(place, received, masses, jnp.asarray(step[:NC]))
    ring = [
        (g * slabs + s, ((g + 1) % groups) * slabs + (s + (g + 1) // groups) % slabs)
        for g in range(groups)
        for s in range(slabs)
    ]
    back = [(j, i) for i, j in ring]
    every = ("bead", "slab", "grp")
    lower = lax.ppermute(last, every, ring)
    upper = lax.ppermute(first, every, back)
    returns = transform(scaled, masses, jnp.asarray(step[NC:]))
    returns, lower, upper = lax.optimization_barrier((returns, lower, upper))
    fields = lax.all_to_all(returns, "bead", split_axis=0, concat_axis=0, tiled=True)

    forces = neural(contracted, lower, upper, block_lists, weights)
    neural_parts, partners = gather_blocks(forces, "bead")
    fields, forces = lax.optimization_barrier((fields, forces))

    new_q, words, fixed, unit, rims = assemble(fields)
    slab_ring = [(s, (s + 1) % slabs) for s in range(slabs)]
    slab_back = [(j, i) for i, j in slab_ring]
    q_lower = lax.ppermute(rims[3], ("slab", "grp"), slab_ring)
    q_upper = lax.ppermute(rims[0], ("slab", "grp"), slab_back)

    pair = pair_inner(words, fixed, unit, lists)
    coefs = (kernel * np.float32(BEADS / NC)).reshape(NC, groups, beads, 1)
    coefs = jnp.asarray(np.broadcast_to(coefs, (NC, groups, beads, LANES)))
    new_p, force = finish(
        place, pair, rims, q_lower, q_upper, lists, fields, neural_parts, partners, coefs
    )
    return tuple(swap(out) for out in (new_q, new_p, force))


def solution(mesh):
    field = P("bead", None, ("slab", "grp"))
    placed = (field,) * 4 + (P(("slab", "grp")), P(("slab", "grp"), None)) + (P(),) * 5
    return jax.shard_map(
        body, mesh=mesh, in_specs=placed, out_specs=(field,) * 3, check_vma=False
    )
```

```python
import math

import jax
import jax.numpy as jnp
import numpy as np
from jax import lax
from jax.experimental import pallas as pl
from jax.experimental.pallas import tpu as pltpu
from jax.sharding import PartitionSpec as P

BEADS = 64
NC = 8
EDGE = 128
LANES = 128

TIME_STEP = 0.1
CYCLE_FREQ = 5.0
CENTROID_FRICTION = 1.0
PAIR_STRENGTH = 0.5

BEST = lax.Precision.HIGHEST


def step_tables():
    b = np.arange(BEADS, dtype=np.float64)
    k = np.arange(BEADS)
    angle = 2.0 * np.pi * ((b[:, None] * b[None, :]) % BEADS) / BEADS
    half = BEADS // 2
    basis = np.where(
        k == 0,
        1.0 / math.sqrt(BEADS),
        np.where(
            k < half,
            math.sqrt(2.0 / BEADS) * np.cos(angle),
            np.where(
                k == half, np.cos(angle) / math.sqrt(BEADS), math.sqrt(2.0 / BEADS) * np.sin(angle)
            ),
        ),
    )
    freq = 2.0 * CYCLE_FREQ * np.sin(np.pi * b / BEADS)
    spacing = b[None, :] / BEADS - np.arange(NC, dtype=np.float64)[:, None] / NC
    kernel = np.ones_like(spacing)
    for order in range(1, NC // 2):
        kernel = kernel + 2.0 * np.cos(2.0 * np.pi * order * spacing)
    kernel = kernel + np.cos(np.pi * NC * spacing)
    contract = kernel / BEADS

    h = 0.5 * TIME_STEP
    safe = np.where(freq > 0.0, freq, 1.0)
    qq = np.where(freq > 0.0, np.cos(safe * h), 1.0)
    qp = np.where(freq > 0.0, np.sin(safe * h) / safe, h)
    pq = np.where(freq > 0.0, -safe * np.sin(safe * h), 0.0)
    pp = qq
    keep = np.exp(-np.where(freq > 0.0, 2.0 * freq, CENTROID_FRICTION) * TIME_STEP)
    kick = np.sqrt(1.0 - keep * keep)
    full_qq = qq * qq + qp * keep * pq
    full_qp = qq * qp + qp * keep * pp
    full_qn = qp * kick
    full_pq = pq * qq + pp * keep * pq
    full_pp = pq * qp + pp * keep * pp
    full_pn = pp * kick
    q_rows = np.concatenate(
        [(basis * full_qq) @ basis.T, (basis * full_qp) @ basis.T, basis * full_qn], axis=1
    )
    p_rows = np.concatenate(
        [(basis * full_pq) @ basis.T, (basis * full_pp) @ basis.T, basis * full_pn], axis=1
    )
    c_rows = contract @ q_rows
    step = np.concatenate([c_rows, q_rows, p_rows], axis=0)
    return step.astype(np.float32), contract.astype(np.float32)


def whole_vmem():
    return pl.BlockSpec(memory_space=pltpu.VMEM)


def params(mebibytes=48):
    return pltpu.CompilerParams(vmem_limit_bytes=mebibytes * 1024 * 1024)


def smem():
    return pl.BlockSpec(memory_space=pltpu.SMEM)


def block_of(place_ref, r, rows):
    return pl.ds(pl.multiple_of((place_ref[0] ^ r) * rows, LANES), rows)


def exchange(blocks, axis):
    count = len(blocks)
    return [blocks[0]] + [
        lax.ppermute(blocks[r], axis, [(i, i ^ r) for i in range(count)]) for r in range(1, count)
    ]


def pack(place, positions, momenta, force_old, noise, groups):
    _, beads, atoms = positions.shape
    rows = atoms // groups

    def kernel(place_ref, q_ref, p_ref, f_ref, n_ref, *rest):
        outs, (p_buf, f_buf, sems) = rest[:groups], rest[groups:]
        loads = [
            pltpu.make_async_copy(p_ref, p_buf, sems.at[0]),
            pltpu.make_async_copy(f_ref, f_buf, sems.at[1]),
        ]
        for r in range(groups):
            at = block_of(place_ref, r, rows)
            for slot, (ref, first) in enumerate(((q_ref, 0), (n_ref, 6))):
                loads.append(
                    pltpu.make_async_copy(
                        ref.at[:, :, at], outs[r].at[pl.ds(first, 3)], sems.at[2 + 2 * r + slot]
                    )
                )
        for load in loads:
            load.start()
        loads[0].wait()
        loads[1].wait()
        for r in range(groups):
            at = block_of(place_ref, r, rows)
            for x in range(3):
                outs[r][3 + x] = p_buf[x, :, at] + 0.5 * TIME_STEP * f_buf[x, :, at]
        for load in loads[2:]:
            load.wait()

    return pl.pallas_call(
        kernel,
        out_shape=[jax.ShapeDtypeStruct((9, beads, rows), jnp.float32)] * groups,
        in_specs=[smem()] + [pl.BlockSpec(memory_space=pltpu.HBM)] * 4,
        out_specs=[whole_vmem()] * groups,
        scratch_shapes=[
            pltpu.VMEM((3, beads, atoms), jnp.float32),
            pltpu.VMEM((3, beads, atoms), jnp.float32),
            pltpu.SemaphoreType.DMA((2 + 2 * groups,)),
        ],
        compiler_params=params(60),
        name="pack",
    )(place, positions, momenta, force_old, noise)


def prepare(pair_list, mass, desc_w, hidden_one, place, rows):
    entries, atoms = pair_list.shape
    desc, env = desc_w.shape
    hid = hidden_one.shape[0]
    order = np.arange(env)
    order = (order % entries) * (env // entries) + order // entries
    permute = jnp.asarray(np.eye(env)[order], jnp.bfloat16)

    def kernel(place_ref, list_ref, mass_ref, w0_ref, w1_ref, order_ref, lists, own, masses, w0, w1):
        for t in range(atoms // LANES):
            at = pl.ds(t * LANES, LANES)
            lists[:, at] = list_ref[:, at] - t * LANES
        block = pl.ds(pl.multiple_of(place_ref[0] * rows, LANES), rows)
        own[...] = lists[:, block]
        masses[...] = mass_ref[:, block]
        w0[...] = lax.dot_general(
            order_ref[...],
            w0_ref[...],
            (((1,), (1,)), ((), ())),
            preferred_element_type=jnp.float32,
        ).astype(w0.dtype)
        w1[...] = w1_ref[...].astype(jnp.float32).T.astype(w1.dtype)

    return pl.pallas_call(
        kernel,
        out_shape=(
            jax.ShapeDtypeStruct((entries, atoms), jnp.int32),
            jax.ShapeDtypeStruct((entries, rows), jnp.int32),
            jax.ShapeDtypeStruct((1, rows), jnp.float32),
            jax.ShapeDtypeStruct((env, desc), jnp.bfloat16),
            jax.ShapeDtypeStruct((desc, hid), jnp.bfloat16),
        ),
        in_specs=[pl.BlockSpec(memory_space=pltpu.SMEM)] + [whole_vmem()] * 5,
        out_specs=(whole_vmem(),) * 5,
        compiler_params=params(),
        cost_estimate=pl.CostEstimate(
            flops=1_000_000_000, bytes_accessed=4_000_000, transcendentals=0
        ),
        name="prepare",
    )(place, pair_list, mass, desc_w, hidden_one, permute)


def contract(place, received, masses, table):
    groups = len(received)
    _, beads, rows = received[0].shape

    def kernel(place_ref, mass_ref, table_ref, own_ref, *rest):
        ins, (c_ref, first, last, fields, own, sem) = rest[: groups - 1], rest[groups - 1 :]

        load = pltpu.make_async_copy(own_ref, own, sem)
        load.start()
        mass = mass_ref[...]
        inverse = 1.0 / mass
        root = lax.rsqrt(mass)

        def scale(g, block):
            for x in range(3):
                fields[x, 0, g] = block[x]
                fields[x, 1, g] = block[3 + x] * inverse
                fields[x, 2, g] = block[6 + x] * root

        for r in range(1, groups):
            scale(place_ref[0] ^ r, ins[r - 1])
        load.wait()
        scale(place_ref[0], own)
        for x in range(3):
            out = jnp.dot(
                table_ref[...],
                fields[x].reshape(3 * BEADS, rows),
                precision=BEST,
                preferred_element_type=jnp.float32,
            )
            c_ref[x] = out
            first[x] = out[:, :EDGE]
            last[x] = out[:, rows - EDGE :]

    edge = jax.ShapeDtypeStruct((3, NC, EDGE), jnp.float32)
    return pl.pallas_call(
        kernel,
        out_shape=(
            jax.ShapeDtypeStruct((3, NC, rows), jnp.float32),
            edge,
            edge,
            jax.ShapeDtypeStruct((3, 3, groups, beads, rows), jnp.float32),
        ),
        in_specs=[smem()]
        + [whole_vmem()] * 2
        + [pl.BlockSpec(memory_space=pltpu.HBM)]
        + [whole_vmem()] * (groups - 1),
        out_specs=(whole_vmem(),) * 4,
        scratch_shapes=[pltpu.VMEM((9, beads, rows), jnp.float32), pltpu.SemaphoreType.DMA],
        compiler_params=params(),
        name="contract",
    )(place, masses, table, *received)


def transform(fields, masses, table):
    _, _, groups, beads, rows = fields.shape

    def kernel(fields_ref, mass_ref, table_ref, out_ref):
        mass = mass_ref[...]
        for x in range(3):
            out = jnp.dot(
                table_ref[...],
                fields_ref[x].reshape(3 * BEADS, rows),
                precision=BEST,
                preferred_element_type=jnp.float32,
            )
            out_ref[:, x] = out[:BEADS].reshape(groups, beads, rows)
            out_ref[:, 3 + x] = (out[BEADS:] * mass).reshape(groups, beads, rows)

    return pl.pallas_call(
        kernel,
        out_shape=jax.ShapeDtypeStruct((groups, 6, beads, rows), jnp.float32),
        in_specs=[whole_vmem()] * 3,
        out_specs=whole_vmem(),
        compiler_params=params(),
        cost_estimate=pl.CostEstimate(
            flops=1_000_000_000, bytes_accessed=2_000_000, transcendentals=0
        ),
        name="transform",
    )(fields, masses, table)


def inverse_of(value):
    estimate = pl.reciprocal(value, approx=True)
    return estimate * (2.0 - value * estimate)


def banded(windows, lane, low, high):
    below, middle, above = [
        jnp.take_along_axis(w, lane, axis=1, mode="promise_in_bounds") for w in windows
    ]
    return jnp.where(low, below, jnp.where(high, above, middle))


def entries_of(list_ref, e, base):
    place = list_ref[pl.ds(e, 8), pl.ds(base, LANES)]
    return place & (LANES - 1), place < LANES, place >= 2 * LANES


def on_sublanes(row):
    return jnp.broadcast_to(row, (8, LANES))


def env_units(windows, list_ref, base, envs, inputs):
    entries = list_ref.shape[0]
    for e in range(0, entries, 8):
        lane, low, high = entries_of(list_ref, e, base)
        for c in range(NC):
            apart = []
            for x in range(3):
                tiles = windows(c, x)
                apart.append(banded(tiles, lane, low, high) - tiles[1])
            square = apart[0] * apart[0] + apart[1] * apart[1] + apart[2] * apart[2]
            close = inverse_of(1.0 + square)
            for x, value in enumerate(apart + [close]):
                envs[pl.ds(x * entries + e, 8), pl.ds(c * LANES, LANES)] = value
            yield
    for c in range(NC):
        at = pl.ds(c * LANES, LANES)
        inputs[at, :] = envs[:, at].T.astype(jnp.bfloat16)
        yield


def network(inputs_ref, weights, out_ref, base, units, chunk=256):
    w0_ref, w1_ref, w2_ref, w3_ref, wo_ref = weights
    desc = w0_ref.shape[1]
    inputs = inputs_ref[...]
    total = None
    for f in range(0, desc, chunk):
        size = min(chunk, desc - f)
        first = jnp.dot(inputs, w0_ref[:, pl.ds(f, size)], preferred_element_type=jnp.float32)
        first = jnp.tanh(first.astype(jnp.bfloat16))
        part = jnp.dot(first, w1_ref[pl.ds(f, size), :], preferred_element_type=jnp.float32)
        total = part if total is None else total + part
        for _ in range(6):
            next(units, None)
    layer = jnp.tanh(total).astype(jnp.bfloat16)
    for ref in (w2_ref, w3_ref):
        layer = jnp.tanh(jnp.dot(layer, ref[...], preferred_element_type=jnp.float32)).astype(
            jnp.bfloat16
        )
    out = lax.dot_general(
        wo_ref[...], layer, (((1,), (1,)), ((), ())), preferred_element_type=jnp.float32
    )
    for c in range(NC):
        for x in range(3):
            out_ref[x, pl.ds(c, 1), pl.ds(base, LANES)] = out[
                x : x + 1, c * LANES : (c + 1) * LANES
            ]


def neural_scratch(env):
    return [
        pltpu.VMEM((2, env, NC * LANES), jnp.float32),
        pltpu.VMEM((2, NC * LANES, env), jnp.bfloat16),
    ]


def neural(contracted, lower, upper, lists, weights):
    _, _, rows = contracted.shape
    tiles = rows // LANES

    def kernel(
        c_ref, low_ref, up_ref, list_ref, w0, w1, w2, w3, wo, out_ref, envs, inputs
    ):
        def tile(x, c, t):
            if t < 0:
                ref, at = low_ref, 0
            elif t >= tiles:
                ref, at = up_ref, 0
            else:
                ref, at = c_ref, t * LANES
            return on_sublanes(ref[x, pl.ds(c, 1), pl.ds(at, LANES)])

        def units_of(t):
            if t >= tiles:
                return iter(())
            windows = lambda c, x: [tile(x, c, t + v) for v in (-1, 0, 1)]
            slot = t % 2
            return env_units(windows, list_ref, t * LANES, envs.at[slot], inputs.at[slot])

        for _ in units_of(0):
            pass
        for t in range(tiles):
            units = units_of(t + 1)
            network(inputs.at[t % 2], (w0, w1, w2, w3, wo), out_ref, t * LANES, units)
            for _ in units:
                pass

    return pl.pallas_call(
        kernel,
        out_shape=jax.ShapeDtypeStruct((3, NC, rows), jnp.float32),
        in_specs=[whole_vmem()] * 9,
        out_specs=whole_vmem(),
        scratch_shapes=neural_scratch(weights[0].shape[0]),
        compiler_params=params(),
        cost_estimate=pl.CostEstimate(
            flops=12_000_000_000, bytes_accessed=4_000_000, transcendentals=0
        ),
        name="neural",
    )(contracted, lower, upper, lists, *weights)


def add_pairs(sums, e, b, apart, close):
    for x in range(3):
        part = apart[x] * close
        sums[x, b] = part if e == 0 else sums[x, b] + part


def total_of(sums, x):
    total = sums[x, :, 0, :]
    for s in range(1, 8):
        total = total + sums[x, :, s, :]
    return total


def assemble(fields):
    groups, _, beads, rows = fields.shape
    atoms = groups * rows
    half = beads // 2
    top = float(2**15 - 1)

    def kernel(in_ref, newq, words, fixed, unit_ref, rims):
        largest = jnp.zeros((beads, rows), jnp.float32)
        for g in range(groups):
            at = pl.ds(g * rows, rows)
            for x in range(3):
                value = in_ref[g, x]
                newq[x, :, at] = value
                largest = jnp.maximum(largest, jnp.abs(value))
        limit = jnp.maximum(jnp.max(largest, keepdims=True), 1e-30)
        to_fixed = top / limit
        unit_ref[...] = jnp.broadcast_to(limit / (top * 65536.0), (beads, LANES))
        for g in range(groups):
            at = pl.ds(g * rows, rows)
            for x in range(3):
                value = jnp.floor(in_ref[g, x] * to_fixed + 0.5)
                fixed[x, :, at] = value * 65536.0
                value = value.astype(jnp.int32)
                words[x, :, at] = (value[:half] << 16) | (value[half:] & 65535)
        for rim, t in enumerate((0, LANES, atoms - 2 * LANES, atoms - LANES)):
            rims[rim] = newq[:, :, pl.ds(t, LANES)]

    return pl.pallas_call(
        kernel,
        out_shape=(
            jax.ShapeDtypeStruct((3, beads, atoms), jnp.float32),
            jax.ShapeDtypeStruct((3, half, atoms), jnp.int32),
            jax.ShapeDtypeStruct((3, beads, atoms), jnp.float32),
            jax.ShapeDtypeStruct((beads, LANES), jnp.float32),
            jax.ShapeDtypeStruct((4, 3, beads, LANES), jnp.float32),
        ),
        in_specs=[whole_vmem()],
        out_specs=(whole_vmem(),) * 5,
        compiler_params=params(),
        name="assemble",
    )(fields)


def pair_inner(words, fixed, unit, lists, part, parts):
    _, beads, atoms = fixed.shape
    half = beads // 2
    tiles = atoms // LANES
    begin, end = part * tiles // parts, (part + 1) * tiles // parts
    entries = lists.shape[0]

    def kernel(words_ref, fixed_ref, unit_ref, list_ref, pair, sums):
        unit_row = unit_ref[...]
        unit_square = on_sublanes(unit_ref[pl.ds(0, 1), :])
        unit_square = unit_square * unit_square

        @pl.loop(max(begin, 1), min(end, tiles - 1))
        def _(t):
            base = pl.multiple_of(t * LANES, LANES)

            def row(ref, x, b, v):
                return on_sublanes(ref[x, pl.ds(b, 1), pl.ds(base + (v - 1) * LANES, LANES)])

            for e in range(0, entries, 8):
                lane, low, high = entries_of(list_ref, e, base)
                for b in range(half):
                    both = [
                        banded([row(words_ref, x, b, v) for v in range(3)], lane, low, high)
                        for x in range(3)
                    ]
                    for bead, near in ((b, [w & -65536 for w in both]),
                                       (b + half, [w << 16 for w in both])):
                        apart = [
                            near[x].astype(jnp.float32) - row(fixed_ref, x, bead, 1)
                            for x in range(3)
                        ]
                        square = apart[0] * apart[0] + apart[1] * apart[1] + apart[2] * apart[2]
                        close = inverse_of(1.0 + square * unit_square)
                        add_pairs(sums, e, bead, apart, close)
            at = pl.ds(pl.multiple_of((t - begin) * LANES, LANES), LANES)
            for x in range(3):
                pair[x, :, at] = (PAIR_STRENGTH * unit_row) * total_of(sums, x)

    return pl.pallas_call(
        kernel,
        out_shape=jax.ShapeDtypeStruct((3, beads, (end - begin) * LANES), jnp.float32),
        in_specs=[whole_vmem()] * 4,
        out_specs=whole_vmem(),
        scratch_shapes=[pltpu.VMEM((3, beads, 8, LANES), jnp.float32)],
        compiler_params=params(),
        cost_estimate=pl.CostEstimate(
            flops=10_000_000_000 // parts, bytes_accessed=2_000_000, transcendentals=0
        ),
        name=f"pair_inner_{part}",
    )(words, fixed, unit, lists)


def finish(place, pairs, rims, lower, upper, lists, fields, neural_parts, partners, coefs):
    groups, _, beads, rows = fields.shape
    atoms = groups * rows
    sizes = [part.shape[0] for part in neural_parts]

    def kernel(place_ref, rims_ref, low_ref, up_ref, list_ref, in_ref, coef_ref, *rest):
        halves, parts = rest[: len(pairs)], rest[len(pairs) : len(pairs) + len(sizes)]
        newp, newf, sums = rest[len(pairs) + len(sizes) :]
        own = place_ref[0]

        def edge(base, tiles):
            for e in range(0, list_ref.shape[0], 8):
                lane, low, high = entries_of(list_ref, e, base)
                for b in range(beads):
                    apart = []
                    for x in range(3):
                        windows = [on_sublanes(tile[x, pl.ds(b, 1), :]) for tile in tiles]
                        apart.append(banded(windows, lane, low, high) - windows[1])
                    square = apart[0] * apart[0] + apart[1] * apart[1] + apart[2] * apart[2]
                    add_pairs(sums, e, b, apart, inverse_of(1.0 + square))
            for x in range(3):
                newf[x, :, pl.ds(base, LANES)] = PAIR_STRENGTH * total_of(sums, x)

        at = 0
        for half in halves:
            newf[:, :, pl.ds(at, half.shape[2])] = half[...]
            at += half.shape[2]
        edge(0, [low_ref, rims_ref.at[0], rims_ref.at[1]])
        edge(atoms - LANES, [rims_ref.at[2], rims_ref.at[3], up_ref])
        coef = [coef_ref[c, own] for c in range(NC)]
        blocks = [part.at[i] for part, size in zip(parts, sizes) for i in range(size)]
        for r, block in zip(partners, blocks):
            g = own ^ r
            for t in range(0, rows, LANES):
                at = pl.ds(pl.multiple_of(g * rows + t, LANES), LANES)
                inner = pl.ds(t, LANES)
                for x in range(3):
                    force = newf[x, :, at]
                    for c in range(NC):
                        force = force + coef[c] * block[x, pl.ds(c, 1), inner]
                    newf[x, :, at] = force
                    newp[x, :, at] = in_ref[g, 3 + x, :, inner] + 0.5 * TIME_STEP * force

    out = jax.ShapeDtypeStruct((3, beads, atoms), jnp.float32)
    return pl.pallas_call(
        kernel,
        out_shape=(out,) * 2,
        in_specs=[smem()] + [whole_vmem()] * (6 + len(pairs) + len(sizes)),
        out_specs=(whole_vmem(),) * 2,
        scratch_shapes=[pltpu.VMEM((3, beads, 8, LANES), jnp.float32)],
        compiler_params=params(),
        name="finish",
    )(place, rims, lower, upper, lists, fields, coefs, *pairs, *neural_parts)


def doubling_step(have, partners, axis, bit):
    count = lax.axis_size(axis)
    got = lax.ppermute(have, axis, [(i, i ^ bit) for i in range(count)])
    return got, partners + [r ^ bit for r in partners]


def body(
    positions,
    momenta,
    force_old,
    noise,
    mass,
    pair_list,
    desc_w,
    hidden_one,
    hidden_two,
    hidden_three,
    out_w,
):
    beads, _, atoms = positions.shape
    groups = lax.axis_size("bead")
    slabs = lax.axis_size(("slab", "grp"))
    rows = atoms // groups
    place = lax.axis_index("bead").astype(jnp.int32)[None]
    step, kernel = step_tables()

    swap = lambda field: jnp.transpose(field, (1, 0, 2))
    sends = pack(place, swap(positions), swap(momenta), swap(force_old), swap(noise), groups)
    received = exchange(sends, "bead")

    lists, block_lists, masses, env_w, w1 = prepare(
        pair_list.T, mass[None, :], desc_w.T, hidden_one.T, place, rows
    )
    received, lists, block_lists, masses, env_w, w1 = lax.optimization_barrier(
        (received, lists, block_lists, masses, env_w, w1)
    )
    weights = (env_w, w1, hidden_two, hidden_three, out_w.T)

    contracted, first, last, scaled = contract(place, received, masses, jnp.asarray(step[:NC]))
    ring = [
        (g * slabs + s, ((g + 1) % groups) * slabs + (s + (g + 1) // groups) % slabs)
        for g in range(groups)
        for s in range(slabs)
    ]
    back = [(j, i) for i, j in ring]
    every = ("bead", "slab", "grp")
    lower = lax.ppermute(last, every, ring)
    upper = lax.ppermute(first, every, back)
    returns = transform(scaled, masses, jnp.asarray(step[NC:]))
    returns, lower, upper = lax.optimization_barrier((returns, lower, upper))
    fields = lax.all_to_all(returns, "bead", split_axis=0, concat_axis=0, tiled=True)

    forces = neural(contracted, lower, upper, block_lists, weights)
    bits = [1 << i for i in range(groups.bit_length() - 2, -1, -1)]
    have = forces[None]
    got, partners = doubling_step(have, [0], "bead", bits[0])
    fields, forces = lax.optimization_barrier((fields, forces))

    new_q, words, fixed, unit, rims = assemble(fields)
    slab_ring = [(s, (s + 1) % slabs) for s in range(slabs)]
    slab_back = [(j, i) for i, j in slab_ring]
    q_lower = lax.ppermute(rims[3], ("slab", "grp"), slab_ring)
    q_upper = lax.ppermute(rims[0], ("slab", "grp"), slab_back)

    words, got = lax.optimization_barrier((words, got))
    pairs = []
    for part, steps in enumerate((bits[1:2], bits[2:])):
        for bit in steps:
            have = jnp.concatenate([have, got], axis=0)
            got, partners = doubling_step(have, partners, "bead", bit)
        pairs.append(pair_inner(words, fixed, unit, lists, part, 2))
        if part == 0:
            words, pairs[0], got = lax.optimization_barrier((words, pairs[0], got))

    coefs = (kernel * np.float32(BEADS / NC)).reshape(NC, groups, beads, 1)
    coefs = jnp.asarray(np.broadcast_to(coefs, (NC, groups, beads, LANES)))
    new_p, force = finish(
        place, pairs, rims, q_lower, q_upper, lists, fields, (have, got), partners, coefs
    )
    return tuple(swap(out) for out in (new_q, new_p, force))


def solution(mesh):
    field = P("bead", None, ("slab", "grp"))
    placed = (field,) * 4 + (P(("slab", "grp")), P(("slab", "grp"), None)) + (P(),) * 5
    return jax.shard_map(
        body, mesh=mesh, in_specs=placed, out_specs=(field,) * 3, check_vma=False
    )
```

```python
import math

import jax
import jax.numpy as jnp
import numpy as np
from jax import lax
from jax.experimental import pallas as pl
from jax.experimental.pallas import tpu as pltpu
from jax.sharding import PartitionSpec as P

BEADS = 64
NC = 8
EDGE = 128
LANES = 128

TIME_STEP = 0.1
CYCLE_FREQ = 5.0
CENTROID_FRICTION = 1.0
PAIR_STRENGTH = 0.5

BEST = lax.Precision.HIGHEST


def step_tables():
    b = np.arange(BEADS, dtype=np.float64)
    k = np.arange(BEADS)
    angle = 2.0 * np.pi * ((b[:, None] * b[None, :]) % BEADS) / BEADS
    half = BEADS // 2
    basis = np.where(
        k == 0,
        1.0 / math.sqrt(BEADS),
        np.where(
            k < half,
            math.sqrt(2.0 / BEADS) * np.cos(angle),
            np.where(
                k == half, np.cos(angle) / math.sqrt(BEADS), math.sqrt(2.0 / BEADS) * np.sin(angle)
            ),
        ),
    )
    freq = 2.0 * CYCLE_FREQ * np.sin(np.pi * b / BEADS)
    spacing = b[None, :] / BEADS - np.arange(NC, dtype=np.float64)[:, None] / NC
    kernel = np.ones_like(spacing)
    for order in range(1, NC // 2):
        kernel = kernel + 2.0 * np.cos(2.0 * np.pi * order * spacing)
    kernel = kernel + np.cos(np.pi * NC * spacing)
    contract = kernel / BEADS

    h = 0.5 * TIME_STEP
    safe = np.where(freq > 0.0, freq, 1.0)
    qq = np.where(freq > 0.0, np.cos(safe * h), 1.0)
    qp = np.where(freq > 0.0, np.sin(safe * h) / safe, h)
    pq = np.where(freq > 0.0, -safe * np.sin(safe * h), 0.0)
    pp = qq
    keep = np.exp(-np.where(freq > 0.0, 2.0 * freq, CENTROID_FRICTION) * TIME_STEP)
    kick = np.sqrt(1.0 - keep * keep)
    full_qq = qq * qq + qp * keep * pq
    full_qp = qq * qp + qp * keep * pp
    full_qn = qp * kick
    full_pq = pq * qq + pp * keep * pq
    full_pp = pq * qp + pp * keep * pp
    full_pn = pp * kick
    q_rows = np.concatenate(
        [(basis * full_qq) @ basis.T, (basis * full_qp) @ basis.T, basis * full_qn], axis=1
    )
    p_rows = np.concatenate(
        [(basis * full_pq) @ basis.T, (basis * full_pp) @ basis.T, basis * full_pn], axis=1
    )
    c_rows = contract @ q_rows
    step = np.concatenate([c_rows, q_rows, p_rows], axis=0)
    return step.astype(np.float32), contract.astype(np.float32)


def whole_vmem():
    return pl.BlockSpec(memory_space=pltpu.VMEM)


def params(mebibytes=48):
    return pltpu.CompilerParams(vmem_limit_bytes=mebibytes * 1024 * 1024)


def smem():
    return pl.BlockSpec(memory_space=pltpu.SMEM)


def block_of(place_ref, r, rows, part=0, parts=1):
    size = rows // parts
    return pl.ds(pl.multiple_of((place_ref[0] ^ r) * rows + part * size, LANES), size)


def exchange(blocks, axis):
    count = len(blocks)
    return [blocks[0]] + [
        lax.ppermute(blocks[r], axis, [(i, i ^ r) for i in range(count)]) for r in range(1, count)
    ]


def pack(place, positions, momenta, force_old, noise, groups, parts):
    _, beads, atoms = positions.shape
    rows = atoms // groups
    count = groups * parts

    def kernel(place_ref, q_ref, p_ref, f_ref, n_ref, *rest):
        outs, (p_buf, f_buf, sems) = rest[:count], rest[count:]
        loads = [
            pltpu.make_async_copy(p_ref, p_buf, sems.at[0]),
            pltpu.make_async_copy(f_ref, f_buf, sems.at[1]),
        ]
        blocks = [
            (outs[part * groups + r], block_of(place_ref, r, rows, part, parts))
            for part in range(parts)
            for r in range(groups)
        ]
        for out, at in blocks:
            for ref, first in ((q_ref, 0), (n_ref, 6)):
                loads.append(
                    pltpu.make_async_copy(
                        ref.at[:, :, at], out.at[pl.ds(first, 3)], sems.at[len(loads)]
                    )
                )
        for load in loads:
            load.start()
        loads[0].wait()
        loads[1].wait()
        for out, at in blocks:
            for x in range(3):
                out[3 + x] = p_buf[x, :, at] + 0.5 * TIME_STEP * f_buf[x, :, at]
        for load in loads[2:]:
            load.wait()

    outs = pl.pallas_call(
        kernel,
        out_shape=[jax.ShapeDtypeStruct((9, beads, rows // parts), jnp.float32)] * count,
        in_specs=[smem()] + [pl.BlockSpec(memory_space=pltpu.HBM)] * 4,
        out_specs=[whole_vmem()] * count,
        scratch_shapes=[
            pltpu.VMEM((3, beads, atoms), jnp.float32),
            pltpu.VMEM((3, beads, atoms), jnp.float32),
            pltpu.SemaphoreType.DMA((2 + 2 * count,)),
        ],
        compiler_params=params(60),
        name="pack",
    )(place, positions, momenta, force_old, noise)
    return [list(outs[part * groups : (part + 1) * groups]) for part in range(parts)]


def prepare(pair_list, mass, desc_w, hidden_one, place, rows):
    entries, atoms = pair_list.shape
    desc, env = desc_w.shape
    hid = hidden_one.shape[0]
    order = np.arange(env)
    order = (order % entries) * (env // entries) + order // entries
    permute = jnp.asarray(np.eye(env)[order], jnp.bfloat16)

    def kernel(place_ref, list_ref, mass_ref, w0_ref, w1_ref, order_ref, lists, own, masses, w0, w1):
        for t in range(atoms // LANES):
            at = pl.ds(t * LANES, LANES)
            lists[:, at] = list_ref[:, at] - t * LANES
        block = pl.ds(pl.multiple_of(place_ref[0] * rows, LANES), rows)
        own[...] = lists[:, block]
        masses[...] = mass_ref[:, block]
        w0[...] = lax.dot_general(
            order_ref[...],
            w0_ref[...],
            (((1,), (1,)), ((), ())),
            preferred_element_type=jnp.float32,
        ).astype(w0.dtype)
        w1[...] = w1_ref[...].astype(jnp.float32).T.astype(w1.dtype)

    return pl.pallas_call(
        kernel,
        out_shape=(
            jax.ShapeDtypeStruct((entries, atoms), jnp.int32),
            jax.ShapeDtypeStruct((entries, rows), jnp.int32),
            jax.ShapeDtypeStruct((1, rows), jnp.float32),
            jax.ShapeDtypeStruct((env, desc), jnp.bfloat16),
            jax.ShapeDtypeStruct((desc, hid), jnp.bfloat16),
        ),
        in_specs=[pl.BlockSpec(memory_space=pltpu.SMEM)] + [whole_vmem()] * 5,
        out_specs=(whole_vmem(),) * 5,
        compiler_params=params(),
        cost_estimate=pl.CostEstimate(
            flops=1_000_000_000, bytes_accessed=4_000_000, transcendentals=0
        ),
        name="prepare",
    )(place, pair_list, mass, desc_w, hidden_one, permute)


def contract(place, received, masses, table, part):
    groups = len(received)
    _, beads, size = received[0].shape

    def kernel(place_ref, mass_ref, table_ref, own_ref, *rest):
        ins, (c_ref, outer, fields, own, sem) = rest[: groups - 1], rest[groups - 1 :]
        load = pltpu.make_async_copy(own_ref, own, sem)
        load.start()
        mass = mass_ref[:, pl.ds(part * size, size)]
        inverse = 1.0 / mass
        root = lax.rsqrt(mass)

        def scale(g, block):
            for x in range(3):
                fields[x, 0, g] = block[x]
                fields[x, 1, g] = block[3 + x] * inverse
                fields[x, 2, g] = block[6 + x] * root

        for r in range(1, groups):
            scale(place_ref[0] ^ r, ins[r - 1])
        load.wait()
        scale(place_ref[0], own)
        for x in range(3):
            out = jnp.dot(
                table_ref[...],
                fields[x].reshape(3 * BEADS, size),
                precision=BEST,
                preferred_element_type=jnp.float32,
            )
            c_ref[x] = out
            outer[x] = out[:, size - EDGE :] if part else out[:, :EDGE]

    return pl.pallas_call(
        kernel,
        out_shape=(
            jax.ShapeDtypeStruct((3, NC, size), jnp.float32),
            jax.ShapeDtypeStruct((3, NC, EDGE), jnp.float32),
            jax.ShapeDtypeStruct((3, 3, groups, beads, size), jnp.float32),
        ),
        in_specs=[smem()]
        + [whole_vmem()] * 2
        + [pl.BlockSpec(memory_space=pltpu.HBM)]
        + [whole_vmem()] * (groups - 1),
        out_specs=(whole_vmem(),) * 3,
        scratch_shapes=[pltpu.VMEM((9, beads, size), jnp.float32), pltpu.SemaphoreType.DMA],
        compiler_params=params(),
        name=f"contract_{part}",
    )(place, masses, table, *received)


def transform(fields, masses, table, part):
    _, _, groups, beads, size = fields.shape

    def kernel(fields_ref, mass_ref, table_ref, out_ref):
        mass = mass_ref[:, pl.ds(part * size, size)]
        for x in range(3):
            out = jnp.dot(
                table_ref[...],
                fields_ref[x].reshape(3 * BEADS, size),
                precision=BEST,
                preferred_element_type=jnp.float32,
            )
            out_ref[:, x] = out[:BEADS].reshape(groups, beads, size)
            out_ref[:, 3 + x] = (out[BEADS:] * mass).reshape(groups, beads, size)

    return pl.pallas_call(
        kernel,
        out_shape=jax.ShapeDtypeStruct((groups, 6, beads, size), jnp.float32),
        in_specs=[whole_vmem()] * 3,
        out_specs=whole_vmem(),
        compiler_params=params(),
        cost_estimate=pl.CostEstimate(
            flops=500_000_000, bytes_accessed=1_000_000, transcendentals=0
        ),
        name=f"transform_{part}",
    )(fields, masses, table)


def inverse_of(value):
    estimate = pl.reciprocal(value, approx=True)
    return estimate * (2.0 - value * estimate)


def banded(windows, lane, low, high):
    below, middle, above = [
        jnp.take_along_axis(w, lane, axis=1, mode="promise_in_bounds") for w in windows
    ]
    return jnp.where(low, below, jnp.where(high, above, middle))


def entries_of(list_ref, e, base):
    place = list_ref[pl.ds(e, 8), pl.ds(base, LANES)]
    return place & (LANES - 1), place < LANES, place >= 2 * LANES


def on_sublanes(row):
    return jnp.broadcast_to(row, (8, LANES))


def env_units(windows, list_ref, base, envs, inputs):
    entries = list_ref.shape[0]
    for e in range(0, entries, 8):
        lane, low, high = entries_of(list_ref, e, base)
        for c in range(NC):
            apart = []
            for x in range(3):
                tiles = windows(c, x)
                apart.append(banded(tiles, lane, low, high) - tiles[1])
            square = apart[0] * apart[0] + apart[1] * apart[1] + apart[2] * apart[2]
            close = inverse_of(1.0 + square)
            for x, value in enumerate(apart + [close]):
                envs[pl.ds(x * entries + e, 8), pl.ds(c * LANES, LANES)] = value
            yield
    for c in range(NC):
        at = pl.ds(c * LANES, LANES)
        inputs[at, :] = envs[:, at].T.astype(jnp.bfloat16)
        yield


def network(inputs_ref, weights, out_ref, base, units, chunk=256):
    w0_ref, w1_ref, w2_ref, w3_ref, wo_ref = weights
    desc = w0_ref.shape[1]
    inputs = inputs_ref[...]
    total = None
    for f in range(0, desc, chunk):
        size = min(chunk, desc - f)
        first = jnp.dot(inputs, w0_ref[:, pl.ds(f, size)], preferred_element_type=jnp.float32)
        first = jnp.tanh(first.astype(jnp.bfloat16))
        part = jnp.dot(first, w1_ref[pl.ds(f, size), :], preferred_element_type=jnp.float32)
        total = part if total is None else total + part
        for _ in range(6):
            next(units, None)
    layer = jnp.tanh(total).astype(jnp.bfloat16)
    for ref in (w2_ref, w3_ref):
        layer = jnp.tanh(jnp.dot(layer, ref[...], preferred_element_type=jnp.float32)).astype(
            jnp.bfloat16
        )
    out = lax.dot_general(
        wo_ref[...], layer, (((1,), (1,)), ((), ())), preferred_element_type=jnp.float32
    )
    for c in range(NC):
        for x in range(3):
            out_ref[x, pl.ds(c, 1), pl.ds(base, LANES)] = out[
                x : x + 1, c * LANES : (c + 1) * LANES
            ]


def neural_scratch(env):
    return [
        pltpu.VMEM((2, env, NC * LANES), jnp.float32),
        pltpu.VMEM((2, NC * LANES, env), jnp.bfloat16),
    ]


def neural(contracted, lower, upper, lists, weights):
    size = contracted[0].shape[2]
    rows = size * len(contracted)
    tiles = rows // LANES

    def kernel(
        low_ref, up_ref, list_ref, w0, w1, w2, w3, wo, *rest
    ):
        c_refs, (out_ref, envs, inputs) = rest[: len(contracted)], rest[len(contracted) :]

        def tile(x, c, t):
            if t < 0:
                ref, at = low_ref, 0
            elif t >= tiles:
                ref, at = up_ref, 0
            else:
                ref, at = c_refs[t * LANES // size], t * LANES % size
            return on_sublanes(ref[x, pl.ds(c, 1), pl.ds(at, LANES)])

        def units_of(t):
            if t >= tiles:
                return iter(())
            windows = lambda c, x: [tile(x, c, t + v) for v in (-1, 0, 1)]
            slot = t % 2
            return env_units(windows, list_ref, t * LANES, envs.at[slot], inputs.at[slot])

        for _ in units_of(0):
            pass
        for t in range(tiles):
            units = units_of(t + 1)
            network(inputs.at[t % 2], (w0, w1, w2, w3, wo), out_ref, t * LANES, units)
            for _ in units:
                pass

    return pl.pallas_call(
        kernel,
        out_shape=jax.ShapeDtypeStruct((3, NC, rows), jnp.float32),
        in_specs=[whole_vmem()] * (8 + len(contracted)),
        out_specs=whole_vmem(),
        scratch_shapes=neural_scratch(weights[0].shape[0]),
        compiler_params=params(),
        cost_estimate=pl.CostEstimate(
            flops=12_000_000_000, bytes_accessed=4_000_000, transcendentals=0
        ),
        name="neural",
    )(lower, upper, lists, *weights, *contracted)


def add_pairs(sums, e, b, apart, close):
    for x in range(3):
        part = apart[x] * close
        sums[x, b] = part if e == 0 else sums[x, b] + part


def total_of(sums, x):
    total = sums[x, :, 0, :]
    for s in range(1, 8):
        total = total + sums[x, :, s, :]
    return total


def assemble(fields):
    groups, _, beads, size = fields[0].shape
    parts = len(fields)
    rows = size * parts
    atoms = groups * rows
    half = beads // 2
    top = float(2**15 - 1)

    def kernel(*refs):
        ins, (newq, words, fixed, unit_ref, rims) = refs[:parts], refs[parts:]
        blocks = [
            (ins[k], g, pl.ds(g * rows + k * size, size)) for g in range(groups) for k in range(parts)
        ]
        largest = jnp.zeros((beads, size), jnp.float32)
        for ref, g, at in blocks:
            for x in range(3):
                value = ref[g, x]
                newq[x, :, at] = value
                largest = jnp.maximum(largest, jnp.abs(value))
        limit = jnp.maximum(jnp.max(largest, keepdims=True), 1e-30)
        to_fixed = top / limit
        unit_ref[...] = jnp.broadcast_to(limit / (top * 65536.0), (beads, LANES))
        for ref, g, at in blocks:
            for x in range(3):
                value = jnp.floor(ref[g, x] * to_fixed + 0.5)
                fixed[x, :, at] = value * 65536.0
                value = value.astype(jnp.int32)
                words[x, :, at] = (value[:half] << 16) | (value[half:] & 65535)
        for rim, t in enumerate((0, LANES, atoms - 2 * LANES, atoms - LANES)):
            rims[rim] = newq[:, :, pl.ds(t, LANES)]

    return pl.pallas_call(
        kernel,
        out_shape=(
            jax.ShapeDtypeStruct((3, beads, atoms), jnp.float32),
            jax.ShapeDtypeStruct((3, half, atoms), jnp.int32),
            jax.ShapeDtypeStruct((3, beads, atoms), jnp.float32),
            jax.ShapeDtypeStruct((beads, LANES), jnp.float32),
            jax.ShapeDtypeStruct((4, 3, beads, LANES), jnp.float32),
        ),
        in_specs=[whole_vmem()] * parts,
        out_specs=(whole_vmem(),) * 5,
        compiler_params=params(),
        name="assemble",
    )(*fields)


def pair_part(words, fixed, unit, lists, begin, end, edges=()):
    _, beads, atoms = fixed.shape
    half = beads // 2
    tiles = atoms // LANES
    entries = lists.shape[0]

    def kernel(words_ref, fixed_ref, unit_ref, list_ref, *rest):
        ends = rest[: len(edges)]
        pair, sums = rest[len(edges)], rest[-1]
        unit_row = unit_ref[...]
        unit_square = on_sublanes(unit_ref[pl.ds(0, 1), :])
        unit_square = unit_square * unit_square

        def edge(out, at, base, near_tiles):
            for e in range(0, entries, 8):
                lane, low, high = entries_of(list_ref, e, base)
                for b in range(beads):
                    apart = []
                    for x in range(3):
                        windows = [on_sublanes(tile[x, pl.ds(b, 1), :]) for tile in near_tiles]
                        apart.append(banded(windows, lane, low, high) - windows[1])
                    square = apart[0] * apart[0] + apart[1] * apart[1] + apart[2] * apart[2]
                    add_pairs(sums, e, b, apart, inverse_of(1.0 + square))
            for x in range(3):
                out[x, :, pl.ds(at, LANES)] = PAIR_STRENGTH * total_of(sums, x)

        @pl.loop(max(begin, 1), min(end, tiles - 1))
        def _(t):
            base = pl.multiple_of(t * LANES, LANES)

            def row(ref, x, b, v):
                return on_sublanes(ref[x, pl.ds(b, 1), pl.ds(base + (v - 1) * LANES, LANES)])

            for e in range(0, entries, 8):
                lane, low, high = entries_of(list_ref, e, base)
                for b in range(half):
                    both = [
                        banded([row(words_ref, x, b, v) for v in range(3)], lane, low, high)
                        for x in range(3)
                    ]
                    for bead, near in ((b, [w & -65536 for w in both]),
                                       (b + half, [w << 16 for w in both])):
                        apart = [
                            near[x].astype(jnp.float32) - row(fixed_ref, x, bead, 1)
                            for x in range(3)
                        ]
                        square = apart[0] * apart[0] + apart[1] * apart[1] + apart[2] * apart[2]
                        close = inverse_of(1.0 + square * unit_square)
                        add_pairs(sums, e, bead, apart, close)
            at = pl.ds(pl.multiple_of((t - begin) * LANES, LANES), LANES)
            for x in range(3):
                pair[x, :, at] = (PAIR_STRENGTH * unit_row) * total_of(sums, x)

        if edges:
            rims, lower, upper = ends
            last = (tiles - 1) * LANES
            edge(rest[len(edges) + 1], 0, 0, [lower, rims.at[0], rims.at[1]])
            edge(pair, last - begin * LANES, last, [rims.at[2], rims.at[3], upper])

    out_shape = [jax.ShapeDtypeStruct((3, beads, (end - begin) * LANES), jnp.float32)]
    if edges:
        out_shape.append(jax.ShapeDtypeStruct((3, beads, LANES), jnp.float32))
    return pl.pallas_call(
        kernel,
        out_shape=out_shape,
        in_specs=[whole_vmem()] * (4 + len(edges)),
        out_specs=[whole_vmem()] * len(out_shape),
        scratch_shapes=[pltpu.VMEM((3, beads, 8, LANES), jnp.float32)],
        compiler_params=params(),
        cost_estimate=pl.CostEstimate(
            flops=300_000_000 * (end - begin), bytes_accessed=2_000_000, transcendentals=0
        ),
        name=f"pair_{begin}",
    )(words, fixed, unit, lists, *edges)


def finish(place, pairs, first, fields, neural_parts, partners, coefs):
    groups, _, beads, size = fields[0].shape
    rows = size * len(fields)
    atoms = groups * rows
    counts = [part.shape[0] for part in neural_parts]

    def kernel(place_ref, first_ref, coef_ref, *rest):
        halves, rest = rest[: len(pairs)], rest[len(pairs) :]
        ins, rest = rest[: len(fields)], rest[len(fields) :]
        blocks, (newp, newf) = rest[: len(counts)], rest[len(counts) :]
        own = place_ref[0]
        at = 0
        for half in halves:
            newf[:, :, pl.ds(at, half.shape[2])] = half[...]
            at += half.shape[2]
        newf[:, :, pl.ds(0, LANES)] = first_ref[...]
        coef = [coef_ref[c, own] for c in range(NC)]
        blocks = [block.at[i] for block, count in zip(blocks, counts) for i in range(count)]
        for r, block in zip(partners, blocks):
            g = own ^ r
            for t in range(0, rows, LANES):
                at = pl.ds(pl.multiple_of(g * rows + t, LANES), LANES)
                moved = ins[t // size].at[g, :, :, pl.ds(t % size, LANES)]
                for x in range(3):
                    force = newf[x, :, at]
                    for c in range(NC):
                        force = force + coef[c] * block[x, pl.ds(c, 1), pl.ds(t, LANES)]
                    newf[x, :, at] = force
                    newp[x, :, at] = moved[3 + x] + 0.5 * TIME_STEP * force

    out = jax.ShapeDtypeStruct((3, beads, atoms), jnp.float32)
    return pl.pallas_call(
        kernel,
        out_shape=(out,) * 2,
        in_specs=[smem()]
        + [whole_vmem()] * (2 + len(pairs) + len(fields) + len(neural_parts)),
        out_specs=(whole_vmem(),) * 2,
        compiler_params=params(),
        name="finish",
    )(place, first, coefs, *pairs, *fields, *neural_parts)


def doubling_step(have, partners, axis, bit):
    count = lax.axis_size(axis)
    got = lax.ppermute(have, axis, [(i, i ^ bit) for i in range(count)])
    return got, partners + [r ^ bit for r in partners]


def body(
    positions,
    momenta,
    force_old,
    noise,
    mass,
    pair_list,
    desc_w,
    hidden_one,
    hidden_two,
    hidden_three,
    out_w,
):
    beads, _, atoms = positions.shape
    groups = lax.axis_size("bead")
    slabs = lax.axis_size(("slab", "grp"))
    rows = atoms // groups
    place = lax.axis_index("bead").astype(jnp.int32)[None]
    step, kernel = step_tables()

    swap = lambda field: jnp.transpose(field, (1, 0, 2))
    parts = 2
    sends = pack(place, swap(positions), swap(momenta), swap(force_old), swap(noise), groups, parts)
    received = exchange(sends[0], "bead")

    lists, block_lists, masses, env_w, w1 = prepare(
        pair_list.T, mass[None, :], desc_w.T, hidden_one.T, place, rows
    )
    received, lists, block_lists, masses, env_w, w1 = lax.optimization_barrier(
        (received, lists, block_lists, masses, env_w, w1)
    )
    weights = (env_w, w1, hidden_two, hidden_three, out_w.T)

    ring = [
        (g * slabs + s, ((g + 1) % groups) * slabs + (s + (g + 1) // groups) % slabs)
        for g in range(groups)
        for s in range(slabs)
    ]
    back = [(j, i) for i, j in ring]
    every = ("bead", "slab", "grp")
    to_contracted, to_new = jnp.asarray(step[:NC]), jnp.asarray(step[NC:])
    ahead, first, scaled = contract(place, received, masses, to_contracted, 0)
    upper = lax.ppermute(first, every, back)
    returns = transform(scaled, masses, to_new, 0)
    near = groups // 2
    sends[1][1:near], returns = lax.optimization_barrier((sends[1][1:near], returns))
    fields = [lax.all_to_all(returns, "bead", split_axis=0, concat_axis=0, tiled=True)]

    received = exchange(sends[1], "bead")
    behind, last, scaled = contract(place, received, masses, to_contracted, 1)
    lower = lax.ppermute(last, every, ring)
    returns = transform(scaled, masses, to_new, 1)
    returns, lower, upper = lax.optimization_barrier((returns, lower, upper))
    fields.append(lax.all_to_all(returns, "bead", split_axis=0, concat_axis=0, tiled=True))
    contracted = (ahead, behind)

    forces = neural(contracted, lower, upper, block_lists, weights)
    bits = [1 << i for i in range(groups.bit_length() - 2, -1, -1)]
    have = forces[None]
    got, partners = doubling_step(have, [0], "bead", bits[0])
    fields, forces = lax.optimization_barrier((fields, forces))

    new_q, words, fixed, unit, rims = assemble(fields)
    slab_ring = [(s, (s + 1) % slabs) for s in range(slabs)]
    slab_back = [(j, i) for i, j in slab_ring]
    q_lower = lax.ppermute(rims[3], ("slab", "grp"), slab_ring)
    q_upper = lax.ppermute(rims[0], ("slab", "grp"), slab_back)

    words, got = lax.optimization_barrier((words, got))
    tiles = atoms // LANES
    cut = 3 * tiles // 8
    for bit in bits[1:2]:
        have = jnp.concatenate([have, got], axis=0)
        got, partners = doubling_step(have, partners, "bead", bit)
    pairs = pair_part(words, fixed, unit, lists, 0, cut)
    words, pairs, got = lax.optimization_barrier((words, pairs, got))
    for bit in bits[2:]:
        have = jnp.concatenate([have, got], axis=0)
        got, partners = doubling_step(have, partners, "bead", bit)
    rest, first = pair_part(
        words, fixed, unit, lists, cut, tiles, (rims, q_lower, q_upper)
    )

    coefs = (kernel * np.float32(BEADS / NC)).reshape(NC, groups, beads, 1)
    coefs = jnp.asarray(np.broadcast_to(coefs, (NC, groups, beads, LANES)))
    new_p, force = finish(
        place, [*pairs, rest], first, fields, (have, got), partners, coefs
    )
    return tuple(swap(out) for out in (new_q, new_p, force))


def solution(mesh):
    field = P("bead", None, ("slab", "grp"))
    placed = (field,) * 4 + (P(("slab", "grp")), P(("slab", "grp"), None)) + (P(),) * 5
    return jax.shard_map(
        body, mesh=mesh, in_specs=placed, out_specs=(field,) * 3, check_vma=False
    )
```

```python
import math

import jax
import jax.numpy as jnp
import numpy as np
from jax import lax
from jax.experimental import pallas as pl
from jax.experimental.pallas import tpu as pltpu
from jax.sharding import PartitionSpec as P

BEADS = 64
NC = 8
EDGE = 128
LANES = 128

TIME_STEP = 0.1
CYCLE_FREQ = 5.0
CENTROID_FRICTION = 1.0
PAIR_STRENGTH = 0.5

BEST = lax.Precision.HIGHEST


def step_tables():
    b = np.arange(BEADS, dtype=np.float64)
    k = np.arange(BEADS)
    angle = 2.0 * np.pi * ((b[:, None] * b[None, :]) % BEADS) / BEADS
    half = BEADS // 2
    basis = np.where(
        k == 0,
        1.0 / math.sqrt(BEADS),
        np.where(
            k < half,
            math.sqrt(2.0 / BEADS) * np.cos(angle),
            np.where(
                k == half, np.cos(angle) / math.sqrt(BEADS), math.sqrt(2.0 / BEADS) * np.sin(angle)
            ),
        ),
    )
    freq = 2.0 * CYCLE_FREQ * np.sin(np.pi * b / BEADS)
    spacing = b[None, :] / BEADS - np.arange(NC, dtype=np.float64)[:, None] / NC
    kernel = np.ones_like(spacing)
    for order in range(1, NC // 2):
        kernel = kernel + 2.0 * np.cos(2.0 * np.pi * order * spacing)
    kernel = kernel + np.cos(np.pi * NC * spacing)
    contract = kernel / BEADS

    h = 0.5 * TIME_STEP
    safe = np.where(freq > 0.0, freq, 1.0)
    qq = np.where(freq > 0.0, np.cos(safe * h), 1.0)
    qp = np.where(freq > 0.0, np.sin(safe * h) / safe, h)
    pq = np.where(freq > 0.0, -safe * np.sin(safe * h), 0.0)
    pp = qq
    keep = np.exp(-np.where(freq > 0.0, 2.0 * freq, CENTROID_FRICTION) * TIME_STEP)
    kick = np.sqrt(1.0 - keep * keep)
    full_qq = qq * qq + qp * keep * pq
    full_qp = qq * qp + qp * keep * pp
    full_qn = qp * kick
    full_pq = pq * qq + pp * keep * pq
    full_pp = pq * qp + pp * keep * pp
    full_pn = pp * kick
    q_rows = np.concatenate(
        [(basis * full_qq) @ basis.T, (basis * full_qp) @ basis.T, basis * full_qn], axis=1
    )
    p_rows = np.concatenate(
        [(basis * full_pq) @ basis.T, (basis * full_pp) @ basis.T, basis * full_pn], axis=1
    )
    c_rows = contract @ q_rows
    step = np.concatenate([c_rows, q_rows, p_rows], axis=0)
    return step.astype(np.float32), contract.astype(np.float32)


def whole_vmem():
    return pl.BlockSpec(memory_space=pltpu.VMEM)


def params(mebibytes=48):
    return pltpu.CompilerParams(vmem_limit_bytes=mebibytes * 1024 * 1024)


def smem():
    return pl.BlockSpec(memory_space=pltpu.SMEM)


def block_of(place_ref, r, rows):
    return pl.ds(pl.multiple_of((place_ref[0] ^ r) * rows, LANES), rows)


def exchange(blocks, axis):
    count = len(blocks)
    return [blocks[0]] + [
        lax.ppermute(blocks[r], axis, [(i, i ^ r) for i in range(count)]) for r in range(1, count)
    ]


def pack(place, positions, momenta, force_old, noise, groups):
    _, beads, atoms = positions.shape
    rows = atoms // groups

    def kernel(place_ref, q_ref, p_ref, f_ref, n_ref, *rest):
        outs, (p_buf, f_buf, sems) = rest[:groups], rest[groups:]
        loads = [
            pltpu.make_async_copy(p_ref, p_buf, sems.at[0]),
            pltpu.make_async_copy(f_ref, f_buf, sems.at[1]),
        ]
        for r in range(groups):
            at = block_of(place_ref, r, rows)
            for slot, (ref, first) in enumerate(((q_ref, 0), (n_ref, 6))):
                loads.append(
                    pltpu.make_async_copy(
                        ref.at[:, :, at], outs[r].at[pl.ds(first, 3)], sems.at[2 + 2 * r + slot]
                    )
                )
        for load in loads:
            load.start()
        loads[0].wait()
        loads[1].wait()
        for r in range(groups):
            at = block_of(place_ref, r, rows)
            for x in range(3):
                outs[r][3 + x] = p_buf[x, :, at] + 0.5 * TIME_STEP * f_buf[x, :, at]
        for load in loads[2:]:
            load.wait()

    return pl.pallas_call(
        kernel,
        out_shape=[jax.ShapeDtypeStruct((9, beads, rows), jnp.float32)] * groups,
        in_specs=[smem()] + [pl.BlockSpec(memory_space=pltpu.HBM)] * 4,
        out_specs=[whole_vmem()] * groups,
        scratch_shapes=[
            pltpu.VMEM((3, beads, atoms), jnp.float32),
            pltpu.VMEM((3, beads, atoms), jnp.float32),
            pltpu.SemaphoreType.DMA((2 + 2 * groups,)),
        ],
        compiler_params=params(60),
        name="pack",
    )(place, positions, momenta, force_old, noise)


def prepare(pair_list, mass, desc_w, hidden_one, place, rows):
    entries, atoms = pair_list.shape
    desc, env = desc_w.shape
    hid = hidden_one.shape[0]
    order = np.arange(env)
    order = (order % entries) * (env // entries) + order // entries
    permute = jnp.asarray(np.eye(env)[order], jnp.bfloat16)

    def kernel(place_ref, list_ref, mass_ref, w0_ref, w1_ref, order_ref, lists, own, masses, w0, w1):
        for t in range(atoms // LANES):
            at = pl.ds(t * LANES, LANES)
            lists[:, at] = list_ref[:, at] - t * LANES
        block = pl.ds(pl.multiple_of(place_ref[0] * rows, LANES), rows)
        own[...] = lists[:, block]
        masses[...] = mass_ref[:, block]
        w0[...] = lax.dot_general(
            order_ref[...],
            w0_ref[...],
            (((1,), (1,)), ((), ())),
            preferred_element_type=jnp.float32,
        ).astype(w0.dtype)
        w1[...] = w1_ref[...].astype(jnp.float32).T.astype(w1.dtype)

    return pl.pallas_call(
        kernel,
        out_shape=(
            jax.ShapeDtypeStruct((entries, atoms), jnp.int32),
            jax.ShapeDtypeStruct((entries, rows), jnp.int32),
            jax.ShapeDtypeStruct((1, rows), jnp.float32),
            jax.ShapeDtypeStruct((env, desc), jnp.bfloat16),
            jax.ShapeDtypeStruct((desc, hid), jnp.bfloat16),
        ),
        in_specs=[pl.BlockSpec(memory_space=pltpu.SMEM)] + [whole_vmem()] * 5,
        out_specs=(whole_vmem(),) * 5,
        compiler_params=params(),
        cost_estimate=pl.CostEstimate(
            flops=1_000_000_000, bytes_accessed=4_000_000, transcendentals=0
        ),
        name="prepare",
    )(place, pair_list, mass, desc_w, hidden_one, permute)


def contract(place, received, masses, table):
    groups = len(received)
    _, beads, rows = received[0].shape

    def kernel(place_ref, mass_ref, table_ref, own_ref, *rest):
        ins, (c_ref, first, last, fields, own, sem) = rest[: groups - 1], rest[groups - 1 :]

        load = pltpu.make_async_copy(own_ref, own, sem)
        load.start()
        mass = mass_ref[...]
        inverse = 1.0 / mass
        root = lax.rsqrt(mass)

        def scale(g, block):
            for x in range(3):
                fields[x, 0, g] = block[x]
                fields[x, 1, g] = block[3 + x] * inverse
                fields[x, 2, g] = block[6 + x] * root

        for r in range(1, groups):
            scale(place_ref[0] ^ r, ins[r - 1])
        load.wait()
        scale(place_ref[0], own)
        for x in range(3):
            out = jnp.dot(
                table_ref[...],
                fields[x].reshape(3 * BEADS, rows),
                precision=BEST,
                preferred_element_type=jnp.float32,
            )
            c_ref[x] = out
            first[x] = out[:, :EDGE]
            last[x] = out[:, rows - EDGE :]

    edge = jax.ShapeDtypeStruct((3, NC, EDGE), jnp.float32)
    return pl.pallas_call(
        kernel,
        out_shape=(
            jax.ShapeDtypeStruct((3, NC, rows), jnp.float32),
            edge,
            edge,
            jax.ShapeDtypeStruct((3, 3, groups, beads, rows), jnp.float32),
        ),
        in_specs=[smem()]
        + [whole_vmem()] * 2
        + [pl.BlockSpec(memory_space=pltpu.HBM)]
        + [whole_vmem()] * (groups - 1),
        out_specs=(whole_vmem(),) * 4,
        scratch_shapes=[pltpu.VMEM((9, beads, rows), jnp.float32), pltpu.SemaphoreType.DMA],
        compiler_params=params(),
        name="contract",
    )(place, masses, table, *received)


def transform(place, fields, masses, table):
    _, _, groups, beads, rows = fields.shape

    def kernel(place_ref, fields_ref, mass_ref, table_ref, *rest):
        outs, news = rest[:groups], rest[groups]
        mass = mass_ref[...]
        for x in range(3):
            out = jnp.dot(
                table_ref[...],
                fields_ref[x].reshape(3 * BEADS, rows),
                precision=BEST,
                preferred_element_type=jnp.float32,
            )
            news[x] = out[:BEADS].reshape(groups, beads, rows)
            news[3 + x] = (out[BEADS:] * mass).reshape(groups, beads, rows)
        for r in range(groups):
            for row in range(6):
                outs[r][row] = news[row, place_ref[0] ^ r]

    return pl.pallas_call(
        kernel,
        out_shape=[jax.ShapeDtypeStruct((6, beads, rows), jnp.float32)] * groups,
        in_specs=[smem()] + [whole_vmem()] * 3,
        out_specs=[whole_vmem()] * groups,
        scratch_shapes=[pltpu.VMEM((6, groups, beads, rows), jnp.float32)],
        compiler_params=params(),
        cost_estimate=pl.CostEstimate(
            flops=1_000_000_000, bytes_accessed=2_000_000, transcendentals=0
        ),
        name="transform",
    )(place, fields, masses, table)


def inverse_of(value):
    estimate = pl.reciprocal(value, approx=True)
    return estimate * (2.0 - value * estimate)


def banded(windows, lane, low, high):
    below, middle, above = [
        jnp.take_along_axis(w, lane, axis=1, mode="promise_in_bounds") for w in windows
    ]
    return jnp.where(low, below, jnp.where(high, above, middle))


def entries_of(list_ref, e, base):
    place = list_ref[pl.ds(e, 8), pl.ds(base, LANES)]
    return place & (LANES - 1), place < LANES, place >= 2 * LANES


def on_sublanes(row):
    return jnp.broadcast_to(row, (8, LANES))


def env_units(windows, list_ref, base, envs, inputs):
    entries = list_ref.shape[0]
    for e in range(0, entries, 8):
        lane, low, high = entries_of(list_ref, e, base)
        for c in range(NC):
            apart = []
            for x in range(3):
                tiles = windows(c, x)
                apart.append(banded(tiles, lane, low, high) - tiles[1])
            square = apart[0] * apart[0] + apart[1] * apart[1] + apart[2] * apart[2]
            close = inverse_of(1.0 + square)
            for x, value in enumerate(apart + [close]):
                envs[pl.ds(x * entries + e, 8), pl.ds(c * LANES, LANES)] = value
            yield
    for c in range(NC):
        at = pl.ds(c * LANES, LANES)
        inputs[at, :] = envs[:, at].T.astype(jnp.bfloat16)
        yield


def network(inputs_ref, weights, out_ref, base, units, chunk=256):
    w0_ref, w1_ref, w2_ref, w3_ref, wo_ref = weights
    desc = w0_ref.shape[1]
    inputs = inputs_ref[...]
    total = None
    for f in range(0, desc, chunk):
        size = min(chunk, desc - f)
        first = jnp.dot(inputs, w0_ref[:, pl.ds(f, size)], preferred_element_type=jnp.float32)
        first = jnp.tanh(first.astype(jnp.bfloat16))
        part = jnp.dot(first, w1_ref[pl.ds(f, size), :], preferred_element_type=jnp.float32)
        total = part if total is None else total + part
        for _ in range(6):
            next(units, None)
    layer = jnp.tanh(total).astype(jnp.bfloat16)
    for ref in (w2_ref, w3_ref):
        layer = jnp.tanh(jnp.dot(layer, ref[...], preferred_element_type=jnp.float32)).astype(
            jnp.bfloat16
        )
    out = lax.dot_general(
        wo_ref[...], layer, (((1,), (1,)), ((), ())), preferred_element_type=jnp.float32
    )
    for c in range(NC):
        for x in range(3):
            out_ref[x, pl.ds(c, 1), pl.ds(base, LANES)] = out[
                x : x + 1, c * LANES : (c + 1) * LANES
            ]


def neural_scratch(env):
    return [
        pltpu.VMEM((2, env, NC * LANES), jnp.float32),
        pltpu.VMEM((2, NC * LANES, env), jnp.bfloat16),
    ]


def neural(contracted, lower, upper, lists, weights, begin, end, done):
    _, _, rows = contracted.shape
    tiles = rows // LANES

    def kernel(
        c_ref, low_ref, up_ref, list_ref, w0, w1, w2, w3, wo, *rest
    ):
        out_ref, envs, inputs = rest[-3:]
        if begin:
            out_ref[:, :, pl.ds(0, begin * LANES)] = rest[0][:, :, pl.ds(0, begin * LANES)]

        def tile(x, c, t):
            if t < 0:
                ref, at = low_ref, 0
            elif t >= tiles:
                ref, at = up_ref, 0
            else:
                ref, at = c_ref, t * LANES
            return on_sublanes(ref[x, pl.ds(c, 1), pl.ds(at, LANES)])

        def units_of(t):
            if t >= end:
                return iter(())
            windows = lambda c, x: [tile(x, c, t + v) for v in (-1, 0, 1)]
            slot = t % 2
            return env_units(windows, list_ref, t * LANES, envs.at[slot], inputs.at[slot])

        for _ in units_of(begin):
            pass
        for t in range(begin, end):
            units = units_of(t + 1)
            network(inputs.at[t % 2], (w0, w1, w2, w3, wo), out_ref, t * LANES, units)
            for _ in units:
                pass

    return pl.pallas_call(
        kernel,
        out_shape=jax.ShapeDtypeStruct((3, NC, rows), jnp.float32),
        in_specs=[whole_vmem()] * (9 + len(done)),
        out_specs=whole_vmem(),
        scratch_shapes=neural_scratch(weights[0].shape[0]),
        compiler_params=params(),
        cost_estimate=pl.CostEstimate(
            flops=3_000_000_000 * (end - begin), bytes_accessed=4_000_000, transcendentals=0
        ),
        name=f"neural_{begin}",
    )(contracted, lower, upper, lists, *weights, *done)


def add_pairs(sums, e, b, apart, close):
    for x in range(3):
        part = apart[x] * close
        sums[x, b] = part if e == 0 else sums[x, b] + part


def total_of(sums, x):
    total = sums[x, :, 0, :]
    for s in range(1, 8):
        total = total + sums[x, :, s, :]
    return total


def assemble(place, fields):
    groups = len(fields)
    _, beads, rows = fields[0].shape
    atoms = groups * rows
    half = beads // 2
    top = float(2**15 - 1)

    def kernel(place_ref, *refs):
        ins, (newq, words, fixed, unit_ref, rims) = refs[:groups], refs[groups:]
        largest = jnp.zeros((beads, rows), jnp.float32)
        for r in range(groups):
            at = block_of(place_ref, r, rows)
            for x in range(3):
                value = ins[r][x]
                newq[x, :, at] = value
                largest = jnp.maximum(largest, jnp.abs(value))
        limit = jnp.maximum(jnp.max(largest, keepdims=True), 1e-30)
        to_fixed = top / limit
        unit_ref[...] = jnp.broadcast_to(limit / (top * 65536.0), (beads, LANES))
        for r in range(groups):
            at = block_of(place_ref, r, rows)
            for x in range(3):
                value = jnp.floor(ins[r][x] * to_fixed + 0.5)
                fixed[x, :, at] = value * 65536.0
                value = value.astype(jnp.int32)
                words[x, :, at] = (value[:half] << 16) | (value[half:] & 65535)
        for rim, t in enumerate((0, LANES, atoms - 2 * LANES, atoms - LANES)):
            rims[rim] = newq[:, :, pl.ds(t, LANES)]

    return pl.pallas_call(
        kernel,
        out_shape=(
            jax.ShapeDtypeStruct((3, beads, atoms), jnp.float32),
            jax.ShapeDtypeStruct((3, half, atoms), jnp.int32),
            jax.ShapeDtypeStruct((3, beads, atoms), jnp.float32),
            jax.ShapeDtypeStruct((beads, LANES), jnp.float32),
            jax.ShapeDtypeStruct((4, 3, beads, LANES), jnp.float32),
        ),
        in_specs=[smem()] + [whole_vmem()] * groups,
        out_specs=(whole_vmem(),) * 5,
        compiler_params=params(),
        name="assemble",
    )(place, *fields)


def pair_part(words, fixed, unit, lists, begin, end, edges=()):
    _, beads, atoms = fixed.shape
    half = beads // 2
    tiles = atoms // LANES
    entries = lists.shape[0]

    def kernel(words_ref, fixed_ref, unit_ref, list_ref, *rest):
        ends = rest[: len(edges)]
        pair, sums = rest[len(edges)], rest[-1]
        unit_row = unit_ref[...]
        unit_square = on_sublanes(unit_ref[pl.ds(0, 1), :])
        unit_square = unit_square * unit_square

        def edge(out, at, base, near_tiles):
            for e in range(0, entries, 8):
                lane, low, high = entries_of(list_ref, e, base)
                for b in range(beads):
                    apart = []
                    for x in range(3):
                        windows = [on_sublanes(tile[x, pl.ds(b, 1), :]) for tile in near_tiles]
                        apart.append(banded(windows, lane, low, high) - windows[1])
                    square = apart[0] * apart[0] + apart[1] * apart[1] + apart[2] * apart[2]
                    add_pairs(sums, e, b, apart, inverse_of(1.0 + square))
            for x in range(3):
                out[x, :, pl.ds(at, LANES)] = PAIR_STRENGTH * total_of(sums, x)

        @pl.loop(max(begin, 1), min(end, tiles - 1))
        def _(t):
            base = pl.multiple_of(t * LANES, LANES)

            def row(ref, x, b, v):
                return on_sublanes(ref[x, pl.ds(b, 1), pl.ds(base + (v - 1) * LANES, LANES)])

            for e in range(0, entries, 8):
                lane, low, high = entries_of(list_ref, e, base)
                for b in range(half):
                    both = [
                        banded([row(words_ref, x, b, v) for v in range(3)], lane, low, high)
                        for x in range(3)
                    ]
                    for bead, near in ((b, [w & -65536 for w in both]),
                                       (b + half, [w << 16 for w in both])):
                        apart = [
                            near[x].astype(jnp.float32) - row(fixed_ref, x, bead, 1)
                            for x in range(3)
                        ]
                        square = apart[0] * apart[0] + apart[1] * apart[1] + apart[2] * apart[2]
                        close = inverse_of(1.0 + square * unit_square)
                        add_pairs(sums, e, bead, apart, close)
            at = pl.ds(pl.multiple_of((t - begin) * LANES, LANES), LANES)
            for x in range(3):
                pair[x, :, at] = (PAIR_STRENGTH * unit_row) * total_of(sums, x)

        if edges:
            rims, lower, upper = ends
            last = (tiles - 1) * LANES
            edge(rest[len(edges) + 1], 0, 0, [lower, rims.at[0], rims.at[1]])
            edge(pair, last - begin * LANES, last, [rims.at[2], rims.at[3], upper])

    out_shape = [jax.ShapeDtypeStruct((3, beads, (end - begin) * LANES), jnp.float32)]
    if edges:
        out_shape.append(jax.ShapeDtypeStruct((3, beads, LANES), jnp.float32))
    return pl.pallas_call(
        kernel,
        out_shape=out_shape,
        in_specs=[whole_vmem()] * (4 + len(edges)),
        out_specs=[whole_vmem()] * len(out_shape),
        scratch_shapes=[pltpu.VMEM((3, beads, 8, LANES), jnp.float32)],
        compiler_params=params(),
        cost_estimate=pl.CostEstimate(
            flops=300_000_000 * (end - begin), bytes_accessed=2_000_000, transcendentals=0
        ),
        name=f"pair_{begin}",
    )(words, fixed, unit, lists, *edges)


def finish(place, pairs, first, moved, neural_parts, partners, coefs):
    groups = len(moved)
    _, beads, rows = moved[0].shape
    atoms = groups * rows
    counts = [part.shape[0] for part in neural_parts]

    def kernel(place_ref, first_ref, coef_ref, *rest):
        halves, rest = rest[: len(pairs)], rest[len(pairs) :]
        ins, rest = rest[:groups], rest[groups:]
        blocks, (newp, newf) = rest[: len(counts)], rest[len(counts) :]
        own = place_ref[0]
        at = 0
        for half in halves:
            newf[:, :, pl.ds(at, half.shape[2])] = half[...]
            at += half.shape[2]
        newf[:, :, pl.ds(0, LANES)] = first_ref[...]
        coef = [coef_ref[c, own] for c in range(NC)]
        blocks = [block.at[i] for block, count in zip(blocks, counts) for i in range(count)]
        for r, block in zip(partners, blocks):
            g = own ^ r
            for t in range(0, rows, LANES):
                at = pl.ds(pl.multiple_of(g * rows + t, LANES), LANES)
                inner = pl.ds(t, LANES)
                for x in range(3):
                    force = newf[x, :, at]
                    for c in range(NC):
                        force = force + coef[c] * block[x, pl.ds(c, 1), inner]
                    newf[x, :, at] = force
                    newp[x, :, at] = ins[r][3 + x, :, inner] + 0.5 * TIME_STEP * force

    out = jax.ShapeDtypeStruct((3, beads, atoms), jnp.float32)
    return pl.pallas_call(
        kernel,
        out_shape=(out,) * 2,
        in_specs=[smem()] + [whole_vmem()] * (2 + len(pairs) + groups + len(neural_parts)),
        out_specs=(whole_vmem(),) * 2,
        compiler_params=params(),
        name="finish",
    )(place, first, coefs, *pairs, *moved, *neural_parts)


def doubling_step(have, partners, axis, bit):
    count = lax.axis_size(axis)
    got = lax.ppermute(have, axis, [(i, i ^ bit) for i in range(count)])
    return got, partners + [r ^ bit for r in partners]


def body(
    positions,
    momenta,
    force_old,
    noise,
    mass,
    pair_list,
    desc_w,
    hidden_one,
    hidden_two,
    hidden_three,
    out_w,
):
    beads, _, atoms = positions.shape
    groups = lax.axis_size("bead")
    slabs = lax.axis_size(("slab", "grp"))
    rows = atoms // groups
    place = lax.axis_index("bead").astype(jnp.int32)[None]
    step, kernel = step_tables()

    swap = lambda field: jnp.transpose(field, (1, 0, 2))
    sends = pack(place, swap(positions), swap(momenta), swap(force_old), swap(noise), groups)
    received = exchange(sends, "bead")

    lists, block_lists, masses, env_w, w1 = prepare(
        pair_list.T, mass[None, :], desc_w.T, hidden_one.T, place, rows
    )
    received, lists, block_lists, masses, env_w, w1 = lax.optimization_barrier(
        (received, lists, block_lists, masses, env_w, w1)
    )
    weights = (env_w, w1, hidden_two, hidden_three, out_w.T)

    contracted, first, last, scaled = contract(place, received, masses, jnp.asarray(step[:NC]))
    ring = [
        (g * slabs + s, ((g + 1) % groups) * slabs + (s + (g + 1) // groups) % slabs)
        for g in range(groups)
        for s in range(slabs)
    ]
    back = [(j, i) for i, j in ring]
    every = ("bead", "slab", "grp")
    lower = lax.ppermute(last, every, ring)
    upper = lax.ppermute(first, every, back)
    returns = transform(place, scaled, masses, jnp.asarray(step[NC:]))
    returns, lower, upper = lax.optimization_barrier((returns, lower, upper))
    fields = exchange(returns, "bead")

    tiles = rows // LANES
    inputs = (contracted, lower, upper, block_lists, weights)
    forces = neural(*inputs, 0, tiles // 2, ())
    forces = neural(*inputs, tiles // 2, tiles, (forces,))
    bits = [1 << i for i in range(groups.bit_length() - 2, -1, -1)]
    have = forces[None]
    got, partners = doubling_step(have, [0], "bead", bits[0])
    fields, forces = lax.optimization_barrier((fields[::-1], forces))
    fields = fields[::-1]

    new_q, words, fixed, unit, rims = assemble(place, fields)
    slab_ring = [(s, (s + 1) % slabs) for s in range(slabs)]
    slab_back = [(j, i) for i, j in slab_ring]
    q_lower = lax.ppermute(rims[3], ("slab", "grp"), slab_ring)
    q_upper = lax.ppermute(rims[0], ("slab", "grp"), slab_back)

    words, got = lax.optimization_barrier((words, got))
    tiles = atoms // LANES
    cut = 3 * tiles // 8
    for bit in bits[1:2]:
        have = jnp.concatenate([have, got], axis=0)
        got, partners = doubling_step(have, partners, "bead", bit)
    pairs = pair_part(words, fixed, unit, lists, 0, cut)
    words, pairs, got = lax.optimization_barrier((words, pairs, got))
    for bit in bits[2:]:
        have = jnp.concatenate([have, got], axis=0)
        got, partners = doubling_step(have, partners, "bead", bit)
    rest, first = pair_part(
        words, fixed, unit, lists, cut, tiles, (rims, q_lower, q_upper)
    )

    coefs = (kernel * np.float32(BEADS / NC)).reshape(NC, groups, beads, 1)
    coefs = jnp.asarray(np.broadcast_to(coefs, (NC, groups, beads, LANES)))
    new_p, force = finish(
        place, [*pairs, rest], first, fields, (have, got), partners, coefs
    )
    return tuple(swap(out) for out in (new_q, new_p, force))


def solution(mesh):
    field = P("bead", None, ("slab", "grp"))
    placed = (field,) * 4 + (P(("slab", "grp")), P(("slab", "grp"), None)) + (P(),) * 5
    return jax.shard_map(
        body, mesh=mesh, in_specs=placed, out_specs=(field,) * 3, check_vma=False
    )
```

```python
import math

import jax
import jax.numpy as jnp
import numpy as np
from jax import lax
from jax.experimental import pallas as pl
from jax.experimental.pallas import tpu as pltpu
from jax.sharding import PartitionSpec as P

BEADS = 64
NC = 8
EDGE = 128
LANES = 128

TIME_STEP = 0.1
CYCLE_FREQ = 5.0
CENTROID_FRICTION = 1.0
PAIR_STRENGTH = 0.5

BEST = lax.Precision.HIGHEST


def step_tables():
    b = np.arange(BEADS, dtype=np.float64)
    k = np.arange(BEADS)
    angle = 2.0 * np.pi * ((b[:, None] * b[None, :]) % BEADS) / BEADS
    half = BEADS // 2
    basis = np.where(
        k == 0,
        1.0 / math.sqrt(BEADS),
        np.where(
            k < half,
            math.sqrt(2.0 / BEADS) * np.cos(angle),
            np.where(
                k == half, np.cos(angle) / math.sqrt(BEADS), math.sqrt(2.0 / BEADS) * np.sin(angle)
            ),
        ),
    )
    freq = 2.0 * CYCLE_FREQ * np.sin(np.pi * b / BEADS)
    spacing = b[None, :] / BEADS - np.arange(NC, dtype=np.float64)[:, None] / NC
    kernel = np.ones_like(spacing)
    for order in range(1, NC // 2):
        kernel = kernel + 2.0 * np.cos(2.0 * np.pi * order * spacing)
    kernel = kernel + np.cos(np.pi * NC * spacing)
    contract = kernel / BEADS

    h = 0.5 * TIME_STEP
    safe = np.where(freq > 0.0, freq, 1.0)
    qq = np.where(freq > 0.0, np.cos(safe * h), 1.0)
    qp = np.where(freq > 0.0, np.sin(safe * h) / safe, h)
    pq = np.where(freq > 0.0, -safe * np.sin(safe * h), 0.0)
    pp = qq
    keep = np.exp(-np.where(freq > 0.0, 2.0 * freq, CENTROID_FRICTION) * TIME_STEP)
    kick = np.sqrt(1.0 - keep * keep)
    full_qq = qq * qq + qp * keep * pq
    full_qp = qq * qp + qp * keep * pp
    full_qn = qp * kick
    full_pq = pq * qq + pp * keep * pq
    full_pp = pq * qp + pp * keep * pp
    full_pn = pp * kick
    q_rows = np.concatenate(
        [(basis * full_qq) @ basis.T, (basis * full_qp) @ basis.T, basis * full_qn], axis=1
    )
    p_rows = np.concatenate(
        [(basis * full_pq) @ basis.T, (basis * full_pp) @ basis.T, basis * full_pn], axis=1
    )
    c_rows = contract @ q_rows
    step = np.concatenate([c_rows, q_rows, p_rows], axis=0)
    return step.astype(np.float32), contract.astype(np.float32)


def whole_vmem():
    return pl.BlockSpec(memory_space=pltpu.VMEM)


def params(mebibytes=48):
    return pltpu.CompilerParams(vmem_limit_bytes=mebibytes * 1024 * 1024)


def smem():
    return pl.BlockSpec(memory_space=pltpu.SMEM)


def block_of(place_ref, r, rows, count):
    return pl.ds(pl.multiple_of(((place_ref[0] ^ r) % count) * rows, LANES), rows)


def swap_with(block, axis, r):
    return lax.ppermute(block, axis, [(i, i ^ r) for i in range(lax.axis_size(axis))])


def exchange(blocks, axis):
    return [blocks[0]] + [swap_with(blocks[r], axis, r) for r in range(1, len(blocks))]


def pack(place, positions, momenta, force_old, noise, groups):
    _, beads, atoms = positions.shape
    rows = atoms // groups

    def kernel(place_ref, q_ref, p_ref, f_ref, n_ref, *rest):
        outs, (p_buf, f_buf, sems) = rest[:groups], rest[groups:]
        loads = [
            pltpu.make_async_copy(p_ref, p_buf, sems.at[0]),
            pltpu.make_async_copy(f_ref, f_buf, sems.at[1]),
        ]
        for r in range(groups):
            at = block_of(place_ref, r, rows, groups)
            for slot, (ref, first) in enumerate(((q_ref, 0), (n_ref, 6))):
                loads.append(
                    pltpu.make_async_copy(
                        ref.at[:, :, at], outs[r].at[pl.ds(first, 3)], sems.at[2 + 2 * r + slot]
                    )
                )
        for load in loads:
            load.start()
        loads[0].wait()
        loads[1].wait()
        for r in range(groups):
            at = block_of(place_ref, r, rows, groups)
            for x in range(3):
                outs[r][3 + x] = p_buf[x, :, at] + 0.5 * TIME_STEP * f_buf[x, :, at]
        for load in loads[2:]:
            load.wait()

    return pl.pallas_call(
        kernel,
        out_shape=[jax.ShapeDtypeStruct((9, beads, rows), jnp.float32)] * groups,
        in_specs=[smem()] + [pl.BlockSpec(memory_space=pltpu.HBM)] * 4,
        out_specs=[whole_vmem()] * groups,
        scratch_shapes=[
            pltpu.VMEM((3, beads, atoms), jnp.float32),
            pltpu.VMEM((3, beads, atoms), jnp.float32),
            pltpu.SemaphoreType.DMA((2 + 2 * groups,)),
        ],
        compiler_params=params(60),
        name="pack",
    )(place, positions, momenta, force_old, noise)


def prepare(pair_list, mass, desc_w, hidden_one, place, rows, half):
    entries, atoms = pair_list.shape
    desc, env = desc_w.shape
    hid = hidden_one.shape[0]
    order = np.arange(env)
    order = (order % entries) * (env // entries) + order // entries
    permute = jnp.asarray(np.eye(env)[order], jnp.bfloat16)

    def kernel(place_ref, list_ref, mass_ref, w0_ref, w1_ref, order_ref, lists, own, masses, w0, w1):
        for t in range(atoms // LANES):
            at = pl.ds(t * LANES, LANES)
            lists[:, at] = list_ref[:, at] - t * LANES
        inner, upper = place_ref[0] % half, place_ref[0] // half
        block = pl.ds(pl.multiple_of((2 * inner + upper) * rows, LANES), rows)
        own[...] = lists[:, block]
        masses[...] = mass_ref[:, pl.ds(pl.multiple_of(2 * inner * rows, LANES), 2 * rows)]
        w0[...] = lax.dot_general(
            order_ref[...],
            w0_ref[...],
            (((1,), (1,)), ((), ())),
            preferred_element_type=jnp.float32,
        ).astype(w0.dtype)
        w1[...] = w1_ref[...].astype(jnp.float32).T.astype(w1.dtype)

    return pl.pallas_call(
        kernel,
        out_shape=(
            jax.ShapeDtypeStruct((entries, atoms), jnp.int32),
            jax.ShapeDtypeStruct((entries, rows), jnp.int32),
            jax.ShapeDtypeStruct((1, 2 * rows), jnp.float32),
            jax.ShapeDtypeStruct((env, desc), jnp.bfloat16),
            jax.ShapeDtypeStruct((desc, hid), jnp.bfloat16),
        ),
        in_specs=[pl.BlockSpec(memory_space=pltpu.SMEM)] + [whole_vmem()] * 5,
        out_specs=(whole_vmem(),) * 5,
        compiler_params=params(),
        cost_estimate=pl.CostEstimate(
            flops=1_000_000_000, bytes_accessed=4_000_000, transcendentals=0
        ),
        name="prepare",
    )(place, pair_list, mass, desc_w, hidden_one, permute)


def contract(place, received, masses, table):
    groups = len(received)
    _, beads, rows = received[0].shape

    def kernel(place_ref, mass_ref, table_ref, own_ref, *rest):
        ins, (c_ref, fields, own, sem) = rest[: groups - 1], rest[groups - 1 :]
        load = pltpu.make_async_copy(own_ref, own, sem)
        load.start()
        mass = mass_ref[...]
        inverse = 1.0 / mass
        root = lax.rsqrt(mass)

        def scale(g, block):
            for x in range(3):
                fields[x, 0, g] = block[x]
                fields[x, 1, g] = block[3 + x] * inverse
                fields[x, 2, g] = block[6 + x] * root

        inner = place_ref[0] % groups
        for r in range(1, groups):
            scale(inner ^ r, ins[r - 1])
        load.wait()
        scale(inner, own)
        for x in range(3):
            c_ref[x] = jnp.dot(
                table_ref[place_ref[0] // groups],
                fields[x].reshape(3 * BEADS // 2, rows),
                precision=BEST,
                preferred_element_type=jnp.float32,
            )

    return pl.pallas_call(
        kernel,
        out_shape=(
            jax.ShapeDtypeStruct((3, NC, rows), jnp.float32),
            jax.ShapeDtypeStruct((3, 3, groups, beads, rows), jnp.float32),
        ),
        in_specs=[smem()]
        + [whole_vmem()] * 2
        + [pl.BlockSpec(memory_space=pltpu.HBM)]
        + [whole_vmem()] * (groups - 1),
        out_specs=(whole_vmem(),) * 2,
        scratch_shapes=[pltpu.VMEM((9, beads, rows), jnp.float32), pltpu.SemaphoreType.DMA],
        compiler_params=params(),
        name="contract",
    )(place, masses, table, *received)


def join_contracted(place, own, other):
    _, _, both = own.shape
    rows = both // 2

    def kernel(upper_ref, own_ref, other_ref, mine, beside, outgoing, total):
        upper = upper_ref[0]
        total[...] = own_ref[...] + other_ref[...]
        mine[...] = total[:, :, pl.ds(pl.multiple_of(upper * rows, LANES), rows)]
        at = pl.multiple_of(rows - upper * EDGE, LANES)
        beside[...] = total[:, :, pl.ds(at, EDGE)]
        at = pl.multiple_of((1 - upper) * (both - EDGE), LANES)
        outgoing[...] = total[:, :, pl.ds(at, EDGE)]

    edge = jax.ShapeDtypeStruct((3, NC, EDGE), jnp.float32)
    return pl.pallas_call(
        kernel,
        out_shape=(jax.ShapeDtypeStruct((3, NC, rows), jnp.float32), edge, edge),
        in_specs=[smem()] + [whole_vmem()] * 2,
        out_specs=(whole_vmem(),) * 3,
        scratch_shapes=[pltpu.VMEM((3, NC, both), jnp.float32)],
        compiler_params=params(),
        name="join_contracted",
    )(place, own, other)


def transform(place, fields, masses, table, name):
    _, _, groups, beads, rows = fields.shape

    def kernel(place_ref, fields_ref, mass_ref, table_ref, cross, own):
        for x in range(3):
            out = jnp.dot(
                table_ref[place_ref[0] // groups],
                fields_ref[x].reshape(3 * BEADS // 2, rows),
                precision=BEST,
                preferred_element_type=jnp.float32,
            )
            if name == "p":
                out = out * mass_ref[...]
            cross[x] = out[: BEADS // 2].reshape(groups, beads, rows)
            own[x] = out[BEADS // 2 :].reshape(groups, beads, rows)

    return pl.pallas_call(
        kernel,
        out_shape=[jax.ShapeDtypeStruct((3, groups, beads, rows), jnp.float32)] * 2,
        in_specs=[smem()] + [whole_vmem()] * 3,
        out_specs=[whole_vmem()] * 2,
        compiler_params=params(),
        cost_estimate=pl.CostEstimate(
            flops=500_000_000, bytes_accessed=1_000_000, transcendentals=0
        ),
        name=f"transform_{name}",
    )(place, fields, masses, table)


def join(place, own, other, name):
    _, groups, beads, rows = own.shape

    def kernel(place_ref, own_ref, other_ref, *outs):
        inner = place_ref[0] % groups
        for r in range(groups):
            for x in range(3):
                outs[r][x] = own_ref[x, inner ^ r] + other_ref[x, inner ^ r]

    return pl.pallas_call(
        kernel,
        out_shape=[jax.ShapeDtypeStruct((3, beads, rows), jnp.float32)] * groups,
        in_specs=[smem()] + [whole_vmem()] * 2,
        out_specs=[whole_vmem()] * groups,
        compiler_params=params(),
        name=f"join_{name}",
    )(place, own, other)


def inverse_of(value):
    estimate = pl.reciprocal(value, approx=True)
    return estimate * (2.0 - value * estimate)


def banded(windows, lane, low, high):
    below, middle, above = [
        jnp.take_along_axis(w, lane, axis=1, mode="promise_in_bounds") for w in windows
    ]
    return jnp.where(low, below, jnp.where(high, above, middle))


def entries_of(list_ref, e, base):
    place = list_ref[pl.ds(e, 8), pl.ds(base, LANES)]
    return place & (LANES - 1), place < LANES, place >= 2 * LANES


def on_sublanes(row):
    return jnp.broadcast_to(row, (8, LANES))


def env_units(windows, list_ref, base, envs, inputs):
    entries = list_ref.shape[0]
    for e in range(0, entries, 8):
        lane, low, high = entries_of(list_ref, e, base)
        for c in range(NC):
            apart = []
            for x in range(3):
                tiles = windows(c, x)
                apart.append(banded(tiles, lane, low, high) - tiles[1])
            square = apart[0] * apart[0] + apart[1] * apart[1] + apart[2] * apart[2]
            close = inverse_of(1.0 + square)
            for x, value in enumerate(apart + [close]):
                envs[pl.ds(x * entries + e, 8), pl.ds(c * LANES, LANES)] = value
            yield
    for c in range(NC):
        at = pl.ds(c * LANES, LANES)
        inputs[at, :] = envs[:, at].T.astype(jnp.bfloat16)
        yield


def network(inputs_ref, weights, out_ref, base, units, chunk=256):
    w0_ref, w1_ref, w2_ref, w3_ref, wo_ref = weights
    desc = w0_ref.shape[1]
    inputs = inputs_ref[...]
    total = None
    for f in range(0, desc, chunk):
        size = min(chunk, desc - f)
        first = jnp.dot(inputs, w0_ref[:, pl.ds(f, size)], preferred_element_type=jnp.float32)
        first = jnp.tanh(first.astype(jnp.bfloat16))
        part = jnp.dot(first, w1_ref[pl.ds(f, size), :], preferred_element_type=jnp.float32)
        total = part if total is None else total + part
        for _ in range(6):
            next(units, None)
    layer = jnp.tanh(total).astype(jnp.bfloat16)
    for ref in (w2_ref, w3_ref):
        layer = jnp.tanh(jnp.dot(layer, ref[...], preferred_element_type=jnp.float32)).astype(
            jnp.bfloat16
        )
    out = lax.dot_general(
        wo_ref[...], layer, (((1,), (1,)), ((), ())), preferred_element_type=jnp.float32
    )
    for c in range(NC):
        for x in range(3):
            out_ref[x, pl.ds(c, 1), pl.ds(base, LANES)] = out[
                x : x + 1, c * LANES : (c + 1) * LANES
            ]


def neural_scratch(env):
    return [
        pltpu.VMEM((2, env, NC * LANES), jnp.float32),
        pltpu.VMEM((2, NC * LANES, env), jnp.bfloat16),
    ]


def neural(upper, contracted, beside, remote, lists, weights):
    _, _, rows = contracted.shape
    tiles = rows // LANES

    def kernel(
        upper_ref, c_ref, beside_ref, remote_ref, list_ref, w0, w1, w2, w3, wo,
        out_ref, halos, envs, inputs,
    ):
        halos[upper_ref[0]] = remote_ref[...]
        halos[1 - upper_ref[0]] = beside_ref[...]

        def tile(x, c, t):
            if t < 0:
                row = halos[0, x, pl.ds(c, 1), :]
            elif t >= tiles:
                row = halos[1, x, pl.ds(c, 1), :]
            else:
                row = c_ref[x, pl.ds(c, 1), pl.ds(t * LANES, LANES)]
            return on_sublanes(row)

        def units_of(t):
            if t >= tiles:
                return iter(())
            windows = lambda c, x: [tile(x, c, t + v) for v in (-1, 0, 1)]
            slot = t % 2
            return env_units(windows, list_ref, t * LANES, envs.at[slot], inputs.at[slot])

        for _ in units_of(0):
            pass
        for t in range(tiles):
            units = units_of(t + 1)
            network(inputs.at[t % 2], (w0, w1, w2, w3, wo), out_ref, t * LANES, units)
            for _ in units:
                pass

    return pl.pallas_call(
        kernel,
        out_shape=jax.ShapeDtypeStruct((3, NC, rows), jnp.float32),
        in_specs=[smem()] + [whole_vmem()] * 9,
        out_specs=whole_vmem(),
        scratch_shapes=[pltpu.VMEM((2, 3, NC, EDGE), jnp.float32)]
        + neural_scratch(weights[0].shape[0]),
        compiler_params=params(),
        cost_estimate=pl.CostEstimate(
            flops=12_000_000_000, bytes_accessed=4_000_000, transcendentals=0
        ),
        name="neural",
    )(upper, contracted, beside, remote, lists, *weights)


def add_pairs(sums, e, b, apart, close):
    for x in range(3):
        part = apart[x] * close
        sums[x, b] = part if e == 0 else sums[x, b] + part


def total_of(sums, x):
    total = sums[x, :, 0, :]
    for s in range(1, 8):
        total = total + sums[x, :, s, :]
    return total


def assemble(place, fields):
    groups = len(fields)
    _, beads, rows = fields[0].shape
    atoms = groups * rows
    half = beads // 2
    top = float(2**15 - 1)

    def kernel(place_ref, *refs):
        ins, (newq, words, fixed, unit_ref, rims) = refs[:groups], refs[groups:]
        largest = jnp.zeros((beads, rows), jnp.float32)
        for r in range(groups):
            at = block_of(place_ref, r, rows, groups)
            for x in range(3):
                value = ins[r][x]
                newq[x, :, at] = value
                largest = jnp.maximum(largest, jnp.abs(value))
        limit = jnp.maximum(jnp.max(largest, keepdims=True), 1e-30)
        to_fixed = top / limit
        unit_ref[...] = jnp.broadcast_to(limit / (top * 65536.0), (beads, LANES))
        for r in range(groups):
            at = block_of(place_ref, r, rows, groups)
            for x in range(3):
                value = jnp.floor(ins[r][x] * to_fixed + 0.5)
                fixed[x, :, at] = value * 65536.0
                value = value.astype(jnp.int32)
                words[x, :, at] = (value[:half] << 16) | (value[half:] & 65535)
        for rim, t in enumerate((0, LANES, atoms - 2 * LANES, atoms - LANES)):
            rims[rim] = newq[:, :, pl.ds(t, LANES)]

    return pl.pallas_call(
        kernel,
        out_shape=(
            jax.ShapeDtypeStruct((3, beads, atoms), jnp.float32),
            jax.ShapeDtypeStruct((3, half, atoms), jnp.int32),
            jax.ShapeDtypeStruct((3, beads, atoms), jnp.float32),
            jax.ShapeDtypeStruct((beads, LANES), jnp.float32),
            jax.ShapeDtypeStruct((4, 3, beads, LANES), jnp.float32),
        ),
        in_specs=[smem()] + [whole_vmem()] * groups,
        out_specs=(whole_vmem(),) * 5,
        compiler_params=params(),
        name="assemble",
    )(place, *fields)


def pair_part(words, fixed, unit, lists, begin, end, edges=()):
    _, beads, atoms = fixed.shape
    half = beads // 2
    tiles = atoms // LANES
    entries = lists.shape[0]

    def kernel(words_ref, fixed_ref, unit_ref, list_ref, *rest):
        ends = rest[: len(edges)]
        pair, sums = rest[len(edges)], rest[-1]
        unit_row = unit_ref[...]
        unit_square = on_sublanes(unit_ref[pl.ds(0, 1), :])
        unit_square = unit_square * unit_square

        def edge(out, at, base, near_tiles):
            for e in range(0, entries, 8):
                lane, low, high = entries_of(list_ref, e, base)
                for b in range(beads):
                    apart = []
                    for x in range(3):
                        windows = [on_sublanes(tile[x, pl.ds(b, 1), :]) for tile in near_tiles]
                        apart.append(banded(windows, lane, low, high) - windows[1])
                    square = apart[0] * apart[0] + apart[1] * apart[1] + apart[2] * apart[2]
                    add_pairs(sums, e, b, apart, inverse_of(1.0 + square))
            for x in range(3):
                out[x, :, pl.ds(at, LANES)] = PAIR_STRENGTH * total_of(sums, x)

        @pl.loop(max(begin, 1), min(end, tiles - 1))
        def _(t):
            base = pl.multiple_of(t * LANES, LANES)

            def row(ref, x, b, v):
                return on_sublanes(ref[x, pl.ds(b, 1), pl.ds(base + (v - 1) * LANES, LANES)])

            for e in range(0, entries, 8):
                lane, low, high = entries_of(list_ref, e, base)
                for b in range(half):
                    both = [
                        banded([row(words_ref, x, b, v) for v in range(3)], lane, low, high)
                        for x in range(3)
                    ]
                    for bead, near in ((b, [w & -65536 for w in both]),
                                       (b + half, [w << 16 for w in both])):
                        apart = [
                            near[x].astype(jnp.float32) - row(fixed_ref, x, bead, 1)
                            for x in range(3)
                        ]
                        square = apart[0] * apart[0] + apart[1] * apart[1] + apart[2] * apart[2]
                        close = inverse_of(1.0 + square * unit_square)
                        add_pairs(sums, e, bead, apart, close)
            at = pl.ds(pl.multiple_of((t - begin) * LANES, LANES), LANES)
            for x in range(3):
                pair[x, :, at] = (PAIR_STRENGTH * unit_row) * total_of(sums, x)

        if edges:
            rims, lower, upper = ends
            last = (tiles - 1) * LANES
            edge(rest[len(edges) + 1], 0, 0, [lower, rims.at[0], rims.at[1]])
            edge(pair, last - begin * LANES, last, [rims.at[2], rims.at[3], upper])

    out_shape = [jax.ShapeDtypeStruct((3, beads, (end - begin) * LANES), jnp.float32)]
    if edges:
        out_shape.append(jax.ShapeDtypeStruct((3, beads, LANES), jnp.float32))
    return pl.pallas_call(
        kernel,
        out_shape=out_shape,
        in_specs=[whole_vmem()] * (4 + len(edges)),
        out_specs=[whole_vmem()] * len(out_shape),
        scratch_shapes=[pltpu.VMEM((3, beads, 8, LANES), jnp.float32)],
        compiler_params=params(),
        cost_estimate=pl.CostEstimate(
            flops=300_000_000 * (end - begin), bytes_accessed=2_000_000, transcendentals=0
        ),
        name=f"pair_{begin}",
    )(words, fixed, unit, lists, *edges)


def finish(place, pairs, first, moved, neural_parts, partners, coefs):
    half = len(moved)
    _, beads, wide = moved[0].shape
    rows = wide // 2
    atoms = half * wide
    counts = [part.shape[0] for part in neural_parts]

    def kernel(place_ref, first_ref, coef_ref, *rest):
        halves, rest = rest[: len(pairs)], rest[len(pairs) :]
        ins, rest = rest[:half], rest[half:]
        blocks, (newp, newf) = rest[: len(counts)], rest[len(counts) :]
        own = place_ref[0]
        at = 0
        for piece in halves:
            newf[:, :, pl.ds(at, piece.shape[2])] = piece[...]
            at += piece.shape[2]
        newf[:, :, pl.ds(0, LANES)] = first_ref[...]
        coef = [coef_ref[c, own] for c in range(NC)]
        blocks = [block.at[i] for block, count in zip(blocks, counts) for i in range(count)]
        for r, block in zip(partners, blocks):
            source = own ^ r
            base = (source % half) * wide + (source // half) * rows
            for t in range(0, rows, LANES):
                at = pl.ds(pl.multiple_of(base + t, LANES), LANES)
                for x in range(3):
                    force = newf[x, :, at]
                    for c in range(NC):
                        force = force + coef[c] * block[x, pl.ds(c, 1), pl.ds(t, LANES)]
                    newf[x, :, at] = force
        for r in range(half):
            at = block_of(place_ref, r, wide, half)
            for x in range(3):
                newp[x, :, at] = ins[r][x] + 0.5 * TIME_STEP * newf[x, :, at]

    out = jax.ShapeDtypeStruct((3, beads, atoms), jnp.float32)
    return pl.pallas_call(
        kernel,
        out_shape=(out,) * 2,
        in_specs=[smem()] + [whole_vmem()] * (2 + len(pairs) + half + len(neural_parts)),
        out_specs=(whole_vmem(),) * 2,
        compiler_params=params(),
        name="finish",
    )(place, first, coefs, *pairs, *moved, *neural_parts)


def doubling_step(have, partners, axis, bit):
    count = lax.axis_size(axis)
    got = lax.ppermute(have, axis, [(i, i ^ bit) for i in range(count)])
    return got, partners + [r ^ bit for r in partners]


def body(
    positions,
    momenta,
    force_old,
    noise,
    mass,
    pair_list,
    desc_w,
    hidden_one,
    hidden_two,
    hidden_three,
    out_w,
):
    beads, _, atoms = positions.shape
    groups = lax.axis_size("bead")
    slabs = lax.axis_size(("slab", "grp"))
    rows = atoms // groups
    half = groups // 2
    index = lax.axis_index("bead").astype(jnp.int32)
    place, upper = index[None], (index // half)[None]
    step, kernel = step_tables()
    sides = step.reshape(-1, 3, 2, BEADS // 2).transpose(2, 0, 1, 3).reshape(2, -1, 3 * BEADS // 2)

    def crossing(first_row):
        rows_of = [sides[:, first_row + s * BEADS // 2 :][:, : BEADS // 2] for s in range(2)]
        return jnp.asarray(
            np.stack(
                [np.concatenate([rows_of[1 - s][s], rows_of[s][s]], axis=0) for s in range(2)]
            )
        )

    swap = lambda field: jnp.transpose(field, (1, 0, 2))
    sends = pack(place, swap(positions), swap(momenta), swap(force_old), swap(noise), half)
    received = exchange(sends, "bead")

    lists, block_lists, masses, env_w, w1 = prepare(
        pair_list.T, mass[None, :], desc_w.T, hidden_one.T, place, rows, half
    )
    received, lists, block_lists, masses, env_w, w1 = lax.optimization_barrier(
        (received, lists, block_lists, masses, env_w, w1)
    )
    weights = (env_w, w1, hidden_two, hidden_three, out_w.T)

    contracted, scaled = contract(place, received, masses, jnp.asarray(sides[:, :NC]))
    other = swap_with(contracted, "bead", half)
    q_cross, q_own = transform(place, scaled, masses, crossing(NC), "q")
    p_cross, p_own = transform(place, scaled, masses, crossing(NC + BEADS), "p")
    contracted, beside, outgoing = join_contracted(upper, contracted, other)
    ring = []
    for s in range(slabs):
        for g in range(half):
            up, down = (g + 1) % half, (g - 1) % half
            up_slab, down_slab = (s + (g + 1) // half) % slabs, (s + (g - 1) // half) % slabs
            ring.append((g * slabs + s, up * slabs + up_slab))
            ring.append(((half + g) * slabs + s, (half + down) * slabs + down_slab))
    remote = lax.ppermute(outgoing, ("bead", "slab", "grp"), ring)
    q_cross, remote = lax.optimization_barrier((q_cross, remote))
    q_other = swap_with(q_cross, "bead", half)

    forces = neural(upper, contracted, beside, remote, block_lists, weights)
    p_cross, q_other, forces = lax.optimization_barrier((p_cross, q_other, forces))
    p_other = swap_with(p_cross, "bead", half)
    fields = exchange(join(place, q_own, q_other, "q"), "bead")
    moved = exchange(join(place, p_own, p_other, "p"), "bead")

    bits = [1 << i for i in range(groups.bit_length() - 2, -1, -1)]
    have = forces[None]
    got, partners = doubling_step(have, [0], "bead", bits[0])
    new_q, words, fixed, unit, rims = assemble(place, fields)
    slab_ring = [(s, (s + 1) % slabs) for s in range(slabs)]
    slab_back = [(j, i) for i, j in slab_ring]
    q_lower = lax.ppermute(rims[3], ("slab", "grp"), slab_ring)
    q_upper = lax.ppermute(rims[0], ("slab", "grp"), slab_back)

    words, got = lax.optimization_barrier((words, got))
    tiles = atoms // LANES
    cut = 3 * tiles // 8
    for bit in bits[1:2]:
        have = jnp.concatenate([have, got], axis=0)
        got, partners = doubling_step(have, partners, "bead", bit)
    pairs = pair_part(words, fixed, unit, lists, 0, cut)
    words, pairs, got = lax.optimization_barrier((words, pairs, got))
    for bit in bits[2:]:
        have = jnp.concatenate([have, got], axis=0)
        got, partners = doubling_step(have, partners, "bead", bit)
    rest, first = pair_part(
        words, fixed, unit, lists, cut, tiles, (rims, q_lower, q_upper)
    )

    coefs = (kernel * np.float32(BEADS / NC)).reshape(NC, groups, beads, 1)
    coefs = jnp.asarray(np.broadcast_to(coefs, (NC, groups, beads, LANES)))
    new_p, force = finish(
        place, [*pairs, rest], first, moved, (have, got), partners, coefs
    )
    return tuple(swap(out) for out in (new_q, new_p, force))


def solution(mesh):
    field = P("bead", None, ("slab", "grp"))
    placed = (field,) * 4 + (P(("slab", "grp")), P(("slab", "grp"), None)) + (P(),) * 5
    return jax.shard_map(
        body, mesh=mesh, in_specs=placed, out_specs=(field,) * 3, check_vma=False
    )
```

```python
import math

import jax
import jax.numpy as jnp
import numpy as np
from jax import lax
from jax.experimental import pallas as pl
from jax.experimental.pallas import tpu as pltpu
from jax.sharding import PartitionSpec as P

BEADS = 64
NC = 8
EDGE = 128
LANES = 128

TIME_STEP = 0.1
CYCLE_FREQ = 5.0
CENTROID_FRICTION = 1.0
PAIR_STRENGTH = 0.5

BEST = lax.Precision.HIGHEST


def step_tables():
    b = np.arange(BEADS, dtype=np.float64)
    k = np.arange(BEADS)
    angle = 2.0 * np.pi * ((b[:, None] * b[None, :]) % BEADS) / BEADS
    half = BEADS // 2
    basis = np.where(
        k == 0,
        1.0 / math.sqrt(BEADS),
        np.where(
            k < half,
            math.sqrt(2.0 / BEADS) * np.cos(angle),
            np.where(
                k == half, np.cos(angle) / math.sqrt(BEADS), math.sqrt(2.0 / BEADS) * np.sin(angle)
            ),
        ),
    )
    freq = 2.0 * CYCLE_FREQ * np.sin(np.pi * b / BEADS)
    spacing = b[None, :] / BEADS - np.arange(NC, dtype=np.float64)[:, None] / NC
    kernel = np.ones_like(spacing)
    for order in range(1, NC // 2):
        kernel = kernel + 2.0 * np.cos(2.0 * np.pi * order * spacing)
    kernel = kernel + np.cos(np.pi * NC * spacing)
    contract = kernel / BEADS

    h = 0.5 * TIME_STEP
    safe = np.where(freq > 0.0, freq, 1.0)
    qq = np.where(freq > 0.0, np.cos(safe * h), 1.0)
    qp = np.where(freq > 0.0, np.sin(safe * h) / safe, h)
    pq = np.where(freq > 0.0, -safe * np.sin(safe * h), 0.0)
    pp = qq
    keep = np.exp(-np.where(freq > 0.0, 2.0 * freq, CENTROID_FRICTION) * TIME_STEP)
    kick = np.sqrt(1.0 - keep * keep)
    full_qq = qq * qq + qp * keep * pq
    full_qp = qq * qp + qp * keep * pp
    full_qn = qp * kick
    full_pq = pq * qq + pp * keep * pq
    full_pp = pq * qp + pp * keep * pp
    full_pn = pp * kick
    q_rows = np.concatenate(
        [(basis * full_qq) @ basis.T, (basis * full_qp) @ basis.T, basis * full_qn], axis=1
    )
    p_rows = np.concatenate(
        [(basis * full_pq) @ basis.T, (basis * full_pp) @ basis.T, basis * full_pn], axis=1
    )
    c_rows = contract @ q_rows
    step = np.concatenate([c_rows, q_rows, p_rows], axis=0)
    return step.astype(np.float32), contract.astype(np.float32)


def whole_vmem():
    return pl.BlockSpec(memory_space=pltpu.VMEM)


def params(mebibytes=48):
    return pltpu.CompilerParams(vmem_limit_bytes=mebibytes * 1024 * 1024)


def smem():
    return pl.BlockSpec(memory_space=pltpu.SMEM)


def block_of(place_ref, r, rows, count):
    return pl.ds(pl.multiple_of(((place_ref[0] ^ r) % count) * rows, LANES), rows)


def swap_with(block, axis, r):
    return lax.ppermute(block, axis, [(i, i ^ r) for i in range(lax.axis_size(axis))])


def exchange(blocks, axis):
    return [blocks[0]] + [swap_with(blocks[r], axis, r) for r in range(1, len(blocks))]


def pack(place, positions, momenta, force_old, noise, groups):
    _, beads, atoms = positions.shape
    rows = atoms // groups

    def kernel(place_ref, q_ref, p_ref, f_ref, n_ref, *rest):
        outs, (p_buf, f_buf, sems) = rest[:groups], rest[groups:]
        loads = [
            pltpu.make_async_copy(p_ref, p_buf, sems.at[0]),
            pltpu.make_async_copy(f_ref, f_buf, sems.at[1]),
        ]
        for r in range(groups):
            at = block_of(place_ref, r, rows, groups)
            for slot, (ref, first) in enumerate(((q_ref, 0), (n_ref, 6))):
                loads.append(
                    pltpu.make_async_copy(
                        ref.at[:, :, at], outs[r].at[pl.ds(first, 3)], sems.at[2 + 2 * r + slot]
                    )
                )
        for load in loads:
            load.start()
        loads[0].wait()
        loads[1].wait()
        for r in range(groups):
            at = block_of(place_ref, r, rows, groups)
            for x in range(3):
                outs[r][3 + x] = p_buf[x, :, at] + 0.5 * TIME_STEP * f_buf[x, :, at]
        for load in loads[2:]:
            load.wait()

    return pl.pallas_call(
        kernel,
        out_shape=[jax.ShapeDtypeStruct((9, beads, rows), jnp.float32)] * groups,
        in_specs=[smem()] + [pl.BlockSpec(memory_space=pltpu.HBM)] * 4,
        out_specs=[whole_vmem()] * groups,
        scratch_shapes=[
            pltpu.VMEM((3, beads, atoms), jnp.float32),
            pltpu.VMEM((3, beads, atoms), jnp.float32),
            pltpu.SemaphoreType.DMA((2 + 2 * groups,)),
        ],
        compiler_params=params(60),
        name="pack",
    )(place, positions, momenta, force_old, noise)


def prepare(pair_list, mass, desc_w, hidden_one, place, rows, half):
    entries, atoms = pair_list.shape
    desc, env = desc_w.shape
    hid = hidden_one.shape[0]
    order = np.arange(env)
    order = (order % entries) * (env // entries) + order // entries
    permute = jnp.asarray(np.eye(env)[order], jnp.bfloat16)

    def kernel(place_ref, list_ref, mass_ref, w0_ref, w1_ref, order_ref, lists, own, masses, w0, w1):
        for t in range(atoms // LANES):
            at = pl.ds(t * LANES, LANES)
            lists[:, at] = list_ref[:, at] - t * LANES
        inner, upper = place_ref[0] % half, place_ref[0] // half
        block = pl.ds(pl.multiple_of((2 * inner + upper) * rows, LANES), rows)
        own[...] = lists[:, block]
        masses[...] = mass_ref[:, pl.ds(pl.multiple_of(2 * inner * rows, LANES), 2 * rows)]
        w0[...] = lax.dot_general(
            order_ref[...],
            w0_ref[...],
            (((1,), (1,)), ((), ())),
            preferred_element_type=jnp.float32,
        ).astype(w0.dtype)
        w1[...] = w1_ref[...].astype(jnp.float32).T.astype(w1.dtype)

    return pl.pallas_call(
        kernel,
        out_shape=(
            jax.ShapeDtypeStruct((entries, atoms), jnp.int32),
            jax.ShapeDtypeStruct((entries, rows), jnp.int32),
            jax.ShapeDtypeStruct((1, 2 * rows), jnp.float32),
            jax.ShapeDtypeStruct((env, desc), jnp.bfloat16),
            jax.ShapeDtypeStruct((desc, hid), jnp.bfloat16),
        ),
        in_specs=[pl.BlockSpec(memory_space=pltpu.SMEM)] + [whole_vmem()] * 5,
        out_specs=(whole_vmem(),) * 5,
        compiler_params=params(),
        cost_estimate=pl.CostEstimate(
            flops=1_000_000_000, bytes_accessed=4_000_000, transcendentals=0
        ),
        name="prepare",
    )(place, pair_list, mass, desc_w, hidden_one, permute)


def contract(place, received, masses, table):
    groups = len(received)
    _, beads, rows = received[0].shape
    taken = rows // 2 + EDGE

    def kernel(place_ref, mass_ref, table_ref, own_ref, *rest):
        ins, (keep, send, fields, own, total, sem) = rest[: groups - 1], rest[groups - 1 :]
        load = pltpu.make_async_copy(own_ref, own, sem)
        load.start()
        mass = mass_ref[...]
        inverse = 1.0 / mass
        root = lax.rsqrt(mass)

        def scale(g, block):
            for x in range(3):
                fields[x, 0, g] = block[x]
                fields[x, 1, g] = block[3 + x] * inverse
                fields[x, 2, g] = block[6 + x] * root

        inner = place_ref[0] % groups
        for r in range(1, groups):
            scale(inner ^ r, ins[r - 1])
        load.wait()
        scale(inner, own)
        upper = place_ref[0] // groups
        for x in range(3):
            total[x] = jnp.dot(
                table_ref[upper],
                fields[x].reshape(3 * BEADS // 2, rows),
                precision=BEST,
                preferred_element_type=jnp.float32,
            )
        keep[...] = total[:, :, pl.ds(pl.multiple_of(upper * (rows - taken), LANES), taken)]
        send[...] = total[:, :, pl.ds(pl.multiple_of((1 - upper) * (rows - taken), LANES), taken)]

    return pl.pallas_call(
        kernel,
        out_shape=(
            jax.ShapeDtypeStruct((3, NC, taken), jnp.float32),
            jax.ShapeDtypeStruct((3, NC, taken), jnp.float32),
            jax.ShapeDtypeStruct((3, 3, groups, beads, rows), jnp.float32),
        ),
        in_specs=[smem()]
        + [whole_vmem()] * 2
        + [pl.BlockSpec(memory_space=pltpu.HBM)]
        + [whole_vmem()] * (groups - 1),
        out_specs=(whole_vmem(),) * 3,
        scratch_shapes=[
            pltpu.VMEM((9, beads, rows), jnp.float32),
            pltpu.VMEM((3, NC, rows), jnp.float32),
            pltpu.SemaphoreType.DMA,
        ],
        compiler_params=params(),
        name="contract",
    )(place, masses, table, *received)


def join_contracted(upper, own, other):
    _, _, taken = own.shape
    rows = taken - EDGE

    def kernel(upper_ref, own_ref, other_ref, extended, outgoing):
        upper = upper_ref[0]
        at = pl.multiple_of((1 - upper) * EDGE, LANES)
        extended[:, :, pl.ds(pl.multiple_of(upper * (rows + EDGE), LANES), EDGE)] = jnp.zeros(
            (3, NC, EDGE), jnp.float32
        )
        extended[:, :, pl.ds(at, taken)] = own_ref[...] + other_ref[...]
        at = pl.multiple_of(EDGE + upper * (rows - EDGE), LANES)
        outgoing[...] = extended[:, :, pl.ds(at, EDGE)]

    return pl.pallas_call(
        kernel,
        out_shape=(
            jax.ShapeDtypeStruct((3, NC, rows + 2 * EDGE), jnp.float32),
            jax.ShapeDtypeStruct((3, NC, EDGE), jnp.float32),
        ),
        in_specs=[smem()] + [whole_vmem()] * 2,
        out_specs=(whole_vmem(),) * 2,
        compiler_params=params(),
        name="join_contracted",
    )(upper, own, other)


def transform(place, fields, masses, table, name):
    _, _, groups, beads, rows = fields.shape

    def kernel(place_ref, fields_ref, mass_ref, table_ref, cross, own):
        for x in range(3):
            out = jnp.dot(
                table_ref[place_ref[0] // groups],
                fields_ref[x].reshape(3 * BEADS // 2, rows),
                precision=BEST,
                preferred_element_type=jnp.float32,
            )
            if name == "p":
                out = out * mass_ref[...]
            cross[x] = out[: BEADS // 2].reshape(groups, beads, rows)
            own[x] = out[BEADS // 2 :].reshape(groups, beads, rows)

    return pl.pallas_call(
        kernel,
        out_shape=[jax.ShapeDtypeStruct((3, groups, beads, rows), jnp.float32)] * 2,
        in_specs=[smem()] + [whole_vmem()] * 3,
        out_specs=[whole_vmem()] * 2,
        compiler_params=params(),
        cost_estimate=pl.CostEstimate(
            flops=500_000_000, bytes_accessed=1_000_000, transcendentals=0
        ),
        name=f"transform_{name}",
    )(place, fields, masses, table)


def join(place, own, other, name):
    _, groups, beads, rows = own.shape

    def kernel(place_ref, own_ref, other_ref, *outs):
        inner = place_ref[0] % groups
        for r in range(groups):
            for x in range(3):
                outs[r][x] = own_ref[x, inner ^ r] + other_ref[x, inner ^ r]

    return pl.pallas_call(
        kernel,
        out_shape=[jax.ShapeDtypeStruct((3, beads, rows), jnp.float32)] * groups,
        in_specs=[smem()] + [whole_vmem()] * 2,
        out_specs=[whole_vmem()] * groups,
        compiler_params=params(),
        name=f"join_{name}",
    )(place, own, other)


def inverse_of(value):
    estimate = pl.reciprocal(value, approx=True)
    return estimate * (2.0 - value * estimate)


def banded(windows, lane, low, high):
    below, middle, above = [
        jnp.take_along_axis(w, lane, axis=1, mode="promise_in_bounds") for w in windows
    ]
    return jnp.where(low, below, jnp.where(high, above, middle))


def entries_of(list_ref, e, base):
    place = list_ref[pl.ds(e, 8), pl.ds(base, LANES)]
    return place & (LANES - 1), place < LANES, place >= 2 * LANES


def on_sublanes(row):
    return jnp.broadcast_to(row, (8, LANES))


def env_units(windows, list_ref, base, envs, inputs):
    entries = list_ref.shape[0]
    for e in range(0, entries, 8):
        lane, low, high = entries_of(list_ref, e, base)
        for c in range(NC):
            apart = []
            for x in range(3):
                tiles = windows(c, x)
                apart.append(banded(tiles, lane, low, high) - tiles[1])
            square = apart[0] * apart[0] + apart[1] * apart[1] + apart[2] * apart[2]
            close = inverse_of(1.0 + square)
            for x, value in enumerate(apart + [close]):
                envs[pl.ds(x * entries + e, 8), pl.ds(c * LANES, LANES)] = value
            yield
    for c in range(NC):
        at = pl.ds(c * LANES, LANES)
        inputs[at, :] = envs[:, at].T.astype(jnp.bfloat16)
        yield


def network(inputs_ref, weights, out_ref, base, units, chunk=256):
    w0_ref, w1_ref, w2_ref, w3_ref, wo_ref = weights
    desc = w0_ref.shape[1]
    inputs = inputs_ref[...]
    total = None
    for f in range(0, desc, chunk):
        size = min(chunk, desc - f)
        first = jnp.dot(inputs, w0_ref[:, pl.ds(f, size)], preferred_element_type=jnp.float32)
        first = jnp.tanh(first.astype(jnp.bfloat16))
        part = jnp.dot(first, w1_ref[pl.ds(f, size), :], preferred_element_type=jnp.float32)
        total = part if total is None else total + part
        for _ in range(6):
            next(units, None)
    layer = jnp.tanh(total).astype(jnp.bfloat16)
    for ref in (w2_ref, w3_ref):
        layer = jnp.tanh(jnp.dot(layer, ref[...], preferred_element_type=jnp.float32)).astype(
            jnp.bfloat16
        )
    out = lax.dot_general(
        wo_ref[...], layer, (((1,), (1,)), ((), ())), preferred_element_type=jnp.float32
    )
    for c in range(NC):
        for x in range(3):
            out_ref[x, pl.ds(c, 1), pl.ds(base, LANES)] = out[
                x : x + 1, c * LANES : (c + 1) * LANES
            ]


def neural_scratch(env):
    return [
        pltpu.VMEM((2, env, NC * LANES), jnp.float32),
        pltpu.VMEM((2, NC * LANES, env), jnp.bfloat16),
    ]


def neural(upper, extended, lists, weights, remote=None, done=None):
    _, _, wide = extended.shape
    rows = wide - 2 * EDGE
    tiles = rows // LANES
    more = () if remote is None else (remote, done)
    count = 1 if more else tiles - 1

    def kernel(upper_ref, ext_ref, list_ref, w0, w1, w2, w3, wo, *rest):
        out_ref, rim, envs, inputs = rest[len(more) :]
        upper = upper_ref[0]
        if more:
            out_ref[...] = rest[1][...]
            rim[1] = rest[0][...]
            own = upper * (tiles - 1)
            at = pl.multiple_of((own + 1) * LANES, LANES)
            rim[0] = ext_ref[:, :, pl.ds(pl.multiple_of(at + (1 - 2 * upper) * LANES, LANES), LANES)]
            middle = at

        def units_of(k):
            if k >= count:
                return iter(())
            if more:
                def windows(c, x):
                    below = rim[1 - upper, x, pl.ds(c, 1), :]
                    above = rim[upper, x, pl.ds(c, 1), :]
                    own_row = ext_ref[x, pl.ds(c, 1), pl.ds(middle, LANES)]
                    return [on_sublanes(row) for row in (below, own_row, above)]

                base = pl.multiple_of(middle - LANES, LANES)
            else:
                base = pl.multiple_of((1 - upper + k) * LANES, LANES)

                def windows(c, x):
                    return [
                        on_sublanes(ext_ref[x, pl.ds(c, 1), pl.ds(base + v * LANES, LANES)])
                        for v in range(3)
                    ]

            return env_units(windows, list_ref, base, envs.at[k % 2], inputs.at[k % 2])

        for _ in units_of(0):
            pass
        for k in range(count):
            units = units_of(k + 1)
            tile = upper * (tiles - 1) if more else 1 - upper + k
            base = pl.multiple_of(tile * LANES, LANES)
            network(inputs.at[k % 2], (w0, w1, w2, w3, wo), out_ref, base, units)
            for _ in units:
                pass

    return pl.pallas_call(
        kernel,
        out_shape=jax.ShapeDtypeStruct((3, NC, rows), jnp.float32),
        in_specs=[smem()] + [whole_vmem()] * (7 + len(more)),
        out_specs=whole_vmem(),
        scratch_shapes=[pltpu.VMEM((2, 3, NC, EDGE), jnp.float32)]
        + neural_scratch(weights[0].shape[0]),
        compiler_params=params(),
        cost_estimate=pl.CostEstimate(
            flops=3_000_000_000 * count, bytes_accessed=2_000_000, transcendentals=0
        ),
        name=f"neural_{count}",
    )(upper, extended, lists, *weights, *more)


def add_pairs(sums, e, b, apart, close):
    for x in range(3):
        part = apart[x] * close
        sums[x, b] = part if e == 0 else sums[x, b] + part


def total_of(sums, x):
    total = sums[x, :, 0, :]
    for s in range(1, 8):
        total = total + sums[x, :, s, :]
    return total


def assemble(place, fields):
    groups = len(fields)
    _, beads, rows = fields[0].shape
    atoms = groups * rows
    half = beads // 2
    top = float(2**15 - 1)

    def kernel(place_ref, *refs):
        ins, (newq, words, fixed, unit_ref, rims) = refs[:groups], refs[groups:]
        largest = jnp.zeros((beads, rows), jnp.float32)
        for r in range(groups):
            at = block_of(place_ref, r, rows, groups)
            for x in range(3):
                value = ins[r][x]
                newq[x, :, at] = value
                largest = jnp.maximum(largest, jnp.abs(value))
        limit = jnp.maximum(jnp.max(largest, keepdims=True), 1e-30)
        to_fixed = top / limit
        unit_ref[...] = jnp.broadcast_to(limit / (top * 65536.0), (beads, LANES))
        for r in range(groups):
            at = block_of(place_ref, r, rows, groups)
            for x in range(3):
                value = jnp.floor(ins[r][x] * to_fixed + 0.5)
                fixed[x, :, at] = value * 65536.0
                value = value.astype(jnp.int32)
                words[x, :, at] = (value[:half] << 16) | (value[half:] & 65535)
        for rim, t in enumerate((0, LANES, atoms - 2 * LANES, atoms - LANES)):
            rims[rim] = newq[:, :, pl.ds(t, LANES)]

    return pl.pallas_call(
        kernel,
        out_shape=(
            jax.ShapeDtypeStruct((3, beads, atoms), jnp.float32),
            jax.ShapeDtypeStruct((3, half, atoms), jnp.int32),
            jax.ShapeDtypeStruct((3, beads, atoms), jnp.float32),
            jax.ShapeDtypeStruct((beads, LANES), jnp.float32),
            jax.ShapeDtypeStruct((4, 3, beads, LANES), jnp.float32),
        ),
        in_specs=[smem()] + [whole_vmem()] * groups,
        out_specs=(whole_vmem(),) * 5,
        compiler_params=params(),
        name="assemble",
    )(place, *fields)


def pair_part(words, fixed, unit, lists, begin, end, edges=()):
    _, beads, atoms = fixed.shape
    half = beads // 2
    tiles = atoms // LANES
    entries = lists.shape[0]

    def kernel(words_ref, fixed_ref, unit_ref, list_ref, *rest):
        ends = rest[: len(edges)]
        pair, sums = rest[len(edges)], rest[-1]
        unit_row = unit_ref[...]
        unit_square = on_sublanes(unit_ref[pl.ds(0, 1), :])
        unit_square = unit_square * unit_square

        def edge(out, at, base, near_tiles):
            for e in range(0, entries, 8):
                lane, low, high = entries_of(list_ref, e, base)
                for b in range(beads):
                    apart = []
                    for x in range(3):
                        windows = [on_sublanes(tile[x, pl.ds(b, 1), :]) for tile in near_tiles]
                        apart.append(banded(windows, lane, low, high) - windows[1])
                    square = apart[0] * apart[0] + apart[1] * apart[1] + apart[2] * apart[2]
                    add_pairs(sums, e, b, apart, inverse_of(1.0 + square))
            for x in range(3):
                out[x, :, pl.ds(at, LANES)] = PAIR_STRENGTH * total_of(sums, x)

        @pl.loop(max(begin, 1), min(end, tiles - 1))
        def _(t):
            base = pl.multiple_of(t * LANES, LANES)

            def row(ref, x, b, v):
                return on_sublanes(ref[x, pl.ds(b, 1), pl.ds(base + (v - 1) * LANES, LANES)])

            for e in range(0, entries, 8):
                lane, low, high = entries_of(list_ref, e, base)
                for b in range(half):
                    both = [
                        banded([row(words_ref, x, b, v) for v in range(3)], lane, low, high)
                        for x in range(3)
                    ]
                    for bead, near in ((b, [w & -65536 for w in both]),
                                       (b + half, [w << 16 for w in both])):
                        apart = [
                            near[x].astype(jnp.float32) - row(fixed_ref, x, bead, 1)
                            for x in range(3)
                        ]
                        square = apart[0] * apart[0] + apart[1] * apart[1] + apart[2] * apart[2]
                        close = inverse_of(1.0 + square * unit_square)
                        add_pairs(sums, e, bead, apart, close)
            at = pl.ds(pl.multiple_of((t - begin) * LANES, LANES), LANES)
            for x in range(3):
                pair[x, :, at] = (PAIR_STRENGTH * unit_row) * total_of(sums, x)

        if edges:
            rims, lower, upper = ends
            last = (tiles - 1) * LANES
            edge(rest[len(edges) + 1], 0, 0, [lower, rims.at[0], rims.at[1]])
            edge(pair, last - begin * LANES, last, [rims.at[2], rims.at[3], upper])

    out_shape = [jax.ShapeDtypeStruct((3, beads, (end - begin) * LANES), jnp.float32)]
    if edges:
        out_shape.append(jax.ShapeDtypeStruct((3, beads, LANES), jnp.float32))
    return pl.pallas_call(
        kernel,
        out_shape=out_shape,
        in_specs=[whole_vmem()] * (4 + len(edges)),
        out_specs=[whole_vmem()] * len(out_shape),
        scratch_shapes=[pltpu.VMEM((3, beads, 8, LANES), jnp.float32)],
        compiler_params=params(),
        cost_estimate=pl.CostEstimate(
            flops=300_000_000 * (end - begin), bytes_accessed=2_000_000, transcendentals=0
        ),
        name=f"pair_{begin}",
    )(words, fixed, unit, lists, *edges)


def finish(place, pairs, first, moved, neural_parts, partners, coefs):
    half = len(moved)
    _, beads, wide = moved[0].shape
    rows = wide // 2
    atoms = half * wide
    counts = [part.shape[0] for part in neural_parts]

    def kernel(place_ref, first_ref, coef_ref, *rest):
        halves, rest = rest[: len(pairs)], rest[len(pairs) :]
        ins, rest = rest[:half], rest[half:]
        blocks, (newp, newf) = rest[: len(counts)], rest[len(counts) :]
        own = place_ref[0]
        at = 0
        for piece in halves:
            newf[:, :, pl.ds(at, piece.shape[2])] = piece[...]
            at += piece.shape[2]
        newf[:, :, pl.ds(0, LANES)] = first_ref[...]
        coef = [coef_ref[c, own] for c in range(NC)]
        blocks = [block.at[i] for block, count in zip(blocks, counts) for i in range(count)]
        for r, block in zip(partners, blocks):
            source = own ^ r
            base = (source % half) * wide + (source // half) * rows
            for t in range(0, rows, LANES):
                at = pl.ds(pl.multiple_of(base + t, LANES), LANES)
                for x in range(3):
                    force = newf[x, :, at]
                    for c in range(NC):
                        force = force + coef[c] * block[x, pl.ds(c, 1), pl.ds(t, LANES)]
                    newf[x, :, at] = force
        for r in range(half):
            at = block_of(place_ref, r, wide, half)
            for x in range(3):
                newp[x, :, at] = ins[r][x] + 0.5 * TIME_STEP * newf[x, :, at]

    out = jax.ShapeDtypeStruct((3, beads, atoms), jnp.float32)
    return pl.pallas_call(
        kernel,
        out_shape=(out,) * 2,
        in_specs=[smem()] + [whole_vmem()] * (2 + len(pairs) + half + len(neural_parts)),
        out_specs=(whole_vmem(),) * 2,
        compiler_params=params(),
        name="finish",
    )(place, first, coefs, *pairs, *moved, *neural_parts)


def doubling_step(have, partners, axis, bit):
    count = lax.axis_size(axis)
    got = lax.ppermute(have, axis, [(i, i ^ bit) for i in range(count)])
    return got, partners + [r ^ bit for r in partners]


def body(
    positions,
    momenta,
    force_old,
    noise,
    mass,
    pair_list,
    desc_w,
    hidden_one,
    hidden_two,
    hidden_three,
    out_w,
):
    beads, _, atoms = positions.shape
    groups = lax.axis_size("bead")
    slabs = lax.axis_size(("slab", "grp"))
    rows = atoms // groups
    half = groups // 2
    index = lax.axis_index("bead").astype(jnp.int32)
    place, upper = index[None], (index // half)[None]
    step, kernel = step_tables()
    sides = step.reshape(-1, 3, 2, BEADS // 2).transpose(2, 0, 1, 3).reshape(2, -1, 3 * BEADS // 2)

    def crossing(first_row):
        rows_of = [sides[:, first_row + s * BEADS // 2 :][:, : BEADS // 2] for s in range(2)]
        return jnp.asarray(
            np.stack(
                [np.concatenate([rows_of[1 - s][s], rows_of[s][s]], axis=0) for s in range(2)]
            )
        )

    swap = lambda field: jnp.transpose(field, (1, 0, 2))
    sends = pack(place, swap(positions), swap(momenta), swap(force_old), swap(noise), half)
    received = exchange(sends, "bead")

    lists, block_lists, masses, env_w, w1 = prepare(
        pair_list.T, mass[None, :], desc_w.T, hidden_one.T, place, rows, half
    )
    received, lists, block_lists, masses, env_w, w1 = lax.optimization_barrier(
        (received, lists, block_lists, masses, env_w, w1)
    )
    weights = (env_w, w1, hidden_two, hidden_three, out_w.T)

    keep, send, scaled = contract(place, received, masses, jnp.asarray(sides[:, :NC]))
    other = swap_with(send, "bead", half)
    q_cross, q_own = transform(place, scaled, masses, crossing(NC), "q")
    p_cross, p_own = transform(place, scaled, masses, crossing(NC + BEADS), "p")
    extended, outgoing = join_contracted(upper, keep, other)
    ring = []
    for s in range(slabs):
        for g in range(half):
            up, down = (g + 1) % half, (g - 1) % half
            up_slab, down_slab = (s + (g + 1) // half) % slabs, (s + (g - 1) // half) % slabs
            ring.append((g * slabs + s, (half + down) * slabs + down_slab))
            ring.append(((half + g) * slabs + s, up * slabs + up_slab))
    remote = lax.ppermute(outgoing, ("bead", "slab", "grp"), ring)
    q_cross, extended = lax.optimization_barrier((q_cross, extended))
    q_other = swap_with(q_cross, "bead", half)

    forces = neural(upper, extended, block_lists, weights)
    forces, remote = lax.optimization_barrier((forces, remote))
    forces = neural(upper, extended, block_lists, weights, remote, forces)

    bits = [1 << i for i in range(groups.bit_length() - 2, -1, -1)]
    have = forces[None]
    got, partners = doubling_step(have, [0], "bead", bits[0])
    q_other, forces = lax.optimization_barrier((q_other, forces))
    p_cross, got = lax.optimization_barrier((p_cross, got))
    p_other = swap_with(p_cross, "bead", half)
    fields = exchange(join(place, q_own, q_other, "q"), "bead")
    moved = exchange(join(place, p_own, p_other, "p"), "bead")
    new_q, words, fixed, unit, rims = assemble(place, fields)
    slab_ring = [(s, (s + 1) % slabs) for s in range(slabs)]
    slab_back = [(j, i) for i, j in slab_ring]
    q_lower = lax.ppermute(rims[3], ("slab", "grp"), slab_ring)
    q_upper = lax.ppermute(rims[0], ("slab", "grp"), slab_back)

    words, got = lax.optimization_barrier((words, got))
    tiles = atoms // LANES
    cut = 3 * tiles // 8
    for bit in bits[1:2]:
        have = jnp.concatenate([have, got], axis=0)
        got, partners = doubling_step(have, partners, "bead", bit)
    pairs = pair_part(words, fixed, unit, lists, 0, cut)
    words, pairs, got = lax.optimization_barrier((words, pairs, got))
    for bit in bits[2:]:
        have = jnp.concatenate([have, got], axis=0)
        got, partners = doubling_step(have, partners, "bead", bit)
    rest, first = pair_part(
        words, fixed, unit, lists, cut, tiles, (rims, q_lower, q_upper)
    )

    coefs = (kernel * np.float32(BEADS / NC)).reshape(NC, groups, beads, 1)
    coefs = jnp.asarray(np.broadcast_to(coefs, (NC, groups, beads, LANES)))
    new_p, force = finish(
        place, [*pairs, rest], first, moved, (have, got), partners, coefs
    )
    return tuple(swap(out) for out in (new_q, new_p, force))


def solution(mesh):
    field = P("bead", None, ("slab", "grp"))
    placed = (field,) * 4 + (P(("slab", "grp")), P(("slab", "grp"), None)) + (P(),) * 5
    return jax.shard_map(
        body, mesh=mesh, in_specs=placed, out_specs=(field,) * 3, check_vma=False
    )
```

```python
import math

import jax
import jax.numpy as jnp
import numpy as np
from jax import lax
from jax.experimental import pallas as pl
from jax.experimental.pallas import tpu as pltpu
from jax.sharding import PartitionSpec as P

BEADS = 64
NC = 8
EDGE = 128
LANES = 128

TIME_STEP = 0.1
CYCLE_FREQ = 5.0
CENTROID_FRICTION = 1.0
PAIR_STRENGTH = 0.5

BEST = lax.Precision.HIGHEST


def step_tables():
    b = np.arange(BEADS, dtype=np.float64)
    k = np.arange(BEADS)
    angle = 2.0 * np.pi * ((b[:, None] * b[None, :]) % BEADS) / BEADS
    half = BEADS // 2
    basis = np.where(
        k == 0,
        1.0 / math.sqrt(BEADS),
        np.where(
            k < half,
            math.sqrt(2.0 / BEADS) * np.cos(angle),
            np.where(
                k == half, np.cos(angle) / math.sqrt(BEADS), math.sqrt(2.0 / BEADS) * np.sin(angle)
            ),
        ),
    )
    freq = 2.0 * CYCLE_FREQ * np.sin(np.pi * b / BEADS)
    spacing = b[None, :] / BEADS - np.arange(NC, dtype=np.float64)[:, None] / NC
    kernel = np.ones_like(spacing)
    for order in range(1, NC // 2):
        kernel = kernel + 2.0 * np.cos(2.0 * np.pi * order * spacing)
    kernel = kernel + np.cos(np.pi * NC * spacing)
    contract = kernel / BEADS

    h = 0.5 * TIME_STEP
    safe = np.where(freq > 0.0, freq, 1.0)
    qq = np.where(freq > 0.0, np.cos(safe * h), 1.0)
    qp = np.where(freq > 0.0, np.sin(safe * h) / safe, h)
    pq = np.where(freq > 0.0, -safe * np.sin(safe * h), 0.0)
    pp = qq
    keep = np.exp(-np.where(freq > 0.0, 2.0 * freq, CENTROID_FRICTION) * TIME_STEP)
    kick = np.sqrt(1.0 - keep * keep)
    full_qq = qq * qq + qp * keep * pq
    full_qp = qq * qp + qp * keep * pp
    full_qn = qp * kick
    full_pq = pq * qq + pp * keep * pq
    full_pp = pq * qp + pp * keep * pp
    full_pn = pp * kick
    q_rows = np.concatenate(
        [(basis * full_qq) @ basis.T, (basis * full_qp) @ basis.T, basis * full_qn], axis=1
    )
    p_rows = np.concatenate(
        [(basis * full_pq) @ basis.T, (basis * full_pp) @ basis.T, basis * full_pn], axis=1
    )
    c_rows = contract @ q_rows
    step = np.concatenate([c_rows, q_rows, p_rows], axis=0)
    return step.astype(np.float32), contract.astype(np.float32)


def whole_vmem():
    return pl.BlockSpec(memory_space=pltpu.VMEM)


def params(mebibytes=48):
    return pltpu.CompilerParams(vmem_limit_bytes=mebibytes * 1024 * 1024)


def smem():
    return pl.BlockSpec(memory_space=pltpu.SMEM)


def block_of(place_ref, r, rows, count):
    return pl.ds(pl.multiple_of(((place_ref[0] ^ r) % count) * rows, LANES), rows)


def swap_with(block, axis, r):
    return lax.ppermute(block, axis, [(i, i ^ r) for i in range(lax.axis_size(axis))])


def exchange(blocks, axis):
    return [blocks[0]] + [swap_with(blocks[r], axis, r) for r in range(1, len(blocks))]


def pack(place, positions, momenta, force_old, noise, groups):
    _, beads, atoms = positions.shape
    rows = atoms // groups

    def kernel(place_ref, q_ref, p_ref, f_ref, n_ref, *rest):
        outs, (p_buf, f_buf, sems) = rest[:groups], rest[groups:]
        loads = [
            pltpu.make_async_copy(p_ref, p_buf, sems.at[0]),
            pltpu.make_async_copy(f_ref, f_buf, sems.at[1]),
        ]
        for r in range(groups):
            at = block_of(place_ref, r, rows, groups)
            for slot, (ref, first) in enumerate(((q_ref, 0), (n_ref, 6))):
                loads.append(
                    pltpu.make_async_copy(
                        ref.at[:, :, at], outs[r].at[pl.ds(first, 3)], sems.at[2 + 2 * r + slot]
                    )
                )
        for load in loads:
            load.start()
        loads[0].wait()
        loads[1].wait()
        for r in range(groups):
            at = block_of(place_ref, r, rows, groups)
            for x in range(3):
                outs[r][3 + x] = p_buf[x, :, at] + 0.5 * TIME_STEP * f_buf[x, :, at]
        for load in loads[2:]:
            load.wait()

    return pl.pallas_call(
        kernel,
        out_shape=[jax.ShapeDtypeStruct((9, beads, rows), jnp.float32)] * groups,
        in_specs=[smem()] + [pl.BlockSpec(memory_space=pltpu.HBM)] * 4,
        out_specs=[whole_vmem()] * groups,
        scratch_shapes=[
            pltpu.VMEM((3, beads, atoms), jnp.float32),
            pltpu.VMEM((3, beads, atoms), jnp.float32),
            pltpu.SemaphoreType.DMA((2 + 2 * groups,)),
        ],
        compiler_params=params(60),
        name="pack",
    )(place, positions, momenta, force_old, noise)


def prepare(pair_list, mass, desc_w, hidden_one, place, rows, half):
    entries, atoms = pair_list.shape
    desc, env = desc_w.shape
    hid = hidden_one.shape[0]
    order = np.arange(env)
    order = (order % entries) * (env // entries) + order // entries
    permute = jnp.asarray(np.eye(env)[order], jnp.bfloat16)

    def kernel(place_ref, list_ref, mass_ref, w0_ref, w1_ref, order_ref, lists, own, masses, w0, w1):
        for t in range(atoms // LANES):
            at = pl.ds(t * LANES, LANES)
            lists[:, at] = list_ref[:, at] - t * LANES
        inner, upper = place_ref[0] % half, place_ref[0] // half
        block = pl.ds(pl.multiple_of((2 * inner + upper) * rows, LANES), rows)
        own[...] = lists[:, block]
        masses[...] = mass_ref[:, pl.ds(pl.multiple_of(2 * inner * rows, LANES), 2 * rows)]
        w0[...] = lax.dot_general(
            order_ref[...],
            w0_ref[...],
            (((1,), (1,)), ((), ())),
            preferred_element_type=jnp.float32,
        ).astype(w0.dtype)
        w1[...] = w1_ref[...].astype(jnp.float32).T.astype(w1.dtype)

    return pl.pallas_call(
        kernel,
        out_shape=(
            jax.ShapeDtypeStruct((entries, atoms), jnp.int32),
            jax.ShapeDtypeStruct((entries, rows), jnp.int32),
            jax.ShapeDtypeStruct((1, 2 * rows), jnp.float32),
            jax.ShapeDtypeStruct((env, desc), jnp.bfloat16),
            jax.ShapeDtypeStruct((desc, hid), jnp.bfloat16),
        ),
        in_specs=[pl.BlockSpec(memory_space=pltpu.SMEM)] + [whole_vmem()] * 5,
        out_specs=(whole_vmem(),) * 5,
        compiler_params=params(),
        cost_estimate=pl.CostEstimate(
            flops=1_000_000_000, bytes_accessed=4_000_000, transcendentals=0
        ),
        name="prepare",
    )(place, pair_list, mass, desc_w, hidden_one, permute)


def contract(place, received, masses, table):
    groups = len(received)
    _, beads, rows = received[0].shape
    taken = rows // 2 + EDGE

    def kernel(place_ref, mass_ref, table_ref, own_ref, *rest):
        ins, (keep, send, fields, own, total, sem) = rest[: groups - 1], rest[groups - 1 :]
        load = pltpu.make_async_copy(own_ref, own, sem)
        load.start()
        mass = mass_ref[...]
        inverse = 1.0 / mass
        root = lax.rsqrt(mass)

        def scale(g, block):
            for x in range(3):
                fields[x, 0, g] = block[x]
                fields[x, 1, g] = block[3 + x] * inverse
                fields[x, 2, g] = block[6 + x] * root

        inner = place_ref[0] % groups
        for r in range(1, groups):
            scale(inner ^ r, ins[r - 1])
        load.wait()
        scale(inner, own)
        upper = place_ref[0] // groups
        for x in range(3):
            total[x] = jnp.dot(
                table_ref[upper],
                fields[x].reshape(3 * BEADS // 2, rows),
                precision=BEST,
                preferred_element_type=jnp.float32,
            )
        keep[...] = total[:, :, pl.ds(pl.multiple_of(upper * (rows - taken), LANES), taken)]
        send[...] = total[:, :, pl.ds(pl.multiple_of((1 - upper) * (rows - taken), LANES), taken)]

    return pl.pallas_call(
        kernel,
        out_shape=(
            jax.ShapeDtypeStruct((3, NC, taken), jnp.float32),
            jax.ShapeDtypeStruct((3, NC, taken), jnp.float32),
            jax.ShapeDtypeStruct((3, 3, groups, beads, rows), jnp.float32),
        ),
        in_specs=[smem()]
        + [whole_vmem()] * 2
        + [pl.BlockSpec(memory_space=pltpu.HBM)]
        + [whole_vmem()] * (groups - 1),
        out_specs=(whole_vmem(),) * 3,
        scratch_shapes=[
            pltpu.VMEM((9, beads, rows), jnp.float32),
            pltpu.VMEM((3, NC, rows), jnp.float32),
            pltpu.SemaphoreType.DMA,
        ],
        compiler_params=params(),
        name="contract",
    )(place, masses, table, *received)


def join_contracted(upper, own, other):
    _, _, taken = own.shape
    rows = taken - EDGE

    def kernel(upper_ref, own_ref, other_ref, extended, outgoing):
        upper = upper_ref[0]
        at = pl.multiple_of((1 - upper) * EDGE, LANES)
        extended[:, :, pl.ds(pl.multiple_of(upper * (rows + EDGE), LANES), EDGE)] = jnp.zeros(
            (3, NC, EDGE), jnp.float32
        )
        extended[:, :, pl.ds(at, taken)] = own_ref[...] + other_ref[...]
        at = pl.multiple_of(EDGE + upper * (rows - EDGE), LANES)
        outgoing[...] = extended[:, :, pl.ds(at, EDGE)]

    return pl.pallas_call(
        kernel,
        out_shape=(
            jax.ShapeDtypeStruct((3, NC, rows + 2 * EDGE), jnp.float32),
            jax.ShapeDtypeStruct((3, NC, EDGE), jnp.float32),
        ),
        in_specs=[smem()] + [whole_vmem()] * 2,
        out_specs=(whole_vmem(),) * 2,
        compiler_params=params(),
        name="join_contracted",
    )(upper, own, other)


def transform(place, fields, masses, table, name):
    _, _, groups, beads, rows = fields.shape

    def kernel(place_ref, fields_ref, mass_ref, table_ref, cross, own):
        for x in range(3):
            out = jnp.dot(
                table_ref[place_ref[0] // groups],
                fields_ref[x].reshape(3 * BEADS // 2, rows),
                precision=BEST,
                preferred_element_type=jnp.float32,
            )
            if name == "p":
                out = out * mass_ref[...]
            cross[x] = out[: BEADS // 2].reshape(groups, beads, rows)
            own[x] = out[BEADS // 2 :].reshape(groups, beads, rows)

    return pl.pallas_call(
        kernel,
        out_shape=[jax.ShapeDtypeStruct((3, groups, beads, rows), jnp.float32)] * 2,
        in_specs=[smem()] + [whole_vmem()] * 3,
        out_specs=[whole_vmem()] * 2,
        compiler_params=params(),
        cost_estimate=pl.CostEstimate(
            flops=500_000_000, bytes_accessed=1_000_000, transcendentals=0
        ),
        name=f"transform_{name}",
    )(place, fields, masses, table)


def join(place, own, other, name):
    _, groups, beads, rows = own.shape

    def kernel(place_ref, own_ref, other_ref, *outs):
        inner = place_ref[0] % groups
        for r in range(groups):
            for x in range(3):
                outs[r][x] = own_ref[x, inner ^ r] + other_ref[x, inner ^ r]

    return pl.pallas_call(
        kernel,
        out_shape=[jax.ShapeDtypeStruct((3, beads, rows), jnp.float32)] * groups,
        in_specs=[smem()] + [whole_vmem()] * 2,
        out_specs=[whole_vmem()] * groups,
        compiler_params=params(),
        name=f"join_{name}",
    )(place, own, other)


def inverse_of(value):
    estimate = pl.reciprocal(value, approx=True)
    return estimate * (2.0 - value * estimate)


def banded(windows, lane, low, high):
    below, middle, above = [
        jnp.take_along_axis(w, lane, axis=1, mode="promise_in_bounds") for w in windows
    ]
    return jnp.where(low, below, jnp.where(high, above, middle))


def entries_of(list_ref, e, base):
    place = list_ref[pl.ds(e, 8), pl.ds(base, LANES)]
    return place & (LANES - 1), place < LANES, place >= 2 * LANES


def on_sublanes(row):
    return jnp.broadcast_to(row, (8, LANES))


def env_units(windows, list_ref, base, envs, inputs):
    entries = list_ref.shape[0]
    for e in range(0, entries, 8):
        lane, low, high = entries_of(list_ref, e, base)
        for c in range(NC):
            apart = []
            for x in range(3):
                tiles = windows(c, x)
                apart.append(banded(tiles, lane, low, high) - tiles[1])
            square = apart[0] * apart[0] + apart[1] * apart[1] + apart[2] * apart[2]
            close = inverse_of(1.0 + square)
            for x, value in enumerate(apart + [close]):
                envs[pl.ds(x * entries + e, 8), pl.ds(c * LANES, LANES)] = value
            yield
    for c in range(NC):
        at = pl.ds(c * LANES, LANES)
        inputs[at, :] = envs[:, at].T.astype(jnp.bfloat16)
        yield


def network(inputs_ref, weights, out_ref, base, units, chunk=256):
    w0_ref, w1_ref, w2_ref, w3_ref, wo_ref = weights
    desc = w0_ref.shape[1]
    inputs = inputs_ref[...]
    total = None
    for f in range(0, desc, chunk):
        size = min(chunk, desc - f)
        first = jnp.dot(inputs, w0_ref[:, pl.ds(f, size)], preferred_element_type=jnp.float32)
        first = jnp.tanh(first.astype(jnp.bfloat16))
        part = jnp.dot(first, w1_ref[pl.ds(f, size), :], preferred_element_type=jnp.float32)
        total = part if total is None else total + part
        for _ in range(6):
            next(units, None)
    layer = jnp.tanh(total).astype(jnp.bfloat16)
    for ref in (w2_ref, w3_ref):
        layer = jnp.tanh(jnp.dot(layer, ref[...], preferred_element_type=jnp.float32)).astype(
            jnp.bfloat16
        )
    out = lax.dot_general(
        wo_ref[...], layer, (((1,), (1,)), ((), ())), preferred_element_type=jnp.float32
    )
    for c in range(NC):
        for x in range(3):
            out_ref[x, pl.ds(c, 1), pl.ds(base, LANES)] = out[
                x : x + 1, c * LANES : (c + 1) * LANES
            ]


def neural_scratch(env):
    return [
        pltpu.VMEM((2, env, NC * LANES), jnp.float32),
        pltpu.VMEM((2, NC * LANES, env), jnp.bfloat16),
    ]


def neural(upper, extended, remote, lists, weights):
    _, _, wide = extended.shape
    rows = wide - 2 * EDGE
    tiles = rows // LANES

    def kernel(
        upper_ref, ext_ref, remote_ref, list_ref, w0, w1, w2, w3, wo, out_ref, ext, envs, inputs
    ):
        ext[...] = ext_ref[...]
        at = pl.multiple_of(upper_ref[0] * (rows + EDGE), LANES)
        ext[:, :, pl.ds(at, EDGE)] = remote_ref[...]

        def units_of(t):
            if t >= tiles:
                return iter(())

            def windows(c, x):
                return [
                    on_sublanes(ext[x, pl.ds(c, 1), pl.ds((t + v) * LANES, LANES)])
                    for v in range(3)
                ]

            slot = t % 2
            return env_units(windows, list_ref, t * LANES, envs.at[slot], inputs.at[slot])

        for _ in units_of(0):
            pass
        for t in range(tiles):
            units = units_of(t + 1)
            network(inputs.at[t % 2], (w0, w1, w2, w3, wo), out_ref, t * LANES, units)
            for _ in units:
                pass

    return pl.pallas_call(
        kernel,
        out_shape=jax.ShapeDtypeStruct((3, NC, rows), jnp.float32),
        in_specs=[smem()] + [whole_vmem()] * 8,
        out_specs=whole_vmem(),
        scratch_shapes=[pltpu.VMEM((3, NC, wide), jnp.float32)]
        + neural_scratch(weights[0].shape[0]),
        compiler_params=params(),
        cost_estimate=pl.CostEstimate(
            flops=12_000_000_000, bytes_accessed=4_000_000, transcendentals=0
        ),
        name="neural",
    )(upper, extended, remote, lists, *weights)


def add_pairs(sums, e, b, apart, close):
    for x in range(3):
        part = apart[x] * close
        sums[x, b] = part if e == 0 else sums[x, b] + part


def total_of(sums, x):
    total = sums[x, :, 0, :]
    for s in range(1, 8):
        total = total + sums[x, :, s, :]
    return total


def assemble(place, fields):
    groups = len(fields)
    _, beads, rows = fields[0].shape
    atoms = groups * rows
    half = beads // 2
    top = float(2**15 - 1)

    def kernel(place_ref, *refs):
        ins, (newq, words, fixed, unit_ref, rims) = refs[:groups], refs[groups:]
        largest = jnp.zeros((beads, rows), jnp.float32)
        for r in range(groups):
            at = block_of(place_ref, r, rows, groups)
            for x in range(3):
                value = ins[r][x]
                newq[x, :, at] = value
                largest = jnp.maximum(largest, jnp.abs(value))
        limit = jnp.maximum(jnp.max(largest, keepdims=True), 1e-30)
        to_fixed = top / limit
        unit_ref[...] = jnp.broadcast_to(limit / (top * 65536.0), (beads, LANES))
        for r in range(groups):
            at = block_of(place_ref, r, rows, groups)
            for x in range(3):
                value = jnp.floor(ins[r][x] * to_fixed + 0.5)
                fixed[x, :, at] = value * 65536.0
                value = value.astype(jnp.int32)
                words[x, :, at] = (value[:half] << 16) | (value[half:] & 65535)
        for rim, t in enumerate((0, LANES, atoms - 2 * LANES, atoms - LANES)):
            rims[rim] = newq[:, :, pl.ds(t, LANES)]

    return pl.pallas_call(
        kernel,
        out_shape=(
            jax.ShapeDtypeStruct((3, beads, atoms), jnp.float32),
            jax.ShapeDtypeStruct((3, half, atoms), jnp.int32),
            jax.ShapeDtypeStruct((3, beads, atoms), jnp.float32),
            jax.ShapeDtypeStruct((beads, LANES), jnp.float32),
            jax.ShapeDtypeStruct((4, 3, beads, LANES), jnp.float32),
        ),
        in_specs=[smem()] + [whole_vmem()] * groups,
        out_specs=(whole_vmem(),) * 5,
        compiler_params=params(),
        name="assemble",
    )(place, *fields)


def pair_part(words, fixed, unit, lists, begin, end, edges=()):
    _, beads, atoms = fixed.shape
    half = beads // 2
    tiles = atoms // LANES
    entries = lists.shape[0]

    def kernel(words_ref, fixed_ref, unit_ref, list_ref, *rest):
        ends = rest[: len(edges)]
        pair, sums = rest[len(edges)], rest[-1]
        unit_row = unit_ref[...]
        unit_square = on_sublanes(unit_ref[pl.ds(0, 1), :])
        unit_square = unit_square * unit_square

        def edge(out, at, base, near_tiles):
            for e in range(0, entries, 8):
                lane, low, high = entries_of(list_ref, e, base)
                for b in range(beads):
                    apart = []
                    for x in range(3):
                        windows = [on_sublanes(tile[x, pl.ds(b, 1), :]) for tile in near_tiles]
                        apart.append(banded(windows, lane, low, high) - windows[1])
                    square = apart[0] * apart[0] + apart[1] * apart[1] + apart[2] * apart[2]
                    add_pairs(sums, e, b, apart, inverse_of(1.0 + square))
            for x in range(3):
                out[x, :, pl.ds(at, LANES)] = PAIR_STRENGTH * total_of(sums, x)

        @pl.loop(max(begin, 1), min(end, tiles - 1))
        def _(t):
            base = pl.multiple_of(t * LANES, LANES)

            def row(ref, x, b, v):
                return on_sublanes(ref[x, pl.ds(b, 1), pl.ds(base + (v - 1) * LANES, LANES)])

            for e in range(0, entries, 8):
                lane, low, high = entries_of(list_ref, e, base)
                for b in range(half):
                    both = [
                        banded([row(words_ref, x, b, v) for v in range(3)], lane, low, high)
                        for x in range(3)
                    ]
                    for bead, near in ((b, [w & -65536 for w in both]),
                                       (b + half, [w << 16 for w in both])):
                        apart = [
                            near[x].astype(jnp.float32) - row(fixed_ref, x, bead, 1)
                            for x in range(3)
                        ]
                        square = apart[0] * apart[0] + apart[1] * apart[1] + apart[2] * apart[2]
                        close = inverse_of(1.0 + square * unit_square)
                        add_pairs(sums, e, bead, apart, close)
            at = pl.ds(pl.multiple_of((t - begin) * LANES, LANES), LANES)
            for x in range(3):
                pair[x, :, at] = (PAIR_STRENGTH * unit_row) * total_of(sums, x)

        if edges:
            rims, lower, upper = ends
            last = (tiles - 1) * LANES
            edge(rest[len(edges) + 1], 0, 0, [lower, rims.at[0], rims.at[1]])
            edge(pair, last - begin * LANES, last, [rims.at[2], rims.at[3], upper])

    out_shape = [jax.ShapeDtypeStruct((3, beads, (end - begin) * LANES), jnp.float32)]
    if edges:
        out_shape.append(jax.ShapeDtypeStruct((3, beads, LANES), jnp.float32))
    return pl.pallas_call(
        kernel,
        out_shape=out_shape,
        in_specs=[whole_vmem()] * (4 + len(edges)),
        out_specs=[whole_vmem()] * len(out_shape),
        scratch_shapes=[pltpu.VMEM((3, beads, 8, LANES), jnp.float32)],
        compiler_params=params(),
        cost_estimate=pl.CostEstimate(
            flops=300_000_000 * (end - begin), bytes_accessed=2_000_000, transcendentals=0
        ),
        name=f"pair_{begin}",
    )(words, fixed, unit, lists, *edges)


def finish(place, pairs, first, moved, neural_parts, partners, coefs):
    half = len(moved)
    _, beads, wide = moved[0].shape
    rows = wide // 2
    atoms = half * wide
    counts = [part.shape[0] for part in neural_parts]

    def kernel(place_ref, first_ref, coef_ref, *rest):
        halves, rest = rest[: len(pairs)], rest[len(pairs) :]
        ins, rest = rest[:half], rest[half:]
        blocks, (newp, newf) = rest[: len(counts)], rest[len(counts) :]
        own = place_ref[0]
        at = 0
        for piece in halves:
            newf[:, :, pl.ds(at, piece.shape[2])] = piece[...]
            at += piece.shape[2]
        newf[:, :, pl.ds(0, LANES)] = first_ref[...]
        coef = [coef_ref[c, own] for c in range(NC)]
        blocks = [block.at[i] for block, count in zip(blocks, counts) for i in range(count)]
        for r, block in zip(partners, blocks):
            source = own ^ r
            base = (source % half) * wide + (source // half) * rows
            for t in range(0, rows, LANES):
                at = pl.ds(pl.multiple_of(base + t, LANES), LANES)
                for x in range(3):
                    force = newf[x, :, at]
                    for c in range(NC):
                        force = force + coef[c] * block[x, pl.ds(c, 1), pl.ds(t, LANES)]
                    newf[x, :, at] = force
        for r in range(half):
            at = block_of(place_ref, r, wide, half)
            for x in range(3):
                newp[x, :, at] = ins[r][x] + 0.5 * TIME_STEP * newf[x, :, at]

    out = jax.ShapeDtypeStruct((3, beads, atoms), jnp.float32)
    return pl.pallas_call(
        kernel,
        out_shape=(out,) * 2,
        in_specs=[smem()] + [whole_vmem()] * (2 + len(pairs) + half + len(neural_parts)),
        out_specs=(whole_vmem(),) * 2,
        compiler_params=params(),
        name="finish",
    )(place, first, coefs, *pairs, *moved, *neural_parts)


def doubling_step(have, partners, axis, bit):
    count = lax.axis_size(axis)
    got = lax.ppermute(have, axis, [(i, i ^ bit) for i in range(count)])
    return got, partners + [r ^ bit for r in partners]


def body(
    positions,
    momenta,
    force_old,
    noise,
    mass,
    pair_list,
    desc_w,
    hidden_one,
    hidden_two,
    hidden_three,
    out_w,
):
    beads, _, atoms = positions.shape
    groups = lax.axis_size("bead")
    slabs = lax.axis_size(("slab", "grp"))
    rows = atoms // groups
    half = groups // 2
    index = lax.axis_index("bead").astype(jnp.int32)
    place, upper = index[None], (index // half)[None]
    step, kernel = step_tables()
    sides = step.reshape(-1, 3, 2, BEADS // 2).transpose(2, 0, 1, 3).reshape(2, -1, 3 * BEADS // 2)

    def crossing(first_row):
        rows_of = [sides[:, first_row + s * BEADS // 2 :][:, : BEADS // 2] for s in range(2)]
        return jnp.asarray(
            np.stack(
                [np.concatenate([rows_of[1 - s][s], rows_of[s][s]], axis=0) for s in range(2)]
            )
        )

    swap = lambda field: jnp.transpose(field, (1, 0, 2))
    sends = pack(place, swap(positions), swap(momenta), swap(force_old), swap(noise), half)
    received = exchange(sends, "bead")

    lists, block_lists, masses, env_w, w1 = prepare(
        pair_list.T, mass[None, :], desc_w.T, hidden_one.T, place, rows, half
    )
    received, lists, block_lists, masses, env_w, w1 = lax.optimization_barrier(
        (received, lists, block_lists, masses, env_w, w1)
    )
    weights = (env_w, w1, hidden_two, hidden_three, out_w.T)

    keep, send, scaled = contract(place, received, masses, jnp.asarray(sides[:, :NC]))
    other = swap_with(send, "bead", half)
    q_cross, q_own = transform(place, scaled, masses, crossing(NC), "q")
    p_cross, p_own = transform(place, scaled, masses, crossing(NC + BEADS), "p")
    extended, outgoing = join_contracted(upper, keep, other)
    ring = []
    for s in range(slabs):
        for g in range(half):
            up, down = (g + 1) % half, (g - 1) % half
            up_slab, down_slab = (s + (g + 1) // half) % slabs, (s + (g - 1) // half) % slabs
            ring.append((g * slabs + s, (half + down) * slabs + down_slab))
            ring.append(((half + g) * slabs + s, up * slabs + up_slab))
    remote = lax.ppermute(outgoing, ("bead", "slab", "grp"), ring)
    q_cross, remote = lax.optimization_barrier((q_cross, remote))
    q_other = swap_with(q_cross, "bead", half)

    forces = neural(upper, extended, remote, block_lists, weights)
    p_cross, forces = lax.optimization_barrier((p_cross, forces))
    p_other = swap_with(p_cross, "bead", half)

    bits = [1 << i for i in range(groups.bit_length() - 2, -1, -1)]
    have = forces[None]
    got, partners = doubling_step(have, [0], "bead", bits[0])
    q_other, forces = lax.optimization_barrier((q_other, forces))
    fields = exchange(join(place, q_own, q_other, "q"), "bead")

    new_q, words, fixed, unit, rims = assemble(place, fields)
    slab_ring = [(s, (s + 1) % slabs) for s in range(slabs)]
    slab_back = [(j, i) for i, j in slab_ring]
    q_lower = lax.ppermute(rims[3], ("slab", "grp"), slab_ring)
    q_upper = lax.ppermute(rims[0], ("slab", "grp"), slab_back)

    words, got = lax.optimization_barrier((words, got))
    tiles = atoms // LANES
    cut = 3 * tiles // 8
    for bit in bits[1:2]:
        have = jnp.concatenate([have, got], axis=0)
        got, partners = doubling_step(have, partners, "bead", bit)
    pairs = pair_part(words, fixed, unit, lists, 0, cut)
    words, pairs, got, p_other = lax.optimization_barrier((words, pairs, got, p_other))
    moved = exchange(join(place, p_own, p_other, "p"), "bead")
    for bit in bits[2:]:
        have = jnp.concatenate([have, got], axis=0)
        got, partners = doubling_step(have, partners, "bead", bit)
    rest, first = pair_part(
        words, fixed, unit, lists, cut, tiles, (rims, q_lower, q_upper)
    )

    coefs = (kernel * np.float32(BEADS / NC)).reshape(NC, groups, beads, 1)
    coefs = jnp.asarray(np.broadcast_to(coefs, (NC, groups, beads, LANES)))
    new_p, force = finish(
        place, [*pairs, rest], first, moved, (have, got), partners, coefs
    )
    return tuple(swap(out) for out in (new_q, new_p, force))


def solution(mesh):
    field = P("bead", None, ("slab", "grp"))
    placed = (field,) * 4 + (P(("slab", "grp")), P(("slab", "grp"), None)) + (P(),) * 5
    return jax.shard_map(
        body, mesh=mesh, in_specs=placed, out_specs=(field,) * 3, check_vma=False
    )
```

```python
import math

import jax
import jax.numpy as jnp
import numpy as np
from jax import lax
from jax.experimental import pallas as pl
from jax.experimental.pallas import tpu as pltpu
from jax.sharding import PartitionSpec as P

BEADS = 64
NC = 8
EDGE = 128
LANES = 128

TIME_STEP = 0.1
CYCLE_FREQ = 5.0
CENTROID_FRICTION = 1.0
PAIR_STRENGTH = 0.5

BEST = lax.Precision.HIGHEST


def step_tables():
    b = np.arange(BEADS, dtype=np.float64)
    k = np.arange(BEADS)
    angle = 2.0 * np.pi * ((b[:, None] * b[None, :]) % BEADS) / BEADS
    half = BEADS // 2
    basis = np.where(
        k == 0,
        1.0 / math.sqrt(BEADS),
        np.where(
            k < half,
            math.sqrt(2.0 / BEADS) * np.cos(angle),
            np.where(
                k == half, np.cos(angle) / math.sqrt(BEADS), math.sqrt(2.0 / BEADS) * np.sin(angle)
            ),
        ),
    )
    freq = 2.0 * CYCLE_FREQ * np.sin(np.pi * b / BEADS)
    spacing = b[None, :] / BEADS - np.arange(NC, dtype=np.float64)[:, None] / NC
    kernel = np.ones_like(spacing)
    for order in range(1, NC // 2):
        kernel = kernel + 2.0 * np.cos(2.0 * np.pi * order * spacing)
    kernel = kernel + np.cos(np.pi * NC * spacing)
    contract = kernel / BEADS

    h = 0.5 * TIME_STEP
    safe = np.where(freq > 0.0, freq, 1.0)
    qq = np.where(freq > 0.0, np.cos(safe * h), 1.0)
    qp = np.where(freq > 0.0, np.sin(safe * h) / safe, h)
    pq = np.where(freq > 0.0, -safe * np.sin(safe * h), 0.0)
    pp = qq
    keep = np.exp(-np.where(freq > 0.0, 2.0 * freq, CENTROID_FRICTION) * TIME_STEP)
    kick = np.sqrt(1.0 - keep * keep)
    full_qq = qq * qq + qp * keep * pq
    full_qp = qq * qp + qp * keep * pp
    full_qn = qp * kick
    full_pq = pq * qq + pp * keep * pq
    full_pp = pq * qp + pp * keep * pp
    full_pn = pp * kick
    q_rows = np.concatenate(
        [(basis * full_qq) @ basis.T, (basis * full_qp) @ basis.T, basis * full_qn], axis=1
    )
    p_rows = np.concatenate(
        [(basis * full_pq) @ basis.T, (basis * full_pp) @ basis.T, basis * full_pn], axis=1
    )
    c_rows = contract @ q_rows
    step = np.concatenate([c_rows, q_rows, p_rows], axis=0)
    return step.astype(np.float32), contract.astype(np.float32)


def whole_vmem():
    return pl.BlockSpec(memory_space=pltpu.VMEM)


def params(mebibytes=48):
    return pltpu.CompilerParams(vmem_limit_bytes=mebibytes * 1024 * 1024)


def smem():
    return pl.BlockSpec(memory_space=pltpu.SMEM)


def block_of(place_ref, r, rows, count):
    return pl.ds(pl.multiple_of(((place_ref[0] ^ r) % count) * rows, LANES), rows)


def swap_with(block, axis, r):
    return lax.ppermute(block, axis, [(i, i ^ r) for i in range(lax.axis_size(axis))])


def exchange(blocks, axis):
    return [blocks[0]] + [swap_with(blocks[r], axis, r) for r in range(1, len(blocks))]


def pack(place, positions, momenta, force_old, noise, groups):
    _, beads, atoms = positions.shape
    rows = atoms // groups

    def kernel(place_ref, q_ref, p_ref, f_ref, n_ref, *rest):
        outs, (p_buf, f_buf, sems) = rest[:groups], rest[groups:]
        loads = [
            pltpu.make_async_copy(p_ref, p_buf, sems.at[0]),
            pltpu.make_async_copy(f_ref, f_buf, sems.at[1]),
        ]
        for r in range(groups):
            at = block_of(place_ref, r, rows, groups)
            for slot, (ref, first) in enumerate(((q_ref, 0), (n_ref, 6))):
                loads.append(
                    pltpu.make_async_copy(
                        ref.at[:, :, at], outs[r].at[pl.ds(first, 3)], sems.at[2 + 2 * r + slot]
                    )
                )
        for load in loads:
            load.start()
        loads[0].wait()
        loads[1].wait()
        for r in range(groups):
            at = block_of(place_ref, r, rows, groups)
            for x in range(3):
                outs[r][3 + x] = p_buf[x, :, at] + 0.5 * TIME_STEP * f_buf[x, :, at]
        for load in loads[2:]:
            load.wait()

    return pl.pallas_call(
        kernel,
        out_shape=[jax.ShapeDtypeStruct((9, beads, rows), jnp.float32)] * groups,
        in_specs=[smem()] + [pl.BlockSpec(memory_space=pltpu.HBM)] * 4,
        out_specs=[whole_vmem()] * groups,
        scratch_shapes=[
            pltpu.VMEM((3, beads, atoms), jnp.float32),
            pltpu.VMEM((3, beads, atoms), jnp.float32),
            pltpu.SemaphoreType.DMA((2 + 2 * groups,)),
        ],
        compiler_params=params(60),
        name="pack",
    )(place, positions, momenta, force_old, noise)


def prepare(pair_list, mass, desc_w, hidden_one, place, rows, half):
    entries, atoms = pair_list.shape
    desc, env = desc_w.shape
    hid = hidden_one.shape[0]
    order = np.arange(env)
    order = (order % entries) * (env // entries) + order // entries
    permute = jnp.asarray(np.eye(env)[order], jnp.bfloat16)

    def kernel(place_ref, list_ref, mass_ref, w0_ref, w1_ref, order_ref, lists, own, masses, w0, w1):
        for t in range(atoms // LANES):
            at = pl.ds(t * LANES, LANES)
            lists[:, at] = list_ref[:, at] - t * LANES
        inner, upper = place_ref[0] % half, place_ref[0] // half
        block = pl.ds(pl.multiple_of((2 * inner + upper) * rows, LANES), rows)
        own[...] = lists[:, block]
        masses[...] = mass_ref[:, pl.ds(pl.multiple_of(2 * inner * rows, LANES), 2 * rows)]
        w0[...] = lax.dot_general(
            order_ref[...],
            w0_ref[...],
            (((1,), (1,)), ((), ())),
            preferred_element_type=jnp.float32,
        ).astype(w0.dtype)
        w1[...] = w1_ref[...].astype(jnp.float32).T.astype(w1.dtype)

    return pl.pallas_call(
        kernel,
        out_shape=(
            jax.ShapeDtypeStruct((entries, atoms), jnp.int32),
            jax.ShapeDtypeStruct((entries, rows), jnp.int32),
            jax.ShapeDtypeStruct((1, 2 * rows), jnp.float32),
            jax.ShapeDtypeStruct((env, desc), jnp.bfloat16),
            jax.ShapeDtypeStruct((desc, hid), jnp.bfloat16),
        ),
        in_specs=[pl.BlockSpec(memory_space=pltpu.SMEM)] + [whole_vmem()] * 5,
        out_specs=(whole_vmem(),) * 5,
        compiler_params=params(),
        cost_estimate=pl.CostEstimate(
            flops=1_000_000_000, bytes_accessed=4_000_000, transcendentals=0
        ),
        name="prepare",
    )(place, pair_list, mass, desc_w, hidden_one, permute)


def contract(place, received, masses, table):
    groups = len(received)
    _, beads, rows = received[0].shape
    taken = rows // 2 + EDGE

    def kernel(place_ref, mass_ref, table_ref, own_ref, *rest):
        ins, (keep, send, fields, own, total, sem) = rest[: groups - 1], rest[groups - 1 :]
        load = pltpu.make_async_copy(own_ref, own, sem)
        load.start()
        mass = mass_ref[...]
        inverse = 1.0 / mass
        root = lax.rsqrt(mass)

        def scale(g, block):
            for x in range(3):
                fields[x, 0, g] = block[x]
                fields[x, 1, g] = block[3 + x] * inverse
                fields[x, 2, g] = block[6 + x] * root

        inner = place_ref[0] % groups
        for r in range(1, groups):
            scale(inner ^ r, ins[r - 1])
        load.wait()
        scale(inner, own)
        upper = place_ref[0] // groups
        for x in range(3):
            total[x] = jnp.dot(
                table_ref[upper],
                fields[x].reshape(3 * BEADS // 2, rows),
                precision=BEST,
                preferred_element_type=jnp.float32,
            )
        keep[...] = total[:, :, pl.ds(pl.multiple_of(upper * (rows - taken), LANES), taken)]
        send[...] = total[:, :, pl.ds(pl.multiple_of((1 - upper) * (rows - taken), LANES), taken)]

    return pl.pallas_call(
        kernel,
        out_shape=(
            jax.ShapeDtypeStruct((3, NC, taken), jnp.float32),
            jax.ShapeDtypeStruct((3, NC, taken), jnp.float32),
            jax.ShapeDtypeStruct((3, 3, groups, beads, rows), jnp.float32),
        ),
        in_specs=[smem()]
        + [whole_vmem()] * 2
        + [pl.BlockSpec(memory_space=pltpu.HBM)]
        + [whole_vmem()] * (groups - 1),
        out_specs=(whole_vmem(),) * 3,
        scratch_shapes=[
            pltpu.VMEM((9, beads, rows), jnp.float32),
            pltpu.VMEM((3, NC, rows), jnp.float32),
            pltpu.SemaphoreType.DMA,
        ],
        compiler_params=params(),
        name="contract",
    )(place, masses, table, *received)


def join_contracted(upper, own, other):
    _, _, taken = own.shape
    rows = taken - EDGE

    def kernel(upper_ref, own_ref, other_ref, extended, outgoing):
        upper = upper_ref[0]
        at = pl.multiple_of((1 - upper) * EDGE, LANES)
        extended[:, :, pl.ds(pl.multiple_of(upper * (rows + EDGE), LANES), EDGE)] = jnp.zeros(
            (3, NC, EDGE), jnp.float32
        )
        extended[:, :, pl.ds(at, taken)] = own_ref[...] + other_ref[...]
        at = pl.multiple_of(EDGE + upper * (rows - EDGE), LANES)
        outgoing[...] = extended[:, :, pl.ds(at, EDGE)]

    return pl.pallas_call(
        kernel,
        out_shape=(
            jax.ShapeDtypeStruct((3, NC, rows + 2 * EDGE), jnp.float32),
            jax.ShapeDtypeStruct((3, NC, EDGE), jnp.float32),
        ),
        in_specs=[smem()] + [whole_vmem()] * 2,
        out_specs=(whole_vmem(),) * 2,
        compiler_params=params(),
        name="join_contracted",
    )(upper, own, other)


def transform(place, fields, masses, table, name):
    _, _, groups, beads, rows = fields.shape

    def kernel(place_ref, fields_ref, mass_ref, table_ref, cross, own):
        for x in range(3):
            out = jnp.dot(
                table_ref[place_ref[0] // groups],
                fields_ref[x].reshape(3 * BEADS // 2, rows),
                precision=BEST,
                preferred_element_type=jnp.float32,
            )
            if name == "p":
                out = out * mass_ref[...]
            cross[x] = out[: BEADS // 2].reshape(groups, beads, rows)
            own[x] = out[BEADS // 2 :].reshape(groups, beads, rows)

    return pl.pallas_call(
        kernel,
        out_shape=[jax.ShapeDtypeStruct((3, groups, beads, rows), jnp.float32)] * 2,
        in_specs=[smem()] + [whole_vmem()] * 3,
        out_specs=[whole_vmem()] * 2,
        compiler_params=params(),
        cost_estimate=pl.CostEstimate(
            flops=500_000_000, bytes_accessed=1_000_000, transcendentals=0
        ),
        name=f"transform_{name}",
    )(place, fields, masses, table)


def join(place, own, other, name):
    _, groups, beads, rows = own.shape

    def kernel(place_ref, own_ref, other_ref, *outs):
        inner = place_ref[0] % groups
        for r in range(groups):
            for x in range(3):
                outs[r][x] = own_ref[x, inner ^ r] + other_ref[x, inner ^ r]

    return pl.pallas_call(
        kernel,
        out_shape=[jax.ShapeDtypeStruct((3, beads, rows), jnp.float32)] * groups,
        in_specs=[smem()] + [whole_vmem()] * 2,
        out_specs=[whole_vmem()] * groups,
        compiler_params=params(),
        name=f"join_{name}",
    )(place, own, other)


def inverse_of(value):
    estimate = pl.reciprocal(value, approx=True)
    return estimate * (2.0 - value * estimate)


def banded(windows, lane, low, high):
    below, middle, above = [
        jnp.take_along_axis(w, lane, axis=1, mode="promise_in_bounds") for w in windows
    ]
    return jnp.where(low, below, jnp.where(high, above, middle))


def entries_of(list_ref, e, base):
    place = list_ref[pl.ds(e, 8), pl.ds(base, LANES)]
    return place & (LANES - 1), place < LANES, place >= 2 * LANES


def on_sublanes(row):
    return jnp.broadcast_to(row, (8, LANES))


def env_units(windows, list_ref, base, envs, inputs):
    entries = list_ref.shape[0]
    for e in range(0, entries, 8):
        lane, low, high = entries_of(list_ref, e, base)
        for c in range(NC):
            apart = []
            for x in range(3):
                tiles = windows(c, x)
                apart.append(banded(tiles, lane, low, high) - tiles[1])
            square = apart[0] * apart[0] + apart[1] * apart[1] + apart[2] * apart[2]
            close = inverse_of(1.0 + square)
            for x, value in enumerate(apart + [close]):
                envs[pl.ds(x * entries + e, 8), pl.ds(c * LANES, LANES)] = value
            yield
    for c in range(NC):
        at = pl.ds(c * LANES, LANES)
        inputs[at, :] = envs[:, at].T.astype(jnp.bfloat16)
        yield


def network(inputs_ref, weights, out_ref, base, units, chunk=256):
    w0_ref, w1_ref, w2_ref, w3_ref, wo_ref = weights
    desc = w0_ref.shape[1]
    inputs = inputs_ref[...]
    total = None
    for f in range(0, desc, chunk):
        size = min(chunk, desc - f)
        first = jnp.dot(inputs, w0_ref[:, pl.ds(f, size)], preferred_element_type=jnp.float32)
        first = jnp.tanh(first.astype(jnp.bfloat16))
        part = jnp.dot(first, w1_ref[pl.ds(f, size), :], preferred_element_type=jnp.float32)
        total = part if total is None else total + part
        for _ in range(6):
            next(units, None)
    layer = jnp.tanh(total).astype(jnp.bfloat16)
    for ref in (w2_ref, w3_ref):
        layer = jnp.tanh(jnp.dot(layer, ref[...], preferred_element_type=jnp.float32)).astype(
            jnp.bfloat16
        )
    out = lax.dot_general(
        wo_ref[...], layer, (((1,), (1,)), ((), ())), preferred_element_type=jnp.float32
    )
    for c in range(NC):
        for x in range(3):
            out_ref[x, pl.ds(c, 1), pl.ds(base, LANES)] = out[
                x : x + 1, c * LANES : (c + 1) * LANES
            ]


def neural_scratch(env):
    return [
        pltpu.VMEM((2, env, NC * LANES), jnp.float32),
        pltpu.VMEM((2, NC * LANES, env), jnp.bfloat16),
    ]


def neural(upper, extended, remote, lists, weights):
    _, _, wide = extended.shape
    rows = wide - 2 * EDGE
    tiles = rows // LANES

    def kernel(
        upper_ref, ext_ref, remote_ref, list_ref, w0, w1, w2, w3, wo, out_ref, ext, envs, inputs
    ):
        ext[...] = ext_ref[...]
        at = pl.multiple_of(upper_ref[0] * (rows + EDGE), LANES)
        ext[:, :, pl.ds(at, EDGE)] = remote_ref[...]

        def units_of(t):
            if t >= tiles:
                return iter(())

            def windows(c, x):
                return [
                    on_sublanes(ext[x, pl.ds(c, 1), pl.ds((t + v) * LANES, LANES)])
                    for v in range(3)
                ]

            slot = t % 2
            return env_units(windows, list_ref, t * LANES, envs.at[slot], inputs.at[slot])

        for _ in units_of(0):
            pass
        for t in range(tiles):
            units = units_of(t + 1)
            network(inputs.at[t % 2], (w0, w1, w2, w3, wo), out_ref, t * LANES, units)
            for _ in units:
                pass

    return pl.pallas_call(
        kernel,
        out_shape=jax.ShapeDtypeStruct((3, NC, rows), jnp.float32),
        in_specs=[smem()] + [whole_vmem()] * 8,
        out_specs=whole_vmem(),
        scratch_shapes=[pltpu.VMEM((3, NC, wide), jnp.float32)]
        + neural_scratch(weights[0].shape[0]),
        compiler_params=params(),
        cost_estimate=pl.CostEstimate(
            flops=12_000_000_000, bytes_accessed=4_000_000, transcendentals=0
        ),
        name="neural",
    )(upper, extended, remote, lists, *weights)


def add_pairs(sums, e, b, apart, close):
    for x in range(3):
        part = apart[x] * close
        sums[x, b] = part if e == 0 else sums[x, b] + part


def total_of(sums, x):
    total = sums[x, :, 0, :]
    for s in range(1, 8):
        total = total + sums[x, :, s, :]
    return total


def assemble(place, fields):
    groups = len(fields)
    _, beads, rows = fields[0].shape
    atoms = groups * rows
    half = beads // 2
    top = float(2**15 - 1)

    def kernel(place_ref, *refs):
        ins, (newq, words, fixed, unit_ref, rims) = refs[:groups], refs[groups:]
        largest = jnp.zeros((beads, rows), jnp.float32)
        for r in range(groups):
            at = block_of(place_ref, r, rows, groups)
            for x in range(3):
                value = ins[r][x]
                newq[x, :, at] = value
                largest = jnp.maximum(largest, jnp.abs(value))
        limit = jnp.maximum(jnp.max(largest, keepdims=True), 1e-30)
        to_fixed = top / limit
        unit_ref[...] = jnp.broadcast_to(limit / (top * 65536.0), (beads, LANES))
        for r in range(groups):
            at = block_of(place_ref, r, rows, groups)
            for x in range(3):
                value = jnp.floor(ins[r][x] * to_fixed + 0.5)
                fixed[x, :, at] = value * 65536.0
                value = value.astype(jnp.int32)
                words[x, :, at] = (value[:half] << 16) | (value[half:] & 65535)
        for rim, t in enumerate((0, LANES, atoms - 2 * LANES, atoms - LANES)):
            rims[rim] = newq[:, :, pl.ds(t, LANES)]

    return pl.pallas_call(
        kernel,
        out_shape=(
            jax.ShapeDtypeStruct((3, beads, atoms), jnp.float32),
            jax.ShapeDtypeStruct((3, half, atoms), jnp.int32),
            jax.ShapeDtypeStruct((3, beads, atoms), jnp.float32),
            jax.ShapeDtypeStruct((beads, LANES), jnp.float32),
            jax.ShapeDtypeStruct((4, 3, beads, LANES), jnp.float32),
        ),
        in_specs=[smem()] + [whole_vmem()] * groups,
        out_specs=(whole_vmem(),) * 5,
        compiler_params=params(),
        name="assemble",
    )(place, *fields)


def pair_part(words, fixed, unit, lists, begin, end, edges=()):
    _, beads, atoms = fixed.shape
    half = beads // 2
    tiles = atoms // LANES
    entries = lists.shape[0]

    def kernel(words_ref, fixed_ref, unit_ref, list_ref, *rest):
        ends = rest[: len(edges)]
        pair, sums = rest[len(edges)], rest[-1]
        unit_row = unit_ref[...]
        unit_square = on_sublanes(unit_ref[pl.ds(0, 1), :])
        unit_square = unit_square * unit_square

        def edge(out, at, base, near_tiles):
            for e in range(0, entries, 8):
                lane, low, high = entries_of(list_ref, e, base)
                for b in range(beads):
                    apart = []
                    for x in range(3):
                        windows = [on_sublanes(tile[x, pl.ds(b, 1), :]) for tile in near_tiles]
                        apart.append(banded(windows, lane, low, high) - windows[1])
                    square = apart[0] * apart[0] + apart[1] * apart[1] + apart[2] * apart[2]
                    add_pairs(sums, e, b, apart, inverse_of(1.0 + square))
            for x in range(3):
                out[x, :, pl.ds(at, LANES)] = PAIR_STRENGTH * total_of(sums, x)

        @pl.loop(max(begin, 1), min(end, tiles - 1))
        def _(t):
            base = pl.multiple_of(t * LANES, LANES)

            def row(ref, x, b, v):
                return on_sublanes(ref[x, pl.ds(b, 1), pl.ds(base + (v - 1) * LANES, LANES)])

            for e in range(0, entries, 8):
                lane, low, high = entries_of(list_ref, e, base)
                for b in range(half):
                    both = [
                        banded([row(words_ref, x, b, v) for v in range(3)], lane, low, high)
                        for x in range(3)
                    ]
                    for bead, near in ((b, [w & -65536 for w in both]),
                                       (b + half, [w << 16 for w in both])):
                        apart = [
                            near[x].astype(jnp.float32) - row(fixed_ref, x, bead, 1)
                            for x in range(3)
                        ]
                        square = apart[0] * apart[0] + apart[1] * apart[1] + apart[2] * apart[2]
                        close = inverse_of(1.0 + square * unit_square)
                        add_pairs(sums, e, bead, apart, close)
            at = pl.ds(pl.multiple_of((t - begin) * LANES, LANES), LANES)
            for x in range(3):
                pair[x, :, at] = (PAIR_STRENGTH * unit_row) * total_of(sums, x)

        if edges:
            rims, lower, upper = ends
            last = (tiles - 1) * LANES
            edge(rest[len(edges) + 1], 0, 0, [lower, rims.at[0], rims.at[1]])
            edge(pair, last - begin * LANES, last, [rims.at[2], rims.at[3], upper])

    out_shape = [jax.ShapeDtypeStruct((3, beads, (end - begin) * LANES), jnp.float32)]
    if edges:
        out_shape.append(jax.ShapeDtypeStruct((3, beads, LANES), jnp.float32))
    return pl.pallas_call(
        kernel,
        out_shape=out_shape,
        in_specs=[whole_vmem()] * (4 + len(edges)),
        out_specs=[whole_vmem()] * len(out_shape),
        scratch_shapes=[pltpu.VMEM((3, beads, 8, LANES), jnp.float32)],
        compiler_params=params(),
        cost_estimate=pl.CostEstimate(
            flops=300_000 * (end - begin), bytes_accessed=1_000, transcendentals=0
        ),
        name=f"pair_{begin}",
    )(words, fixed, unit, lists, *edges)


def finish(place, pairs, first, moved, neural_parts, partners, coefs):
    half = len(moved)
    _, beads, wide = moved[0].shape
    rows = wide // 2
    atoms = half * wide
    counts = [part.shape[0] for part in neural_parts]

    def kernel(place_ref, first_ref, coef_ref, *rest):
        halves, rest = rest[: len(pairs)], rest[len(pairs) :]
        ins, rest = rest[:half], rest[half:]
        blocks, (newp, newf) = rest[: len(counts)], rest[len(counts) :]
        own = place_ref[0]
        at = 0
        for piece in halves:
            newf[:, :, pl.ds(at, piece.shape[2])] = piece[...]
            at += piece.shape[2]
        newf[:, :, pl.ds(0, LANES)] = first_ref[...]
        coef = [coef_ref[c, own] for c in range(NC)]
        blocks = [block.at[i] for block, count in zip(blocks, counts) for i in range(count)]
        for r, block in zip(partners, blocks):
            source = own ^ r
            base = (source % half) * wide + (source // half) * rows
            for t in range(0, rows, LANES):
                at = pl.ds(pl.multiple_of(base + t, LANES), LANES)
                for x in range(3):
                    force = newf[x, :, at]
                    for c in range(NC):
                        force = force + coef[c] * block[x, pl.ds(c, 1), pl.ds(t, LANES)]
                    newf[x, :, at] = force
        for r in range(half):
            at = block_of(place_ref, r, wide, half)
            for x in range(3):
                newp[x, :, at] = ins[r][x] + 0.5 * TIME_STEP * newf[x, :, at]

    out = jax.ShapeDtypeStruct((3, beads, atoms), jnp.float32)
    return pl.pallas_call(
        kernel,
        out_shape=(out,) * 2,
        in_specs=[smem()] + [whole_vmem()] * (2 + len(pairs) + half + len(neural_parts)),
        out_specs=(whole_vmem(),) * 2,
        compiler_params=params(),
        name="finish",
    )(place, first, coefs, *pairs, *moved, *neural_parts)


def doubling_step(have, partners, axis, bit):
    count = lax.axis_size(axis)
    got = lax.ppermute(have, axis, [(i, i ^ bit) for i in range(count)])
    return got, partners + [r ^ bit for r in partners]


def body(
    positions,
    momenta,
    force_old,
    noise,
    mass,
    pair_list,
    desc_w,
    hidden_one,
    hidden_two,
    hidden_three,
    out_w,
):
    beads, _, atoms = positions.shape
    groups = lax.axis_size("bead")
    slabs = lax.axis_size(("slab", "grp"))
    rows = atoms // groups
    half = groups // 2
    index = lax.axis_index("bead").astype(jnp.int32)
    place, upper = index[None], (index // half)[None]
    step, kernel = step_tables()
    sides = step.reshape(-1, 3, 2, BEADS // 2).transpose(2, 0, 1, 3).reshape(2, -1, 3 * BEADS // 2)

    def crossing(first_row):
        rows_of = [sides[:, first_row + s * BEADS // 2 :][:, : BEADS // 2] for s in range(2)]
        return jnp.asarray(
            np.stack(
                [np.concatenate([rows_of[1 - s][s], rows_of[s][s]], axis=0) for s in range(2)]
            )
        )

    swap = lambda field: jnp.transpose(field, (1, 0, 2))
    sends = pack(place, swap(positions), swap(momenta), swap(force_old), swap(noise), half)
    received = exchange(sends, "bead")

    lists, block_lists, masses, env_w, w1 = prepare(
        pair_list.T, mass[None, :], desc_w.T, hidden_one.T, place, rows, half
    )
    received, lists, block_lists, masses, env_w, w1 = lax.optimization_barrier(
        (received, lists, block_lists, masses, env_w, w1)
    )
    weights = (env_w, w1, hidden_two, hidden_three, out_w.T)

    keep, send, scaled = contract(place, received, masses, jnp.asarray(sides[:, :NC]))
    other = swap_with(send, "bead", half)
    q_cross, q_own = transform(place, scaled, masses, crossing(NC), "q")
    p_cross, p_own = transform(place, scaled, masses, crossing(NC + BEADS), "p")
    extended, outgoing = join_contracted(upper, keep, other)
    ring = []
    for s in range(slabs):
        for g in range(half):
            up, down = (g + 1) % half, (g - 1) % half
            up_slab, down_slab = (s + (g + 1) // half) % slabs, (s + (g - 1) // half) % slabs
            ring.append((g * slabs + s, (half + down) * slabs + down_slab))
            ring.append(((half + g) * slabs + s, up * slabs + up_slab))
    remote = lax.ppermute(outgoing, ("bead", "slab", "grp"), ring)
    q_cross, remote = lax.optimization_barrier((q_cross, remote))
    q_other = swap_with(q_cross, "bead", half)

    forces = neural(upper, extended, remote, block_lists, weights)

    bits = [1 << i for i in range(groups.bit_length() - 2, -1, -1)]
    have = forces[None]
    got, partners = doubling_step(have, [0], "bead", bits[0])
    q_other, p_cross, got = lax.optimization_barrier((q_other, p_cross, got))
    p_other = swap_with(p_cross, "bead", half)
    fields = exchange(join(place, q_own, q_other, "q"), "bead")

    new_q, words, fixed, unit, rims = assemble(place, fields)
    slab_ring = [(s, (s + 1) % slabs) for s in range(slabs)]
    slab_back = [(j, i) for i, j in slab_ring]
    q_lower = lax.ppermute(rims[3], ("slab", "grp"), slab_ring)
    q_upper = lax.ppermute(rims[0], ("slab", "grp"), slab_back)

    tiles = atoms // LANES
    cuts = [0, 3 * tiles // 8, 11 * tiles // 16, tiles]
    for bit in bits[1:2]:
        have = jnp.concatenate([have, got], axis=0)
        got, partners = doubling_step(have, partners, "bead", bit)
    (head,) = pair_part(words, fixed, unit, lists, *cuts[:2])
    words, head, got, q_lower, q_upper = lax.optimization_barrier(
        (words, head, got, q_lower, q_upper)
    )
    for bit in bits[2:]:
        have = jnp.concatenate([have, got], axis=0)
        got, partners = doubling_step(have, partners, "bead", bit)
    (middle,) = pair_part(words, fixed, unit, lists, *cuts[1:3])
    words, middle, p_other = lax.optimization_barrier((words, middle, p_other))
    moved = exchange(join(place, p_own, p_other, "p"), "bead")
    rest, first = pair_part(words, fixed, unit, lists, *cuts[2:], (rims, q_lower, q_upper))
    pairs = [head, middle]

    coefs = (kernel * np.float32(BEADS / NC)).reshape(NC, groups, beads, 1)
    coefs = jnp.asarray(np.broadcast_to(coefs, (NC, groups, beads, LANES)))
    new_p, force = finish(
        place, [*pairs, rest], first, moved, (have, got), partners, coefs
    )
    return tuple(swap(out) for out in (new_q, new_p, force))


def solution(mesh):
    field = P("bead", None, ("slab", "grp"))
    placed = (field,) * 4 + (P(("slab", "grp")), P(("slab", "grp"), None)) + (P(),) * 5
    return jax.shard_map(
        body, mesh=mesh, in_specs=placed, out_specs=(field,) * 3, check_vma=False
    )
```

```python
import math

import jax
import jax.numpy as jnp
import numpy as np
from jax import lax
from jax.experimental import pallas as pl
from jax.experimental.pallas import tpu as pltpu
from jax.sharding import PartitionSpec as P

BEADS = 64
NC = 8
EDGE = 128
LANES = 128

TIME_STEP = 0.1
CYCLE_FREQ = 5.0
CENTROID_FRICTION = 1.0
PAIR_STRENGTH = 0.5

BEST = lax.Precision.HIGHEST


def step_tables():
    b = np.arange(BEADS, dtype=np.float64)
    k = np.arange(BEADS)
    angle = 2.0 * np.pi * ((b[:, None] * b[None, :]) % BEADS) / BEADS
    half = BEADS // 2
    basis = np.where(
        k == 0,
        1.0 / math.sqrt(BEADS),
        np.where(
            k < half,
            math.sqrt(2.0 / BEADS) * np.cos(angle),
            np.where(
                k == half, np.cos(angle) / math.sqrt(BEADS), math.sqrt(2.0 / BEADS) * np.sin(angle)
            ),
        ),
    )
    freq = 2.0 * CYCLE_FREQ * np.sin(np.pi * b / BEADS)
    spacing = b[None, :] / BEADS - np.arange(NC, dtype=np.float64)[:, None] / NC
    kernel = np.ones_like(spacing)
    for order in range(1, NC // 2):
        kernel = kernel + 2.0 * np.cos(2.0 * np.pi * order * spacing)
    kernel = kernel + np.cos(np.pi * NC * spacing)
    contract = kernel / BEADS

    h = 0.5 * TIME_STEP
    safe = np.where(freq > 0.0, freq, 1.0)
    qq = np.where(freq > 0.0, np.cos(safe * h), 1.0)
    qp = np.where(freq > 0.0, np.sin(safe * h) / safe, h)
    pq = np.where(freq > 0.0, -safe * np.sin(safe * h), 0.0)
    pp = qq
    keep = np.exp(-np.where(freq > 0.0, 2.0 * freq, CENTROID_FRICTION) * TIME_STEP)
    kick = np.sqrt(1.0 - keep * keep)
    full_qq = qq * qq + qp * keep * pq
    full_qp = qq * qp + qp * keep * pp
    full_qn = qp * kick
    full_pq = pq * qq + pp * keep * pq
    full_pp = pq * qp + pp * keep * pp
    full_pn = pp * kick
    q_rows = np.concatenate(
        [(basis * full_qq) @ basis.T, (basis * full_qp) @ basis.T, basis * full_qn], axis=1
    )
    p_rows = np.concatenate(
        [(basis * full_pq) @ basis.T, (basis * full_pp) @ basis.T, basis * full_pn], axis=1
    )
    c_rows = contract @ q_rows
    step = np.concatenate([c_rows, q_rows, p_rows], axis=0)
    return step.astype(np.float32), contract.astype(np.float32)


def whole_vmem():
    return pl.BlockSpec(memory_space=pltpu.VMEM)


def params(mebibytes=48):
    return pltpu.CompilerParams(vmem_limit_bytes=mebibytes * 1024 * 1024)


def smem():
    return pl.BlockSpec(memory_space=pltpu.SMEM)


def block_of(place_ref, r, rows):
    return pl.ds(pl.multiple_of((place_ref[0] ^ r) * rows, LANES), rows)


def exchange(blocks, axis):
    count = len(blocks)
    return [blocks[0]] + [
        lax.ppermute(blocks[r], axis, [(i, i ^ r) for i in range(count)]) for r in range(1, count)
    ]


def pack(place, positions, momenta, force_old, noise, groups):
    _, beads, atoms = positions.shape
    rows = atoms // groups

    def kernel(place_ref, q_ref, p_ref, f_ref, n_ref, *rest):
        outs, (p_buf, f_buf, sems) = rest[:groups], rest[groups:]
        loads = [
            pltpu.make_async_copy(p_ref, p_buf, sems.at[0]),
            pltpu.make_async_copy(f_ref, f_buf, sems.at[1]),
        ]
        for r in range(groups):
            at = block_of(place_ref, r, rows)
            for slot, (ref, first) in enumerate(((q_ref, 0), (n_ref, 6))):
                loads.append(
                    pltpu.make_async_copy(
                        ref.at[:, :, at], outs[r].at[pl.ds(first, 3)], sems.at[2 + 2 * r + slot]
                    )
                )
        for load in loads:
            load.start()
        loads[0].wait()
        loads[1].wait()
        for r in range(groups):
            at = block_of(place_ref, r, rows)
            for x in range(3):
                outs[r][3 + x] = p_buf[x, :, at] + 0.5 * TIME_STEP * f_buf[x, :, at]
        for load in loads[2:]:
            load.wait()

    return pl.pallas_call(
        kernel,
        out_shape=[jax.ShapeDtypeStruct((9, beads, rows), jnp.float32)] * groups,
        in_specs=[smem()] + [pl.BlockSpec(memory_space=pltpu.HBM)] * 4,
        out_specs=[whole_vmem()] * groups,
        scratch_shapes=[
            pltpu.VMEM((3, beads, atoms), jnp.float32),
            pltpu.VMEM((3, beads, atoms), jnp.float32),
            pltpu.SemaphoreType.DMA((2 + 2 * groups,)),
        ],
        compiler_params=params(60),
        name="pack",
    )(place, positions, momenta, force_old, noise)


def prepare(pair_list, mass, desc_w, hidden_one, place, rows):
    entries, atoms = pair_list.shape
    desc, env = desc_w.shape
    hid = hidden_one.shape[0]
    order = np.arange(env)
    order = (order % entries) * (env // entries) + order // entries
    permute = jnp.asarray(np.eye(env)[order], jnp.bfloat16)

    def kernel(place_ref, list_ref, mass_ref, w0_ref, w1_ref, order_ref, lists, own, masses, w0, w1):
        for t in range(atoms // LANES):
            at = pl.ds(t * LANES, LANES)
            lists[:, at] = list_ref[:, at] - t * LANES
        block = pl.ds(pl.multiple_of(place_ref[0] * rows, LANES), rows)
        own[...] = lists[:, block]
        masses[...] = mass_ref[:, block]
        w0[...] = lax.dot_general(
            order_ref[...],
            w0_ref[...],
            (((1,), (1,)), ((), ())),
            preferred_element_type=jnp.float32,
        ).astype(w0.dtype)
        w1[...] = w1_ref[...].astype(jnp.float32).T.astype(w1.dtype)

    return pl.pallas_call(
        kernel,
        out_shape=(
            jax.ShapeDtypeStruct((entries, atoms), jnp.int32),
            jax.ShapeDtypeStruct((entries, rows), jnp.int32),
            jax.ShapeDtypeStruct((1, rows), jnp.float32),
            jax.ShapeDtypeStruct((env, desc), jnp.bfloat16),
            jax.ShapeDtypeStruct((desc, hid), jnp.bfloat16),
        ),
        in_specs=[pl.BlockSpec(memory_space=pltpu.SMEM)] + [whole_vmem()] * 5,
        out_specs=(whole_vmem(),) * 5,
        compiler_params=params(),
        cost_estimate=pl.CostEstimate(
            flops=1_000_000_000, bytes_accessed=4_000_000, transcendentals=0
        ),
        name="prepare",
    )(place, pair_list, mass, desc_w, hidden_one, permute)


def contract(place, received, masses, table):
    groups = len(received)
    _, beads, rows = received[0].shape

    def kernel(place_ref, mass_ref, table_ref, own_ref, *rest):
        ins, (c_ref, first, last, fields, own, sem) = rest[: groups - 1], rest[groups - 1 :]

        load = pltpu.make_async_copy(own_ref, own, sem)
        load.start()
        mass = mass_ref[...]
        inverse = 1.0 / mass
        root = lax.rsqrt(mass)

        def scale(g, block):
            for x in range(3):
                fields[x, 0, g] = block[x]
                fields[x, 1, g] = block[3 + x] * inverse
                fields[x, 2, g] = block[6 + x] * root

        for r in range(1, groups):
            scale(place_ref[0] ^ r, ins[r - 1])
        load.wait()
        scale(place_ref[0], own)
        for x in range(3):
            out = jnp.dot(
                table_ref[...],
                fields[x].reshape(3 * BEADS, rows),
                precision=BEST,
                preferred_element_type=jnp.float32,
            )
            c_ref[x] = out
            first[x] = out[:, :EDGE]
            last[x] = out[:, rows - EDGE :]

    edge = jax.ShapeDtypeStruct((3, NC, EDGE), jnp.float32)
    return pl.pallas_call(
        kernel,
        out_shape=(
            jax.ShapeDtypeStruct((3, NC, rows), jnp.float32),
            edge,
            edge,
            jax.ShapeDtypeStruct((3, 3, groups, beads, rows), jnp.float32),
        ),
        in_specs=[smem()]
        + [whole_vmem()] * 2
        + [pl.BlockSpec(memory_space=pltpu.HBM)]
        + [whole_vmem()] * (groups - 1),
        out_specs=(whole_vmem(),) * 4,
        scratch_shapes=[pltpu.VMEM((9, beads, rows), jnp.float32), pltpu.SemaphoreType.DMA],
        compiler_params=params(),
        name="contract",
    )(place, masses, table, *received)


def transform(fields, masses, table):
    _, _, groups, beads, rows = fields.shape

    def kernel(fields_ref, mass_ref, table_ref, out_ref, news, sems):
        mass = mass_ref[...]
        copies = []
        for x in range(3):
            out = jnp.dot(
                table_ref[...],
                fields_ref[x].reshape(3 * BEADS, rows),
                precision=BEST,
                preferred_element_type=jnp.float32,
            )
            news[x] = out[:BEADS].reshape(groups, beads, rows)
            news[3 + x] = (out[BEADS:] * mass).reshape(groups, beads, rows)
            for row in (x, 3 + x):
                copy = pltpu.make_async_copy(news.at[row], out_ref.at[:, row], sems.at[row])
                copy.start()
                copies.append(copy)
        for copy in copies:
            copy.wait()

    return pl.pallas_call(
        kernel,
        out_shape=jax.ShapeDtypeStruct((groups, 6, beads, rows), jnp.float32),
        in_specs=[whole_vmem()] * 3,
        out_specs=pl.BlockSpec(memory_space=pltpu.HBM),
        scratch_shapes=[
            pltpu.VMEM((6, groups, beads, rows), jnp.float32),
            pltpu.SemaphoreType.DMA((6,)),
        ],
        compiler_params=params(),
        cost_estimate=pl.CostEstimate(
            flops=1_000_000_000, bytes_accessed=2_000_000, transcendentals=0
        ),
        name="transform",
    )(fields, masses, table)


def inverse_of(value):
    estimate = pl.reciprocal(value, approx=True)
    return estimate * (2.0 - value * estimate)


def banded(windows, lane, low, high):
    below, middle, above = [
        jnp.take_along_axis(w, lane, axis=1, mode="promise_in_bounds") for w in windows
    ]
    return jnp.where(low, below, jnp.where(high, above, middle))


def entries_of(list_ref, e, base):
    place = list_ref[pl.ds(e, 8), pl.ds(base, LANES)]
    return place & (LANES - 1), place < LANES, place >= 2 * LANES


def on_sublanes(row):
    return jnp.broadcast_to(row, (8, LANES))


def env_units(windows, list_ref, base, envs, inputs):
    entries = list_ref.shape[0]
    for e in range(0, entries, 8):
        lane, low, high = entries_of(list_ref, e, base)
        for c in range(NC):
            apart = []
            for x in range(3):
                tiles = windows(c, x)
                apart.append(banded(tiles, lane, low, high) - tiles[1])
            square = apart[0] * apart[0] + apart[1] * apart[1] + apart[2] * apart[2]
            close = inverse_of(1.0 + square)
            for x, value in enumerate(apart + [close]):
                envs[pl.ds(x * entries + e, 8), pl.ds(c * LANES, LANES)] = value
            yield
    for c in range(NC):
        at = pl.ds(c * LANES, LANES)
        inputs[at, :] = envs[:, at].T.astype(jnp.bfloat16)
        yield


def network(inputs_ref, weights, out_ref, base, units, chunk=256):
    w0_ref, w1_ref, w2_ref, w3_ref, wo_ref = weights
    desc = w0_ref.shape[1]
    inputs = inputs_ref[...]
    total = None
    for f in range(0, desc, chunk):
        size = min(chunk, desc - f)
        first = jnp.dot(inputs, w0_ref[:, pl.ds(f, size)], preferred_element_type=jnp.float32)
        first = jnp.tanh(first.astype(jnp.bfloat16))
        part = jnp.dot(first, w1_ref[pl.ds(f, size), :], preferred_element_type=jnp.float32)
        total = part if total is None else total + part
        for _ in range(6):
            next(units, None)
    layer = jnp.tanh(total).astype(jnp.bfloat16)
    for ref in (w2_ref, w3_ref):
        layer = jnp.tanh(jnp.dot(layer, ref[...], preferred_element_type=jnp.float32)).astype(
            jnp.bfloat16
        )
    out = lax.dot_general(
        wo_ref[...], layer, (((1,), (1,)), ((), ())), preferred_element_type=jnp.float32
    )
    for c in range(NC):
        for x in range(3):
            out_ref[x, pl.ds(c, 1), pl.ds(base, LANES)] = out[
                x : x + 1, c * LANES : (c + 1) * LANES
            ]


def neural_scratch(env):
    return [
        pltpu.VMEM((2, env, NC * LANES), jnp.float32),
        pltpu.VMEM((2, NC * LANES, env), jnp.bfloat16),
    ]


def neural(contracted, lower, upper, lists, weights):
    _, _, rows = contracted.shape
    tiles = rows // LANES

    def kernel(
        c_ref, low_ref, up_ref, list_ref, w0, w1, w2, w3, wo, out_ref, envs, inputs
    ):
        def tile(x, c, t):
            if t < 0:
                ref, at = low_ref, 0
            elif t >= tiles:
                ref, at = up_ref, 0
            else:
                ref, at = c_ref, t * LANES
            return on_sublanes(ref[x, pl.ds(c, 1), pl.ds(at, LANES)])

        def units_of(t):
            if t >= tiles:
                return iter(())
            windows = lambda c, x: [tile(x, c, t + v) for v in (-1, 0, 1)]
            slot = t % 2
            return env_units(windows, list_ref, t * LANES, envs.at[slot], inputs.at[slot])

        for _ in units_of(0):
            pass
        for t in range(tiles):
            units = units_of(t + 1)
            network(inputs.at[t % 2], (w0, w1, w2, w3, wo), out_ref, t * LANES, units)
            for _ in units:
                pass

    return pl.pallas_call(
        kernel,
        out_shape=jax.ShapeDtypeStruct((3, NC, rows), jnp.float32),
        in_specs=[whole_vmem()] * 9,
        out_specs=whole_vmem(),
        scratch_shapes=neural_scratch(weights[0].shape[0]),
        compiler_params=params(),
        cost_estimate=pl.CostEstimate(
            flops=12_000_000_000, bytes_accessed=4_000_000, transcendentals=0
        ),
        name="neural",
    )(contracted, lower, upper, lists, *weights)


def add_pairs(sums, e, b, apart, close):
    for x in range(3):
        part = apart[x] * close
        sums[x, b] = part if e == 0 else sums[x, b] + part


def total_of(sums, x):
    total = sums[x, :, 0, :]
    for s in range(1, 8):
        total = total + sums[x, :, s, :]
    return total


def assemble(fields):
    groups, _, beads, rows = fields.shape
    atoms = groups * rows
    half = beads // 2
    top = float(2**15 - 1)

    def kernel(in_ref, newq, words, fixed, unit_ref, rims):
        largest = jnp.zeros((beads, rows), jnp.float32)
        for g in range(groups):
            at = pl.ds(g * rows, rows)
            for x in range(3):
                value = in_ref[g, x]
                newq[x, :, at] = value
                largest = jnp.maximum(largest, jnp.abs(value))
        limit = jnp.maximum(jnp.max(largest, keepdims=True), 1e-30)
        to_fixed = top / limit
        unit_ref[...] = jnp.broadcast_to(limit / (top * 65536.0), (beads, LANES))
        for g in range(groups):
            at = pl.ds(g * rows, rows)
            for x in range(3):
                value = jnp.floor(in_ref[g, x] * to_fixed + 0.5)
                fixed[x, :, at] = value * 65536.0
                value = value.astype(jnp.int32)
                words[x, :, at] = (value[:half] << 16) | (value[half:] & 65535)
        for rim, t in enumerate((0, LANES, atoms - 2 * LANES, atoms - LANES)):
            rims[rim] = newq[:, :, pl.ds(t, LANES)]

    return pl.pallas_call(
        kernel,
        out_shape=(
            jax.ShapeDtypeStruct((3, beads, atoms), jnp.float32),
            jax.ShapeDtypeStruct((3, half, atoms), jnp.int32),
            jax.ShapeDtypeStruct((3, beads, atoms), jnp.float32),
            jax.ShapeDtypeStruct((beads, LANES), jnp.float32),
            jax.ShapeDtypeStruct((4, 3, beads, LANES), jnp.float32),
        ),
        in_specs=[whole_vmem()],
        out_specs=(whole_vmem(),) * 5,
        compiler_params=params(),
        name="assemble",
    )(fields)


def pair_part(words, fixed, unit, lists, begin, end, edges=()):
    _, beads, atoms = fixed.shape
    half = beads // 2
    tiles = atoms // LANES
    entries = lists.shape[0]

    def kernel(words_ref, fixed_ref, unit_ref, list_ref, *rest):
        ends = rest[: len(edges)]
        pair, sums = rest[len(edges)], rest[-1]
        unit_row = unit_ref[...]
        unit_square = on_sublanes(unit_ref[pl.ds(0, 1), :])
        unit_square = unit_square * unit_square

        def edge(out, at, base, near_tiles):
            for e in range(0, entries, 8):
                lane, low, high = entries_of(list_ref, e, base)
                for b in range(beads):
                    apart = []
                    for x in range(3):
                        windows = [on_sublanes(tile[x, pl.ds(b, 1), :]) for tile in near_tiles]
                        apart.append(banded(windows, lane, low, high) - windows[1])
                    square = apart[0] * apart[0] + apart[1] * apart[1] + apart[2] * apart[2]
                    add_pairs(sums, e, b, apart, inverse_of(1.0 + square))
            for x in range(3):
                out[x, :, pl.ds(at, LANES)] = PAIR_STRENGTH * total_of(sums, x)

        @pl.loop(max(begin, 1), min(end, tiles - 1))
        def _(t):
            base = pl.multiple_of(t * LANES, LANES)

            def row(ref, x, b, v):
                return on_sublanes(ref[x, pl.ds(b, 1), pl.ds(base + (v - 1) * LANES, LANES)])

            for e in range(0, entries, 8):
                lane, low, high = entries_of(list_ref, e, base)
                for b in range(half):
                    both = [
                        banded([row(words_ref, x, b, v) for v in range(3)], lane, low, high)
                        for x in range(3)
                    ]
                    for bead, near in ((b, [w & -65536 for w in both]),
                                       (b + half, [w << 16 for w in both])):
                        apart = [
                            near[x].astype(jnp.float32) - row(fixed_ref, x, bead, 1)
                            for x in range(3)
                        ]
                        square = apart[0] * apart[0] + apart[1] * apart[1] + apart[2] * apart[2]
                        close = inverse_of(1.0 + square * unit_square)
                        add_pairs(sums, e, bead, apart, close)
            at = pl.ds(pl.multiple_of((t - begin) * LANES, LANES), LANES)
            for x in range(3):
                pair[x, :, at] = (PAIR_STRENGTH * unit_row) * total_of(sums, x)

        if edges:
            rims, lower, upper = ends
            last = (tiles - 1) * LANES
            edge(rest[len(edges) + 1], 0, 0, [lower, rims.at[0], rims.at[1]])
            edge(pair, last - begin * LANES, last, [rims.at[2], rims.at[3], upper])

    out_shape = [jax.ShapeDtypeStruct((3, beads, (end - begin) * LANES), jnp.float32)]
    if edges:
        out_shape.append(jax.ShapeDtypeStruct((3, beads, LANES), jnp.float32))
    return pl.pallas_call(
        kernel,
        out_shape=out_shape,
        in_specs=[whole_vmem()] * (4 + len(edges)),
        out_specs=[whole_vmem()] * len(out_shape),
        scratch_shapes=[pltpu.VMEM((3, beads, 8, LANES), jnp.float32)],
        compiler_params=params(),
        cost_estimate=pl.CostEstimate(
            flops=300_000_000 * (end - begin), bytes_accessed=2_000_000, transcendentals=0
        ),
        name=f"pair_{begin}",
    )(words, fixed, unit, lists, *edges)


def finish(place, pairs, first, fields, neural_parts, partners, coefs):
    groups, _, beads, size = fields[0].shape
    rows = size * len(fields)
    atoms = groups * rows
    counts = [part.shape[0] for part in neural_parts]

    def kernel(place_ref, first_ref, coef_ref, *rest):
        halves, rest = rest[: len(pairs)], rest[len(pairs) :]
        ins, rest = rest[: len(fields)], rest[len(fields) :]
        blocks, (newp, newf) = rest[: len(counts)], rest[len(counts) :]
        own = place_ref[0]
        at = 0
        for half in halves:
            newf[:, :, pl.ds(at, half.shape[2])] = half[...]
            at += half.shape[2]
        newf[:, :, pl.ds(0, LANES)] = first_ref[...]
        coef = [coef_ref[c, own] for c in range(NC)]
        blocks = [block.at[i] for block, count in zip(blocks, counts) for i in range(count)]
        for r, block in zip(partners, blocks):
            g = own ^ r
            for t in range(0, rows, LANES):
                at = pl.ds(pl.multiple_of(g * rows + t, LANES), LANES)
                moved = ins[t // size].at[g, :, :, pl.ds(t % size, LANES)]
                for x in range(3):
                    force = newf[x, :, at]
                    for c in range(NC):
                        force = force + coef[c] * block[x, pl.ds(c, 1), pl.ds(t, LANES)]
                    newf[x, :, at] = force
                    newp[x, :, at] = moved[3 + x] + 0.5 * TIME_STEP * force

    out = jax.ShapeDtypeStruct((3, beads, atoms), jnp.float32)
    return pl.pallas_call(
        kernel,
        out_shape=(out,) * 2,
        in_specs=[smem()]
        + [whole_vmem()] * (2 + len(pairs) + len(fields) + len(neural_parts)),
        out_specs=(whole_vmem(),) * 2,
        compiler_params=params(),
        name="finish",
    )(place, first, coefs, *pairs, *fields, *neural_parts)


def doubling_step(have, partners, axis, bit):
    count = lax.axis_size(axis)
    got = lax.ppermute(have, axis, [(i, i ^ bit) for i in range(count)])
    return got, partners + [r ^ bit for r in partners]


def body(
    positions,
    momenta,
    force_old,
    noise,
    mass,
    pair_list,
    desc_w,
    hidden_one,
    hidden_two,
    hidden_three,
    out_w,
):
    beads, _, atoms = positions.shape
    groups = lax.axis_size("bead")
    slabs = lax.axis_size(("slab", "grp"))
    rows = atoms // groups
    place = lax.axis_index("bead").astype(jnp.int32)[None]
    step, kernel = step_tables()

    swap = lambda field: jnp.transpose(field, (1, 0, 2))
    sends = pack(place, swap(positions), swap(momenta), swap(force_old), swap(noise), groups)
    received = exchange(sends, "bead")

    lists, block_lists, masses, env_w, w1 = prepare(
        pair_list.T, mass[None, :], desc_w.T, hidden_one.T, place, rows
    )
    received, lists, block_lists, masses, env_w, w1 = lax.optimization_barrier(
        (received, lists, block_lists, masses, env_w, w1)
    )
    weights = (env_w, w1, hidden_two, hidden_three, out_w.T)

    contracted, first, last, scaled = contract(place, received, masses, jnp.asarray(step[:NC]))
    ring = [
        (g * slabs + s, ((g + 1) % groups) * slabs + (s + (g + 1) // groups) % slabs)
        for g in range(groups)
        for s in range(slabs)
    ]
    back = [(j, i) for i, j in ring]
    every = ("bead", "slab", "grp")
    lower = lax.ppermute(last, every, ring)
    upper = lax.ppermute(first, every, back)
    returns = transform(scaled, masses, jnp.asarray(step[NC:]))
    returns, lower, upper = lax.optimization_barrier((returns, lower, upper))
    fields = lax.all_to_all(returns, "bead", split_axis=0, concat_axis=0, tiled=True)

    forces = neural(contracted, lower, upper, block_lists, weights)
    bits = [1 << i for i in range(groups.bit_length() - 2, -1, -1)]
    have = forces[None]
    got, partners = doubling_step(have, [0], "bead", bits[0])
    fields, forces = lax.optimization_barrier((fields, forces))

    new_q, words, fixed, unit, rims = assemble(fields)
    slab_ring = [(s, (s + 1) % slabs) for s in range(slabs)]
    slab_back = [(j, i) for i, j in slab_ring]
    q_lower = lax.ppermute(rims[3], ("slab", "grp"), slab_ring)
    q_upper = lax.ppermute(rims[0], ("slab", "grp"), slab_back)

    words, got = lax.optimization_barrier((words, got))
    tiles = atoms // LANES
    cut = 3 * tiles // 8
    for bit in bits[1:2]:
        have = jnp.concatenate([have, got], axis=0)
        got, partners = doubling_step(have, partners, "bead", bit)
    pairs = pair_part(words, fixed, unit, lists, 0, cut)
    words, pairs, got = lax.optimization_barrier((words, pairs, got))
    for bit in bits[2:]:
        have = jnp.concatenate([have, got], axis=0)
        got, partners = doubling_step(have, partners, "bead", bit)
    rest, first = pair_part(
        words, fixed, unit, lists, cut, tiles, (rims, q_lower, q_upper)
    )

    coefs = (kernel * np.float32(BEADS / NC)).reshape(NC, groups, beads, 1)
    coefs = jnp.asarray(np.broadcast_to(coefs, (NC, groups, beads, LANES)))
    new_p, force = finish(
        place, [*pairs, rest], first, [fields], (have, got), partners, coefs
    )
    return tuple(swap(out) for out in (new_q, new_p, force))


def solution(mesh):
    field = P("bead", None, ("slab", "grp"))
    placed = (field,) * 4 + (P(("slab", "grp")), P(("slab", "grp"), None)) + (P(),) * 5
    return jax.shard_map(
        body, mesh=mesh, in_specs=placed, out_specs=(field,) * 3, check_vma=False
    )
```

```python
import math

import jax
import jax.numpy as jnp
import numpy as np
from jax import lax
from jax.experimental import pallas as pl
from jax.experimental.pallas import tpu as pltpu
from jax.sharding import PartitionSpec as P

BEADS = 64
NC = 8
EDGE = 128
LANES = 128

TIME_STEP = 0.1
CYCLE_FREQ = 5.0
CENTROID_FRICTION = 1.0
PAIR_STRENGTH = 0.5

BEST = lax.Precision.HIGHEST


def step_tables():
    b = np.arange(BEADS, dtype=np.float64)
    k = np.arange(BEADS)
    angle = 2.0 * np.pi * ((b[:, None] * b[None, :]) % BEADS) / BEADS
    half = BEADS // 2
    basis = np.where(
        k == 0,
        1.0 / math.sqrt(BEADS),
        np.where(
            k < half,
            math.sqrt(2.0 / BEADS) * np.cos(angle),
            np.where(
                k == half, np.cos(angle) / math.sqrt(BEADS), math.sqrt(2.0 / BEADS) * np.sin(angle)
            ),
        ),
    )
    freq = 2.0 * CYCLE_FREQ * np.sin(np.pi * b / BEADS)
    spacing = b[None, :] / BEADS - np.arange(NC, dtype=np.float64)[:, None] / NC
    kernel = np.ones_like(spacing)
    for order in range(1, NC // 2):
        kernel = kernel + 2.0 * np.cos(2.0 * np.pi * order * spacing)
    kernel = kernel + np.cos(np.pi * NC * spacing)
    contract = kernel / BEADS

    h = 0.5 * TIME_STEP
    safe = np.where(freq > 0.0, freq, 1.0)
    qq = np.where(freq > 0.0, np.cos(safe * h), 1.0)
    qp = np.where(freq > 0.0, np.sin(safe * h) / safe, h)
    pq = np.where(freq > 0.0, -safe * np.sin(safe * h), 0.0)
    pp = qq
    keep = np.exp(-np.where(freq > 0.0, 2.0 * freq, CENTROID_FRICTION) * TIME_STEP)
    kick = np.sqrt(1.0 - keep * keep)
    full_qq = qq * qq + qp * keep * pq
    full_qp = qq * qp + qp * keep * pp
    full_qn = qp * kick
    full_pq = pq * qq + pp * keep * pq
    full_pp = pq * qp + pp * keep * pp
    full_pn = pp * kick
    q_rows = np.concatenate(
        [(basis * full_qq) @ basis.T, (basis * full_qp) @ basis.T, basis * full_qn], axis=1
    )
    p_rows = np.concatenate(
        [(basis * full_pq) @ basis.T, (basis * full_pp) @ basis.T, basis * full_pn], axis=1
    )
    c_rows = contract @ q_rows
    step = np.concatenate([c_rows, q_rows, p_rows], axis=0)
    return step.astype(np.float32), contract.astype(np.float32)


def whole_vmem():
    return pl.BlockSpec(memory_space=pltpu.VMEM)


def params(mebibytes=48):
    return pltpu.CompilerParams(vmem_limit_bytes=mebibytes * 1024 * 1024)


def smem():
    return pl.BlockSpec(memory_space=pltpu.SMEM)


def block_of(place_ref, r, rows):
    return pl.ds(pl.multiple_of((place_ref[0] ^ r) * rows, LANES), rows)


def exchange(blocks, axis):
    count = len(blocks)
    return [blocks[0]] + [
        lax.ppermute(blocks[r], axis, [(i, i ^ r) for i in range(count)]) for r in range(1, count)
    ]


def pack(place, positions, momenta, force_old, noise, groups):
    _, beads, atoms = positions.shape
    rows = atoms // groups

    def kernel(place_ref, q_ref, p_ref, f_ref, n_ref, *rest):
        outs, (blocks, kicks, loaded, stored) = rest[:groups], rest[groups:]
        loads = []
        for r in range(groups):
            at = block_of(place_ref, r, rows)
            targets = [blocks.at[r, pl.ds(first, 3)] for first in (0, 3, 6)] + [kicks.at[r]]
            loads.append(
                [
                    pltpu.make_async_copy(ref.at[:, :, at], target, loaded.at[4 * r + i])
                    for i, (ref, target) in enumerate(zip((q_ref, p_ref, n_ref, f_ref), targets))
                ]
            )
            for load in loads[r]:
                load.start()
        stores = []
        for r in range(groups):
            for load in loads[r]:
                load.wait()
            for x in range(3):
                blocks[r, 3 + x] = blocks[r, 3 + x] + 0.5 * TIME_STEP * kicks[r, x]
            stores.append(pltpu.make_async_copy(blocks.at[r], outs[r], stored.at[r]))
            stores[r].start()
        for store in stores:
            store.wait()

    hbm = pl.BlockSpec(memory_space=pltpu.HBM)
    return pl.pallas_call(
        kernel,
        out_shape=[jax.ShapeDtypeStruct((9, beads, rows), jnp.float32)] * groups,
        in_specs=[smem()] + [hbm] * 4,
        out_specs=[hbm] * groups,
        scratch_shapes=[
            pltpu.VMEM((groups, 9, beads, rows), jnp.float32),
            pltpu.VMEM((groups, 3, beads, rows), jnp.float32),
            pltpu.SemaphoreType.DMA((4 * groups,)),
            pltpu.SemaphoreType.DMA((groups,)),
        ],
        compiler_params=params(60),
        name="pack",
    )(place, positions, momenta, force_old, noise)


def prepare(pair_list, mass, desc_w, hidden_one, place, rows):
    entries, atoms = pair_list.shape
    desc, env = desc_w.shape
    hid = hidden_one.shape[0]
    order = np.arange(env)
    order = (order % entries) * (env // entries) + order // entries
    permute = jnp.asarray(np.eye(env)[order], jnp.bfloat16)

    def kernel(place_ref, list_ref, mass_ref, w0_ref, w1_ref, order_ref, lists, own, masses, w0, w1):
        for t in range(atoms // LANES):
            at = pl.ds(t * LANES, LANES)
            lists[:, at] = list_ref[:, at] - t * LANES
        block = pl.ds(pl.multiple_of(place_ref[0] * rows, LANES), rows)
        own[...] = lists[:, block]
        masses[...] = mass_ref[:, block]
        w0[...] = lax.dot_general(
            order_ref[...],
            w0_ref[...],
            (((1,), (1,)), ((), ())),
            preferred_element_type=jnp.float32,
        ).astype(w0.dtype)
        w1[...] = w1_ref[...].astype(jnp.float32).T.astype(w1.dtype)

    return pl.pallas_call(
        kernel,
        out_shape=(
            jax.ShapeDtypeStruct((entries, atoms), jnp.int32),
            jax.ShapeDtypeStruct((entries, rows), jnp.int32),
            jax.ShapeDtypeStruct((1, rows), jnp.float32),
            jax.ShapeDtypeStruct((env, desc), jnp.bfloat16),
            jax.ShapeDtypeStruct((desc, hid), jnp.bfloat16),
        ),
        in_specs=[pl.BlockSpec(memory_space=pltpu.SMEM)] + [whole_vmem()] * 5,
        out_specs=(whole_vmem(),) * 5,
        compiler_params=params(),
        cost_estimate=pl.CostEstimate(
            flops=1_000_000_000, bytes_accessed=4_000_000, transcendentals=0
        ),
        name="prepare",
    )(place, pair_list, mass, desc_w, hidden_one, permute)


def contract(place, received, masses, table):
    groups = len(received)
    _, beads, rows = received[0].shape

    def kernel(place_ref, mass_ref, table_ref, own_ref, *rest):
        ins, (c_ref, first, last, fields, own, sem) = rest[: groups - 1], rest[groups - 1 :]

        load = pltpu.make_async_copy(own_ref, own, sem)
        load.start()
        mass = mass_ref[...]
        inverse = 1.0 / mass
        root = lax.rsqrt(mass)

        def scale(g, block):
            for x in range(3):
                fields[x, 0, g] = block[x]
                fields[x, 1, g] = block[3 + x] * inverse
                fields[x, 2, g] = block[6 + x] * root

        for r in range(1, groups):
            scale(place_ref[0] ^ r, ins[r - 1])
        load.wait()
        scale(place_ref[0], own)
        for x in range(3):
            out = jnp.dot(
                table_ref[...],
                fields[x].reshape(3 * BEADS, rows),
                precision=BEST,
                preferred_element_type=jnp.float32,
            )
            c_ref[x] = out
            first[x] = out[:, :EDGE]
            last[x] = out[:, rows - EDGE :]

    edge = jax.ShapeDtypeStruct((3, NC, EDGE), jnp.float32)
    return pl.pallas_call(
        kernel,
        out_shape=(
            jax.ShapeDtypeStruct((3, NC, rows), jnp.float32),
            edge,
            edge,
            jax.ShapeDtypeStruct((3, 3, groups, beads, rows), jnp.float32),
        ),
        in_specs=[smem()]
        + [whole_vmem()] * 2
        + [pl.BlockSpec(memory_space=pltpu.HBM)]
        + [whole_vmem()] * (groups - 1),
        out_specs=(whole_vmem(),) * 4,
        scratch_shapes=[pltpu.VMEM((9, beads, rows), jnp.float32), pltpu.SemaphoreType.DMA],
        compiler_params=params(),
        name="contract",
    )(place, masses, table, *received)


def transform(fields, masses, table):
    _, _, groups, beads, rows = fields.shape

    def kernel(fields_ref, mass_ref, table_ref, out_ref, news, sems):
        mass = mass_ref[...]
        copies = []
        for x in range(3):
            out = jnp.dot(
                table_ref[...],
                fields_ref[x].reshape(3 * BEADS, rows),
                precision=BEST,
                preferred_element_type=jnp.float32,
            )
            news[x] = out[:BEADS].reshape(groups, beads, rows)
            news[3 + x] = (out[BEADS:] * mass).reshape(groups, beads, rows)
            for row in (x, 3 + x):
                copy = pltpu.make_async_copy(news.at[row], out_ref.at[:, row], sems.at[row])
                copy.start()
                copies.append(copy)
        for copy in copies:
            copy.wait()

    return pl.pallas_call(
        kernel,
        out_shape=jax.ShapeDtypeStruct((groups, 6, beads, rows), jnp.float32),
        in_specs=[whole_vmem()] * 3,
        out_specs=pl.BlockSpec(memory_space=pltpu.HBM),
        scratch_shapes=[
            pltpu.VMEM((6, groups, beads, rows), jnp.float32),
            pltpu.SemaphoreType.DMA((6,)),
        ],
        compiler_params=params(),
        cost_estimate=pl.CostEstimate(
            flops=1_000_000_000, bytes_accessed=2_000_000, transcendentals=0
        ),
        name="transform",
    )(fields, masses, table)


def inverse_of(value):
    estimate = pl.reciprocal(value, approx=True)
    return estimate * (2.0 - value * estimate)


def banded(windows, lane, low, high):
    below, middle, above = [
        jnp.take_along_axis(w, lane, axis=1, mode="promise_in_bounds") for w in windows
    ]
    return jnp.where(low, below, jnp.where(high, above, middle))


def entries_of(list_ref, e, base):
    place = list_ref[pl.ds(e, 8), pl.ds(base, LANES)]
    return place & (LANES - 1), place < LANES, place >= 2 * LANES


def on_sublanes(row):
    return jnp.broadcast_to(row, (8, LANES))


def env_units(windows, list_ref, base, envs, inputs):
    entries = list_ref.shape[0]
    for e in range(0, entries, 8):
        lane, low, high = entries_of(list_ref, e, base)
        for c in range(NC):
            apart = []
            for x in range(3):
                tiles = windows(c, x)
                apart.append(banded(tiles, lane, low, high) - tiles[1])
            square = apart[0] * apart[0] + apart[1] * apart[1] + apart[2] * apart[2]
            close = inverse_of(1.0 + square)
            for x, value in enumerate(apart + [close]):
                envs[pl.ds(x * entries + e, 8), pl.ds(c * LANES, LANES)] = value
            yield
    for c in range(NC):
        at = pl.ds(c * LANES, LANES)
        inputs[at, :] = envs[:, at].T.astype(jnp.bfloat16)
        yield


def network(inputs_ref, weights, out_ref, base, units, chunk=256):
    w0_ref, w1_ref, w2_ref, w3_ref, wo_ref = weights
    desc = w0_ref.shape[1]
    inputs = inputs_ref[...]
    total = None
    for f in range(0, desc, chunk):
        size = min(chunk, desc - f)
        first = jnp.dot(inputs, w0_ref[:, pl.ds(f, size)], preferred_element_type=jnp.float32)
        first = jnp.tanh(first.astype(jnp.bfloat16))
        part = jnp.dot(first, w1_ref[pl.ds(f, size), :], preferred_element_type=jnp.float32)
        total = part if total is None else total + part
        for _ in range(6):
            next(units, None)
    layer = jnp.tanh(total).astype(jnp.bfloat16)
    for ref in (w2_ref, w3_ref):
        layer = jnp.tanh(jnp.dot(layer, ref[...], preferred_element_type=jnp.float32)).astype(
            jnp.bfloat16
        )
    out = lax.dot_general(
        wo_ref[...], layer, (((1,), (1,)), ((), ())), preferred_element_type=jnp.float32
    )
    for c in range(NC):
        for x in range(3):
            out_ref[x, pl.ds(c, 1), pl.ds(base, LANES)] = out[
                x : x + 1, c * LANES : (c + 1) * LANES
            ]


def neural_scratch(env):
    return [
        pltpu.VMEM((2, env, NC * LANES), jnp.float32),
        pltpu.VMEM((2, NC * LANES, env), jnp.bfloat16),
    ]


def neural(contracted, lower, upper, lists, weights):
    _, _, rows = contracted.shape
    tiles = rows // LANES

    def kernel(
        c_ref, low_ref, up_ref, list_ref, w0, w1, w2, w3, wo, out_ref, envs, inputs
    ):
        def tile(x, c, t):
            if t < 0:
                ref, at = low_ref, 0
            elif t >= tiles:
                ref, at = up_ref, 0
            else:
                ref, at = c_ref, t * LANES
            return on_sublanes(ref[x, pl.ds(c, 1), pl.ds(at, LANES)])

        def units_of(t):
            if t >= tiles:
                return iter(())
            windows = lambda c, x: [tile(x, c, t + v) for v in (-1, 0, 1)]
            slot = t % 2
            return env_units(windows, list_ref, t * LANES, envs.at[slot], inputs.at[slot])

        for _ in units_of(0):
            pass
        for t in range(tiles):
            units = units_of(t + 1)
            network(inputs.at[t % 2], (w0, w1, w2, w3, wo), out_ref, t * LANES, units)
            for _ in units:
                pass

    return pl.pallas_call(
        kernel,
        out_shape=jax.ShapeDtypeStruct((3, NC, rows), jnp.float32),
        in_specs=[whole_vmem()] * 9,
        out_specs=whole_vmem(),
        scratch_shapes=neural_scratch(weights[0].shape[0]),
        compiler_params=params(),
        cost_estimate=pl.CostEstimate(
            flops=12_000_000_000, bytes_accessed=4_000_000, transcendentals=0
        ),
        name="neural",
    )(contracted, lower, upper, lists, *weights)


def add_pairs(sums, e, b, apart, close):
    for x in range(3):
        part = apart[x] * close
        sums[x, b] = part if e == 0 else sums[x, b] + part


def total_of(sums, x):
    total = sums[x, :, 0, :]
    for s in range(1, 8):
        total = total + sums[x, :, s, :]
    return total


def assemble(fields):
    groups, _, beads, rows = fields.shape
    atoms = groups * rows
    half = beads // 2
    top = float(2**15 - 1)

    def kernel(in_ref, newq, words, fixed, unit_ref, rims):
        largest = jnp.zeros((beads, rows), jnp.float32)
        for g in range(groups):
            at = pl.ds(g * rows, rows)
            for x in range(3):
                value = in_ref[g, x]
                newq[x, :, at] = value
                largest = jnp.maximum(largest, jnp.abs(value))
        limit = jnp.maximum(jnp.max(largest, keepdims=True), 1e-30)
        to_fixed = top / limit
        unit_ref[...] = jnp.broadcast_to(limit / (top * 65536.0), (beads, LANES))
        for g in range(groups):
            at = pl.ds(g * rows, rows)
            for x in range(3):
                value = jnp.floor(in_ref[g, x] * to_fixed + 0.5)
                fixed[x, :, at] = value * 65536.0
                value = value.astype(jnp.int32)
                words[x, :, at] = (value[:half] << 16) | (value[half:] & 65535)
        for rim, t in enumerate((0, LANES, atoms - 2 * LANES, atoms - LANES)):
            rims[rim] = newq[:, :, pl.ds(t, LANES)]

    return pl.pallas_call(
        kernel,
        out_shape=(
            jax.ShapeDtypeStruct((3, beads, atoms), jnp.float32),
            jax.ShapeDtypeStruct((3, half, atoms), jnp.int32),
            jax.ShapeDtypeStruct((3, beads, atoms), jnp.float32),
            jax.ShapeDtypeStruct((beads, LANES), jnp.float32),
            jax.ShapeDtypeStruct((4, 3, beads, LANES), jnp.float32),
        ),
        in_specs=[whole_vmem()],
        out_specs=(whole_vmem(),) * 5,
        compiler_params=params(),
        name="assemble",
    )(fields)


def pair_part(words, fixed, unit, lists, begin, end, edges=()):
    _, beads, atoms = fixed.shape
    half = beads // 2
    tiles = atoms // LANES
    entries = lists.shape[0]

    def kernel(words_ref, fixed_ref, unit_ref, list_ref, *rest):
        ends = rest[: len(edges)]
        pair, sums = rest[len(edges)], rest[-1]
        unit_row = unit_ref[...]
        unit_square = on_sublanes(unit_ref[pl.ds(0, 1), :])
        unit_square = unit_square * unit_square

        def edge(out, at, base, near_tiles):
            for e in range(0, entries, 8):
                lane, low, high = entries_of(list_ref, e, base)
                for b in range(beads):
                    apart = []
                    for x in range(3):
                        windows = [on_sublanes(tile[x, pl.ds(b, 1), :]) for tile in near_tiles]
                        apart.append(banded(windows, lane, low, high) - windows[1])
                    square = apart[0] * apart[0] + apart[1] * apart[1] + apart[2] * apart[2]
                    add_pairs(sums, e, b, apart, inverse_of(1.0 + square))
            for x in range(3):
                out[x, :, pl.ds(at, LANES)] = PAIR_STRENGTH * total_of(sums, x)

        @pl.loop(max(begin, 1), min(end, tiles - 1))
        def _(t):
            base = pl.multiple_of(t * LANES, LANES)

            def row(ref, x, b, v):
                return on_sublanes(ref[x, pl.ds(b, 1), pl.ds(base + (v - 1) * LANES, LANES)])

            for e in range(0, entries, 8):
                lane, low, high = entries_of(list_ref, e, base)
                for b in range(half):
                    both = [
                        banded([row(words_ref, x, b, v) for v in range(3)], lane, low, high)
                        for x in range(3)
                    ]
                    for bead, near in ((b, [w & -65536 for w in both]),
                                       (b + half, [w << 16 for w in both])):
                        apart = [
                            near[x].astype(jnp.float32) - row(fixed_ref, x, bead, 1)
                            for x in range(3)
                        ]
                        square = apart[0] * apart[0] + apart[1] * apart[1] + apart[2] * apart[2]
                        close = inverse_of(1.0 + square * unit_square)
                        add_pairs(sums, e, bead, apart, close)
            at = pl.ds(pl.multiple_of((t - begin) * LANES, LANES), LANES)
            for x in range(3):
                pair[x, :, at] = (PAIR_STRENGTH * unit_row) * total_of(sums, x)

        if edges:
            rims, lower, upper = ends
            last = (tiles - 1) * LANES
            edge(rest[len(edges) + 1], 0, 0, [lower, rims.at[0], rims.at[1]])
            edge(pair, last - begin * LANES, last, [rims.at[2], rims.at[3], upper])

    out_shape = [jax.ShapeDtypeStruct((3, beads, (end - begin) * LANES), jnp.float32)]
    if edges:
        out_shape.append(jax.ShapeDtypeStruct((3, beads, LANES), jnp.float32))
    return pl.pallas_call(
        kernel,
        out_shape=out_shape,
        in_specs=[whole_vmem()] * (4 + len(edges)),
        out_specs=[whole_vmem()] * len(out_shape),
        scratch_shapes=[pltpu.VMEM((3, beads, 8, LANES), jnp.float32)],
        compiler_params=params(),
        cost_estimate=pl.CostEstimate(
            flops=300_000_000 * (end - begin), bytes_accessed=2_000_000, transcendentals=0
        ),
        name=f"pair_{begin}",
    )(words, fixed, unit, lists, *edges)


def finish(place, pairs, first, fields, neural_parts, partners, coefs):
    groups, _, beads, rows = fields.shape
    atoms = groups * rows
    counts = [part.shape[0] for part in neural_parts]

    def kernel(place_ref, first_ref, coef_ref, in_ref, *rest):
        halves, rest = rest[: len(pairs)], rest[len(pairs) :]
        blocks, (newp, newf, pair, momenta, forces, sems) = rest[: len(counts)], rest[len(counts) :]
        own = place_ref[0]
        at = 0
        for half in halves:
            pair[:, :, pl.ds(at, half.shape[2])] = half[...]
            at += half.shape[2]
        pair[:, :, pl.ds(0, LANES)] = first_ref[...]
        coef = [coef_ref[c, own] for c in range(NC)]
        blocks = [block.at[i] for block, count in zip(blocks, counts) for i in range(count)]
        copies = []
        for slot, (r, block) in enumerate(zip(partners, blocks)):
            g = own ^ r
            for t in range(0, rows, LANES):
                at = pl.ds(pl.multiple_of(g * rows + t, LANES), LANES)
                inner = pl.ds(t, LANES)
                for x in range(3):
                    force = pair[x, :, at]
                    for c in range(NC):
                        force = force + coef[c] * block[x, pl.ds(c, 1), inner]
                    forces[slot, x, :, inner] = force
                    momenta[slot, x, :, inner] = in_ref[g, 3 + x, :, inner] + 0.5 * TIME_STEP * force
            at = block_of(place_ref, r, rows)
            for i, (source, out) in enumerate(((forces, newf), (momenta, newp))):
                copy = pltpu.make_async_copy(
                    source.at[slot], out.at[:, :, at], sems.at[2 * slot + i]
                )
                copy.start()
                copies.append(copy)
        for copy in copies:
            copy.wait()

    out = jax.ShapeDtypeStruct((3, beads, atoms), jnp.float32)
    return pl.pallas_call(
        kernel,
        out_shape=(out,) * 2,
        in_specs=[smem()] + [whole_vmem()] * (3 + len(pairs) + len(neural_parts)),
        out_specs=(pl.BlockSpec(memory_space=pltpu.HBM),) * 2,
        scratch_shapes=[
            pltpu.VMEM((3, beads, atoms), jnp.float32),
            pltpu.VMEM((groups, 3, beads, rows), jnp.float32),
            pltpu.VMEM((groups, 3, beads, rows), jnp.float32),
            pltpu.SemaphoreType.DMA((2 * groups,)),
        ],
        compiler_params=params(),
        name="finish",
    )(place, first, coefs, fields, *pairs, *neural_parts)


def doubling_step(have, partners, axis, bit):
    count = lax.axis_size(axis)
    got = lax.ppermute(have, axis, [(i, i ^ bit) for i in range(count)])
    return got, partners + [r ^ bit for r in partners]


def body(
    positions,
    momenta,
    force_old,
    noise,
    mass,
    pair_list,
    desc_w,
    hidden_one,
    hidden_two,
    hidden_three,
    out_w,
):
    beads, _, atoms = positions.shape
    groups = lax.axis_size("bead")
    slabs = lax.axis_size(("slab", "grp"))
    rows = atoms // groups
    place = lax.axis_index("bead").astype(jnp.int32)[None]
    step, kernel = step_tables()

    swap = lambda field: jnp.transpose(field, (1, 0, 2))
    sends = pack(place, swap(positions), swap(momenta), swap(force_old), swap(noise), groups)
    received = exchange(sends, "bead")

    lists, block_lists, masses, env_w, w1 = prepare(
        pair_list.T, mass[None, :], desc_w.T, hidden_one.T, place, rows
    )
    received, lists, block_lists, masses, env_w, w1 = lax.optimization_barrier(
        (received, lists, block_lists, masses, env_w, w1)
    )
    weights = (env_w, w1, hidden_two, hidden_three, out_w.T)

    contracted, first, last, scaled = contract(place, received, masses, jnp.asarray(step[:NC]))
    ring = [
        (g * slabs + s, ((g + 1) % groups) * slabs + (s + (g + 1) // groups) % slabs)
        for g in range(groups)
        for s in range(slabs)
    ]
    back = [(j, i) for i, j in ring]
    every = ("bead", "slab", "grp")
    lower = lax.ppermute(last, every, ring)
    upper = lax.ppermute(first, every, back)
    returns = transform(scaled, masses, jnp.asarray(step[NC:]))
    returns, lower, upper = lax.optimization_barrier((returns, lower, upper))
    fields = lax.all_to_all(returns, "bead", split_axis=0, concat_axis=0, tiled=True)

    forces = neural(contracted, lower, upper, block_lists, weights)
    bits = [1 << i for i in range(groups.bit_length() - 2, -1, -1)]
    have = forces[None]
    got, partners = doubling_step(have, [0], "bead", bits[0])
    fields, forces = lax.optimization_barrier((fields, forces))

    new_q, words, fixed, unit, rims = assemble(fields)
    slab_ring = [(s, (s + 1) % slabs) for s in range(slabs)]
    slab_back = [(j, i) for i, j in slab_ring]
    q_lower = lax.ppermute(rims[3], ("slab", "grp"), slab_ring)
    q_upper = lax.ppermute(rims[0], ("slab", "grp"), slab_back)

    words, got = lax.optimization_barrier((words, got))
    tiles = atoms // LANES
    cut = 3 * tiles // 8
    for bit in bits[1:2]:
        have = jnp.concatenate([have, got], axis=0)
        got, partners = doubling_step(have, partners, "bead", bit)
    pairs = pair_part(words, fixed, unit, lists, 0, cut)
    words, pairs, got = lax.optimization_barrier((words, pairs, got))
    for bit in bits[2:]:
        have = jnp.concatenate([have, got], axis=0)
        got, partners = doubling_step(have, partners, "bead", bit)
    rest, first = pair_part(
        words, fixed, unit, lists, cut, tiles, (rims, q_lower, q_upper)
    )

    coefs = (kernel * np.float32(BEADS / NC)).reshape(NC, groups, beads, 1)
    coefs = jnp.asarray(np.broadcast_to(coefs, (NC, groups, beads, LANES)))
    new_p, force = finish(
        place, [*pairs, rest], first, fields, (have, got), partners, coefs
    )
    return tuple(swap(out) for out in (new_q, new_p, force))


def solution(mesh):
    field = P("bead", None, ("slab", "grp"))
    placed = (field,) * 4 + (P(("slab", "grp")), P(("slab", "grp"), None)) + (P(),) * 5
    return jax.shard_map(
        body, mesh=mesh, in_specs=placed, out_specs=(field,) * 3, check_vma=False
    )
```

```python
import math

import jax
import jax.numpy as jnp
import numpy as np
from jax import lax
from jax.experimental import pallas as pl
from jax.experimental.pallas import tpu as pltpu
from jax.sharding import PartitionSpec as P

BEADS = 64
NC = 8
EDGE = 128
LANES = 128

TIME_STEP = 0.1
CYCLE_FREQ = 5.0
CENTROID_FRICTION = 1.0
PAIR_STRENGTH = 0.5

BEST = lax.Precision.HIGHEST


def step_tables():
    b = np.arange(BEADS, dtype=np.float64)
    k = np.arange(BEADS)
    angle = 2.0 * np.pi * ((b[:, None] * b[None, :]) % BEADS) / BEADS
    half = BEADS // 2
    basis = np.where(
        k == 0,
        1.0 / math.sqrt(BEADS),
        np.where(
            k < half,
            math.sqrt(2.0 / BEADS) * np.cos(angle),
            np.where(
                k == half, np.cos(angle) / math.sqrt(BEADS), math.sqrt(2.0 / BEADS) * np.sin(angle)
            ),
        ),
    )
    freq = 2.0 * CYCLE_FREQ * np.sin(np.pi * b / BEADS)
    spacing = b[None, :] / BEADS - np.arange(NC, dtype=np.float64)[:, None] / NC
    kernel = np.ones_like(spacing)
    for order in range(1, NC // 2):
        kernel = kernel + 2.0 * np.cos(2.0 * np.pi * order * spacing)
    kernel = kernel + np.cos(np.pi * NC * spacing)
    contract = kernel / BEADS

    h = 0.5 * TIME_STEP
    safe = np.where(freq > 0.0, freq, 1.0)
    qq = np.where(freq > 0.0, np.cos(safe * h), 1.0)
    qp = np.where(freq > 0.0, np.sin(safe * h) / safe, h)
    pq = np.where(freq > 0.0, -safe * np.sin(safe * h), 0.0)
    pp = qq
    keep = np.exp(-np.where(freq > 0.0, 2.0 * freq, CENTROID_FRICTION) * TIME_STEP)
    kick = np.sqrt(1.0 - keep * keep)
    full_qq = qq * qq + qp * keep * pq
    full_qp = qq * qp + qp * keep * pp
    full_qn = qp * kick
    full_pq = pq * qq + pp * keep * pq
    full_pp = pq * qp + pp * keep * pp
    full_pn = pp * kick
    q_rows = np.concatenate(
        [(basis * full_qq) @ basis.T, (basis * full_qp) @ basis.T, basis * full_qn], axis=1
    )
    p_rows = np.concatenate(
        [(basis * full_pq) @ basis.T, (basis * full_pp) @ basis.T, basis * full_pn], axis=1
    )
    c_rows = contract @ q_rows
    step = np.concatenate([c_rows, q_rows, p_rows], axis=0)
    return step.astype(np.float32), contract.astype(np.float32)


def whole_vmem():
    return pl.BlockSpec(memory_space=pltpu.VMEM)


def params(mebibytes=48):
    return pltpu.CompilerParams(vmem_limit_bytes=mebibytes * 1024 * 1024)


def smem():
    return pl.BlockSpec(memory_space=pltpu.SMEM)


def block_of(place_ref, r, rows):
    return pl.ds(pl.multiple_of((place_ref[0] ^ r) * rows, LANES), rows)


def exchange(blocks, axis):
    count = len(blocks)
    return [blocks[0]] + [
        lax.ppermute(blocks[r], axis, [(i, i ^ r) for i in range(count)]) for r in range(1, count)
    ]


def pack(place, positions, momenta, force_old, noise, groups):
    _, beads, atoms = positions.shape
    rows = atoms // groups

    def kernel(place_ref, q_ref, p_ref, f_ref, n_ref, *rest):
        outs, (blocks, kicks, loaded, stored) = rest[:groups], rest[groups:]
        loads = []
        for r in range(groups):
            at = block_of(place_ref, r, rows)
            targets = [blocks.at[r, pl.ds(first, 3)] for first in (0, 3, 6)] + [kicks.at[r]]
            loads.append(
                [
                    pltpu.make_async_copy(ref.at[:, :, at], target, loaded.at[4 * r + i])
                    for i, (ref, target) in enumerate(zip((q_ref, p_ref, n_ref, f_ref), targets))
                ]
            )
            for load in loads[r]:
                load.start()
        stores = []
        for r in range(groups):
            for load in loads[r]:
                load.wait()
            for x in range(3):
                blocks[r, 3 + x] = blocks[r, 3 + x] + 0.5 * TIME_STEP * kicks[r, x]
            stores.append(pltpu.make_async_copy(blocks.at[r], outs[r], stored.at[r]))
            stores[r].start()
        for store in stores:
            store.wait()

    hbm = pl.BlockSpec(memory_space=pltpu.HBM)
    return pl.pallas_call(
        kernel,
        out_shape=[jax.ShapeDtypeStruct((9, beads, rows), jnp.float32)] * groups,
        in_specs=[smem()] + [hbm] * 4,
        out_specs=[hbm] * groups,
        scratch_shapes=[
            pltpu.VMEM((groups, 9, beads, rows), jnp.float32),
            pltpu.VMEM((groups, 3, beads, rows), jnp.float32),
            pltpu.SemaphoreType.DMA((4 * groups,)),
            pltpu.SemaphoreType.DMA((groups,)),
        ],
        compiler_params=params(60),
        name="pack",
    )(place, positions, momenta, force_old, noise)


def prepare(pair_list, mass, desc_w, hidden_one, place, rows):
    entries, atoms = pair_list.shape
    desc, env = desc_w.shape
    hid = hidden_one.shape[0]
    order = np.arange(env)
    order = (order % entries) * (env // entries) + order // entries
    permute = jnp.asarray(np.eye(env)[order], jnp.bfloat16)

    def kernel(place_ref, list_ref, mass_ref, w0_ref, w1_ref, order_ref, lists, own, masses, w0, w1):
        for t in range(atoms // LANES):
            at = pl.ds(t * LANES, LANES)
            lists[:, at] = list_ref[:, at] - t * LANES
        block = pl.ds(pl.multiple_of(place_ref[0] * rows, LANES), rows)
        own[...] = lists[:, block]
        masses[...] = mass_ref[:, block]
        w0[...] = lax.dot_general(
            order_ref[...],
            w0_ref[...],
            (((1,), (1,)), ((), ())),
            preferred_element_type=jnp.float32,
        ).astype(w0.dtype)
        w1[...] = w1_ref[...].astype(jnp.float32).T.astype(w1.dtype)

    return pl.pallas_call(
        kernel,
        out_shape=(
            jax.ShapeDtypeStruct((entries, atoms), jnp.int32),
            jax.ShapeDtypeStruct((entries, rows), jnp.int32),
            jax.ShapeDtypeStruct((1, rows), jnp.float32),
            jax.ShapeDtypeStruct((env, desc), jnp.bfloat16),
            jax.ShapeDtypeStruct((desc, hid), jnp.bfloat16),
        ),
        in_specs=[pl.BlockSpec(memory_space=pltpu.SMEM)] + [whole_vmem()] * 5,
        out_specs=(whole_vmem(),) * 5,
        compiler_params=params(),
        cost_estimate=pl.CostEstimate(
            flops=1_000_000_000, bytes_accessed=4_000_000, transcendentals=0
        ),
        name="prepare",
    )(place, pair_list, mass, desc_w, hidden_one, permute)


def contract(place, received, masses, table):
    groups = len(received)
    _, beads, rows = received[0].shape

    def kernel(place_ref, mass_ref, table_ref, own_ref, *rest):
        ins, (c_ref, first, last, fields, own, sem) = rest[: groups - 1], rest[groups - 1 :]

        load = pltpu.make_async_copy(own_ref, own, sem)
        load.start()
        mass = mass_ref[...]
        inverse = 1.0 / mass
        root = lax.rsqrt(mass)

        def scale(g, block):
            for x in range(3):
                fields[x, 0, g] = block[x]
                fields[x, 1, g] = block[3 + x] * inverse
                fields[x, 2, g] = block[6 + x] * root

        for r in range(1, groups):
            scale(place_ref[0] ^ r, ins[r - 1])
        load.wait()
        scale(place_ref[0], own)
        for x in range(3):
            out = jnp.dot(
                table_ref[...],
                fields[x].reshape(3 * BEADS, rows),
                precision=BEST,
                preferred_element_type=jnp.float32,
            )
            c_ref[x] = out
            first[x] = out[:, :EDGE]
            last[x] = out[:, rows - EDGE :]

    edge = jax.ShapeDtypeStruct((3, NC, EDGE), jnp.float32)
    return pl.pallas_call(
        kernel,
        out_shape=(
            jax.ShapeDtypeStruct((3, NC, rows), jnp.float32),
            edge,
            edge,
            jax.ShapeDtypeStruct((3, 3, groups, beads, rows), jnp.float32),
        ),
        in_specs=[smem()]
        + [whole_vmem()] * 2
        + [pl.BlockSpec(memory_space=pltpu.HBM)]
        + [whole_vmem()] * (groups - 1),
        out_specs=(whole_vmem(),) * 4,
        scratch_shapes=[pltpu.VMEM((9, beads, rows), jnp.float32), pltpu.SemaphoreType.DMA],
        compiler_params=params(),
        name="contract",
    )(place, masses, table, *received)


def transform(fields, masses, table):
    _, _, groups, beads, rows = fields.shape

    def kernel(fields_ref, mass_ref, table_ref, out_ref, news, sems):
        mass = mass_ref[...]
        copies = []
        for x in range(3):
            out = jnp.dot(
                table_ref[...],
                fields_ref[x].reshape(3 * BEADS, rows),
                precision=BEST,
                preferred_element_type=jnp.float32,
            )
            news[x] = out[:BEADS].reshape(groups, beads, rows)
            news[3 + x] = (out[BEADS:] * mass).reshape(groups, beads, rows)
            for row in (x, 3 + x):
                copy = pltpu.make_async_copy(news.at[row], out_ref.at[:, row], sems.at[row])
                copy.start()
                copies.append(copy)
        for copy in copies:
            copy.wait()

    return pl.pallas_call(
        kernel,
        out_shape=jax.ShapeDtypeStruct((groups, 6, beads, rows), jnp.float32),
        in_specs=[whole_vmem()] * 3,
        out_specs=pl.BlockSpec(memory_space=pltpu.HBM),
        scratch_shapes=[
            pltpu.VMEM((6, groups, beads, rows), jnp.float32),
            pltpu.SemaphoreType.DMA((6,)),
        ],
        compiler_params=params(),
        cost_estimate=pl.CostEstimate(
            flops=1_000_000_000, bytes_accessed=2_000_000, transcendentals=0
        ),
        name="transform",
    )(fields, masses, table)


def inverse_of(value):
    estimate = pl.reciprocal(value, approx=True)
    return estimate * (2.0 - value * estimate)


def banded(windows, lane, low, high):
    below, middle, above = [
        jnp.take_along_axis(w, lane, axis=1, mode="promise_in_bounds") for w in windows
    ]
    return jnp.where(low, below, jnp.where(high, above, middle))


def entries_of(list_ref, e, base):
    place = list_ref[pl.ds(e, 8), pl.ds(base, LANES)]
    return place & (LANES - 1), place < LANES, place >= 2 * LANES


def on_sublanes(row):
    return jnp.broadcast_to(row, (8, LANES))


def env_units(windows, list_ref, base, envs, inputs):
    entries = list_ref.shape[0]
    for e in range(0, entries, 8):
        lane, low, high = entries_of(list_ref, e, base)
        for c in range(NC):
            apart = []
            for x in range(3):
                tiles = windows(c, x)
                apart.append(banded(tiles, lane, low, high) - tiles[1])
            square = apart[0] * apart[0] + apart[1] * apart[1] + apart[2] * apart[2]
            close = inverse_of(1.0 + square)
            for x, value in enumerate(apart + [close]):
                envs[pl.ds(x * entries + e, 8), pl.ds(c * LANES, LANES)] = value
            yield
    for c in range(NC):
        at = pl.ds(c * LANES, LANES)
        inputs[at, :] = envs[:, at].T.astype(jnp.bfloat16)
        yield


def network(inputs_ref, weights, out_ref, base, units, chunk=256):
    w0_ref, w1_ref, w2_ref, w3_ref, wo_ref = weights
    desc = w0_ref.shape[1]
    inputs = inputs_ref[...]
    total = None
    for f in range(0, desc, chunk):
        size = min(chunk, desc - f)
        first = jnp.dot(inputs, w0_ref[:, pl.ds(f, size)], preferred_element_type=jnp.float32)
        first = jnp.tanh(first).astype(jnp.bfloat16)
        part = jnp.dot(first, w1_ref[pl.ds(f, size), :], preferred_element_type=jnp.float32)
        total = part if total is None else total + part
        for _ in range(6):
            next(units, None)
    layer = jnp.tanh(total).astype(jnp.bfloat16)
    for ref in (w2_ref, w3_ref):
        layer = jnp.tanh(jnp.dot(layer, ref[...], preferred_element_type=jnp.float32)).astype(
            jnp.bfloat16
        )
    out = lax.dot_general(
        wo_ref[...], layer, (((1,), (1,)), ((), ())), preferred_element_type=jnp.float32
    )
    for c in range(NC):
        for x in range(3):
            out_ref[x, pl.ds(c, 1), pl.ds(base, LANES)] = out[
                x : x + 1, c * LANES : (c + 1) * LANES
            ]


def neural_scratch(env):
    return [
        pltpu.VMEM((2, env, NC * LANES), jnp.float32),
        pltpu.VMEM((2, NC * LANES, env), jnp.bfloat16),
    ]


def neural(contracted, lower, upper, lists, weights):
    _, _, rows = contracted.shape
    tiles = rows // LANES

    def kernel(
        c_ref, low_ref, up_ref, list_ref, w0, w1, w2, w3, wo, out_ref, envs, inputs
    ):
        def tile(x, c, t):
            if t < 0:
                ref, at = low_ref, 0
            elif t >= tiles:
                ref, at = up_ref, 0
            else:
                ref, at = c_ref, t * LANES
            return on_sublanes(ref[x, pl.ds(c, 1), pl.ds(at, LANES)])

        def units_of(t):
            if t >= tiles:
                return iter(())
            windows = lambda c, x: [tile(x, c, t + v) for v in (-1, 0, 1)]
            slot = t % 2
            return env_units(windows, list_ref, t * LANES, envs.at[slot], inputs.at[slot])

        for _ in units_of(0):
            pass
        for t in range(tiles):
            units = units_of(t + 1)
            network(inputs.at[t % 2], (w0, w1, w2, w3, wo), out_ref, t * LANES, units)
            for _ in units:
                pass

    return pl.pallas_call(
        kernel,
        out_shape=jax.ShapeDtypeStruct((3, NC, rows), jnp.float32),
        in_specs=[whole_vmem()] * 9,
        out_specs=whole_vmem(),
        scratch_shapes=neural_scratch(weights[0].shape[0]),
        compiler_params=params(),
        cost_estimate=pl.CostEstimate(
            flops=12_000_000_000, bytes_accessed=4_000_000, transcendentals=0
        ),
        name="neural",
    )(contracted, lower, upper, lists, *weights)


def add_pairs(sums, e, b, apart, close):
    for x in range(3):
        part = apart[x] * close
        sums[x, b] = part if e == 0 else sums[x, b] + part


def total_of(sums, x):
    total = sums[x, :, 0, :]
    for s in range(1, 8):
        total = total + sums[x, :, s, :]
    return total


def assemble(fields):
    groups, _, beads, rows = fields.shape
    atoms = groups * rows
    half = beads // 2
    top = float(2**15 - 1)

    def kernel(in_ref, newq, words, fixed, unit_ref, rims):
        largest = jnp.zeros((beads, rows), jnp.float32)
        for g in range(groups):
            at = pl.ds(g * rows, rows)
            for x in range(3):
                value = in_ref[g, x]
                newq[x, :, at] = value
                largest = jnp.maximum(largest, jnp.abs(value))
        limit = jnp.maximum(jnp.max(largest, keepdims=True), 1e-30)
        to_fixed = top / limit
        unit_ref[...] = jnp.broadcast_to(limit / (top * 65536.0), (beads, LANES))
        for g in range(groups):
            at = pl.ds(g * rows, rows)
            for x in range(3):
                value = jnp.floor(in_ref[g, x] * to_fixed + 0.5)
                fixed[x, :, at] = value * 65536.0
                value = value.astype(jnp.int32)
                words[x, :, at] = (value[:half] << 16) | (value[half:] & 65535)
        for rim, t in enumerate((0, LANES, atoms - 2 * LANES, atoms - LANES)):
            rims[rim] = newq[:, :, pl.ds(t, LANES)]

    return pl.pallas_call(
        kernel,
        out_shape=(
            jax.ShapeDtypeStruct((3, beads, atoms), jnp.float32),
            jax.ShapeDtypeStruct((3, half, atoms), jnp.int32),
            jax.ShapeDtypeStruct((3, beads, atoms), jnp.float32),
            jax.ShapeDtypeStruct((beads, LANES), jnp.float32),
            jax.ShapeDtypeStruct((4, 3, beads, LANES), jnp.float32),
        ),
        in_specs=[whole_vmem()],
        out_specs=(whole_vmem(),) * 5,
        compiler_params=params(),
        name="assemble",
    )(fields)


def pair_part(words, fixed, unit, lists, begin, end, edges=()):
    _, beads, atoms = fixed.shape
    half = beads // 2
    tiles = atoms // LANES
    entries = lists.shape[0]

    def kernel(words_ref, fixed_ref, unit_ref, list_ref, *rest):
        ends = rest[: len(edges)]
        pair, sums = rest[len(edges)], rest[-1]
        unit_row = unit_ref[...]
        unit_square = on_sublanes(unit_ref[pl.ds(0, 1), :])
        unit_square = unit_square * unit_square

        def edge(out, at, base, near_tiles):
            for e in range(0, entries, 8):
                lane, low, high = entries_of(list_ref, e, base)
                for b in range(beads):
                    apart = []
                    for x in range(3):
                        windows = [on_sublanes(tile[x, pl.ds(b, 1), :]) for tile in near_tiles]
                        apart.append(banded(windows, lane, low, high) - windows[1])
                    square = apart[0] * apart[0] + apart[1] * apart[1] + apart[2] * apart[2]
                    add_pairs(sums, e, b, apart, inverse_of(1.0 + square))
            for x in range(3):
                out[x, :, pl.ds(at, LANES)] = PAIR_STRENGTH * total_of(sums, x)

        @pl.loop(max(begin, 1), min(end, tiles - 1))
        def _(t):
            base = pl.multiple_of(t * LANES, LANES)

            def row(ref, x, b, v):
                return on_sublanes(ref[x, pl.ds(b, 1), pl.ds(base + (v - 1) * LANES, LANES)])

            for e in range(0, entries, 8):
                lane, low, high = entries_of(list_ref, e, base)
                for b in range(half):
                    both = [
                        banded([row(words_ref, x, b, v) for v in range(3)], lane, low, high)
                        for x in range(3)
                    ]
                    for bead, near in ((b, [w & -65536 for w in both]),
                                       (b + half, [w << 16 for w in both])):
                        apart = [
                            near[x].astype(jnp.float32) - row(fixed_ref, x, bead, 1)
                            for x in range(3)
                        ]
                        square = apart[0] * apart[0] + apart[1] * apart[1] + apart[2] * apart[2]
                        close = inverse_of(1.0 + square * unit_square)
                        add_pairs(sums, e, bead, apart, close)
            at = pl.ds(pl.multiple_of((t - begin) * LANES, LANES), LANES)
            for x in range(3):
                pair[x, :, at] = (PAIR_STRENGTH * unit_row) * total_of(sums, x)

        if edges:
            rims, lower, upper = ends
            last = (tiles - 1) * LANES
            edge(rest[len(edges) + 1], 0, 0, [lower, rims.at[0], rims.at[1]])
            edge(pair, last - begin * LANES, last, [rims.at[2], rims.at[3], upper])

    out_shape = [jax.ShapeDtypeStruct((3, beads, (end - begin) * LANES), jnp.float32)]
    if edges:
        out_shape.append(jax.ShapeDtypeStruct((3, beads, LANES), jnp.float32))
    return pl.pallas_call(
        kernel,
        out_shape=out_shape,
        in_specs=[whole_vmem()] * (4 + len(edges)),
        out_specs=[whole_vmem()] * len(out_shape),
        scratch_shapes=[pltpu.VMEM((3, beads, 8, LANES), jnp.float32)],
        compiler_params=params(),
        cost_estimate=pl.CostEstimate(
            flops=300_000_000 * (end - begin), bytes_accessed=2_000_000, transcendentals=0
        ),
        name=f"pair_{begin}",
    )(words, fixed, unit, lists, *edges)


def finish(place, pairs, first, fields, neural_parts, partners, coefs):
    groups, _, beads, rows = fields.shape
    atoms = groups * rows
    counts = [part.shape[0] for part in neural_parts]

    def kernel(place_ref, first_ref, coef_ref, in_ref, *rest):
        halves, rest = rest[: len(pairs)], rest[len(pairs) :]
        blocks, (newp, newf, pair, momenta, forces, sems) = rest[: len(counts)], rest[len(counts) :]
        own = place_ref[0]
        at = 0
        for half in halves:
            pair[:, :, pl.ds(at, half.shape[2])] = half[...]
            at += half.shape[2]
        pair[:, :, pl.ds(0, LANES)] = first_ref[...]
        coef = [coef_ref[c, own] for c in range(NC)]
        blocks = [block.at[i] for block, count in zip(blocks, counts) for i in range(count)]
        copies = []
        for slot, (r, block) in enumerate(zip(partners, blocks)):
            g = own ^ r
            for t in range(0, rows, LANES):
                at = pl.ds(pl.multiple_of(g * rows + t, LANES), LANES)
                inner = pl.ds(t, LANES)
                for x in range(3):
                    force = pair[x, :, at]
                    for c in range(NC):
                        force = force + coef[c] * block[x, pl.ds(c, 1), inner]
                    forces[slot, x, :, inner] = force
                    momenta[slot, x, :, inner] = in_ref[g, 3 + x, :, inner] + 0.5 * TIME_STEP * force
            at = block_of(place_ref, r, rows)
            for i, (source, out) in enumerate(((forces, newf), (momenta, newp))):
                copy = pltpu.make_async_copy(
                    source.at[slot], out.at[:, :, at], sems.at[2 * slot + i]
                )
                copy.start()
                copies.append(copy)
        for copy in copies:
            copy.wait()

    out = jax.ShapeDtypeStruct((3, beads, atoms), jnp.float32)
    return pl.pallas_call(
        kernel,
        out_shape=(out,) * 2,
        in_specs=[smem()] + [whole_vmem()] * (3 + len(pairs) + len(neural_parts)),
        out_specs=(pl.BlockSpec(memory_space=pltpu.HBM),) * 2,
        scratch_shapes=[
            pltpu.VMEM((3, beads, atoms), jnp.float32),
            pltpu.VMEM((groups, 3, beads, rows), jnp.float32),
            pltpu.VMEM((groups, 3, beads, rows), jnp.float32),
            pltpu.SemaphoreType.DMA((2 * groups,)),
        ],
        compiler_params=params(),
        name="finish",
    )(place, first, coefs, fields, *pairs, *neural_parts)


def doubling_step(have, partners, axis, bit):
    count = lax.axis_size(axis)
    got = lax.ppermute(have, axis, [(i, i ^ bit) for i in range(count)])
    return got, partners + [r ^ bit for r in partners]


def body(
    positions,
    momenta,
    force_old,
    noise,
    mass,
    pair_list,
    desc_w,
    hidden_one,
    hidden_two,
    hidden_three,
    out_w,
):
    beads, _, atoms = positions.shape
    groups = lax.axis_size("bead")
    slabs = lax.axis_size(("slab", "grp"))
    rows = atoms // groups
    place = lax.axis_index("bead").astype(jnp.int32)[None]
    step, kernel = step_tables()

    swap = lambda field: jnp.transpose(field, (1, 0, 2))
    sends = pack(place, swap(positions), swap(momenta), swap(force_old), swap(noise), groups)
    received = exchange(sends, "bead")

    lists, block_lists, masses, env_w, w1 = prepare(
        pair_list.T, mass[None, :], desc_w.T, hidden_one.T, place, rows
    )
    received, lists, block_lists, masses, env_w, w1 = lax.optimization_barrier(
        (received, lists, block_lists, masses, env_w, w1)
    )
    weights = (env_w, w1, hidden_two, hidden_three, out_w.T)

    contracted, first, last, scaled = contract(place, received, masses, jnp.asarray(step[:NC]))
    ring = [
        (g * slabs + s, ((g + 1) % groups) * slabs + (s + (g + 1) // groups) % slabs)
        for g in range(groups)
        for s in range(slabs)
    ]
    back = [(j, i) for i, j in ring]
    every = ("bead", "slab", "grp")
    lower = lax.ppermute(last, every, ring)
    upper = lax.ppermute(first, every, back)
    returns = transform(scaled, masses, jnp.asarray(step[NC:]))
    returns, lower, upper = lax.optimization_barrier((returns, lower, upper))
    fields = lax.all_to_all(returns, "bead", split_axis=0, concat_axis=0, tiled=True)

    forces = neural(contracted, lower, upper, block_lists, weights)
    bits = [1 << i for i in range(groups.bit_length() - 2, -1, -1)]
    have = forces[None]
    got, partners = doubling_step(have, [0], "bead", bits[0])
    fields, forces = lax.optimization_barrier((fields, forces))

    new_q, words, fixed, unit, rims = assemble(fields)
    slab_ring = [(s, (s + 1) % slabs) for s in range(slabs)]
    slab_back = [(j, i) for i, j in slab_ring]
    q_lower = lax.ppermute(rims[3], ("slab", "grp"), slab_ring)
    q_upper = lax.ppermute(rims[0], ("slab", "grp"), slab_back)

    words, got = lax.optimization_barrier((words, got))
    tiles = atoms // LANES
    cut = 3 * tiles // 8
    for bit in bits[1:2]:
        have = jnp.concatenate([have, got], axis=0)
        got, partners = doubling_step(have, partners, "bead", bit)
    pairs = pair_part(words, fixed, unit, lists, 0, cut)
    words, pairs, got = lax.optimization_barrier((words, pairs, got))
    for bit in bits[2:]:
        have = jnp.concatenate([have, got], axis=0)
        got, partners = doubling_step(have, partners, "bead", bit)
    rest, first = pair_part(
        words, fixed, unit, lists, cut, tiles, (rims, q_lower, q_upper)
    )

    coefs = (kernel * np.float32(BEADS / NC)).reshape(NC, groups, beads, 1)
    coefs = jnp.asarray(np.broadcast_to(coefs, (NC, groups, beads, LANES)))
    new_p, force = finish(
        place, [*pairs, rest], first, fields, (have, got), partners, coefs
    )
    return tuple(swap(out) for out in (new_q, new_p, force))


def solution(mesh):
    field = P("bead", None, ("slab", "grp"))
    placed = (field,) * 4 + (P(("slab", "grp")), P(("slab", "grp"), None)) + (P(),) * 5
    return jax.shard_map(
        body, mesh=mesh, in_specs=placed, out_specs=(field,) * 3, check_vma=False
    )
```
